32 devices in a mesh: seq: 8 (over z, y), dp: 4 (over x, core).
Axes of the slice: x: 2, y: 2, z: 4, core: 2. Of those that a mesh axis runs over, the one named last changes fastest.
Arguments:
- tokens: bfloat16 [4, 8192, 768], P('dp', 'seq'), may hold values from -6 to 6
- input_weight: bfloat16 [768, 2304], P('dp'), may hold values from -0.21875 to 0.21875
- output_weight: bfloat16 [768, 768], P('dp'), may hold values from -0.875 to 0.875
- up_weight: bfloat16 [768, 3072], P('dp'), may hold values from -0.21875 to 0.21875
- down_weight: bfloat16 [3072, 768], P('dp'), may hold values from -0.109375 to 0.109375
- output_bias: bfloat16 [768], P('dp'), may hold values from -3 to 3
- up_bias: bfloat16 [3072], P('dp'), may hold values from -3 to 3
- down_bias: bfloat16 [768], P('dp'), may hold values from -3 to 3
- first_gain: bfloat16 [768], P('dp'), may hold values from 0.099609375 to 1.8984375
- first_shift: bfloat16 [768], P('dp'), may hold values from -2 to 2
- second_gain: bfloat16 [768], P('dp'), may hold values from 0.099609375 to 1.8984375
- second_shift: bfloat16 [768], P('dp'), may hold values from -2 to 2
- document_runs: int32 [4, 8], P('dp'), may hold values from 1 to 16, as said below
- document_trim: int32 [4, 8], P('dp'), may hold values from 0 to 63
- cluster_order: int32 [4, 12, 8192], P('dp'), may hold values from 0 to 8191, as said below
- cotangent: bfloat16 [4, 8192, 768], P('dp', 'seq'), may hold values from -6 to 6
Outputs:
- output: bfloat16 [4, 8192, 768], P('dp', 'seq')
- input_gradient: float32 [4, 8192, 768], P('dp', 'seq')
- input_weight_gradient: float32 [768, 2304], P('dp')
- output_weight_gradient: float32 [768, 768], P('dp')
- up_weight_gradient: float32 [768, 3072], P('dp')
- down_weight_gradient: float32 [3072, 768], P('dp')
- output_bias_gradient: float32 [768], P('dp')
- up_bias_gradient: float32 [3072], P('dp')
- down_bias_gradient: float32 [768], P('dp')
- first_gain_gradient: float32 [768], P('dp')
- first_shift_gradient: float32 [768], P('dp')
- second_gain_gradient: float32 [768], P('dp')
- second_shift_gradient: float32 [768], P('dp')
The draws below stay inside these ranges and needn't reach their ends.
Inputs may be any that keep to these rules, and one draw needn't show every extreme that they name: `document_runs`: each group's row sums to 64, and one document of each group has 16. `cluster_order`: for each group and head a permutation of the 8192 positions that maps the positions of each document onto positions of the same document.
All inputs are finite; a program needn't handle non-finite values.
Results may differ from the reference program's by a relative error of at most 0.018.
Values may be sent and summed in bfloat16 or wider, within the bound.
No kernel may reach another device: no remote copies, remote signals or barrier semaphores. Data moves between devices by JAX's collectives and lax.ppermute only.
A program may use at most 192 MiB of HBM per device.

```python
import jax
import jax.numpy as jnp
from jax import lax

D = 768
FF = 3072
HEADS = 12
HD = 64
CL = 128
GROUP = 8192
DOCS = 8
N_DP = 4


def shared_runs(key):
    first_key, second_key = jax.random.split(key)
    wobble = jax.random.randint(first_key, (N_DP, DOCS), -3, 4)
    peak = jax.random.randint(second_key, (N_DP, 1), 0, DOCS)
    index = jnp.arange(DOCS, dtype=jnp.int32)[None, :]
    after = (peak + 1) % DOCS
    wobble = jnp.where(index == peak, 4, jnp.where(index == after, -4, wobble))
    runs = 8 + wobble - jnp.roll(wobble, -1, axis=1)
    return runs.astype(jnp.int32)


def draw_document_runs(key, part):
    return shared_runs(key)


def draw_cluster_order(key, part):
    runs = shared_runs(key)
    key = jax.random.fold_in(key, 7)
    ends = jnp.cumsum(runs, axis=1) * CL
    positions = jnp.arange(GROUP, dtype=jnp.int32)
    doc_index = jnp.sum((positions[None, :, None] >= ends[:, None, :]).astype(jnp.int32), axis=-1)
    noise = jax.random.randint(key, (N_DP, HEADS, GROUP), 0, 64)
    ranking = (doc_index[:, None, :] * 64 + noise) * GROUP + positions
    return jnp.argsort(ranking, axis=-1).astype(jnp.int32)


def with_ends(values, own_key, smallest, largest):
    dims = values.shape
    index_at = [jax.random.randint(jax.random.fold_in(own_key, axis), (), 0, dims[axis]) for axis in range(len(dims))]
    values = values.at[tuple(index_at)].set(smallest)
    longest = dims.index(max(dims))
    index_at[longest] = (index_at[longest] + 1) % dims[longest]
    return values.at[tuple(index_at)].set(largest)


def shard_levels(own_key, dims, shards, smallest, top_value):
    level = 1.0
    for dim, shards_of in shards:
        steps = jax.random.uniform(jax.random.fold_in(jax.random.fold_in(own_key, 6), dim), (shards_of,), jnp.float32, smallest / len(shards), top_value / len(shards))
        level = level * jnp.repeat(jnp.exp(steps), dims[dim] // shards_of).reshape((-1,) + (1,) * (len(dims) - 1 - dim))
    return level


def centred(stream_key, shape, deviation, limit, shards=(), held_as=jnp.bfloat16):
    array = deviation * jax.random.normal(stream_key, shape, jnp.float32)
    if shards:
        array = array * shard_levels(stream_key, shape, shards, -0.22, 0.18)
    return jnp.clip(array, -limit, limit).astype(held_as)


def setup_inputs(seed: int = 0) -> dict:
    key_of = jax.random.split(jax.random.key(seed), 17)
    tokens = centred(key_of[0], (N_DP, GROUP, D), 1.0, 6.0, ((0, 4), (1, 8)))
    input_weight = centred(key_of[1], (D, 3 * D), D ** -0.5, 0.21875, ((0, 4),))
    output_weight = centred(key_of[2], (D, D), (D // 16) ** -0.5, 0.875, ((0, 4),))
    up_weight = centred(key_of[3], (D, FF), D ** -0.5, 0.21875, ((0, 4),))
    down_weight = centred(key_of[4], (FF, D), FF ** -0.5, 0.109375, ((0, 4),))
    output_bias = centred(key_of[5], (D,), 0.5, 3.0, ((0, 4),))
    up_bias = centred(key_of[6], (FF,), 0.5, 3.0, ((0, 4),))
    down_bias = centred(key_of[7], (D,), 0.5, 3.0, ((0, 4),))
    first_gain = jnp.clip(1.0 + 0.18 * jax.random.normal(key_of[8], (D,), jnp.float32), 0.099609375, 1.8984375).astype(jnp.bfloat16)
    first_shift = centred(key_of[9], (D,), 0.3, 2.0, ((0, 4),))
    second_gain = jnp.clip(1.0 + 0.18 * jax.random.normal(key_of[10], (D,), jnp.float32), 0.099609375, 1.8984375).astype(jnp.bfloat16)
    second_shift = centred(key_of[11], (D,), 0.3, 2.0, ((0, 4),))
    document_runs = draw_document_runs(jax.random.fold_in(key_of[16], 71), 0)
    document_trim = with_ends(jax.random.randint(key_of[13], (N_DP, DOCS), 0, CL // 2), jax.random.fold_in(key_of[13], 1), 0, (CL // 2) - 1).astype(jnp.int32)
    cluster_order = draw_cluster_order(jax.random.fold_in(key_of[16], 71), 0)
    cotangent = centred(key_of[15], (N_DP, GROUP, D), 1.0, 6.0, ((0, 4), (1, 8)))
    return {"tokens": tokens, "input_weight": input_weight, "output_weight": output_weight, "up_weight": up_weight, "down_weight": down_weight, "output_bias": output_bias, "up_bias": up_bias, "down_bias": down_bias, "first_gain": first_gain, "first_shift": first_shift, "second_gain": second_gain, "second_shift": second_shift, "document_runs": document_runs, "document_trim": document_trim, "cluster_order": cluster_order, "cotangent": cotangent}


@jax.custom_vjp
def low(v):
    return lax.optimization_barrier(v.astype(jnp.bfloat16)).astype(jnp.float32)

@jax.custom_vjp
def low_back(v):
    return v

def low_keep(v):
    return (low(v), None)

def low_pass(kept, grad):
    return (grad,)

def back_keep(v):
    return (v, None)

def back_low(kept, grad):
    return (low(grad),)
low.defvjp(low_keep, low_pass)
low_back.defvjp(back_keep, back_low)
EPSILON = 1e-05

def product(left, right):
    return jnp.dot(left, right, precision=lax.Precision.HIGHEST)

def layer_norm(values, gain, shift):
    centre = values - lax.optimization_barrier(jnp.mean(values, axis=-1, keepdims=True))
    spread = lax.optimization_barrier(jnp.mean(centre * centre, axis=-1, keepdims=True))
    return centre * lax.rsqrt(spread + EPSILON) * gain + shift

def live_tokens(runs, trim, positions):
    ends = jnp.cumsum(runs) * CL
    starts = ends - runs * CL
    lengths = runs * CL - trim
    inside = (positions[..., None] >= starts) & (positions[..., None] < starts + lengths)
    return jnp.any(inside, axis=-1).astype(jnp.float32)

def head_attend(queries, key_rows, values, live_mask):
    query_blocks = queries.reshape(-1, CL, HD)
    key_blocks = key_rows.reshape(-1, CL, HD)
    value_blocks = values.reshape(-1, CL, HD)
    scores = jnp.einsum('cqd,ckd->cqk', query_blocks, key_blocks, precision=lax.Precision.HIGHEST) * HD ** (-0.5)
    scores = jnp.where(live_mask.reshape(-1, 1, CL) > 0.5, scores, -1e+30)
    row_top = lax.optimization_barrier(jnp.max(scores, axis=-1, keepdims=True))
    weights = jnp.exp(scores - row_top)
    probs_rounded = low(weights / lax.optimization_barrier(jnp.sum(weights, axis=-1, keepdims=True)))
    result = jnp.einsum('cqk,ckd->cqd', probs_rounded, value_blocks, precision=lax.Precision.HIGHEST)
    return (result * live_mask.reshape(-1, CL, 1)).reshape(-1, HD)

def group_attend(projected, group_order, live_mask):
    parts = projected.reshape(GROUP, 3, HEADS, HD).transpose(2, 1, 0, 3)
    clustered = jnp.take_along_axis(parts, group_order[:, None, :, None], axis=2)
    live_rows = live_mask[group_order]
    attend = jax.checkpoint(head_attend)
    results = lax.map(lambda packed: attend(*packed), (clustered[:, 0], clustered[:, 1], clustered[:, 2], live_rows))
    results = low_back(low(results))
    head_index = jnp.arange(HEADS, dtype=jnp.int32)[:, None]
    placed = jnp.zeros((HEADS, GROUP, HD), results.dtype).at[head_index, group_order].set(results)
    return placed.transpose(1, 0, 2).reshape(GROUP, D)

def forward(tokens, input_weight, output_weight, up_weight, down_weight, output_bias, up_bias, down_bias, first_gain, first_shift, second_gain, second_shift, cluster_order, live_mask):
    flat = tokens.reshape(-1, D)
    projected = low_back(low(product(flat, input_weight))).reshape(N_DP, GROUP, 3 * D)
    attended = lax.map(lambda packed: group_attend(*packed), (projected, cluster_order, live_mask)).reshape(-1, D)
    mixed = low_back(product(attended, output_weight)) + output_bias + flat
    hidden = layer_norm(mixed, first_gain, first_shift)
    up_sum = low_back(product(low(hidden), up_weight)) + up_bias
    active = low(jax.nn.gelu(up_sum, approximate=False))
    down_sum = low_back(product(active, down_weight)) + down_bias
    return layer_norm(down_sum + hidden, second_gain, second_shift).reshape(N_DP, GROUP, D)

def reference(tokens, input_weight, output_weight, up_weight, down_weight, output_bias, up_bias, down_bias, first_gain, first_shift, second_gain, second_shift, document_runs, document_trim, cluster_order, cotangent):
    positions = jnp.arange(GROUP, dtype=jnp.int32)
    live_mask = jax.vmap(lambda runs, trim: live_tokens(runs, trim, positions))(document_runs, document_trim)
    floats = [source.astype(jnp.float32) for source in (tokens, input_weight, output_weight, up_weight, down_weight, output_bias, up_bias, down_bias, first_gain, first_shift, second_gain, second_shift)]

    def run(*params):
        return forward(*params, cluster_order, live_mask)
    result, pullback = jax.vjp(run, *floats)
    gradients = pullback(cotangent.astype(jnp.float32))
    return (result.astype(jnp.bfloat16), gradients[0], gradients[1], gradients[2], gradients[3], gradients[4], gradients[5], gradients[6], gradients[7], gradients[8], gradients[9], gradients[10], gradients[11])
```

```python
import functools

import jax
import jax.numpy as jnp
from jax import lax
from jax.experimental import pallas as pl
from jax.experimental.pallas import tpu as pltpu
from jax.sharding import PartitionSpec as P

D = 768
HEADS = 12
HD = 64
CL = 128
MOSTB = 16
PAIRS = HEADS // 2
WINDOW = MOSTB * CL
HALO = (MOSTB - 1) * CL
CHUNK = 512
NEG = -1e30
SCALE2 = HD ** (-0.5) * 1.4426950408889634

EPSILON = 1e-05


def shifted(value, axis, by):
    devices = lax.axis_size(axis)
    pairs = [(i, i + by) for i in range(devices) if 0 <= i + by < devices]
    return lax.ppermute(value, axis, pairs)


def halo_rows(value, axis, row_axis):
    own = value.shape[row_axis]
    parts = [value]
    left = HALO
    distance = 1
    while left > 0:
        take = min(own, left)
        before = shifted(lax.slice_in_dim(value, own - take, own, axis=row_axis), axis, distance)
        after = shifted(lax.slice_in_dim(value, 0, take, axis=row_axis), axis, -distance)
        parts = [before] + parts + [after]
        left -= take
        distance += 1
    return jnp.concatenate(parts, axis=row_axis)


def layer_norm(values, gain, shift):
    centre = values - jnp.mean(values, axis=-1, keepdims=True)
    spread = jnp.mean(centre * centre, axis=-1, keepdims=True)
    return centre * lax.rsqrt(spread + EPSILON) * gain + shift


def gelu_exact(values):
    return jax.nn.gelu(values, approximate=False)


def live_tokens(runs, trim, positions):
    ends = jnp.cumsum(runs) * CL
    starts = ends - runs * CL
    lengths = runs * CL - trim
    inside = (positions[..., None] >= starts) & (positions[..., None] < starts + lengths)
    return jnp.any(inside, axis=-1)


def outer_sum(left, right):
    return lax.dot_general(
        left, right, (((0,), (0,)), ((), ())), preferred_element_type=jnp.float32
    )


def back_product(left, right):
    return lax.dot_general(
        left, right, (((1,), (1,)), ((), ())), preferred_element_type=jnp.float32
    )


def plain_product(left, right):
    return jnp.dot(left, right, preferred_element_type=jnp.float32)


def stacked(tile):
    lane = lax.broadcasted_iota(jnp.int32, tile.shape, 1)
    zero = jnp.zeros_like(tile)
    return jnp.concatenate(
        [jnp.where(lane < HD, tile, zero), jnp.where(lane < HD, zero, tile)], axis=0
    )


def unstacked(both):
    lane = lax.broadcasted_iota(jnp.int32, (CL, 2 * HD), 1)
    return jnp.where(lane < HD, both[:CL], both[CL:])


def as_column(row):
    return jnp.broadcast_to(row, (CL, CL)).T


def as_row(column):
    return jnp.broadcast_to(column, (CL, CL)).T[0:1]


def masked(scores, col_pair, row_ref, begin):
    parts = []
    for half in range(2):
        row = row_ref[0, half : half + 1, pl.ds(begin, CHUNK)]
        block = scores[half * CL : (half + 1) * CL]
        col = jnp.concatenate([col_pair[half]] * (CHUNK // CL), axis=1)
        parts.append(jnp.where(col == row, block, NEG))
    return jnp.concatenate(parts, axis=0)


def attend_kernel(tiles, starts, q_ref, k_ref, v_ref, qid_ref, kid_ref, out_ref, lse_ref, s_ref):
    def one_tile(tile, carry):
        begin = pl.multiple_of(starts[tile] * CL, CL)
        own = pl.multiple_of(HALO + tile * CL, CL)
        here = pl.multiple_of(tile * CL, CL)
        query = stacked(q_ref[pl.ds(own, CL), :])
        cols = [as_column(qid_ref[0, half : half + 1, pl.ds(own, CL)]) for half in range(2)]
        top = jnp.full((2 * CL, CL), NEG, jnp.float32)
        for j in range(WINDOW // CHUNK):
            at = pl.multiple_of(begin + j * CHUNK, CL)
            scores = masked(
                back_product(query, k_ref[pl.ds(at, CHUNK), :]), cols, kid_ref, at
            )
            s_ref[:, j * CHUNK : (j + 1) * CHUNK] = scores
            for i in range(CHUNK // CL):
                top = jnp.maximum(top, scores[:, i * CL : (i + 1) * CL])
        peak = jnp.max(top, axis=1, keepdims=True)
        total = jnp.zeros((2 * CL, CL), jnp.float32)
        result = jnp.zeros((2 * CL, 2 * HD), jnp.float32)
        for j in range(WINDOW // CHUNK):
            at = pl.multiple_of(begin + j * CHUNK, CL)
            weights = jnp.exp2((s_ref[:, j * CHUNK : (j + 1) * CHUNK] - peak) * SCALE2)
            for i in range(CHUNK // CL):
                total = total + weights[:, i * CL : (i + 1) * CL]
            result = result + plain_product(
                weights.astype(jnp.bfloat16), v_ref[pl.ds(at, CHUNK), :]
            )
        total = jnp.sum(total, axis=1, keepdims=True)
        result = result / total
        lse = peak * SCALE2 + jnp.log2(total)
        live = [(col >= 0.0).astype(jnp.float32) for col in cols]
        result = result * jnp.concatenate(live, axis=0)
        out_ref[pl.ds(here, CL), :] = unstacked(result).astype(jnp.bfloat16)
        for half in range(2):
            lse_ref[0, half : half + 1, pl.ds(here, CL)] = as_row(lse[half * CL : (half + 1) * CL])
        return carry

    lax.fori_loop(0, tiles, one_tile, 0)


def query_kernel(
    tiles, starts, q_ref, k_ref, v_ref, g_ref, qid_ref, kid_ref, lse_ref, delta_ref, out_ref
):
    def one_tile(tile, carry):
        begin = pl.multiple_of(starts[tile] * CL, CL)
        own = pl.multiple_of(HALO + tile * CL, CL)
        here = pl.multiple_of(tile * CL, CL)
        query = stacked(q_ref[pl.ds(own, CL), :])
        back = stacked(g_ref[pl.ds(here, CL), :])
        cols = [as_column(qid_ref[0, half : half + 1, pl.ds(own, CL)]) for half in range(2)]
        lse = jnp.concatenate(
            [as_column(lse_ref[0, half : half + 1, pl.ds(here, CL)]) for half in range(2)], axis=0
        )
        delta = jnp.concatenate(
            [as_column(delta_ref[0, half : half + 1, pl.ds(here, CL)]) for half in range(2)], axis=0
        )
        lse = jnp.concatenate([lse] * (CHUNK // CL), axis=1)
        delta = jnp.concatenate([delta] * (CHUNK // CL), axis=1)
        result = jnp.zeros((2 * CL, 2 * HD), jnp.float32)
        for j in range(WINDOW // CHUNK):
            at = pl.multiple_of(begin + j * CHUNK, CL)
            keys = k_ref[pl.ds(at, CHUNK), :]
            scores = masked(back_product(query, keys) * SCALE2, cols, kid_ref, at)
            probs = jnp.exp2(scores - lse)
            back_probs = back_product(back, v_ref[pl.ds(at, CHUNK), :])
            back_scores = probs * (back_probs - delta)
            result = result + plain_product(back_scores.astype(jnp.bfloat16), keys)
        out_ref[pl.ds(here, CL), :] = (unstacked(result) * HD ** (-0.5)).astype(jnp.bfloat16)
        return carry

    lax.fori_loop(0, tiles, one_tile, 0)


def key_kernel(
    tiles,
    starts,
    q_ref,
    k_ref,
    v_ref,
    g_ref,
    qid_ref,
    kid_ref,
    lse_ref,
    delta_ref,
    key_out_ref,
    value_out_ref,
):
    def one_tile(tile, carry):
        begin = pl.multiple_of(starts[tile] * CL, CL)
        own = pl.multiple_of(HALO + tile * CL, CL)
        here = pl.multiple_of(tile * CL, CL)
        keys = stacked(k_ref[pl.ds(own, CL), :])
        values = stacked(v_ref[pl.ds(own, CL), :])
        cols = [as_column(kid_ref[0, half : half + 1, pl.ds(own, CL)]) for half in range(2)]
        key_sum = jnp.zeros((2 * CL, 2 * HD), jnp.float32)
        value_sum = jnp.zeros((2 * CL, 2 * HD), jnp.float32)
        for j in range(WINDOW // CHUNK):
            at = pl.multiple_of(begin + j * CHUNK, CL)
            queries = q_ref[pl.ds(at, CHUNK), :]
            back = g_ref[pl.ds(at, CHUNK), :]
            scores = masked(back_product(keys, queries) * SCALE2, cols, qid_ref, at)
            lse = [lse_ref[0, half : half + 1, pl.ds(at, CHUNK)] for half in range(2)]
            delta = [delta_ref[0, half : half + 1, pl.ds(at, CHUNK)] for half in range(2)]
            back_probs = back_product(values, back)
            probs, back_scores = [], []
            for half in range(2):
                rows = slice(half * CL, (half + 1) * CL)
                prob = jnp.exp2(scores[rows] - lse[half])
                probs.append(prob.astype(jnp.bfloat16))
                back_scores.append((prob * (back_probs[rows] - delta[half])).astype(jnp.bfloat16))
            value_sum = value_sum + plain_product(jnp.concatenate(probs, axis=0), back)
            key_sum = key_sum + plain_product(jnp.concatenate(back_scores, axis=0), queries)
        key_out_ref[pl.ds(here, CL), :] = (unstacked(key_sum) * HD ** (-0.5)).astype(jnp.bfloat16)
        value_out_ref[pl.ds(here, CL), :] = unstacked(value_sum).astype(jnp.bfloat16)
        return carry

    lax.fori_loop(0, tiles, one_tile, 0)


def lane_block(rows, first):
    return pl.BlockSpec((rows, 2 * HD), lambda pair, starts: (0, first + pair))


def row_block(columns):
    return pl.BlockSpec((1, 2, columns), lambda pair, starts: (pair, 0, 0))


VMEM_LIMIT = 56 * 1024 * 1024


def strip_call(kernel, tiles, in_specs, out_specs, out_shape, scratch, args):
    return pl.pallas_call(
        functools.partial(kernel, tiles),
        out_shape=out_shape,
        grid_spec=pltpu.PrefetchScalarGridSpec(
            num_scalar_prefetch=1,
            grid=(PAIRS,),
            in_specs=in_specs,
            out_specs=out_specs,
            scratch_shapes=scratch,
        ),
        compiler_params=pltpu.CompilerParams(vmem_limit_bytes=VMEM_LIMIT),
    )(*args)


def cluster_ids(group_order, own_start, span):
    padded = jnp.pad(group_order, ((0, 0), (HALO, HALO)), constant_values=-(1 << 24))
    wanted = lax.dynamic_slice_in_dim(padded, own_start, span, 1) - (own_start - HALO)
    tile_of = wanted >> 7
    lane_of = wanted & (CL - 1)
    cluster = (jnp.arange(span, dtype=jnp.int32) >> 7) + 1
    tile_hot = jnp.where(
        tile_of[:, :, None] == jnp.arange(span // CL, dtype=jnp.int32), cluster[None, :, None], 0
    ).astype(jnp.bfloat16)
    lane_hot = (lane_of[:, :, None] == jnp.arange(CL, dtype=jnp.int32)).astype(jnp.bfloat16)
    table = jnp.einsum("hpt,hpl->htl", tile_hot, lane_hot, preferred_element_type=jnp.float32)
    return table.reshape(HEADS, span) - 1.0


def on_device(
    tokens,
    input_weight,
    output_weight,
    up_weight,
    down_weight,
    output_bias,
    up_bias,
    down_bias,
    first_gain,
    first_shift,
    second_gain,
    second_shift,
    document_runs,
    document_trim,
    cluster_order,
    cotangent,
):
    gathered = [
        lax.all_gather(member, "dp", axis=0, tiled=True)
        for member in (
            input_weight,
            output_weight,
            up_weight,
            down_weight,
            output_bias,
            up_bias,
            down_bias,
            first_gain,
            first_shift,
            second_gain,
            second_shift,
        )
    ]
    weight_in, weight_mix, weight_up, weight_down = gathered[:4]
    bias_mix, bias_up, bias_down, gain_one, shift_one, gain_two, shift_two = [
        member.astype(jnp.float32) for member in gathered[4:]
    ]
    inputs = tokens[0]
    tok_dev = inputs.shape[0]
    tiles = tok_dev // CL
    span = tok_dev + 2 * HALO
    seq_rank = lax.axis_index("seq")
    own_start = seq_rank * tok_dev

    runs = document_runs[0]
    first_cluster = jnp.cumsum(runs) - runs
    own_clusters = seq_rank * tiles + jnp.arange(tiles, dtype=jnp.int32)
    doc_start = jnp.max(
        jnp.where(first_cluster[None, :] <= own_clusters[:, None], first_cluster[None, :], 0), axis=1
    )
    starts = (doc_start - seq_rank * tiles + (MOSTB - 1)).astype(jnp.int32)

    cids = cluster_ids(cluster_order[0], own_start, span)
    positions = own_start - HALO + jnp.arange(span, dtype=jnp.int32)
    live = live_tokens(runs, document_trim[0], positions)
    usable = live[None, :] & (cids >= 0.0)
    key_ids = jnp.where(usable, cids, -1.0).reshape(PAIRS, 2, span)
    query_ids = jnp.where(usable, cids, -2.0).reshape(PAIRS, 2, span)
    own_live = live[HALO : HALO + tok_dev, None].astype(jnp.float32)

    window_tokens = halo_rows(inputs, "seq", 0)
    projected = plain_product(window_tokens, weight_in).astype(jnp.bfloat16)

    full = [lane_block(span, i * PAIRS) for i in range(3)]
    attended, lse = strip_call(
        attend_kernel,
        tiles,
        full + [row_block(span), row_block(span)],
        [lane_block(tok_dev, 0), row_block(tok_dev)],
        [
            jax.ShapeDtypeStruct((tok_dev, D), jnp.bfloat16),
            jax.ShapeDtypeStruct((PAIRS, 2, tok_dev), jnp.float32),
        ],
        [pltpu.VMEM((2 * CL, WINDOW), jnp.float32)],
        (starts, projected, projected, projected, query_ids, key_ids),
    )

    mixed = plain_product(attended, weight_mix) + bias_mix + inputs.astype(jnp.float32)
    hidden, first_back = jax.vjp(layer_norm, mixed, gain_one, shift_one)
    hidden_rounded = hidden.astype(jnp.bfloat16)
    up_sum = plain_product(hidden_rounded, weight_up) + bias_up
    active_full, gelu_back = jax.vjp(gelu_exact, up_sum)
    active = active_full.astype(jnp.bfloat16)
    down_sum = plain_product(active, weight_down) + bias_down
    result, second_back = jax.vjp(layer_norm, down_sum + hidden, gain_two, shift_two)
    back_pre, grad_gain_two, grad_shift_two = second_back(cotangent[0].astype(jnp.float32))
    pre_rounded = back_pre.astype(jnp.bfloat16)
    grad_down = outer_sum(active, pre_rounded)
    grad_bias_down = jnp.sum(back_pre, axis=0)
    (back_up,) = gelu_back(back_product(pre_rounded, weight_down))
    up_rounded = back_up.astype(jnp.bfloat16)
    grad_up = outer_sum(hidden_rounded, up_rounded)
    grad_bias_up = jnp.sum(back_up, axis=0)
    back_hidden = back_pre + back_product(up_rounded, weight_up)
    back_mixed, grad_gain_one, grad_shift_one = first_back(back_hidden)
    mixed_rounded = back_mixed.astype(jnp.bfloat16)
    grad_mix = outer_sum(attended, mixed_rounded)
    grad_bias_mix = jnp.sum(back_mixed, axis=0)
    back_attended = back_product(mixed_rounded, weight_mix).astype(jnp.bfloat16)
    back_masked = (back_attended * own_live).astype(jnp.bfloat16)

    delta_terms = back_masked.astype(jnp.float32) * attended.astype(jnp.float32)
    delta = jnp.sum(delta_terms.reshape(tok_dev, HEADS, HD), axis=-1).T.reshape(PAIRS, 2, tok_dev)

    window_back = halo_rows(back_masked, "seq", 0)
    window_rows = halo_rows(
        jnp.concatenate([lse.reshape(HEADS, tok_dev), delta.reshape(HEADS, tok_dev)], 0), "seq", 1
    )
    window_lse = window_rows[:HEADS].reshape(PAIRS, 2, span)
    window_delta = window_rows[HEADS:].reshape(PAIRS, 2, span)

    back_queries = strip_call(
        query_kernel,
        tiles,
        full
        + [
            lane_block(tok_dev, 0),
            row_block(span),
            row_block(span),
            row_block(tok_dev),
            row_block(tok_dev),
        ],
        lane_block(tok_dev, 0),
        jax.ShapeDtypeStruct((tok_dev, D), jnp.bfloat16),
        [],
        (starts, projected, projected, projected, back_masked, query_ids, key_ids, lse, delta),
    )
    back_keys, back_values = strip_call(
        key_kernel,
        tiles,
        full
        + [
            lane_block(span, 0),
            row_block(span),
            row_block(span),
            row_block(span),
            row_block(span),
        ],
        [lane_block(tok_dev, 0), lane_block(tok_dev, 0)],
        [jax.ShapeDtypeStruct((tok_dev, D), jnp.bfloat16)] * 2,
        [],
        (
            starts,
            projected,
            projected,
            projected,
            window_back,
            query_ids,
            key_ids,
            window_lse,
            window_delta,
        ),
    )
    back_projected = jnp.concatenate([back_queries, back_keys, back_values], axis=1)
    grad_in = outer_sum(inputs, back_projected)
    input_grad = back_mixed + back_product(back_projected, weight_in)

    totals = []
    for grad in (
        grad_in,
        grad_mix,
        grad_up,
        grad_down,
        grad_bias_mix,
        grad_bias_up,
        grad_bias_down,
        grad_gain_one,
        grad_shift_one,
        grad_gain_two,
        grad_shift_two,
    ):
        share = lax.psum_scatter(
            grad.astype(jnp.bfloat16), "dp", scatter_dimension=0, tiled=True
        )
        totals.append(lax.psum(share, "seq").astype(jnp.float32))
    return (result.astype(jnp.bfloat16)[None], input_grad[None], *totals)


def solution(mesh):
    placed = (
        P("dp", "seq", None),
        P("dp", None),
        P("dp", None),
        P("dp", None),
        P("dp", None),
        P("dp"),
        P("dp"),
        P("dp"),
        P("dp"),
        P("dp"),
        P("dp"),
        P("dp"),
        P("dp", None),
        P("dp", None),
        P("dp", None, None),
        P("dp", "seq", None),
    )
    return jax.shard_map(
        on_device,
        mesh=mesh,
        in_specs=placed,
        out_specs=(
            P("dp", "seq", None),
            P("dp", "seq", None),
            P("dp", None),
            P("dp", None),
            P("dp", None),
            P("dp", None),
            P("dp"),
            P("dp"),
            P("dp"),
            P("dp"),
            P("dp"),
            P("dp"),
            P("dp"),
        ),
        check_vma=False,
    )
```

```python
import functools

import jax
import jax.numpy as jnp
from jax import lax
from jax.experimental import pallas as pl
from jax.experimental.pallas import tpu as pltpu
from jax.sharding import PartitionSpec as P

D = 768
HEADS = 12
HD = 64
CL = 128
MOSTB = 16
PAIRS = HEADS // 2
WINDOW = MOSTB * CL
HALO = (MOSTB - 1) * CL
CHUNK = 512
NEG = -1e30
TERMS = 5
FF = 3072
RTILE = 256
FCHUNK = 768
SCALE2 = HD ** (-0.5) * 1.4426950408889634

EPSILON = 1e-05


def shifted(value, axis, by):
    devices = lax.axis_size(axis)
    pairs = [(i, i + by) for i in range(devices) if 0 <= i + by < devices]
    return lax.ppermute(value, axis, pairs)


def halo_parts(value):
    own = value.shape[0]
    parts = [value]
    left = HALO
    distance = 1
    while left > 0:
        take = min(own, left)
        before = shifted(value[own - take :], "seq", distance)
        after = shifted(value[:take], "seq", -distance)
        parts = [before] + parts + [after]
        left -= take
        distance += 1
    return parts


def live_tokens(runs, trim, positions):
    ends = jnp.cumsum(runs) * CL
    starts = ends - runs * CL
    lengths = runs * CL - trim
    inside = (positions[..., None] >= starts) & (positions[..., None] < starts + lengths)
    return jnp.any(inside, axis=-1)


def outer_sum(left, right):
    return lax.dot_general(
        left, right, (((0,), (0,)), ((), ())), preferred_element_type=jnp.float32
    )


def back_product(left, right):
    return lax.dot_general(
        left, right, (((1,), (1,)), ((), ())), preferred_element_type=jnp.float32
    )


def plain_product(left, right):
    return jnp.dot(left, right, preferred_element_type=jnp.float32)


def stacked(tile):
    lane = lax.broadcasted_iota(jnp.int32, tile.shape, 1)
    zero = jnp.zeros_like(tile)
    return jnp.concatenate(
        [jnp.where(lane < HD, tile, zero), jnp.where(lane < HD, zero, tile)], axis=0
    )


def unstacked(both):
    lane = lax.broadcasted_iota(jnp.int32, (CL, 2 * HD), 1)
    return jnp.where(lane < HD, both[:CL], both[CL:])


def as_column(row):
    return jnp.broadcast_to(row, (CL, CL)).T


def lane_of(tile, lane):
    lanes = lax.broadcasted_iota(jnp.int32, tile.shape, 1)
    return jnp.sum(jnp.where(lanes == lane, tile, 0.0), axis=1, keepdims=True)


def masked(scores, col_pair, row_ref, begin):
    parts = []
    for half in range(2):
        row = row_ref[0, half : half + 1, pl.ds(begin, CHUNK)]
        block = scores[half * CL : (half + 1) * CL]
        col = jnp.concatenate([col_pair[half]] * (CHUNK // CL), axis=1)
        parts.append(jnp.where(col == row, block, NEG))
    return jnp.concatenate(parts, axis=0)


def assemble(parts, whole):
    at = 0
    for part in parts:
        rows = part.shape[0]
        whole[at : at + rows, :] = part[...]
        at += rows


def attend_kernel(tiles, n_parts, starts, q_ref, *refs):
    k_parts, refs = refs[:n_parts], refs[n_parts:]
    v_parts, refs = refs[:n_parts], refs[n_parts:]
    qid_ref, kid_ref, out_ref, lse_ref, k_ref, v_ref, s_ref = refs
    pair = pl.program_id(0)
    assemble(k_parts, k_ref)
    assemble(v_parts, v_ref)

    def one_tile(tile, carry):
        begin = pl.multiple_of(starts[tile] * CL, CL)
        own = pl.multiple_of(HALO + tile * CL, CL)
        here = pl.multiple_of(tile * CL, CL)
        query = stacked(q_ref[pl.ds(here, CL), :])
        cols = [as_column(qid_ref[0, half : half + 1, pl.ds(own, CL)]) for half in range(2)]
        top = jnp.full((2 * CL, CL), NEG, jnp.float32)
        for j in range(WINDOW // CHUNK):
            at = pl.multiple_of(begin + j * CHUNK, CL)
            scores = masked(
                back_product(query, k_ref[pl.ds(at, CHUNK), :]), cols, kid_ref, at
            )
            s_ref[:, j * CHUNK : (j + 1) * CHUNK] = scores
            for i in range(CHUNK // CL):
                top = jnp.maximum(top, scores[:, i * CL : (i + 1) * CL])
        peak = jnp.max(top, axis=1, keepdims=True)
        total = jnp.zeros((2 * CL, CL), jnp.float32)
        result = jnp.zeros((2 * CL, 2 * HD), jnp.float32)
        for j in range(WINDOW // CHUNK):
            at = pl.multiple_of(begin + j * CHUNK, CL)
            weights = jnp.exp2((s_ref[:, j * CHUNK : (j + 1) * CHUNK] - peak) * SCALE2)
            for i in range(CHUNK // CL):
                total = total + weights[:, i * CL : (i + 1) * CL]
            result = result + plain_product(
                weights.astype(jnp.bfloat16), v_ref[pl.ds(at, CHUNK), :]
            )
        total = jnp.sum(total, axis=1, keepdims=True)
        result = result / total
        lse = peak + jnp.log(total) * HD**0.5
        live = [(col >= 0.0).astype(jnp.float32) for col in cols]
        result = result * jnp.concatenate(live, axis=0)
        out_ref[pl.ds(here, CL), :] = unstacked(result).astype(jnp.bfloat16)
        lane = lax.broadcasted_iota(jnp.int32, (CL, CL), 1)
        kept = lse_ref[pl.ds(here, CL), :]
        for half in range(2):
            first = (2 * pair + half) * TERMS
            kept = jnp.where(
                (lane >= first) & (lane < first + TERMS), lse[half * CL : (half + 1) * CL], kept
            )
        lse_ref[pl.ds(here, CL), :] = kept
        return carry

    @pl.when(pair == 0)
    def _():
        lse_ref[...] = jnp.zeros_like(lse_ref)

    lax.fori_loop(0, tiles, one_tile, 0)


def query_kernel(tiles, n_parts, first_pair, starts, q_ref, *refs):
    k_parts, refs = refs[:n_parts], refs[n_parts:]
    v_parts, refs = refs[:n_parts], refs[n_parts:]
    g_ref, qid_ref, kid_ref, lse_ref, delta_ref, out_ref, k_ref, v_ref = refs
    pair = first_pair + pl.program_id(0)
    assemble(k_parts, k_ref)
    assemble(v_parts, v_ref)

    def one_tile(tile, carry):
        begin = pl.multiple_of(starts[tile] * CL, CL)
        own = pl.multiple_of(HALO + tile * CL, CL)
        here = pl.multiple_of(tile * CL, CL)
        query = stacked(q_ref[pl.ds(here, CL), :])
        back = stacked(g_ref[pl.ds(here, CL), :])
        cols = [as_column(qid_ref[0, half : half + 1, pl.ds(own, CL)]) for half in range(2)]
        lse_tile = lse_ref[pl.ds(here, CL), :]
        delta_tile = delta_ref[pl.ds(here, CL), :]
        lse = jnp.concatenate(
            [lane_of(lse_tile, (2 * pair + half) * TERMS) for half in range(2)], axis=0
        )
        delta = jnp.concatenate(
            [lane_of(delta_tile, (2 * pair + half) * TERMS) for half in range(2)], axis=0
        )
        result = jnp.zeros((2 * CL, 2 * HD), jnp.float32)
        for j in range(WINDOW // CHUNK):
            at = pl.multiple_of(begin + j * CHUNK, CL)
            keys = k_ref[pl.ds(at, CHUNK), :]
            scores = masked((back_product(query, keys) - lse) * SCALE2, cols, kid_ref, at)
            probs = jnp.exp2(scores)
            back_probs = back_product(back, v_ref[pl.ds(at, CHUNK), :])
            back_scores = probs * (back_probs - delta)
            result = result + plain_product(back_scores.astype(jnp.bfloat16), keys)
        out_ref[pl.ds(here, CL), :] = (unstacked(result) * HD ** (-0.5)).astype(jnp.bfloat16)
        return carry

    lax.fori_loop(0, tiles, one_tile, 0)


def key_kernel(tiles, n_parts, first_pair, starts, k_ref, v_ref, *refs):
    q_parts, refs = refs[:n_parts], refs[n_parts:]
    g_parts, refs = refs[:n_parts], refs[n_parts:]
    a_parts, refs = refs[:n_parts], refs[n_parts:]
    qid_ref, kid_ref, key_out_ref, value_out_ref, q_ref, g_ref = refs
    pair = first_pair + pl.program_id(0)
    at = 0
    for q_part, g_part, a_part in zip(q_parts, g_parts, a_parts):
        rows = q_part.shape[0]
        q_ref[at : at + rows, : 2 * HD] = q_part[...]
        q_ref[at : at + rows, 2 * HD :] = a_part[...]
        g_ref[at : at + rows, : 2 * HD] = g_part[...]
        g_ref[at : at + rows, 2 * HD :] = a_part[...]
        at += rows

    lane = lax.broadcasted_iota(jnp.int32, (CL, CL), 1)
    lse_pick, delta_pick = [], []
    for half in range(2):
        first = (2 * pair + half) * TERMS
        lse_pick.append(jnp.where((lane >= first) & (lane < first + 3), -1.0, 0.0))
        delta_pick.append(jnp.where((lane >= first + 3) & (lane < first + TERMS), -1.0, 0.0))
    lse_pick = jnp.concatenate(lse_pick, axis=0).astype(jnp.bfloat16)
    delta_pick = jnp.concatenate(delta_pick, axis=0).astype(jnp.bfloat16)

    def one_tile(tile, carry):
        begin = pl.multiple_of(starts[tile] * CL, CL)
        own = pl.multiple_of(HALO + tile * CL, CL)
        here = pl.multiple_of(tile * CL, CL)
        keys = jnp.concatenate([stacked(k_ref[pl.ds(here, CL), :]), lse_pick], axis=1)
        values = jnp.concatenate([stacked(v_ref[pl.ds(here, CL), :]), delta_pick], axis=1)
        cols = [as_column(kid_ref[0, half : half + 1, pl.ds(own, CL)]) for half in range(2)]
        key_sum = jnp.zeros((2 * CL, 2 * HD), jnp.float32)
        value_sum = jnp.zeros((2 * CL, 2 * HD), jnp.float32)
        for j in range(WINDOW // CHUNK):
            at = pl.multiple_of(begin + j * CHUNK, CL)
            queries = q_ref[pl.ds(at, CHUNK), :]
            back = g_ref[pl.ds(at, CHUNK), :]
            scores = masked(back_product(keys, queries) * SCALE2, cols, qid_ref, at)
            probs = jnp.exp2(scores)
            back_scores = probs * back_product(values, back)
            value_sum = value_sum + plain_product(probs.astype(jnp.bfloat16), back[:, : 2 * HD])
            key_sum = key_sum + plain_product(
                back_scores.astype(jnp.bfloat16), queries[:, : 2 * HD]
            )
        key_out_ref[pl.ds(here, CL), :] = (unstacked(key_sum) * HD ** (-0.5)).astype(jnp.bfloat16)
        value_out_ref[pl.ds(here, CL), :] = unstacked(value_sum).astype(jnp.bfloat16)
        return carry

    lax.fori_loop(0, tiles, one_tile, 0)


def lane_block(rows, first):
    return pl.BlockSpec((rows, 2 * HD), lambda pair, starts: (0, first + pair))


def fixed_lanes(rows, block):
    return pl.BlockSpec((rows, 2 * HD), lambda pair, starts: (0, block))


def row_block(columns, first):
    return pl.BlockSpec((1, 2, columns), lambda pair, starts: (first + pair, 0, 0))


VMEM_LIMIT = 60 * 1024 * 1024


def strip_call(kernel, pairs, in_specs, out_specs, out_shape, scratch, args):
    return pl.pallas_call(
        kernel,
        out_shape=out_shape,
        grid_spec=pltpu.PrefetchScalarGridSpec(
            num_scalar_prefetch=1,
            grid=(pairs,),
            in_specs=in_specs,
            out_specs=out_specs,
            scratch_shapes=scratch,
        ),
        compiler_params=pltpu.CompilerParams(vmem_limit_bytes=VMEM_LIMIT),
    )(*args)


def gelu_terms(value):
    t = 1.0 / (1.0 + (0.3275911 * 0.7071067811865476) * jnp.abs(value))
    bell = jnp.exp2(value * value * (-0.5 * 1.4426950408889634))
    tail = 0.5 * 1.061405429
    for term in (-0.5 * 1.453152027, 0.5 * 1.421413741, -0.5 * 0.284496736, 0.5 * 0.254829592):
        tail = tail * t + term
    tail = tail * t * bell
    cdf = jnp.where(value >= 0.0, 1.0 - tail, tail)
    return value * cdf, cdf + value * (0.3989422804014327 * bell)


def normalised(values):
    mean = jnp.mean(values, axis=-1, keepdims=True)
    centre = values - mean
    rate = lax.rsqrt(jnp.mean(centre * centre, axis=-1, keepdims=True) + EPSILON)
    return centre * rate, rate


def norm_back(scaled, unit, rate):
    first = jnp.mean(scaled, axis=-1, keepdims=True)
    second = jnp.mean(scaled * unit, axis=-1, keepdims=True)
    return rate * (scaled - first - unit * second)


def row_sums(values):
    rows, columns = values.shape
    return jnp.sum(values.reshape(rows // 8, 8, columns), axis=0)


def chain_kernel(
    att_ref,
    tok_ref,
    cot_ref,
    live_ref,
    lse_ref,
    mix_ref,
    up_ref,
    down_ref,
    vec_ref,
    bias_up_ref,
    spread_ref,
    out_ref,
    act_ref,
    upr_ref,
    hid_ref,
    pre_ref,
    mixr_ref,
    mixed_ref,
    back_ref,
    delta_ref,
    sum_ref,
    sum_up_ref,
    slope_ref,
):
    width = up_ref.shape[1]
    bias_mix, bias_down = vec_ref[0:1], vec_ref[1:2]
    gain_one, shift_one = vec_ref[2:3], vec_ref[3:4]
    gain_two, shift_two = vec_ref[4:5], vec_ref[5:6]

    @pl.when(pl.program_id(0) == 0)
    def _():
        sum_ref[...] = jnp.zeros_like(sum_ref)
        sum_up_ref[...] = jnp.zeros_like(sum_up_ref)

    attended = att_ref[...]
    mixed = plain_product(attended, mix_ref[...]) + bias_mix + tok_ref[...].astype(jnp.float32)
    unit_one, rate_one = normalised(mixed)
    hidden = unit_one * gain_one + shift_one
    hidden_rounded = hidden.astype(jnp.bfloat16)
    hid_ref[...] = hidden_rounded
    down_sum = bias_down + hidden
    for f in range(0, width, FCHUNK):
        up_sum = plain_product(hidden_rounded, up_ref[:, f : f + FCHUNK]) + (
            bias_up_ref[0:1, f : f + FCHUNK]
        )
        active, slope = gelu_terms(up_sum)
        active = active.astype(jnp.bfloat16)
        act_ref[:, f : f + FCHUNK] = active
        slope_ref[:, f : f + FCHUNK] = slope
        down_sum = down_sum + plain_product(active, down_ref[f : f + FCHUNK, :])
    unit_two, rate_two = normalised(down_sum)
    out_ref[...] = (unit_two * gain_two + shift_two).astype(jnp.bfloat16)
    cot = cot_ref[...].astype(jnp.float32)
    back_pre = norm_back(cot * gain_two, unit_two, rate_two)
    pre_rounded = back_pre.astype(jnp.bfloat16)
    pre_ref[...] = pre_rounded
    sum_ref[4] += row_sums(cot * unit_two)
    sum_ref[5] += row_sums(cot)
    sum_ref[1] += row_sums(back_pre)
    back_hidden = back_pre
    for f in range(0, width, FCHUNK):
        back_up = back_product(pre_rounded, down_ref[f : f + FCHUNK, :]) * (
            slope_ref[:, f : f + FCHUNK]
        )
        sum_up_ref[:, f : f + FCHUNK] += row_sums(back_up)
        up_rounded = back_up.astype(jnp.bfloat16)
        upr_ref[:, f : f + FCHUNK] = up_rounded
        back_hidden = back_hidden + back_product(up_rounded, up_ref[:, f : f + FCHUNK])
    sum_ref[2] += row_sums(back_hidden * unit_one)
    sum_ref[3] += row_sums(back_hidden)
    back_mixed = norm_back(back_hidden * gain_one, unit_one, rate_one)
    sum_ref[0] += row_sums(back_mixed)
    mixed_ref[...] = back_mixed
    mixed_rounded = back_mixed.astype(jnp.bfloat16)
    mixr_ref[...] = mixed_rounded
    back = back_product(mixed_rounded, mix_ref[...]).astype(jnp.bfloat16)
    back = jnp.where(live_ref[...] > 0.5, back, jnp.zeros_like(back))
    back_ref[:, : back.shape[1]] = back
    terms = back.astype(jnp.float32) * attended.astype(jnp.float32)
    high = terms.astype(jnp.bfloat16)
    low = (terms - high.astype(jnp.float32)).astype(jnp.bfloat16)
    delta = plain_product(high, spread_ref[...]) + plain_product(low, spread_ref[...])
    delta_ref[...] = delta
    lane = lax.broadcasted_iota(jnp.int32, delta.shape, 1)
    term = lane % TERMS
    whole = jnp.where(term < 3, lse_ref[...], delta)
    first = whole.astype(jnp.bfloat16)
    rest = whole - first.astype(jnp.float32)
    second = rest.astype(jnp.bfloat16)
    third = (rest - second.astype(jnp.float32)).astype(jnp.bfloat16)
    picked = jnp.where(
        (term == 0) | (term == 3),
        first.astype(jnp.float32),
        jnp.where((term == 2), third.astype(jnp.float32), second.astype(jnp.float32)),
    )
    picked = jnp.where(lane < TERMS * HEADS, picked, 0.0)
    back_ref[:, back.shape[1] :] = picked.astype(jnp.bfloat16)


def chain_call(att, tok, cot, live, lse, mix, up, down, vectors, bias_up):
    rows, width = tok.shape
    wide = up.shape[1]
    head_of = jnp.arange(width, dtype=jnp.int32)[:, None] // HD
    spread = (head_of == jnp.arange(2 * HD, dtype=jnp.int32)[None, :] // TERMS).astype(jnp.bfloat16)

    def tile(columns):
        return pl.BlockSpec((RTILE, columns), lambda i: (i, 0))

    def fixed(*shape):
        return pl.BlockSpec(shape, lambda i: (0,) * len(shape))

    bf16, f32 = jnp.bfloat16, jnp.float32
    return pl.pallas_call(
        chain_kernel,
        grid=(rows // RTILE,),
        in_specs=[
            tile(width),
            tile(width),
            tile(width),
            tile(1),
            tile(2 * HD),
            fixed(*mix.shape),
            fixed(*up.shape),
            fixed(*down.shape),
            fixed(*vectors.shape),
            fixed(*bias_up.shape),
            fixed(*spread.shape),
        ],
        out_specs=[
            tile(width),
            tile(wide),
            tile(wide),
            tile(width),
            tile(width),
            tile(width),
            tile(width),
            tile(width + 2 * HD),
            tile(2 * HD),
            fixed(6, 8, width),
            fixed(8, wide),
        ],
        out_shape=[
            jax.ShapeDtypeStruct((rows, width), bf16),
            jax.ShapeDtypeStruct((rows, wide), bf16),
            jax.ShapeDtypeStruct((rows, wide), bf16),
            jax.ShapeDtypeStruct((rows, width), bf16),
            jax.ShapeDtypeStruct((rows, width), bf16),
            jax.ShapeDtypeStruct((rows, width), bf16),
            jax.ShapeDtypeStruct((rows, width), f32),
            jax.ShapeDtypeStruct((rows, width + 2 * HD), bf16),
            jax.ShapeDtypeStruct((rows, 2 * HD), f32),
            jax.ShapeDtypeStruct((6, 8, width), f32),
            jax.ShapeDtypeStruct((8, wide), f32),
        ],
        scratch_shapes=[pltpu.VMEM((RTILE, wide), f32)],
        compiler_params=pltpu.CompilerParams(vmem_limit_bytes=VMEM_LIMIT),
    )(att, tok, cot, live, lse, mix, up, down, vectors, bias_up, spread)


def weight_kernel(n_dp, core_ref, act, pre, hid, upr, att, mixr, small, send, keep, tmp):
    step = pl.program_id(0)
    core = core_ref[0]
    pieces = FF // D
    down_rows = FF // n_dp
    part_rows = D // n_dp

    def put(x, row, rows, begin):
        mine = pl.multiple_of(begin + core * rows, 16)
        other = pl.multiple_of(begin + (1 - core) * rows, 16)
        keep[pl.ds(x, 1), pl.ds(row, rows), :] = tmp[pl.ds(mine, rows), :][None]
        send[pl.ds(x, 1), pl.ds(row, rows), :] = tmp[pl.ds(other, rows), :][None]

    @pl.when(step < pieces)
    def _():
        tmp[...] = outer_sum(act[...], pre[...]).astype(jnp.bfloat16)
        per = D // down_rows
        for b in range(per):
            block = step * per + b
            x = block // 2
            rows = tmp[b * down_rows : (b + 1) * down_rows, :]

            @pl.when(lax.rem(block, 2) == core)
            def _():
                keep[pl.ds(x, 1), 0:down_rows, :] = rows[None]

            @pl.when(lax.rem(block, 2) != core)
            def _():
                send[pl.ds(x, 1), 0:down_rows, :] = rows[None]

    @pl.when((step >= pieces) & (step < 2 * pieces))
    def _():
        tmp[...] = outer_sum(hid[...], upr[...]).astype(jnp.bfloat16)
        row = pl.multiple_of(down_rows + (step - pieces) * part_rows, 16)
        for x in range(n_dp // 2):
            put(x, row, part_rows, 2 * x * part_rows)

    @pl.when(step == 2 * pieces)
    def _():
        tmp[...] = outer_sum(att[...], mixr[...]).astype(jnp.bfloat16)
        row = down_rows + pieces * part_rows
        for x in range(n_dp // 2):
            put(x, row, part_rows, 2 * x * part_rows)
            last = row + part_rows
            rows = keep.shape[1] - last
            keep[x, last:, :] = small[pl.ds(2 * x + core, 1), :, :][0]
            send[x, last:, :] = small[pl.ds(2 * x + 1 - core, 1), :, :][0]


def weight_call(n_dp, core, act, pre, hid, upr, att, mixr, small):
    rows = act.shape[0]
    pieces = FF // D
    out_rows = FF // n_dp + (pieces + 1) * (D // n_dp) + small.shape[1]

    def fixed(*shape):
        return pl.BlockSpec(shape, lambda i, c: (0,) * len(shape))

    def stepped(first):
        return pl.BlockSpec((rows, D), lambda i, c: (0, jnp.clip(i - first, 0, pieces - 1)))

    shape = (n_dp // 2, out_rows, D)
    return pl.pallas_call(
        functools.partial(weight_kernel, n_dp),
        out_shape=[jax.ShapeDtypeStruct(shape, jnp.bfloat16)] * 2,
        grid_spec=pltpu.PrefetchScalarGridSpec(
            num_scalar_prefetch=1,
            grid=(2 * pieces + 1,),
            in_specs=[
                stepped(0),
                fixed(rows, D),
                fixed(rows, D),
                stepped(pieces),
                fixed(rows, D),
                fixed(rows, D),
                fixed(*small.shape),
            ],
            out_specs=[fixed(*shape)] * 2,
            scratch_shapes=[pltpu.VMEM((D, D), jnp.bfloat16)],
        ),
        compiler_params=pltpu.CompilerParams(vmem_limit_bytes=VMEM_LIMIT),
    )(core, act, pre, hid, upr, att, mixr, small)


def swap(value, axis, bit):
    devices = lax.axis_size(axis)
    return lax.ppermute(value, axis, [(i, i ^ bit) for i in range(devices)])


def half_of(blocks, which):
    paired = blocks.reshape((blocks.shape[0] // 2, 2) + blocks.shape[1:])
    return lax.dynamic_index_in_dim(paired, which, 1, keepdims=False)


def added(left, right):
    return (left.astype(jnp.float32) + right.astype(jnp.float32)).astype(jnp.bfloat16)


def dp_rest(blocks, dp_rank):
    bit = 2
    while blocks.shape[0] > 1:
        mine = (dp_rank // bit) % 2
        got = swap(half_of(blocks, 1 - mine), "dp", bit)
        blocks = added(half_of(blocks, mine), got)
        bit *= 2
    return blocks[0]


def cluster_ids(group_order, own_start, span):
    padded = jnp.pad(group_order, ((0, 0), (HALO, HALO)), constant_values=-(1 << 24))
    wanted = lax.dynamic_slice_in_dim(padded, own_start, span, 1) - (own_start - HALO)
    tile_of = wanted >> 7
    lane_of_token = wanted & (CL - 1)
    cluster = (jnp.arange(span, dtype=jnp.int32) >> 7) + 1
    tile_hot = jnp.where(
        tile_of[:, :, None] == jnp.arange(span // CL, dtype=jnp.int32), cluster[None, :, None], 0
    ).astype(jnp.bfloat16)
    lane_hot = (lane_of_token[:, :, None] == jnp.arange(CL, dtype=jnp.int32)).astype(jnp.bfloat16)
    table = jnp.einsum("hpt,hpl->htl", tile_hot, lane_hot, preferred_element_type=jnp.float32)
    return table.reshape(HEADS, span) - 1.0


def after(values, *others):
    return lax.optimization_barrier((values, others))[0]


def on_device(
    tokens,
    input_weight,
    output_weight,
    up_weight,
    down_weight,
    output_bias,
    up_bias,
    down_bias,
    first_gain,
    first_shift,
    second_gain,
    second_shift,
    document_runs,
    document_trim,
    cluster_order,
    cotangent,
):
    bf16, f32 = jnp.bfloat16, jnp.float32
    n_dp = lax.axis_size("dp")
    n_seq = lax.axis_size("seq")
    dp_rank = lax.axis_index("dp")
    seq_rank = lax.axis_index("seq")
    inputs = tokens[0]
    tok_dev = inputs.shape[0]
    tiles = tok_dev // CL
    span = tok_dev + 2 * HALO
    own_start = seq_rank * tok_dev

    token_parts = halo_parts(inputs)
    n_parts = len(token_parts)

    weight_in = lax.all_gather(input_weight, "dp", axis=0, tiled=True)
    vectors = [output_bias, down_bias, first_gain, first_shift, second_gain, second_shift]
    packed = jnp.concatenate(vectors + [up_bias])
    pad_rows = -(-packed.shape[0] // (16 * D)) * 16
    packed = jnp.pad(packed, (0, pad_rows * D - packed.shape[0])).reshape(pad_rows, D)
    mix_rows = output_weight.shape[0]
    mix_all = lax.all_gather(jnp.concatenate([output_weight, packed], 0), "dp", axis=0)
    weight_up = lax.all_gather(up_weight, "dp", axis=0, tiled=True)
    weight_down = lax.all_gather(down_weight, "dp", axis=0, tiled=True)
    weight_mix = mix_all[:, :mix_rows].reshape(D, D)
    small_all = mix_all[:, mix_rows:].reshape(n_dp, -1).astype(f32)
    vec = small_all[:, : 6 * mix_rows].reshape(n_dp, 6, mix_rows).transpose(1, 0, 2).reshape(6, D)
    vec = jnp.pad(vec, ((0, 2), (0, 0)))
    up_part = up_bias.shape[0]
    bias_up = small_all[:, 6 * mix_rows : 6 * mix_rows + up_part].reshape(1, n_dp * up_part)
    bias_up = jnp.pad(bias_up, ((0, 7), (0, 0)))

    runs = document_runs[0]
    first_cluster = jnp.cumsum(runs) - runs
    own_clusters = seq_rank * tiles + jnp.arange(tiles, dtype=jnp.int32)
    doc_start = jnp.max(
        jnp.where(first_cluster[None, :] <= own_clusters[:, None], first_cluster[None, :], 0), axis=1
    )
    starts = (doc_start - seq_rank * tiles + (MOSTB - 1)).astype(jnp.int32)

    cids = cluster_ids(cluster_order[0], own_start, span)
    positions = own_start - HALO + jnp.arange(span, dtype=jnp.int32)
    live = live_tokens(runs, document_trim[0], positions)
    usable = live[None, :] & (cids >= 0.0)
    key_ids = jnp.where(usable, cids, -1.0).reshape(PAIRS, 2, span)
    query_ids = jnp.where(usable, cids, -2.0).reshape(PAIRS, 2, span)
    own_live = live[HALO : HALO + tok_dev, None].astype(f32)

    projected = [plain_product(part, weight_in).astype(bf16) for part in token_parts]
    own = projected[n_parts // 2]
    heights = [part.shape[0] for part in token_parts]

    def over_parts(third, first):
        return [lane_block(rows, third * PAIRS + first) for rows in heights]

    wide_scratch = pltpu.VMEM((span, 2 * HD), bf16)
    attended, lse = strip_call(
        functools.partial(attend_kernel, tiles, n_parts),
        PAIRS,
        [lane_block(tok_dev, 0)]
        + over_parts(1, 0)
        + over_parts(2, 0)
        + [row_block(span, 0), row_block(span, 0)],
        [lane_block(tok_dev, 0), fixed_lanes(tok_dev, 0)],
        [
            jax.ShapeDtypeStruct((tok_dev, D), bf16),
            jax.ShapeDtypeStruct((tok_dev, 2 * HD), f32),
        ],
        [wide_scratch, wide_scratch, pltpu.VMEM((2 * CL, WINDOW), f32)],
        (starts, own, *projected, *projected, query_ids, key_ids),
    )

    (
        result,
        active,
        up_rounded,
        hidden_rounded,
        pre_rounded,
        mixed_rounded,
        back_mixed,
        back_own,
        delta,
        sums,
        sums_up,
    ) = chain_call(
        attended,
        inputs,
        cotangent[0],
        own_live,
        lse,
        weight_mix,
        weight_up,
        weight_down,
        vec,
        bias_up,
    )
    back_parts = halo_parts(back_own)

    small = jnp.concatenate(
        [
            jnp.sum(sums, axis=1).reshape(6, n_dp, mix_rows).transpose(1, 0, 2).reshape(n_dp, -1),
            jnp.sum(sums_up, axis=0).reshape(n_dp, -1),
        ],
        axis=1,
    ).astype(bf16)
    fixed_rows = FF // n_dp + (FF // D + 1) * (D // n_dp)
    unit = 16 * n_seq // 2
    small_rows = -(-(fixed_rows + -(-small.shape[1] // D)) // unit) * unit - fixed_rows
    small = jnp.pad(small, ((0, 0), (0, small_rows * D - small.shape[1])))
    small = small.reshape(n_dp, small_rows, D)
    core = (dp_rank % 2).astype(jnp.int32).reshape(1)
    send, keep = weight_call(
        n_dp,
        core,
        active,
        pre_rounded,
        hidden_rounded,
        up_rounded,
        attended,
        mixed_rounded,
        small,
    )
    core_got = swap(send, "dp", 1)

    half_pairs = PAIRS // 2

    def query_strip(first, starts_now):
        return strip_call(
            functools.partial(query_kernel, tiles, n_parts, first),
            half_pairs,
            [lane_block(tok_dev, first)]
            + over_parts(1, first)
            + over_parts(2, first)
            + [
                lane_block(tok_dev, first),
                row_block(span, first),
                row_block(span, first),
                fixed_lanes(tok_dev, 0),
                fixed_lanes(tok_dev, 0),
            ],
            lane_block(tok_dev, 0),
            jax.ShapeDtypeStruct((tok_dev, half_pairs * 2 * HD), bf16),
            [wide_scratch, wide_scratch],
            (
                starts_now,
                own,
                *projected,
                *projected,
                back_own,
                query_ids,
                key_ids,
                lse,
                delta_at_lse,
            ),
        )

    def key_strip(first, starts_now):
        return strip_call(
            functools.partial(key_kernel, tiles, n_parts, first),
            half_pairs,
            [lane_block(tok_dev, PAIRS + first), lane_block(tok_dev, 2 * PAIRS + first)]
            + over_parts(0, first)
            + over_parts(0, first)
            + [fixed_lanes(rows, PAIRS) for rows in heights]
            + [row_block(span, first), row_block(span, first)],
            [lane_block(tok_dev, 0), lane_block(tok_dev, 0)],
            [jax.ShapeDtypeStruct((tok_dev, half_pairs * 2 * HD), bf16)] * 2,
            [pltpu.VMEM((span, 4 * HD), bf16), pltpu.VMEM((span, 4 * HD), bf16)],
            (
                starts_now,
                own,
                own,
                *projected,
                *back_parts,
                *back_parts,
                query_ids,
                key_ids,
            ),
        )

    delta_at_lse = delta
    queries_a = query_strip(0, after(starts, send))
    core_sum = added(keep, after(core_got, queries_a))
    queries_b = query_strip(half_pairs, after(starts, core_sum))
    keys_a, values_a = key_strip(0, after(starts, queries_b))
    share = dp_rest(core_sum, dp_rank)
    share_rows = share.shape[0]
    scattered = lax.all_to_all(
        share.reshape(n_seq, share_rows // n_seq, D), "seq", split_axis=0, concat_axis=0
    )
    keys_b, values_b = key_strip(half_pairs, after(starts, share, keys_a))
    mine = jnp.sum(scattered.astype(f32), axis=0).astype(bf16)
    early = lax.all_gather(mine, "seq", axis=0, tiled=True)

    back_projected = jnp.concatenate(
        [queries_a, queries_b, keys_a, keys_b, values_a, values_b], axis=1
    )
    grad_in = outer_sum(inputs, back_projected).astype(bf16)
    grad_in_share = lax.psum_scatter(grad_in, "dp", scatter_dimension=0, tiled=True)
    grad_in_total = lax.psum(grad_in_share, "seq").astype(f32)
    input_grad = back_mixed + back_product(back_projected, weight_in)

    down_rows = FF // n_dp
    part_rows = D // n_dp
    grad_down = early[:down_rows].astype(f32)
    grad_up = (
        early[down_rows : down_rows + (FF // D) * part_rows]
        .reshape(FF // D, part_rows, D)
        .transpose(1, 0, 2)
        .reshape(part_rows, FF)
        .astype(f32)
    )
    at = down_rows + (FF // D) * part_rows
    grad_mix = early[at : at + part_rows].astype(f32)
    flat = early[at + part_rows :].reshape(-1).astype(f32)
    vectors_out = [flat[i * part_rows : (i + 1) * part_rows] for i in range(6)]
    bias_up_out = flat[6 * part_rows : 6 * part_rows + down_rows]
    return (
        result[None],
        input_grad[None],
        grad_in_total,
        grad_mix,
        grad_up,
        grad_down,
        vectors_out[0],
        bias_up_out,
        vectors_out[1],
        *vectors_out[2:],
    )


def solution(mesh):
    placed = (
        P("dp", "seq", None),
        P("dp", None),
        P("dp", None),
        P("dp", None),
        P("dp", None),
        P("dp"),
        P("dp"),
        P("dp"),
        P("dp"),
        P("dp"),
        P("dp"),
        P("dp"),
        P("dp", None),
        P("dp", None),
        P("dp", None, None),
        P("dp", "seq", None),
    )
    return jax.shard_map(
        on_device,
        mesh=mesh,
        in_specs=placed,
        out_specs=(
            P("dp", "seq", None),
            P("dp", "seq", None),
            P("dp", None),
            P("dp", None),
            P("dp", None),
            P("dp", None),
            P("dp"),
            P("dp"),
            P("dp"),
            P("dp"),
            P("dp"),
            P("dp"),
            P("dp"),
        ),
        check_vma=False,
    )
```

```python
import functools

import jax
import jax.numpy as jnp
from jax import lax
from jax.experimental import pallas as pl
from jax.experimental.pallas import tpu as pltpu
from jax.sharding import PartitionSpec as P

D = 768
HEADS = 12
HD = 64
CL = 128
MOSTB = 16
PAIRS = HEADS // 2
WINDOW = MOSTB * CL
HALO = (MOSTB - 1) * CL
CHUNK = 512
KCHUNK = 256
PACK = 4
NEG = -1e30
TERMS = 5
FF = 3072
RTILE = 256
FCHUNK = 768
SCALE2 = HD ** (-0.5) * 1.4426950408889634

EPSILON = 1e-05


def shifted(value, axis, by):
    devices = lax.axis_size(axis)
    pairs = [(i, i + by) for i in range(devices) if 0 <= i + by < devices]
    return lax.ppermute(value, axis, pairs)


def halo_parts(value):
    own = value.shape[0]
    parts = [value]
    left = HALO
    distance = 1
    while left > 0:
        take = min(own, left)
        before = shifted(value[own - take :], "seq", distance)
        after = shifted(value[:take], "seq", -distance)
        parts = [before] + parts + [after]
        left -= take
        distance += 1
    return parts


def live_tokens(runs, trim, positions):
    ends = jnp.cumsum(runs) * CL
    starts = ends - runs * CL
    lengths = runs * CL - trim
    inside = (positions[..., None] >= starts) & (positions[..., None] < starts + lengths)
    return jnp.any(inside, axis=-1)


def outer_sum(left, right):
    return lax.dot_general(
        left, right, (((0,), (0,)), ((), ())), preferred_element_type=jnp.float32
    )


def back_product(left, right):
    return lax.dot_general(
        left, right, (((1,), (1,)), ((), ())), preferred_element_type=jnp.float32
    )


def plain_product(left, right):
    return jnp.dot(left, right, preferred_element_type=jnp.float32)


def stacked(tile):
    lane = lax.broadcasted_iota(jnp.int32, tile.shape, 1)
    zero = jnp.zeros_like(tile)
    heads = tile.shape[1] // HD
    return jnp.concatenate(
        [
            jnp.where((lane >= h * HD) & (lane < (h + 1) * HD), tile, zero)
            for h in range(heads)
        ],
        axis=0,
    )


def unstacked(stack):
    heads = stack.shape[1] // HD
    lane = lax.broadcasted_iota(jnp.int32, (CL, heads * HD), 1)
    result = stack[:CL]
    for h in range(1, heads):
        result = jnp.where(lane >= h * HD, stack[h * CL : (h + 1) * CL], result)
    return result


def as_column(row):
    return jnp.broadcast_to(row, (CL, CL)).T


def lane_of(tile, lane):
    lanes = lax.broadcasted_iota(jnp.int32, tile.shape, 1)
    return jnp.sum(jnp.where(lanes == lane, tile, 0.0), axis=1, keepdims=True)


def masked(scores, cols, row_ref, begin):
    parts = []
    wide = scores.shape[1]
    for half, one in enumerate(cols):
        row = row_ref[0, half : half + 1, pl.ds(begin, wide)]
        block = scores[half * CL : (half + 1) * CL]
        col = jnp.concatenate([one] * (wide // CL), axis=1)
        parts.append(jnp.where(col == row, block, NEG))
    return jnp.concatenate(parts, axis=0)


def assemble(parts, whole):
    at = 0
    for part in parts:
        rows = part.shape[0]
        whole[at : at + rows, :] = part[...]
        at += rows


def attend_kernel(tiles, n_parts, starts, q_ref, *refs):
    k_parts, refs = refs[:n_parts], refs[n_parts:]
    v_parts, refs = refs[:n_parts], refs[n_parts:]
    qid_ref, kid_ref, out_ref, lse_ref, k_ref, v_ref, s_ref = refs
    pair = pl.program_id(0)
    assemble(k_parts, k_ref)
    assemble(v_parts, v_ref)

    def one_tile(tile, slot):
        begin = pl.multiple_of(starts[tile] * CL, CL)
        own = pl.multiple_of(HALO + tile * CL, CL)
        here = pl.multiple_of(tile * CL, CL)
        query = stacked(q_ref[pl.ds(here, CL), :])
        cols = [as_column(qid_ref[0, half : half + 1, pl.ds(own, CL)]) for half in range(2)]
        top = jnp.full((2 * CL, CL), NEG, jnp.float32)
        for j in range(WINDOW // CHUNK):
            at = pl.multiple_of(begin + j * CHUNK, CL)
            scores = masked(
                back_product(query, k_ref[pl.ds(at, CHUNK), :]), cols, kid_ref, at
            )
            s_ref[slot, :, j * CHUNK : (j + 1) * CHUNK] = scores
            for i in range(CHUNK // CL):
                top = jnp.maximum(top, scores[:, i * CL : (i + 1) * CL])
        peak = jnp.max(top, axis=1, keepdims=True)
        total = jnp.zeros((2 * CL, CL), jnp.float32)
        result = jnp.zeros((2 * CL, 2 * HD), jnp.float32)
        for j in range(WINDOW // CHUNK):
            at = pl.multiple_of(begin + j * CHUNK, CL)
            weights = jnp.exp2((s_ref[slot, :, j * CHUNK : (j + 1) * CHUNK] - peak) * SCALE2)
            for i in range(CHUNK // CL):
                total = total + weights[:, i * CL : (i + 1) * CL]
            result = result + plain_product(
                weights.astype(jnp.bfloat16), v_ref[pl.ds(at, CHUNK), :]
            )
        total = jnp.sum(total, axis=1, keepdims=True)
        result = result / total
        lse = peak + jnp.log(total) * HD**0.5
        live = [(col >= 0.0).astype(jnp.float32) for col in cols]
        result = result * jnp.concatenate(live, axis=0)
        out_ref[pl.ds(here, CL), :] = unstacked(result).astype(jnp.bfloat16)
        lane = lax.broadcasted_iota(jnp.int32, (CL, CL), 1)
        kept = lse_ref[pl.ds(here, CL), :]
        for half in range(2):
            first = (2 * pair + half) * TERMS
            kept = jnp.where(
                (lane >= first) & (lane < first + TERMS), lse[half * CL : (half + 1) * CL], kept
            )
        lse_ref[pl.ds(here, CL), :] = kept

    def two_tiles(step, carry):
        for slot in range(2):
            one_tile(2 * step + slot, slot)
        return carry

    @pl.when(pair == 0)
    def _():
        lse_ref[...] = jnp.zeros_like(lse_ref)

    lax.fori_loop(0, tiles // 2, two_tiles, 0)


def query_kernel(tiles, n_parts, first_head, starts, q_ref, *refs):
    k_parts, refs = refs[:n_parts], refs[n_parts:]
    v_parts, refs = refs[:n_parts], refs[n_parts:]
    g_ref, qid_ref, kid_ref, lse_ref, delta_ref = refs[:5]
    out_ref, k_ref, v_ref = refs[-3:]
    heads = q_ref.shape[1] // HD
    head = first_head + heads * pl.program_id(0)
    assemble(k_parts, k_ref)
    assemble(v_parts, v_ref)

    def one_tile(tile, carry):
        begin = pl.multiple_of(starts[tile] * CL, CL)
        own = pl.multiple_of(HALO + tile * CL, CL)
        here = pl.multiple_of(tile * CL, CL)
        query = stacked(q_ref[pl.ds(here, CL), :])
        back = stacked(g_ref[pl.ds(here, CL), :])
        cols = [as_column(qid_ref[0, half : half + 1, pl.ds(own, CL)]) for half in range(heads)]
        lse_tile = lse_ref[pl.ds(here, CL), :]
        delta_tile = delta_ref[pl.ds(here, CL), :]
        lse = jnp.concatenate(
            [lane_of(lse_tile, (head + half) * TERMS) for half in range(heads)], axis=0
        )
        delta = jnp.concatenate(
            [lane_of(delta_tile, (head + half) * TERMS) for half in range(heads)], axis=0
        )
        result = jnp.zeros((heads * CL, heads * HD), jnp.float32)
        for j in range(WINDOW // CHUNK):
            at = pl.multiple_of(begin + j * CHUNK, CL)
            keys = k_ref[pl.ds(at, CHUNK), :]
            scores = masked((back_product(query, keys) - lse) * SCALE2, cols, kid_ref, at)
            probs = jnp.exp2(scores)
            back_probs = back_product(back, v_ref[pl.ds(at, CHUNK), :])
            back_scores = probs * (back_probs - delta)
            result = result + plain_product(back_scores.astype(jnp.bfloat16), keys)
        out_ref[pl.ds(here, CL), :] = (unstacked(result) * HD ** (-0.5)).astype(jnp.bfloat16)
        return carry

    lax.fori_loop(0, tiles, one_tile, 0)


def key_kernel(tiles, n_parts, first_pair, starts, k_ref, v_ref, *refs):
    q_parts, refs = refs[:n_parts], refs[n_parts:]
    g_parts, refs = refs[:n_parts], refs[n_parts:]
    a_parts, refs = refs[:n_parts], refs[n_parts:]
    qid_ref, kid_ref = refs[:2]
    key_out_ref, value_out_ref, q_ref, g_ref = refs[-4:]
    pair = first_pair + pl.program_id(0)
    at = 0
    for q_part, g_part, a_part in zip(q_parts, g_parts, a_parts):
        rows = q_part.shape[0]
        q_ref[at : at + rows, : 2 * HD] = q_part[...]
        q_ref[at : at + rows, 2 * HD :] = a_part[...]
        g_ref[at : at + rows, : 2 * HD] = g_part[...]
        g_ref[at : at + rows, 2 * HD :] = a_part[...]
        at += rows

    lane = lax.broadcasted_iota(jnp.int32, (CL, CL), 1)
    lse_pick, delta_pick = [], []
    for half in range(2):
        first = (2 * pair + half) * TERMS
        lse_pick.append(jnp.where((lane >= first) & (lane < first + 3), -1.0, 0.0))
        delta_pick.append(jnp.where((lane >= first + 3) & (lane < first + TERMS), -1.0, 0.0))
    lse_pick = jnp.concatenate(lse_pick, axis=0).astype(jnp.bfloat16)
    delta_pick = jnp.concatenate(delta_pick, axis=0).astype(jnp.bfloat16)

    def one_tile(tile, carry):
        begin = pl.multiple_of(starts[tile] * CL, CL)
        own = pl.multiple_of(HALO + tile * CL, CL)
        here = pl.multiple_of(tile * CL, CL)
        keys = jnp.concatenate([stacked(k_ref[pl.ds(here, CL), :]), lse_pick], axis=1)
        values = jnp.concatenate([stacked(v_ref[pl.ds(here, CL), :]), delta_pick], axis=1)
        cols = [as_column(kid_ref[0, half : half + 1, pl.ds(own, CL)]) for half in range(2)]
        key_sum = jnp.zeros((2 * CL, 2 * HD), jnp.float32)
        value_sum = jnp.zeros((2 * CL, 2 * HD), jnp.float32)
        for j in range(WINDOW // KCHUNK):
            at = pl.multiple_of(begin + j * KCHUNK, CL)
            queries = q_ref[pl.ds(at, KCHUNK), :]
            back = g_ref[pl.ds(at, KCHUNK), :]
            scores = masked(back_product(keys, queries) * SCALE2, cols, qid_ref, at)
            probs = jnp.exp2(scores)
            back_scores = probs * back_product(values, back)
            value_sum = value_sum + plain_product(probs.astype(jnp.bfloat16), back[:, : 2 * HD])
            key_sum = key_sum + plain_product(
                back_scores.astype(jnp.bfloat16), queries[:, : 2 * HD]
            )
        key_out_ref[pl.ds(here, CL), :] = (unstacked(key_sum) * HD ** (-0.5)).astype(jnp.bfloat16)
        value_out_ref[pl.ds(here, CL), :] = unstacked(value_sum).astype(jnp.bfloat16)
        return carry

    lax.fori_loop(0, tiles, one_tile, 0)


def lane_block(rows, first, heads=2):
    return pl.BlockSpec((rows, heads * HD), lambda pair, starts: (0, first + pair))


def fixed_lanes(rows, block):
    return pl.BlockSpec((rows, 2 * HD), lambda pair, starts: (0, block))


def row_block(columns, first, heads=2):
    return pl.BlockSpec((1, heads, columns), lambda pair, starts: (first + pair, 0, 0))


UNREAD = pl.BlockSpec(memory_space=pl.ANY)


VMEM_LIMIT = 60 * 1024 * 1024


def strip_call(kernel, pairs, in_specs, out_specs, out_shape, scratch, args):
    return pl.pallas_call(
        kernel,
        out_shape=out_shape,
        grid_spec=pltpu.PrefetchScalarGridSpec(
            num_scalar_prefetch=1,
            grid=(pairs,),
            in_specs=in_specs,
            out_specs=out_specs,
            scratch_shapes=scratch,
        ),
        compiler_params=pltpu.CompilerParams(vmem_limit_bytes=VMEM_LIMIT),
    )(*args)


def gelu_terms(value):
    t = 1.0 / (1.0 + (0.3275911 * 0.7071067811865476) * jnp.abs(value))
    bell = jnp.exp2(value * value * (-0.5 * 1.4426950408889634))
    tail = 0.5 * 1.061405429
    for term in (-0.5 * 1.453152027, 0.5 * 1.421413741, -0.5 * 0.284496736, 0.5 * 0.254829592):
        tail = tail * t + term
    tail = tail * t * bell
    cdf = jnp.where(value >= 0.0, 1.0 - tail, tail)
    return value * cdf, cdf + value * (0.3989422804014327 * bell)


def normalised(values):
    mean = jnp.mean(values, axis=-1, keepdims=True)
    centre = values - mean
    rate = lax.rsqrt(jnp.mean(centre * centre, axis=-1, keepdims=True) + EPSILON)
    return centre * rate, rate


def norm_back(scaled, unit, rate):
    first = jnp.mean(scaled, axis=-1, keepdims=True)
    second = jnp.mean(scaled * unit, axis=-1, keepdims=True)
    return rate * (scaled - first - unit * second)


def row_sums(values):
    rows, columns = values.shape
    return jnp.sum(values.reshape(rows // 8, 8, columns), axis=0)


def chain_kernel(
    att_ref,
    tok_ref,
    cot_ref,
    live_ref,
    lse_ref,
    mix_ref,
    up_ref,
    down_ref,
    vec_ref,
    bias_up_ref,
    spread_ref,
    out_ref,
    act_ref,
    upr_ref,
    hid_ref,
    pre_ref,
    mixr_ref,
    mixed_ref,
    back_ref,
    delta_ref,
    sum_ref,
    sum_up_ref,
    slope_ref,
):
    width = up_ref.shape[1]
    bias_mix, bias_down = vec_ref[0:1], vec_ref[1:2]
    gain_one, shift_one = vec_ref[2:3], vec_ref[3:4]
    gain_two, shift_two = vec_ref[4:5], vec_ref[5:6]

    @pl.when(pl.program_id(0) == 0)
    def _():
        sum_ref[...] = jnp.zeros_like(sum_ref)
        sum_up_ref[...] = jnp.zeros_like(sum_up_ref)

    attended = att_ref[...]
    mixed = plain_product(attended, mix_ref[...]) + bias_mix + tok_ref[...].astype(jnp.float32)
    unit_one, rate_one = normalised(mixed)
    hidden = unit_one * gain_one + shift_one
    hidden_rounded = hidden.astype(jnp.bfloat16)
    hid_ref[...] = hidden_rounded
    down_sum = bias_down + hidden
    for f in range(0, width, FCHUNK):
        up_sum = plain_product(hidden_rounded, up_ref[:, f : f + FCHUNK]) + (
            bias_up_ref[0:1, f : f + FCHUNK]
        )
        active, slope = gelu_terms(up_sum)
        active = active.astype(jnp.bfloat16)
        act_ref[:, f : f + FCHUNK] = active
        slope_ref[:, f : f + FCHUNK] = slope
        down_sum = down_sum + plain_product(active, down_ref[f : f + FCHUNK, :])
    unit_two, rate_two = normalised(down_sum)
    out_ref[...] = (unit_two * gain_two + shift_two).astype(jnp.bfloat16)
    cot = cot_ref[...].astype(jnp.float32)
    back_pre = norm_back(cot * gain_two, unit_two, rate_two)
    pre_rounded = back_pre.astype(jnp.bfloat16)
    pre_ref[...] = pre_rounded
    sum_ref[4] += row_sums(cot * unit_two)
    sum_ref[5] += row_sums(cot)
    sum_ref[1] += row_sums(back_pre)
    back_hidden = back_pre
    for f in range(0, width, FCHUNK):
        back_up = back_product(pre_rounded, down_ref[f : f + FCHUNK, :]) * (
            slope_ref[:, f : f + FCHUNK]
        )
        sum_up_ref[:, f : f + FCHUNK] += row_sums(back_up)
        up_rounded = back_up.astype(jnp.bfloat16)
        upr_ref[:, f : f + FCHUNK] = up_rounded
        back_hidden = back_hidden + back_product(up_rounded, up_ref[:, f : f + FCHUNK])
    sum_ref[2] += row_sums(back_hidden * unit_one)
    sum_ref[3] += row_sums(back_hidden)
    back_mixed = norm_back(back_hidden * gain_one, unit_one, rate_one)
    sum_ref[0] += row_sums(back_mixed)
    mixed_ref[...] = back_mixed
    mixed_rounded = back_mixed.astype(jnp.bfloat16)
    mixr_ref[...] = mixed_rounded
    back = back_product(mixed_rounded, mix_ref[...]).astype(jnp.bfloat16)
    back = jnp.where(live_ref[...] > 0.5, back, jnp.zeros_like(back))
    back_ref[:, : back.shape[1]] = back
    terms = back.astype(jnp.float32) * attended.astype(jnp.float32)
    high = terms.astype(jnp.bfloat16)
    low = (terms - high.astype(jnp.float32)).astype(jnp.bfloat16)
    delta = plain_product(high, spread_ref[...]) + plain_product(low, spread_ref[...])
    delta_ref[...] = delta
    lane = lax.broadcasted_iota(jnp.int32, delta.shape, 1)
    term = lane % TERMS
    whole = jnp.where(term < 3, lse_ref[...], delta)
    first = whole.astype(jnp.bfloat16)
    rest = whole - first.astype(jnp.float32)
    second = rest.astype(jnp.bfloat16)
    third = (rest - second.astype(jnp.float32)).astype(jnp.bfloat16)
    picked = jnp.where(
        (term == 0) | (term == 3),
        first.astype(jnp.float32),
        jnp.where((term == 2), third.astype(jnp.float32), second.astype(jnp.float32)),
    )
    picked = jnp.where(lane < TERMS * HEADS, picked, 0.0)
    back_ref[:, back.shape[1] :] = picked.astype(jnp.bfloat16)


def chain_call(att, tok, cot, live, lse, mix, up, down, vectors, bias_up):
    rows, width = tok.shape
    wide = up.shape[1]
    head_of = jnp.arange(width, dtype=jnp.int32)[:, None] // HD
    spread = (head_of == jnp.arange(2 * HD, dtype=jnp.int32)[None, :] // TERMS).astype(jnp.bfloat16)

    def tile(columns):
        return pl.BlockSpec((RTILE, columns), lambda i: (i, 0))

    def fixed(*shape):
        return pl.BlockSpec(shape, lambda i: (0,) * len(shape))

    bf16, f32 = jnp.bfloat16, jnp.float32
    return pl.pallas_call(
        chain_kernel,
        grid=(rows // RTILE,),
        in_specs=[
            tile(width),
            tile(width),
            tile(width),
            tile(1),
            tile(2 * HD),
            fixed(*mix.shape),
            fixed(*up.shape),
            fixed(*down.shape),
            fixed(*vectors.shape),
            fixed(*bias_up.shape),
            fixed(*spread.shape),
        ],
        out_specs=[
            tile(width),
            tile(wide),
            tile(wide),
            tile(width),
            tile(width),
            tile(width),
            tile(width),
            tile(width + 2 * HD),
            tile(2 * HD),
            fixed(6, 8, width),
            fixed(8, wide),
        ],
        out_shape=[
            jax.ShapeDtypeStruct((rows, width), bf16),
            jax.ShapeDtypeStruct((rows, wide), bf16),
            jax.ShapeDtypeStruct((rows, wide), bf16),
            jax.ShapeDtypeStruct((rows, width), bf16),
            jax.ShapeDtypeStruct((rows, width), bf16),
            jax.ShapeDtypeStruct((rows, width), bf16),
            jax.ShapeDtypeStruct((rows, width), f32),
            jax.ShapeDtypeStruct((rows, width + 2 * HD), bf16),
            jax.ShapeDtypeStruct((rows, 2 * HD), f32),
            jax.ShapeDtypeStruct((6, 8, width), f32),
            jax.ShapeDtypeStruct((8, wide), f32),
        ],
        scratch_shapes=[pltpu.VMEM((RTILE, wide), f32)],
        compiler_params=pltpu.CompilerParams(vmem_limit_bytes=VMEM_LIMIT),
    )(att, tok, cot, live, lse, mix, up, down, vectors, bias_up, spread)


def down_kernel(n_dp, core_ref, act, pre, send, keep, tmp):
    step = pl.program_id(0)
    core = core_ref[0]
    down_rows = FF // n_dp
    tmp[...] = outer_sum(act[...], pre[...]).astype(jnp.bfloat16)
    per = D // down_rows
    for b in range(per):
        block = step * per + b
        x = block // 2
        rows = tmp[b * down_rows : (b + 1) * down_rows, :]

        @pl.when(lax.rem(block, 2) == core)
        def _():
            keep[pl.ds(x, 1)] = rows[None]

        @pl.when(lax.rem(block, 2) != core)
        def _():
            send[pl.ds(x, 1)] = rows[None]


def up_kernel(n_dp, core_ref, hid, upr, att, mixr, small, send, keep, tmp):
    step = pl.program_id(0)
    core = core_ref[0]
    pieces = FF // D
    part_rows = D // n_dp

    def put(x, row, rows, begin):
        mine = pl.multiple_of(begin + core * rows, 16)
        other = pl.multiple_of(begin + (1 - core) * rows, 16)
        keep[x, pl.ds(row, rows), :] = tmp[pl.ds(mine, rows), :]
        send[x, pl.ds(row, rows), :] = tmp[pl.ds(other, rows), :]

    @pl.when(step < pieces)
    def _():
        tmp[...] = outer_sum(hid[...], upr[...]).astype(jnp.bfloat16)
        row = pl.multiple_of(step * part_rows, 16)
        for x in range(n_dp // 2):
            put(x, row, part_rows, 2 * x * part_rows)

    @pl.when(step == pieces)
    def _():
        tmp[...] = outer_sum(att[...], mixr[...]).astype(jnp.bfloat16)
        row = pieces * part_rows
        for x in range(n_dp // 2):
            put(x, row, part_rows, 2 * x * part_rows)
            last = row + part_rows
            keep[x, last:, :] = small[pl.ds(2 * x + core, 1), :, :][0]
            send[x, last:, :] = small[pl.ds(2 * x + 1 - core, 1), :, :][0]


def split_call(kernel, n_dp, steps, out_rows, in_specs, args):
    shape = (n_dp // 2, out_rows, D)
    return pl.pallas_call(
        functools.partial(kernel, n_dp),
        out_shape=[jax.ShapeDtypeStruct(shape, jnp.bfloat16)] * 2,
        grid_spec=pltpu.PrefetchScalarGridSpec(
            num_scalar_prefetch=1,
            grid=(steps,),
            in_specs=in_specs,
            out_specs=[pl.BlockSpec(shape, lambda i, c: (0, 0, 0))] * 2,
            scratch_shapes=[pltpu.VMEM((D, D), jnp.bfloat16)],
        ),
        compiler_params=pltpu.CompilerParams(vmem_limit_bytes=VMEM_LIMIT),
    )(*args)


def whole_block(*shape):
    return pl.BlockSpec(shape, lambda i, c: (0,) * len(shape))


def down_call(n_dp, core, act, pre):
    rows = act.shape[0]
    specs = [pl.BlockSpec((rows, D), lambda i, c: (0, i)), whole_block(rows, D)]
    return split_call(down_kernel, n_dp, FF // D, FF // n_dp, specs, (core, act, pre))


def up_call(n_dp, core, hid, upr, att, mixr, small):
    rows = hid.shape[0]
    pieces = FF // D
    specs = [
        whole_block(rows, D),
        pl.BlockSpec((rows, D), lambda i, c: (0, jnp.minimum(i, pieces - 1))),
        whole_block(rows, D),
        whole_block(rows, D),
        whole_block(*small.shape),
    ]
    out_rows = (pieces + 1) * (D // n_dp) + small.shape[1]
    return split_call(
        up_kernel, n_dp, pieces + 1, out_rows, specs, (core, hid, upr, att, mixr, small)
    )


def gate_kernel(first, *refs):
    half = len(refs) // 2
    for source, target in zip(refs[:half], refs[half:]):
        target[...] = source[...]


def gated(first, *arrays):
    return pl.pallas_call(
        gate_kernel,
        in_specs=[UNREAD] + [pl.BlockSpec(memory_space=pltpu.VMEM)] * len(arrays),
        out_specs=[pl.BlockSpec(memory_space=pltpu.VMEM)] * len(arrays),
        out_shape=[jax.ShapeDtypeStruct(one.shape, one.dtype) for one in arrays],
        compiler_params=pltpu.CompilerParams(vmem_limit_bytes=VMEM_LIMIT),
    )(first, *arrays)


def swap(value, axis, bit):
    devices = lax.axis_size(axis)
    return lax.ppermute(value, axis, [(i, i ^ bit) for i in range(devices)])


def half_of(blocks, which):
    paired = blocks.reshape((blocks.shape[0] // 2, 2) + blocks.shape[1:])
    return lax.dynamic_index_in_dim(paired, which, 1, keepdims=False)


def added(left, right):
    return (left.astype(jnp.float32) + right.astype(jnp.float32)).astype(jnp.bfloat16)


def dp_rest(blocks, dp_rank):
    bit = 2
    while blocks.shape[0] > 1:
        mine = (dp_rank // bit) % 2
        got = swap(half_of(blocks, 1 - mine), "dp", bit)
        blocks = added(half_of(blocks, mine), got)
        bit *= 2
    return blocks[0]


def cluster_ids(group_order, own_start, span):
    padded = jnp.pad(group_order, ((0, 0), (HALO, HALO)), constant_values=-(1 << 24))
    wanted = lax.dynamic_slice_in_dim(padded, own_start, span, 1) - (own_start - HALO)
    tile_of = wanted >> 7
    lane_of_token = wanted & (CL - 1)
    cluster = (jnp.arange(span, dtype=jnp.int32) >> 7) + 1
    tile_hot = jnp.where(
        tile_of[:, :, None] == jnp.arange(span // CL, dtype=jnp.int32), cluster[None, :, None], 0
    ).astype(jnp.bfloat16)
    lane_hot = (lane_of_token[:, :, None] == jnp.arange(CL, dtype=jnp.int32)).astype(jnp.bfloat16)
    table = jnp.einsum("hpt,hpl->htl", tile_hot, lane_hot, preferred_element_type=jnp.float32)
    return table.reshape(HEADS, span) - 1.0


def on_device(
    tokens,
    input_weight,
    output_weight,
    up_weight,
    down_weight,
    output_bias,
    up_bias,
    down_bias,
    first_gain,
    first_shift,
    second_gain,
    second_shift,
    document_runs,
    document_trim,
    cluster_order,
    cotangent,
):
    bf16, f32 = jnp.bfloat16, jnp.float32
    n_dp = lax.axis_size("dp")
    n_seq = lax.axis_size("seq")
    dp_rank = lax.axis_index("dp")
    seq_rank = lax.axis_index("seq")
    inputs = tokens[0]
    tok_dev = inputs.shape[0]
    tiles = tok_dev // CL
    span = tok_dev + 2 * HALO
    own_start = seq_rank * tok_dev

    token_parts = halo_parts(inputs)
    n_parts = len(token_parts)

    weight_in = lax.all_gather(input_weight, "dp", axis=0, tiled=True)
    vectors = [output_bias, down_bias, first_gain, first_shift, second_gain, second_shift]
    packed = jnp.concatenate(vectors + [up_bias])
    pad_rows = -(-packed.shape[0] // (16 * D)) * 16
    packed = jnp.pad(packed, (0, pad_rows * D - packed.shape[0])).reshape(pad_rows, D)
    mix_rows = output_weight.shape[0]
    mix_shard, up_shard, down_shard = gated(
        weight_in, jnp.concatenate([output_weight, packed], 0), up_weight, down_weight
    )
    mix_all = lax.all_gather(mix_shard, "dp", axis=0)
    weight_up = lax.all_gather(up_shard, "dp", axis=0, tiled=True)
    weight_down = lax.all_gather(down_shard, "dp", axis=0, tiled=True)
    weight_mix = mix_all[:, :mix_rows].reshape(D, D)
    small_all = mix_all[:, mix_rows:].reshape(n_dp, -1).astype(f32)
    vec = small_all[:, : 6 * mix_rows].reshape(n_dp, 6, mix_rows).transpose(1, 0, 2).reshape(6, D)
    vec = jnp.pad(vec, ((0, 2), (0, 0)))
    up_part = up_bias.shape[0]
    bias_up = small_all[:, 6 * mix_rows : 6 * mix_rows + up_part].reshape(1, n_dp * up_part)
    bias_up = jnp.pad(bias_up, ((0, 7), (0, 0)))

    runs = document_runs[0]
    first_cluster = jnp.cumsum(runs) - runs
    own_clusters = seq_rank * tiles + jnp.arange(tiles, dtype=jnp.int32)
    doc_start = jnp.max(
        jnp.where(first_cluster[None, :] <= own_clusters[:, None], first_cluster[None, :], 0), axis=1
    )
    starts = (doc_start - seq_rank * tiles + (MOSTB - 1)).astype(jnp.int32)

    cids = cluster_ids(cluster_order[0], own_start, span)
    positions = own_start - HALO + jnp.arange(span, dtype=jnp.int32)
    live = live_tokens(runs, document_trim[0], positions)
    usable = live[None, :] & (cids >= 0.0)
    key_ids = jnp.where(usable, cids, -1.0).reshape(PAIRS, 2, span)
    query_ids = jnp.where(usable, cids, -2.0).reshape(PAIRS, 2, span)
    own_live = live[HALO : HALO + tok_dev, None].astype(f32)

    projected = [plain_product(part, weight_in).astype(bf16) for part in token_parts]
    own = projected[n_parts // 2]
    heights = [part.shape[0] for part in token_parts]

    def over_parts(third, first):
        return [lane_block(rows, third * PAIRS + first) for rows in heights]

    wide_scratch = pltpu.VMEM((span, 2 * HD), bf16)
    attended, lse = strip_call(
        functools.partial(attend_kernel, tiles, n_parts),
        PAIRS,
        [lane_block(tok_dev, 0)]
        + over_parts(1, 0)
        + over_parts(2, 0)
        + [row_block(span, 0), row_block(span, 0)],
        [lane_block(tok_dev, 0), fixed_lanes(tok_dev, 0)],
        [
            jax.ShapeDtypeStruct((tok_dev, D), bf16),
            jax.ShapeDtypeStruct((tok_dev, 2 * HD), f32),
        ],
        [wide_scratch, wide_scratch, pltpu.VMEM((2, 2 * CL, WINDOW), f32)],
        (starts, own, *projected, *projected, query_ids, key_ids),
    )

    (
        result,
        active,
        up_rounded,
        hidden_rounded,
        pre_rounded,
        mixed_rounded,
        back_mixed,
        back_own,
        delta,
        sums,
        sums_up,
    ) = chain_call(
        attended,
        inputs,
        cotangent[0],
        own_live,
        lse,
        weight_mix,
        weight_up,
        weight_down,
        vec,
        bias_up,
    )
    back_parts = halo_parts(back_own)

    small = jnp.concatenate(
        [
            jnp.sum(sums, axis=1).reshape(6, n_dp, mix_rows).transpose(1, 0, 2).reshape(n_dp, -1),
            jnp.sum(sums_up, axis=0).reshape(n_dp, -1),
        ],
        axis=1,
    ).astype(bf16)
    unit = 8 * n_seq
    fixed_rows = (FF // D + 1) * (D // n_dp)
    small_rows = -(-(fixed_rows + -(-small.shape[1] // D)) // unit) * unit - fixed_rows
    small = jnp.pad(small, ((0, 0), (0, small_rows * D - small.shape[1])))
    small = small.reshape(n_dp, small_rows, D)
    core = (dp_rank % 2).astype(jnp.int32).reshape(1)
    down_send, down_keep = down_call(n_dp, core, active, pre_rounded)
    up_send, up_keep = up_call(
        n_dp, core, hidden_rounded, up_rounded, attended, mixed_rounded, small
    )
    down_got = swap(down_send, "dp", 1)
    up_got = swap(up_send, "dp", 1)

    groups = HEADS // PACK
    group_key_ids = key_ids.reshape(groups, PACK, span)
    group_query_ids = query_ids.reshape(groups, PACK, span)
    group_scratch = pltpu.VMEM((span, PACK * HD), bf16)

    def query_strip(first, *needs):
        def parts(third):
            return [lane_block(rows, third * groups + first, PACK) for rows in heights]

        return strip_call(
            functools.partial(query_kernel, tiles, n_parts, first * PACK),
            1,
            [lane_block(tok_dev, first, PACK)]
            + parts(1)
            + parts(2)
            + [
                lane_block(tok_dev, first, PACK),
                row_block(span, first, PACK),
                row_block(span, first, PACK),
                fixed_lanes(tok_dev, 0),
                fixed_lanes(tok_dev, 0),
            ]
            + [UNREAD] * len(needs),
            lane_block(tok_dev, 0, PACK),
            jax.ShapeDtypeStruct((tok_dev, PACK * HD), bf16),
            [group_scratch, group_scratch],
            (
                starts,
                own,
                *projected,
                *projected,
                back_own,
                group_query_ids,
                group_key_ids,
                lse,
                delta,
                *needs,
            ),
        )

    key_pairs = 2

    def key_strip(first, *needs):
        return strip_call(
            functools.partial(key_kernel, tiles, n_parts, first),
            key_pairs,
            [lane_block(tok_dev, PAIRS + first), lane_block(tok_dev, 2 * PAIRS + first)]
            + over_parts(0, first)
            + over_parts(0, first)
            + [fixed_lanes(rows, PAIRS) for rows in heights]
            + [row_block(span, first), row_block(span, first)]
            + [UNREAD] * len(needs),
            [lane_block(tok_dev, 0), lane_block(tok_dev, 0)],
            [jax.ShapeDtypeStruct((tok_dev, key_pairs * 2 * HD), bf16)] * 2,
            [pltpu.VMEM((span, 4 * HD), bf16), pltpu.VMEM((span, 4 * HD), bf16)],
            (
                starts,
                own,
                own,
                *projected,
                *back_parts,
                *back_parts,
                query_ids,
                key_ids,
                *needs,
            ),
        )

    def scatter(share):
        rows, columns = share.shape
        return lax.all_to_all(
            share.reshape(n_seq, rows // n_seq, columns), "seq", split_axis=0, concat_axis=0
        )

    def gather(pieces):
        mine = jnp.sum(pieces.astype(f32), axis=0).astype(bf16)
        return mine, lax.all_gather(mine, "seq", axis=0, tiled=True)

    def core_split(grad):
        blocks = grad.astype(bf16).reshape((n_dp, D // n_dp) + grad.shape[1:])
        return half_of(blocks, 1 - core[0]), half_of(blocks, core[0])

    q_strips = [query_strip(0, down_send, up_send)]
    down_sum = added(down_keep, down_got)
    up_sum = added(up_keep, up_got)
    q_strips.append(query_strip(1, q_strips[0], down_sum, up_sum))
    down_share = dp_rest(down_sum, dp_rank)
    q_strips.append(query_strip(2, q_strips[1], down_share))
    down_pieces = scatter(down_share)
    k_strips = [key_strip(0, q_strips[2])]
    up_share = dp_rest(up_sum, dp_rank)
    up_pieces = scatter(up_share)
    k_strips.append(key_strip(key_pairs, k_strips[0][0], up_share))
    down_mine, down_all = gather(down_pieces)
    early_cols = jnp.concatenate(
        q_strips + [k_strips[0][0], k_strips[1][0], k_strips[0][1], k_strips[1][1]], axis=1
    )
    early_send, early_keep = core_split(outer_sum(inputs, early_cols))
    early_got = swap(early_send, "dp", 1)
    k_strips.append(key_strip(2 * key_pairs, down_mine, early_send))
    late_cols = jnp.concatenate(k_strips[2], axis=1)
    late_send, late_keep = core_split(outer_sum(inputs, late_cols))
    late_got = swap(late_send, "dp", 1)
    early_share = dp_rest(added(early_keep, early_got), dp_rank)
    late_share = dp_rest(added(late_keep, late_got), dp_rank)
    _, up_all = gather(up_pieces)
    _, early_all = gather(scatter(early_share))
    _, late_all = gather(scatter(late_share))

    back_projected = jnp.concatenate(
        q_strips + [pair[0] for pair in k_strips] + [pair[1] for pair in k_strips], axis=1
    )
    input_grad = back_mixed + back_product(back_projected, weight_in)

    third = key_pairs * 2 * HD
    grad_in_total = jnp.concatenate(
        [
            early_all[:, : D + 2 * third],
            late_all[:, :third],
            early_all[:, D + 2 * third :],
            late_all[:, third:],
        ],
        axis=1,
    ).astype(f32)
    part_rows = D // n_dp
    up_rows = (FF // D) * part_rows
    grad_down = down_all.astype(f32)
    grad_up = (
        up_all[:up_rows]
        .reshape(FF // D, part_rows, D)
        .transpose(1, 0, 2)
        .reshape(part_rows, FF)
        .astype(f32)
    )
    grad_mix = up_all[up_rows : up_rows + part_rows].astype(f32)
    flat = up_all[up_rows + part_rows :].reshape(-1).astype(f32)
    vectors_out = [flat[i * part_rows : (i + 1) * part_rows] for i in range(6)]
    bias_up_out = flat[6 * part_rows : 6 * part_rows + FF // n_dp]
    return (
        result[None],
        input_grad[None],
        grad_in_total,
        grad_mix,
        grad_up,
        grad_down,
        vectors_out[0],
        bias_up_out,
        vectors_out[1],
        *vectors_out[2:],
    )


def solution(mesh):
    placed = (
        P("dp", "seq", None),
        P("dp", None),
        P("dp", None),
        P("dp", None),
        P("dp", None),
        P("dp"),
        P("dp"),
        P("dp"),
        P("dp"),
        P("dp"),
        P("dp"),
        P("dp"),
        P("dp", None),
        P("dp", None),
        P("dp", None, None),
        P("dp", "seq", None),
    )
    return jax.shard_map(
        on_device,
        mesh=mesh,
        in_specs=placed,
        out_specs=(
            P("dp", "seq", None),
            P("dp", "seq", None),
            P("dp", None),
            P("dp", None),
            P("dp", None),
            P("dp", None),
            P("dp"),
            P("dp"),
            P("dp"),
            P("dp"),
            P("dp"),
            P("dp"),
            P("dp"),
        ),
        check_vma=False,
    )
```

```python
import functools

import jax
import jax.numpy as jnp
from jax import lax
from jax.experimental import pallas as pl
from jax.experimental.pallas import tpu as pltpu
from jax.sharding import PartitionSpec as P

D = 768
HEADS = 12
HD = 64
CL = 128
MOSTB = 16
PAIRS = HEADS // 2
WINDOW = MOSTB * CL
HALO = (MOSTB - 1) * CL
CHUNK = 512
KCHUNK = 512
TILES_AT_ONCE = 2
PACK = 4
NEG = -1e30
TERMS = 5
FF = 3072
RTILE = 256
FCHUNK = 768
SCALE2 = HD ** (-0.5) * 1.4426950408889634

EPSILON = 1e-05


def shifted(value, axis, by):
    devices = lax.axis_size(axis)
    pairs = [(i, i + by) for i in range(devices) if 0 <= i + by < devices]
    return lax.ppermute(value, axis, pairs)


def halo_parts(value):
    own = value.shape[0]
    parts = [value]
    left = HALO
    distance = 1
    while left > 0:
        take = min(own, left)
        before = shifted(value[own - take :], "seq", distance)
        after = shifted(value[:take], "seq", -distance)
        parts = [before] + parts + [after]
        left -= take
        distance += 1
    return parts


def live_tokens(runs, trim, positions):
    ends = jnp.cumsum(runs) * CL
    starts = ends - runs * CL
    lengths = runs * CL - trim
    inside = (positions[..., None] >= starts) & (positions[..., None] < starts + lengths)
    return jnp.any(inside, axis=-1)


def outer_sum(left, right):
    return lax.dot_general(
        left, right, (((0,), (0,)), ((), ())), preferred_element_type=jnp.float32
    )


def back_product(left, right):
    return lax.dot_general(
        left, right, (((1,), (1,)), ((), ())), preferred_element_type=jnp.float32
    )


def plain_product(left, right):
    return jnp.dot(left, right, preferred_element_type=jnp.float32)


def stacked(tile):
    lane = lax.broadcasted_iota(jnp.int32, tile.shape, 1)
    zero = jnp.zeros_like(tile)
    heads = tile.shape[1] // HD
    return jnp.concatenate(
        [
            jnp.where((lane >= h * HD) & (lane < (h + 1) * HD), tile, zero)
            for h in range(heads)
        ],
        axis=0,
    )


def unstacked(stack):
    heads = stack.shape[1] // HD
    lane = lax.broadcasted_iota(jnp.int32, (CL, heads * HD), 1)
    result = stack[:CL]
    for h in range(1, heads):
        result = jnp.where(lane >= h * HD, stack[h * CL : (h + 1) * CL], result)
    return result


def as_column(row):
    return jnp.broadcast_to(row, (CL, CL)).T


def lane_of(tile, lane):
    lanes = lax.broadcasted_iota(jnp.int32, tile.shape, 1)
    return jnp.sum(jnp.where(lanes == lane, tile, 0.0), axis=1, keepdims=True)


def masked(scores, cols, row_ref, begin):
    parts = []
    wide = scores.shape[1]
    for half, one in enumerate(cols):
        row = row_ref[0, half : half + 1, pl.ds(begin, wide)]
        block = scores[half * CL : (half + 1) * CL]
        col = jnp.concatenate([one] * (wide // CL), axis=1)
        parts.append(jnp.where(col == row, block, NEG))
    return jnp.concatenate(parts, axis=0)


def assemble(parts, whole):
    at = 0
    for part in parts:
        rows = part.shape[0]
        whole[at : at + rows, :] = part[...]
        at += rows


def ahead(steps, produce, consume):
    held = produce(*steps[0])
    for i, step in enumerate(steps):
        following = produce(*steps[i + 1]) if i + 1 < len(steps) else None
        consume(*step, held)
        held = following


def attend_kernel(tiles, n_parts, starts, q_ref, *refs):
    k_parts, refs = refs[:n_parts], refs[n_parts:]
    v_parts, refs = refs[:n_parts], refs[n_parts:]
    qid_ref, kid_ref, out_ref, lse_ref, k_ref, v_ref, *slots = refs
    s_refs, top_refs = slots[:2], slots[2:]
    group = pl.program_id(0)
    heads = q_ref.shape[1] // HD
    chunks = WINDOW // CHUNK
    assemble(k_parts, k_ref)
    assemble(v_parts, v_ref)

    def first_half(tile):
        begin = pl.multiple_of(starts[tile] * CL, CL)
        own = pl.multiple_of(HALO + tile * CL, CL)
        here = pl.multiple_of(tile * CL, CL)
        query = stacked(q_ref[pl.ds(here, CL), :])
        cols = [as_column(qid_ref[0, half : half + 1, pl.ds(own, CL)]) for half in range(heads)]
        return begin, query, cols

    def score(state, slot, j):
        begin, query, cols = state
        at = pl.multiple_of(begin + j * CHUNK, CL)
        scores = masked(back_product(query, k_ref[pl.ds(at, CHUNK), :]), cols, kid_ref, at)
        s_refs[slot][:, j * CHUNK : (j + 1) * CHUNK] = scores
        top = scores[:, :CL]
        for i in range(1, CHUNK // CL):
            top = jnp.maximum(top, scores[:, i * CL : (i + 1) * CL])
        if j > 0:
            top = jnp.maximum(top, top_refs[slot][...])
        top_refs[slot][...] = top

    def both(tile, slot, next_tile):
        state = first_half(next_tile)
        begin = pl.multiple_of(starts[tile] * CL, CL)
        own = pl.multiple_of(HALO + tile * CL, CL)
        here = pl.multiple_of(tile * CL, CL)
        peak = jnp.max(top_refs[slot][...], axis=1, keepdims=True)
        total = jnp.zeros((heads * CL, CL), jnp.float32)
        result = jnp.zeros((heads * CL, heads * HD), jnp.float32)
        for j in range(chunks):
            score(state, 1 - slot, j)
            at = pl.multiple_of(begin + j * CHUNK, CL)
            weights = jnp.exp2((s_refs[slot][:, j * CHUNK : (j + 1) * CHUNK] - peak) * SCALE2)
            for i in range(CHUNK // CL):
                total = total + weights[:, i * CL : (i + 1) * CL]
            result = result + plain_product(
                weights.astype(jnp.bfloat16), v_ref[pl.ds(at, CHUNK), :]
            )
        total = jnp.sum(total, axis=1, keepdims=True)
        result = result / total
        lse = peak + jnp.log(total) * HD**0.5
        cols = [as_column(qid_ref[0, half : half + 1, pl.ds(own, CL)]) for half in range(heads)]
        live = (cols[0] >= 0.0).astype(jnp.float32)
        live = jnp.concatenate([live] * (heads * HD // CL), axis=1)
        out_ref[pl.ds(here, CL), :] = (unstacked(result) * live).astype(jnp.bfloat16)
        lane = lax.broadcasted_iota(jnp.int32, (CL, CL), 1)
        kept = lse_ref[pl.ds(here, CL), :]
        for half in range(heads):
            first = (heads * group + half) * TERMS
            kept = jnp.where(
                (lane >= first) & (lane < first + TERMS), lse[half * CL : (half + 1) * CL], kept
            )
        lse_ref[pl.ds(here, CL), :] = kept

    def two_tiles(step, carry):
        both(2 * step, 0, 2 * step + 1)
        both(2 * step + 1, 1, jnp.minimum(2 * step + 2, tiles - 1))
        return carry

    @pl.when(group == 0)
    def _():
        lse_ref[...] = jnp.zeros_like(lse_ref)

    state = first_half(0)
    for j in range(chunks):
        score(state, 0, j)
    lax.fori_loop(0, tiles // 2, two_tiles, 0)


def query_kernel(tiles, n_parts, first_head, starts, q_ref, *refs):
    k_parts, refs = refs[:n_parts], refs[n_parts:]
    v_parts, refs = refs[:n_parts], refs[n_parts:]
    g_ref, qid_ref, kid_ref, lse_ref, delta_ref = refs[:5]
    out_ref, k_ref, v_ref = refs[-3:]
    heads = q_ref.shape[1] // HD
    head = first_head + heads * pl.program_id(0)
    assemble(k_parts, k_ref)
    assemble(v_parts, v_ref)

    def some_tiles(step, carry):
        states = {}

        def state_of(slot):
            if slot not in states:
                tile = TILES_AT_ONCE * step + slot
                own = pl.multiple_of(HALO + tile * CL, CL)
                here = pl.multiple_of(tile * CL, CL)
                lse_tile = lse_ref[pl.ds(here, CL), :]
                delta_tile = delta_ref[pl.ds(here, CL), :]
                states[slot] = dict(
                    begin=pl.multiple_of(starts[tile] * CL, CL),
                    here=here,
                    query=stacked(q_ref[pl.ds(here, CL), :]),
                    back=stacked(g_ref[pl.ds(here, CL), :]),
                    cols=[
                        as_column(qid_ref[0, half : half + 1, pl.ds(own, CL)])
                        for half in range(heads)
                    ],
                    lse=jnp.concatenate(
                        [lane_of(lse_tile, (head + half) * TERMS) for half in range(heads)], axis=0
                    ),
                    delta=jnp.concatenate(
                        [lane_of(delta_tile, (head + half) * TERMS) for half in range(heads)],
                        axis=0,
                    ),
                    result=jnp.zeros((heads * CL, heads * HD), jnp.float32),
                )
            return states[slot]

        def produce(slot, j):
            state = state_of(slot)
            at = pl.multiple_of(state["begin"] + j * CHUNK, CL)
            scores = back_product(state["query"], k_ref[pl.ds(at, CHUNK), :])
            return scores, back_product(state["back"], v_ref[pl.ds(at, CHUNK), :])

        def consume(slot, j, held):
            state = state_of(slot)
            at = pl.multiple_of(state["begin"] + j * CHUNK, CL)
            scores, back_probs = held
            scores = masked((scores - state["lse"]) * SCALE2, state["cols"], kid_ref, at)
            back_scores = jnp.exp2(scores) * (back_probs - state["delta"])
            state["result"] = state["result"] + plain_product(
                back_scores.astype(jnp.bfloat16), k_ref[pl.ds(at, CHUNK), :]
            )
            if j == WINDOW // CHUNK - 1:
                out_ref[pl.ds(state["here"], CL), :] = (
                    unstacked(state["result"]) * HD ** (-0.5)
                ).astype(jnp.bfloat16)

        ahead(
            [(slot, j) for slot in range(TILES_AT_ONCE) for j in range(WINDOW // CHUNK)],
            produce,
            consume,
        )
        return carry

    lax.fori_loop(0, tiles // TILES_AT_ONCE, some_tiles, 0)


def key_kernel(tiles, n_parts, first_pair, starts, k_ref, v_ref, *refs):
    q_parts, refs = refs[:n_parts], refs[n_parts:]
    g_parts, refs = refs[:n_parts], refs[n_parts:]
    a_parts, refs = refs[:n_parts], refs[n_parts:]
    qid_ref, kid_ref = refs[:2]
    out_ref, q_ref, g_ref = refs[-3:]
    step_pair = pl.program_id(0)
    pair = first_pair + step_pair
    at = 0
    for q_part, g_part, a_part in zip(q_parts, g_parts, a_parts):
        rows = q_part.shape[0]
        q_ref[at : at + rows, : 2 * HD] = q_part[...]
        q_ref[at : at + rows, 2 * HD :] = a_part[...]
        g_ref[at : at + rows, : 2 * HD] = g_part[...]
        g_ref[at : at + rows, 2 * HD :] = a_part[...]
        at += rows

    lane = lax.broadcasted_iota(jnp.int32, (CL, CL), 1)
    lse_pick, delta_pick = [], []
    for half in range(2):
        first = (2 * pair + half) * TERMS
        lse_pick.append(jnp.where((lane >= first) & (lane < first + 3), -1.0, 0.0))
        delta_pick.append(jnp.where((lane >= first + 3) & (lane < first + TERMS), -1.0, 0.0))
    lse_pick = jnp.concatenate(lse_pick, axis=0).astype(jnp.bfloat16)
    delta_pick = jnp.concatenate(delta_pick, axis=0).astype(jnp.bfloat16)
    key_lanes = pl.ds(pl.multiple_of(step_pair * 2 * HD, 2 * HD), 2 * HD)
    value_lanes = pl.ds(
        pl.multiple_of(out_ref.shape[1] // 2 + step_pair * 2 * HD, 2 * HD), 2 * HD
    )

    def some_tiles(step, carry):
        states = {}

        def state_of(slot):
            if slot not in states:
                tile = TILES_AT_ONCE * step + slot
                own = pl.multiple_of(HALO + tile * CL, CL)
                here = pl.multiple_of(tile * CL, CL)
                states[slot] = dict(
                    begin=pl.multiple_of(starts[tile] * CL, CL),
                    here=here,
                    keys=jnp.concatenate([stacked(k_ref[pl.ds(here, CL), :]), lse_pick], axis=1),
                    values=jnp.concatenate(
                        [stacked(v_ref[pl.ds(here, CL), :]), delta_pick], axis=1
                    ),
                    cols=[
                        as_column(kid_ref[0, half : half + 1, pl.ds(own, CL)]) for half in range(2)
                    ],
                    key_sum=jnp.zeros((2 * CL, 2 * HD), jnp.float32),
                    value_sum=jnp.zeros((2 * CL, 2 * HD), jnp.float32),
                )
            return states[slot]

        def produce(slot, j):
            state = state_of(slot)
            at = pl.multiple_of(state["begin"] + j * KCHUNK, CL)
            scores = back_product(state["keys"], q_ref[pl.ds(at, KCHUNK), :])
            return scores, back_product(state["values"], g_ref[pl.ds(at, KCHUNK), :])

        def consume(slot, j, held):
            state = state_of(slot)
            at = pl.multiple_of(state["begin"] + j * KCHUNK, CL)
            scores, back_probs = held
            probs = jnp.exp2(masked(scores * SCALE2, state["cols"], qid_ref, at))
            back_scores = probs * back_probs
            state["value_sum"] = state["value_sum"] + plain_product(
                probs.astype(jnp.bfloat16), g_ref[pl.ds(at, KCHUNK), : 2 * HD]
            )
            state["key_sum"] = state["key_sum"] + plain_product(
                back_scores.astype(jnp.bfloat16), q_ref[pl.ds(at, KCHUNK), : 2 * HD]
            )
            if j == WINDOW // KCHUNK - 1:
                rows = pl.ds(state["here"], CL)
                out_ref[rows, key_lanes] = (
                    unstacked(state["key_sum"]) * HD ** (-0.5)
                ).astype(jnp.bfloat16)
                out_ref[rows, value_lanes] = unstacked(state["value_sum"]).astype(jnp.bfloat16)

        ahead(
            [(slot, j) for slot in range(TILES_AT_ONCE) for j in range(WINDOW // KCHUNK)],
            produce,
            consume,
        )
        return carry

    lax.fori_loop(0, tiles // TILES_AT_ONCE, some_tiles, 0)


def lane_block(rows, first, heads=2):
    return pl.BlockSpec((rows, heads * HD), lambda pair, starts: (0, first + pair))


def fixed_lanes(rows, block):
    return pl.BlockSpec((rows, 2 * HD), lambda pair, starts: (0, block))


def row_block(columns, first, heads=2):
    return pl.BlockSpec((1, heads, columns), lambda pair, starts: (first + pair, 0, 0))


UNREAD = pl.BlockSpec(memory_space=pl.ANY)


VMEM_LIMIT = 60 * 1024 * 1024


def strip_call(kernel, pairs, in_specs, out_specs, out_shape, scratch, args, aliases=None):
    return pl.pallas_call(
        kernel,
        out_shape=out_shape,
        grid_spec=pltpu.PrefetchScalarGridSpec(
            num_scalar_prefetch=1,
            grid=(pairs,),
            in_specs=in_specs,
            out_specs=out_specs,
            scratch_shapes=scratch,
        ),
        input_output_aliases=aliases or {},
        compiler_params=pltpu.CompilerParams(vmem_limit_bytes=VMEM_LIMIT),
    )(*args)


def gelu_terms(value):
    t = 1.0 / (1.0 + (0.3275911 * 0.7071067811865476) * jnp.abs(value))
    bell = jnp.exp2(value * value * (-0.5 * 1.4426950408889634))
    tail = 0.5 * 1.061405429
    for term in (-0.5 * 1.453152027, 0.5 * 1.421413741, -0.5 * 0.284496736, 0.5 * 0.254829592):
        tail = tail * t + term
    tail = tail * t * bell
    cdf = jnp.where(value >= 0.0, 1.0 - tail, tail)
    return value * cdf, cdf + value * (0.3989422804014327 * bell)


def normalised(values):
    mean = jnp.mean(values, axis=-1, keepdims=True)
    centre = values - mean
    rate = lax.rsqrt(jnp.mean(centre * centre, axis=-1, keepdims=True) + EPSILON)
    return centre * rate, rate


def norm_back(scaled, unit, rate):
    first = jnp.mean(scaled, axis=-1, keepdims=True)
    second = jnp.mean(scaled * unit, axis=-1, keepdims=True)
    return rate * (scaled - first - unit * second)


def row_sums(values):
    rows, columns = values.shape
    return jnp.sum(values.reshape(rows // 8, 8, columns), axis=0)


def chain_kernel(
    att_ref,
    tok_ref,
    cot_ref,
    live_ref,
    lse_ref,
    mix_ref,
    up_ref,
    down_ref,
    vec_ref,
    bias_up_ref,
    spread_ref,
    out_ref,
    act_ref,
    upr_ref,
    hid_ref,
    pre_ref,
    mixr_ref,
    mixed_ref,
    back_ref,
    delta_ref,
    sum_ref,
    sum_up_ref,
    slope_ref,
):
    width = up_ref.shape[1]
    bias_mix, bias_down = vec_ref[0:1], vec_ref[1:2]
    gain_one, shift_one = vec_ref[2:3], vec_ref[3:4]
    gain_two, shift_two = vec_ref[4:5], vec_ref[5:6]

    @pl.when(pl.program_id(0) == 0)
    def _():
        sum_ref[...] = jnp.zeros_like(sum_ref)
        sum_up_ref[...] = jnp.zeros_like(sum_up_ref)

    attended = att_ref[...]
    mixed = plain_product(attended, mix_ref[...]) + bias_mix + tok_ref[...].astype(jnp.float32)
    unit_one, rate_one = normalised(mixed)
    hidden = unit_one * gain_one + shift_one
    hidden_rounded = hidden.astype(jnp.bfloat16)
    hid_ref[...] = hidden_rounded
    down_sum = bias_down + hidden
    for f in range(0, width, FCHUNK):
        up_sum = plain_product(hidden_rounded, up_ref[:, f : f + FCHUNK]) + (
            bias_up_ref[0:1, f : f + FCHUNK]
        )
        active, slope = gelu_terms(up_sum)
        active = active.astype(jnp.bfloat16)
        act_ref[:, f : f + FCHUNK] = active
        slope_ref[:, f : f + FCHUNK] = slope
        down_sum = down_sum + plain_product(active, down_ref[f : f + FCHUNK, :])
    unit_two, rate_two = normalised(down_sum)
    out_ref[...] = (unit_two * gain_two + shift_two).astype(jnp.bfloat16)
    cot = cot_ref[...].astype(jnp.float32)
    back_pre = norm_back(cot * gain_two, unit_two, rate_two)
    pre_rounded = back_pre.astype(jnp.bfloat16)
    pre_ref[...] = pre_rounded
    sum_ref[4] += row_sums(cot * unit_two)
    sum_ref[5] += row_sums(cot)
    sum_ref[1] += row_sums(back_pre)
    back_hidden = back_pre
    for f in range(0, width, FCHUNK):
        back_up = back_product(pre_rounded, down_ref[f : f + FCHUNK, :]) * (
            slope_ref[:, f : f + FCHUNK]
        )
        sum_up_ref[:, f : f + FCHUNK] += row_sums(back_up)
        up_rounded = back_up.astype(jnp.bfloat16)
        upr_ref[:, f : f + FCHUNK] = up_rounded
        back_hidden = back_hidden + back_product(up_rounded, up_ref[:, f : f + FCHUNK])
    sum_ref[2] += row_sums(back_hidden * unit_one)
    sum_ref[3] += row_sums(back_hidden)
    back_mixed = norm_back(back_hidden * gain_one, unit_one, rate_one)
    sum_ref[0] += row_sums(back_mixed)
    mixed_ref[...] = back_mixed
    mixed_rounded = back_mixed.astype(jnp.bfloat16)
    mixr_ref[...] = mixed_rounded
    back = back_product(mixed_rounded, mix_ref[...]).astype(jnp.bfloat16)
    back = jnp.where(live_ref[...] > 0.5, back, jnp.zeros_like(back))
    back_ref[:, : back.shape[1]] = back
    terms = back.astype(jnp.float32) * attended.astype(jnp.float32)
    high = terms.astype(jnp.bfloat16)
    low = (terms - high.astype(jnp.float32)).astype(jnp.bfloat16)
    delta = plain_product(high, spread_ref[...]) + plain_product(low, spread_ref[...])
    delta_ref[...] = delta
    lane = lax.broadcasted_iota(jnp.int32, delta.shape, 1)
    term = lane % TERMS
    whole = jnp.where(term < 3, lse_ref[...], delta)
    first = whole.astype(jnp.bfloat16)
    rest = whole - first.astype(jnp.float32)
    second = rest.astype(jnp.bfloat16)
    third = (rest - second.astype(jnp.float32)).astype(jnp.bfloat16)
    picked = jnp.where(
        (term == 0) | (term == 3),
        first.astype(jnp.float32),
        jnp.where((term == 2), third.astype(jnp.float32), second.astype(jnp.float32)),
    )
    picked = jnp.where(lane < TERMS * HEADS, picked, 0.0)
    back_ref[:, back.shape[1] :] = picked.astype(jnp.bfloat16)


def chain_call(att, tok, cot, live, lse, mix, up, down, vectors, bias_up):
    rows, width = tok.shape
    wide = up.shape[1]
    head_of = jnp.arange(width, dtype=jnp.int32)[:, None] // HD
    spread = (head_of == jnp.arange(2 * HD, dtype=jnp.int32)[None, :] // TERMS).astype(jnp.bfloat16)

    def tile(columns):
        return pl.BlockSpec((RTILE, columns), lambda i: (i, 0))

    def fixed(*shape):
        return pl.BlockSpec(shape, lambda i: (0,) * len(shape))

    bf16, f32 = jnp.bfloat16, jnp.float32
    return pl.pallas_call(
        chain_kernel,
        grid=(rows // RTILE,),
        in_specs=[
            tile(width),
            tile(width),
            tile(width),
            tile(1),
            tile(2 * HD),
            fixed(*mix.shape),
            fixed(*up.shape),
            fixed(*down.shape),
            fixed(*vectors.shape),
            fixed(*bias_up.shape),
            fixed(*spread.shape),
        ],
        out_specs=[
            tile(width),
            tile(wide),
            tile(wide),
            tile(width),
            tile(width),
            tile(width),
            tile(width),
            tile(width + 2 * HD),
            tile(2 * HD),
            fixed(6, 8, width),
            fixed(8, wide),
        ],
        out_shape=[
            jax.ShapeDtypeStruct((rows, width), bf16),
            jax.ShapeDtypeStruct((rows, wide), bf16),
            jax.ShapeDtypeStruct((rows, wide), bf16),
            jax.ShapeDtypeStruct((rows, width), bf16),
            jax.ShapeDtypeStruct((rows, width), bf16),
            jax.ShapeDtypeStruct((rows, width), bf16),
            jax.ShapeDtypeStruct((rows, width), f32),
            jax.ShapeDtypeStruct((rows, width + 2 * HD), bf16),
            jax.ShapeDtypeStruct((rows, 2 * HD), f32),
            jax.ShapeDtypeStruct((6, 8, width), f32),
            jax.ShapeDtypeStruct((8, wide), f32),
        ],
        scratch_shapes=[pltpu.VMEM((RTILE, wide), f32)],
        compiler_params=pltpu.CompilerParams(vmem_limit_bytes=VMEM_LIMIT),
    )(att, tok, cot, live, lse, mix, up, down, vectors, bias_up, spread)


def down_kernel(n_dp, core_ref, act, pre, send, keep, tmp):
    step = pl.program_id(0)
    core = core_ref[0]
    down_rows = FF // n_dp
    tmp[...] = outer_sum(act[...], pre[...]).astype(jnp.bfloat16)
    per = D // down_rows
    for b in range(per):
        block = step * per + b
        x = block // 2
        rows = tmp[b * down_rows : (b + 1) * down_rows, :]

        @pl.when(lax.rem(block, 2) == core)
        def _():
            keep[pl.ds(x, 1)] = rows[None]

        @pl.when(lax.rem(block, 2) != core)
        def _():
            send[pl.ds(x, 1)] = rows[None]


def up_kernel(n_dp, core_ref, hid, upr, att, mixr, small, send, keep, tmp):
    step = pl.program_id(0)
    core = core_ref[0]
    pieces = FF // D
    part_rows = D // n_dp

    def put(x, row, rows, begin):
        mine = pl.multiple_of(begin + core * rows, 16)
        other = pl.multiple_of(begin + (1 - core) * rows, 16)
        keep[x, pl.ds(row, rows), :] = tmp[pl.ds(mine, rows), :]
        send[x, pl.ds(row, rows), :] = tmp[pl.ds(other, rows), :]

    @pl.when(step < pieces)
    def _():
        tmp[...] = outer_sum(hid[...], upr[...]).astype(jnp.bfloat16)
        row = pl.multiple_of(step * part_rows, 16)
        for x in range(n_dp // 2):
            put(x, row, part_rows, 2 * x * part_rows)

    @pl.when(step == pieces)
    def _():
        tmp[...] = outer_sum(att[...], mixr[...]).astype(jnp.bfloat16)
        row = pieces * part_rows
        for x in range(n_dp // 2):
            put(x, row, part_rows, 2 * x * part_rows)
            last = row + part_rows
            keep[x, last:, :] = small[pl.ds(2 * x + core, 1), :, :][0]
            send[x, last:, :] = small[pl.ds(2 * x + 1 - core, 1), :, :][0]


def split_call(kernel, n_dp, steps, out_rows, in_specs, args):
    shape = (n_dp // 2, out_rows, D)
    return pl.pallas_call(
        functools.partial(kernel, n_dp),
        out_shape=[jax.ShapeDtypeStruct(shape, jnp.bfloat16)] * 2,
        grid_spec=pltpu.PrefetchScalarGridSpec(
            num_scalar_prefetch=1,
            grid=(steps,),
            in_specs=in_specs,
            out_specs=[pl.BlockSpec(shape, lambda i, c: (0, 0, 0))] * 2,
            scratch_shapes=[pltpu.VMEM((D, D), jnp.bfloat16)],
        ),
        compiler_params=pltpu.CompilerParams(vmem_limit_bytes=VMEM_LIMIT),
    )(*args)


def whole_block(*shape):
    return pl.BlockSpec(shape, lambda i, c: (0,) * len(shape))


def down_call(n_dp, core, act, pre):
    rows = act.shape[0]
    specs = [pl.BlockSpec((rows, D), lambda i, c: (0, i)), whole_block(rows, D)]
    return split_call(down_kernel, n_dp, FF // D, FF // n_dp, specs, (core, act, pre))


def up_call(n_dp, core, hid, upr, att, mixr, small):
    rows = hid.shape[0]
    pieces = FF // D
    specs = [
        whole_block(rows, D),
        pl.BlockSpec((rows, D), lambda i, c: (0, jnp.minimum(i, pieces - 1))),
        whole_block(rows, D),
        whole_block(rows, D),
        whole_block(*small.shape),
    ]
    out_rows = (pieces + 1) * (D // n_dp) + small.shape[1]
    return split_call(
        up_kernel, n_dp, pieces + 1, out_rows, specs, (core, hid, upr, att, mixr, small)
    )


def swap(value, axis, bit):
    devices = lax.axis_size(axis)
    return lax.ppermute(value, axis, [(i, i ^ bit) for i in range(devices)])


def half_of(blocks, which):
    paired = blocks.reshape((blocks.shape[0] // 2, 2) + blocks.shape[1:])
    return lax.dynamic_index_in_dim(paired, which, 1, keepdims=False)


def added(left, right):
    return (left.astype(jnp.float32) + right.astype(jnp.float32)).astype(jnp.bfloat16)


def dp_gather(shard, dp_rank):
    blocks = shard[None]
    bit = lax.axis_size("dp") // 2
    while bit >= 1:
        got = swap(blocks, "dp", bit)
        high = ((dp_rank // bit) % 2) == 1
        first = jnp.where(high, got, blocks)
        second = jnp.where(high, blocks, got)
        blocks = jnp.stack([first, second], axis=1).reshape((-1,) + shard.shape)
        bit //= 2
    return blocks.reshape((-1,) + shard.shape[1:])


def dp_rest(blocks, dp_rank):
    bit = 2
    while blocks.shape[0] > 1:
        mine = (dp_rank // bit) % 2
        got = swap(half_of(blocks, 1 - mine), "dp", bit)
        blocks = added(half_of(blocks, mine), got)
        bit *= 2
    return blocks[0]


def cluster_ids(group_order, own_start, span):
    padded = jnp.pad(group_order, ((0, 0), (HALO, HALO)), constant_values=-(1 << 24))
    wanted = lax.dynamic_slice_in_dim(padded, own_start, span, 1) - (own_start - HALO)
    tile_of = wanted >> 7
    lane_of_token = wanted & (CL - 1)
    cluster = (jnp.arange(span, dtype=jnp.int32) >> 7) + 1
    tile_hot = jnp.where(
        tile_of[:, :, None] == jnp.arange(span // CL, dtype=jnp.int32), cluster[None, :, None], 0
    ).astype(jnp.bfloat16)
    lane_hot = (lane_of_token[:, :, None] == jnp.arange(CL, dtype=jnp.int32)).astype(jnp.bfloat16)
    table = jnp.einsum("hpt,hpl->htl", tile_hot, lane_hot, preferred_element_type=jnp.float32)
    return table.reshape(HEADS, span) - 1.0


def on_device(
    tokens,
    input_weight,
    output_weight,
    up_weight,
    down_weight,
    output_bias,
    up_bias,
    down_bias,
    first_gain,
    first_shift,
    second_gain,
    second_shift,
    document_runs,
    document_trim,
    cluster_order,
    cotangent,
):
    bf16, f32 = jnp.bfloat16, jnp.float32
    n_dp = lax.axis_size("dp")
    n_seq = lax.axis_size("seq")
    dp_rank = lax.axis_index("dp")
    seq_rank = lax.axis_index("seq")
    inputs = tokens[0]
    tok_dev = inputs.shape[0]
    tiles = tok_dev // CL
    span = tok_dev + 2 * HALO
    own_start = seq_rank * tok_dev

    token_parts = halo_parts(inputs)
    n_parts = len(token_parts)

    weight_in = dp_gather(input_weight, dp_rank)
    vectors = [output_bias, down_bias, first_gain, first_shift, second_gain, second_shift]
    packed = jnp.concatenate(vectors + [up_bias])
    pad_rows = -(-packed.shape[0] // (16 * D)) * 16
    packed = jnp.pad(packed, (0, pad_rows * D - packed.shape[0])).reshape(pad_rows, D)
    mix_rows = output_weight.shape[0]
    mix_all = lax.all_gather(jnp.concatenate([output_weight, packed], 0), "dp", axis=0)
    weight_up = lax.all_gather(up_weight, "dp", axis=0, tiled=True)
    weight_down = lax.all_gather(down_weight, "dp", axis=0, tiled=True)
    weight_mix = mix_all[:, :mix_rows].reshape(D, D)
    small_all = mix_all[:, mix_rows:].reshape(n_dp, -1).astype(f32)
    vec = small_all[:, : 6 * mix_rows].reshape(n_dp, 6, mix_rows).transpose(1, 0, 2).reshape(6, D)
    vec = jnp.pad(vec, ((0, 2), (0, 0)))
    up_part = up_bias.shape[0]
    bias_up = small_all[:, 6 * mix_rows : 6 * mix_rows + up_part].reshape(1, n_dp * up_part)
    bias_up = jnp.pad(bias_up, ((0, 7), (0, 0)))

    runs = document_runs[0]
    first_cluster = jnp.cumsum(runs) - runs
    own_clusters = seq_rank * tiles + jnp.arange(tiles, dtype=jnp.int32)
    doc_start = jnp.max(
        jnp.where(first_cluster[None, :] <= own_clusters[:, None], first_cluster[None, :], 0), axis=1
    )
    starts = (doc_start - seq_rank * tiles + (MOSTB - 1)).astype(jnp.int32)

    cids = cluster_ids(cluster_order[0], own_start, span)
    positions = own_start - HALO + jnp.arange(span, dtype=jnp.int32)
    live = live_tokens(runs, document_trim[0], positions)
    usable = live[None, :] & (cids >= 0.0)
    key_ids = jnp.where(usable, cids, -1.0).reshape(PAIRS, 2, span)
    query_ids = jnp.where(usable, cids, -2.0).reshape(PAIRS, 2, span)
    own_live = live[HALO : HALO + tok_dev, None].astype(f32)

    projected = [plain_product(part, weight_in).astype(bf16) for part in token_parts]
    own = projected[n_parts // 2]
    heights = [part.shape[0] for part in token_parts]

    groups = HEADS // PACK
    group_lanes = PACK * HD
    group_key_ids = key_ids.reshape(groups, PACK, span)
    group_query_ids = query_ids.reshape(groups, PACK, span)
    group_scratch = pltpu.VMEM((span, group_lanes), bf16)

    def group_parts(third, first):
        return [lane_block(rows, third * groups + first, PACK) for rows in heights]

    attended, lse = strip_call(
        functools.partial(attend_kernel, tiles, n_parts),
        groups,
        [lane_block(tok_dev, 0, PACK)]
        + group_parts(1, 0)
        + group_parts(2, 0)
        + [row_block(span, 0, PACK), row_block(span, 0, PACK)],
        [lane_block(tok_dev, 0, PACK), fixed_lanes(tok_dev, 0)],
        [
            jax.ShapeDtypeStruct((tok_dev, D), bf16),
            jax.ShapeDtypeStruct((tok_dev, 2 * HD), f32),
        ],
        [group_scratch, group_scratch]
        + [pltpu.VMEM((PACK * CL, WINDOW), f32)] * 2
        + [pltpu.VMEM((PACK * CL, CL), f32)] * 2,
        (starts, own, *projected, *projected, group_query_ids, group_key_ids),
    )

    (
        result,
        active,
        up_rounded,
        hidden_rounded,
        pre_rounded,
        mixed_rounded,
        back_mixed,
        back_own,
        delta,
        sums,
        sums_up,
    ) = chain_call(
        attended,
        inputs,
        cotangent[0],
        own_live,
        lse,
        weight_mix,
        weight_up,
        weight_down,
        vec,
        bias_up,
    )
    back_parts = halo_parts(back_own)

    small = jnp.concatenate(
        [
            jnp.sum(sums, axis=1).reshape(6, n_dp, mix_rows).transpose(1, 0, 2).reshape(n_dp, -1),
            jnp.sum(sums_up, axis=0).reshape(n_dp, -1),
        ],
        axis=1,
    ).astype(bf16)
    unit = 8 * n_seq
    fixed_rows = (FF // D + 1) * (D // n_dp)
    small_rows = -(-(fixed_rows + -(-small.shape[1] // D)) // unit) * unit - fixed_rows
    small = jnp.pad(small, ((0, 0), (0, small_rows * D - small.shape[1])))
    small = small.reshape(n_dp, small_rows, D)
    core = (dp_rank % 2).astype(jnp.int32).reshape(1)
    down_send, down_keep = down_call(n_dp, core, active, pre_rounded)
    up_send, up_keep = up_call(
        n_dp, core, hidden_rounded, up_rounded, attended, mixed_rounded, small
    )
    down_got = swap(down_send, "dp", 1)
    up_got = swap(up_send, "dp", 1)

    def query_strip(first, *needs):
        buffer = needs[:1] if first > 0 else ()
        in_specs = (
            [lane_block(tok_dev, first, PACK)]
            + group_parts(1, first)
            + group_parts(2, first)
            + [
                lane_block(tok_dev, first, PACK),
                row_block(span, first, PACK),
                row_block(span, first, PACK),
                fixed_lanes(tok_dev, 0),
                fixed_lanes(tok_dev, 0),
            ]
            + [UNREAD] * len(needs)
        )
        return strip_call(
            functools.partial(query_kernel, tiles, n_parts, first * PACK),
            1,
            in_specs,
            lane_block(tok_dev, first, PACK),
            jax.ShapeDtypeStruct((tok_dev, D), bf16),
            [group_scratch, group_scratch],
            (
                starts,
                own,
                *projected,
                *projected,
                back_own,
                group_query_ids,
                group_key_ids,
                lse,
                delta,
                *needs,
            ),
            {len(in_specs) + 1 - len(needs): 0} if buffer else None,
        )

    key_pairs = PACK // 2
    pair_scratch = pltpu.VMEM((span, 4 * HD), bf16)

    def key_strip(first, *needs):
        buffer = needs[:1] if first > 0 else ()
        pair = first * key_pairs

        def parts(third):
            return [lane_block(rows, third * PAIRS + pair) for rows in heights]

        in_specs = (
            [lane_block(tok_dev, PAIRS + pair), lane_block(tok_dev, 2 * PAIRS + pair)]
            + parts(0)
            + parts(0)
            + [fixed_lanes(rows, PAIRS) for rows in heights]
            + [row_block(span, pair), row_block(span, pair)]
            + [UNREAD] * len(needs)
        )
        return strip_call(
            functools.partial(key_kernel, tiles, n_parts, pair),
            key_pairs,
            in_specs,
            pl.BlockSpec((tok_dev, 2 * group_lanes), lambda step, starts: (0, first)),
            jax.ShapeDtypeStruct((tok_dev, 2 * D), bf16),
            [pair_scratch, pair_scratch],
            (
                starts,
                own,
                own,
                *projected,
                *back_parts,
                *back_parts,
                query_ids,
                key_ids,
                *needs,
            ),
            {len(in_specs) + 1 - len(needs): 0} if buffer else None,
        )

    def scatter(share):
        rows, columns = share.shape
        return lax.all_to_all(
            share.reshape(n_seq, rows // n_seq, columns), "seq", split_axis=0, concat_axis=0
        )

    def summed(pieces):
        return jnp.sum(pieces.astype(f32), axis=0).astype(bf16)

    def copies(mine):
        rows, columns = mine.shape
        sent = jnp.broadcast_to(mine[None], (n_seq, rows, columns))
        got = lax.all_to_all(sent, "seq", split_axis=0, concat_axis=0)
        return got.reshape(n_seq * rows, columns)

    def scatter_all(grad):
        rows, columns = grad.shape
        parts = n_dp * n_seq
        return lax.all_to_all(
            grad.astype(bf16).reshape(parts, rows // parts, columns),
            ("dp", "seq"),
            split_axis=0,
            concat_axis=0,
        )

    back_q = query_strip(0, down_send, up_send)
    down_sum = added(down_keep, down_got)
    up_sum = added(up_keep, up_got)
    back_q = query_strip(1, back_q, down_sum, up_sum)
    down_share = dp_rest(down_sum, dp_rank)
    back_q = query_strip(2, back_q, down_share)
    down_pieces = scatter(down_share)
    grad_q = outer_sum(inputs, back_q).astype(bf16)
    q_pieces = scatter_all(grad_q)
    up_share = dp_rest(up_sum, dp_rank)
    back_kv = key_strip(0, back_q, grad_q)
    up_pieces = scatter(up_share)
    down_mine = summed(down_pieces)
    back_kv = key_strip(1, back_kv, up_share, down_mine)
    down_all = lax.all_gather(down_mine, "seq", axis=0, tiled=True)
    cut = 2 * group_lanes * (groups - 1)
    grad_early = outer_sum(inputs, back_kv[:, :cut]).astype(bf16)
    early_pieces = scatter_all(grad_early)
    q_mine = summed(q_pieces)
    up_mine = summed(up_pieces)
    back_kv = key_strip(2, back_kv, grad_early, q_mine, up_mine)
    up_all = copies(up_mine)
    q_all = copies(q_mine)
    grad_late = outer_sum(inputs, back_kv[:, cut:]).astype(bf16)
    late_pieces = scatter_all(grad_late)
    early_all = copies(summed(early_pieces))
    late_all = copies(summed(late_pieces))

    kv_weight = (
        weight_in[:, D:]
        .reshape(D, 2, groups, group_lanes)
        .transpose(0, 2, 1, 3)
        .reshape(D, 2 * D)
    )
    input_grad = (
        back_mixed + back_product(back_q, weight_in[:, :D]) + back_product(back_kv, kv_weight)
    )
    kv_all = jnp.concatenate([early_all, late_all], axis=1)
    kv_all = kv_all.reshape(-1, groups, 2, group_lanes).transpose(0, 2, 1, 3).reshape(-1, 2 * D)
    grad_in_total = jnp.concatenate([q_all, kv_all], axis=1).astype(f32)
    part_rows = D // n_dp
    up_rows = (FF // D) * part_rows
    grad_down = down_all.astype(f32)
    grad_up = (
        up_all[:up_rows]
        .reshape(FF // D, part_rows, D)
        .transpose(1, 0, 2)
        .reshape(part_rows, FF)
        .astype(f32)
    )
    grad_mix = up_all[up_rows : up_rows + part_rows].astype(f32)
    flat = up_all[up_rows + part_rows :].reshape(-1).astype(f32)
    vectors_out = [flat[i * part_rows : (i + 1) * part_rows] for i in range(6)]
    bias_up_out = flat[6 * part_rows : 6 * part_rows + FF // n_dp]
    return (
        result[None],
        input_grad[None],
        grad_in_total,
        grad_mix,
        grad_up,
        grad_down,
        vectors_out[0],
        bias_up_out,
        vectors_out[1],
        *vectors_out[2:],
    )


def solution(mesh):
    placed = (
        P("dp", "seq", None),
        P("dp", None),
        P("dp", None),
        P("dp", None),
        P("dp", None),
        P("dp"),
        P("dp"),
        P("dp"),
        P("dp"),
        P("dp"),
        P("dp"),
        P("dp"),
        P("dp", None),
        P("dp", None),
        P("dp", None, None),
        P("dp", "seq", None),
    )
    return jax.shard_map(
        on_device,
        mesh=mesh,
        in_specs=placed,
        out_specs=(
            P("dp", "seq", None),
            P("dp", "seq", None),
            P("dp", None),
            P("dp", None),
            P("dp", None),
            P("dp", None),
            P("dp"),
            P("dp"),
            P("dp"),
            P("dp"),
            P("dp"),
            P("dp"),
            P("dp"),
        ),
        check_vma=False,
    )
```

```python
import functools

import jax
import jax.numpy as jnp
from jax import lax
from jax.experimental import pallas as pl
from jax.experimental.pallas import tpu as pltpu
from jax.sharding import PartitionSpec as P

D = 768
HEADS = 12
HD = 64
CL = 128
MOSTB = 16
PAIRS = HEADS // 2
WINDOW = MOSTB * CL
HALO = (MOSTB - 1) * CL
CHUNK = 512
KCHUNK = 512
TILES_AT_ONCE = 2
PACK = 4
NEG = -1e30
TERMS = 5
FF = 3072
RTILE = 256
FCHUNK = 768
SCALE2 = HD ** (-0.5) * 1.4426950408889634

EPSILON = 1e-05


def shifted(value, axis, by):
    devices = lax.axis_size(axis)
    pairs = [(i, i + by) for i in range(devices) if 0 <= i + by < devices]
    return lax.ppermute(value, axis, pairs)


def halo_parts(value):
    own = value.shape[0]
    parts = [value]
    left = HALO
    distance = 1
    while left > 0:
        take = min(own, left)
        before = shifted(value[own - take :], "seq", distance)
        after = shifted(value[:take], "seq", -distance)
        parts = [before] + parts + [after]
        left -= take
        distance += 1
    return parts


def live_tokens(runs, trim, positions):
    ends = jnp.cumsum(runs) * CL
    starts = ends - runs * CL
    lengths = runs * CL - trim
    inside = (positions[..., None] >= starts) & (positions[..., None] < starts + lengths)
    return jnp.any(inside, axis=-1)


def outer_sum(left, right):
    return lax.dot_general(
        left, right, (((0,), (0,)), ((), ())), preferred_element_type=jnp.float32
    )


def back_product(left, right):
    return lax.dot_general(
        left, right, (((1,), (1,)), ((), ())), preferred_element_type=jnp.float32
    )


def plain_product(left, right):
    return jnp.dot(left, right, preferred_element_type=jnp.float32)


def stacked(tile):
    lane = lax.broadcasted_iota(jnp.int32, tile.shape, 1)
    zero = jnp.zeros_like(tile)
    heads = tile.shape[1] // HD
    return jnp.concatenate(
        [
            jnp.where((lane >= h * HD) & (lane < (h + 1) * HD), tile, zero)
            for h in range(heads)
        ],
        axis=0,
    )


def unstacked(stack):
    heads = stack.shape[1] // HD
    lane = lax.broadcasted_iota(jnp.int32, (CL, heads * HD), 1)
    result = stack[:CL]
    for h in range(1, heads):
        result = jnp.where(lane >= h * HD, stack[h * CL : (h + 1) * CL], result)
    return result


def as_column(row):
    return jnp.broadcast_to(row, (CL, CL)).T


def lane_of(tile, lane):
    lanes = lax.broadcasted_iota(jnp.int32, tile.shape, 1)
    return jnp.sum(jnp.where(lanes == lane, tile, 0.0), axis=1, keepdims=True)


def masked(scores, cols, row_ref, begin):
    parts = []
    wide = scores.shape[1]
    for half, one in enumerate(cols):
        row = row_ref[0, half : half + 1, pl.ds(begin, wide)]
        block = scores[half * CL : (half + 1) * CL]
        col = jnp.concatenate([one] * (wide // CL), axis=1)
        parts.append(jnp.where(col == row, block, NEG))
    return jnp.concatenate(parts, axis=0)


def assemble(parts, whole):
    at = 0
    for part in parts:
        rows = part.shape[0]
        whole[at : at + rows, :] = part[...]
        at += rows


def ahead(steps, produce, consume):
    held = produce(*steps[0])
    for i, step in enumerate(steps):
        following = produce(*steps[i + 1]) if i + 1 < len(steps) else None
        consume(*step, held)
        held = following


def attend_kernel(tiles, n_parts, starts, q_ref, *refs):
    k_parts, refs = refs[:n_parts], refs[n_parts:]
    v_parts, refs = refs[:n_parts], refs[n_parts:]
    qid_ref, kid_ref, out_ref, lse_ref, k_ref, v_ref, *slots = refs
    s_refs, top_refs = slots[:2], slots[2:]
    group = pl.program_id(0)
    heads = q_ref.shape[1] // HD
    chunks = WINDOW // CHUNK
    assemble(k_parts, k_ref)
    assemble(v_parts, v_ref)

    def first_half(tile):
        begin = pl.multiple_of(starts[tile] * CL, CL)
        own = pl.multiple_of(HALO + tile * CL, CL)
        here = pl.multiple_of(tile * CL, CL)
        query = stacked(q_ref[pl.ds(here, CL), :])
        cols = [as_column(qid_ref[0, half : half + 1, pl.ds(own, CL)]) for half in range(heads)]
        return begin, query, cols

    def score(state, slot, j):
        begin, query, cols = state
        at = pl.multiple_of(begin + j * CHUNK, CL)
        scores = masked(back_product(query, k_ref[pl.ds(at, CHUNK), :]), cols, kid_ref, at)
        s_refs[slot][:, j * CHUNK : (j + 1) * CHUNK] = scores
        top = scores[:, :CL]
        for i in range(1, CHUNK // CL):
            top = jnp.maximum(top, scores[:, i * CL : (i + 1) * CL])
        if j > 0:
            top = jnp.maximum(top, top_refs[slot][...])
        top_refs[slot][...] = top

    def both(tile, slot, next_tile):
        state = first_half(next_tile)
        begin = pl.multiple_of(starts[tile] * CL, CL)
        own = pl.multiple_of(HALO + tile * CL, CL)
        here = pl.multiple_of(tile * CL, CL)
        peak = jnp.max(top_refs[slot][...], axis=1, keepdims=True)
        total = jnp.zeros((heads * CL, CL), jnp.float32)
        result = jnp.zeros((heads * CL, heads * HD), jnp.float32)
        for j in range(chunks):
            score(state, 1 - slot, j)
            at = pl.multiple_of(begin + j * CHUNK, CL)
            weights = jnp.exp2((s_refs[slot][:, j * CHUNK : (j + 1) * CHUNK] - peak) * SCALE2)
            for i in range(CHUNK // CL):
                total = total + weights[:, i * CL : (i + 1) * CL]
            result = result + plain_product(
                weights.astype(jnp.bfloat16), v_ref[pl.ds(at, CHUNK), :]
            )
        total = jnp.sum(total, axis=1, keepdims=True)
        result = result / total
        lse = peak + jnp.log(total) * HD**0.5
        cols = [as_column(qid_ref[0, half : half + 1, pl.ds(own, CL)]) for half in range(heads)]
        live = (cols[0] >= 0.0).astype(jnp.float32)
        live = jnp.concatenate([live] * (heads * HD // CL), axis=1)
        out_ref[pl.ds(here, CL), :] = (unstacked(result) * live).astype(jnp.bfloat16)
        lane = lax.broadcasted_iota(jnp.int32, (CL, CL), 1)
        kept = lse_ref[pl.ds(here, CL), :]
        for half in range(heads):
            first = (heads * group + half) * TERMS
            kept = jnp.where(
                (lane >= first) & (lane < first + TERMS), lse[half * CL : (half + 1) * CL], kept
            )
        lse_ref[pl.ds(here, CL), :] = kept

    def two_tiles(step, carry):
        both(2 * step, 0, 2 * step + 1)
        both(2 * step + 1, 1, jnp.minimum(2 * step + 2, tiles - 1))
        return carry

    @pl.when(group == 0)
    def _():
        lse_ref[...] = jnp.zeros_like(lse_ref)

    state = first_half(0)
    for j in range(chunks):
        score(state, 0, j)
    lax.fori_loop(0, tiles // 2, two_tiles, 0)


def query_kernel(tiles, n_parts, first_head, starts, q_ref, *refs):
    k_parts, refs = refs[:n_parts], refs[n_parts:]
    v_parts, refs = refs[:n_parts], refs[n_parts:]
    g_ref, qid_ref, kid_ref, lse_ref, delta_ref = refs[:5]
    out_ref, k_ref, v_ref = refs[-3:]
    heads = q_ref.shape[1] // HD
    head = first_head + heads * pl.program_id(0)
    assemble(k_parts, k_ref)
    assemble(v_parts, v_ref)

    def some_tiles(step, carry):
        states = {}

        def state_of(slot):
            if slot not in states:
                tile = TILES_AT_ONCE * step + slot
                own = pl.multiple_of(HALO + tile * CL, CL)
                here = pl.multiple_of(tile * CL, CL)
                lse_tile = lse_ref[pl.ds(here, CL), :]
                delta_tile = delta_ref[pl.ds(here, CL), :]
                states[slot] = dict(
                    begin=pl.multiple_of(starts[tile] * CL, CL),
                    here=here,
                    query=stacked(q_ref[pl.ds(here, CL), :]),
                    back=stacked(g_ref[pl.ds(here, CL), :]),
                    cols=[
                        as_column(qid_ref[0, half : half + 1, pl.ds(own, CL)])
                        for half in range(heads)
                    ],
                    lse=jnp.concatenate(
                        [lane_of(lse_tile, (head + half) * TERMS) for half in range(heads)], axis=0
                    ),
                    delta=jnp.concatenate(
                        [lane_of(delta_tile, (head + half) * TERMS) for half in range(heads)],
                        axis=0,
                    ),
                    result=jnp.zeros((heads * CL, heads * HD), jnp.float32),
                )
            return states[slot]

        def produce(slot, j):
            state = state_of(slot)
            at = pl.multiple_of(state["begin"] + j * CHUNK, CL)
            scores = back_product(state["query"], k_ref[pl.ds(at, CHUNK), :])
            return scores, back_product(state["back"], v_ref[pl.ds(at, CHUNK), :])

        def consume(slot, j, held):
            state = state_of(slot)
            at = pl.multiple_of(state["begin"] + j * CHUNK, CL)
            scores, back_probs = held
            scores = masked((scores - state["lse"]) * SCALE2, state["cols"], kid_ref, at)
            back_scores = jnp.exp2(scores) * (back_probs - state["delta"])
            state["result"] = state["result"] + plain_product(
                back_scores.astype(jnp.bfloat16), k_ref[pl.ds(at, CHUNK), :]
            )
            if j == WINDOW // CHUNK - 1:
                out_ref[pl.ds(state["here"], CL), :] = (
                    unstacked(state["result"]) * HD ** (-0.5)
                ).astype(jnp.bfloat16)

        ahead(
            [(slot, j) for slot in range(TILES_AT_ONCE) for j in range(WINDOW // CHUNK)],
            produce,
            consume,
        )
        return carry

    lax.fori_loop(0, tiles // TILES_AT_ONCE, some_tiles, 0)


def key_kernel(tiles, n_parts, first_pair, starts, k_ref, v_ref, *refs):
    q_parts, refs = refs[:n_parts], refs[n_parts:]
    g_parts, refs = refs[:n_parts], refs[n_parts:]
    a_parts, refs = refs[:n_parts], refs[n_parts:]
    qid_ref, kid_ref = refs[:2]
    out_ref, q_ref, g_ref = refs[-3:]
    step_pair = pl.program_id(0)
    pair = first_pair + step_pair
    at = 0
    for q_part, g_part, a_part in zip(q_parts, g_parts, a_parts):
        rows = q_part.shape[0]
        q_ref[at : at + rows, : 2 * HD] = q_part[...]
        q_ref[at : at + rows, 2 * HD :] = a_part[...]
        g_ref[at : at + rows, : 2 * HD] = g_part[...]
        g_ref[at : at + rows, 2 * HD :] = a_part[...]
        at += rows

    lane = lax.broadcasted_iota(jnp.int32, (CL, CL), 1)
    lse_pick, delta_pick = [], []
    for half in range(2):
        first = (2 * pair + half) * TERMS
        lse_pick.append(jnp.where((lane >= first) & (lane < first + 3), -1.0, 0.0))
        delta_pick.append(jnp.where((lane >= first + 3) & (lane < first + TERMS), -1.0, 0.0))
    lse_pick = jnp.concatenate(lse_pick, axis=0).astype(jnp.bfloat16)
    delta_pick = jnp.concatenate(delta_pick, axis=0).astype(jnp.bfloat16)
    key_lanes = pl.ds(pl.multiple_of(step_pair * 2 * HD, 2 * HD), 2 * HD)
    value_lanes = pl.ds(
        pl.multiple_of(out_ref.shape[1] // 2 + step_pair * 2 * HD, 2 * HD), 2 * HD
    )

    def some_tiles(step, carry):
        states = {}

        def state_of(slot):
            if slot not in states:
                tile = TILES_AT_ONCE * step + slot
                own = pl.multiple_of(HALO + tile * CL, CL)
                here = pl.multiple_of(tile * CL, CL)
                states[slot] = dict(
                    begin=pl.multiple_of(starts[tile] * CL, CL),
                    here=here,
                    keys=jnp.concatenate([stacked(k_ref[pl.ds(here, CL), :]), lse_pick], axis=1),
                    values=jnp.concatenate(
                        [stacked(v_ref[pl.ds(here, CL), :]), delta_pick], axis=1
                    ),
                    cols=[
                        as_column(kid_ref[0, half : half + 1, pl.ds(own, CL)]) for half in range(2)
                    ],
                    key_sum=jnp.zeros((2 * CL, 2 * HD), jnp.float32),
                    value_sum=jnp.zeros((2 * CL, 2 * HD), jnp.float32),
                )
            return states[slot]

        def produce(slot, j):
            state = state_of(slot)
            at = pl.multiple_of(state["begin"] + j * KCHUNK, CL)
            scores = back_product(state["keys"], q_ref[pl.ds(at, KCHUNK), :])
            return scores, back_product(state["values"], g_ref[pl.ds(at, KCHUNK), :])

        def consume(slot, j, held):
            state = state_of(slot)
            at = pl.multiple_of(state["begin"] + j * KCHUNK, CL)
            scores, back_probs = held
            probs = jnp.exp2(masked(scores * SCALE2, state["cols"], qid_ref, at))
            back_scores = probs * back_probs
            state["value_sum"] = state["value_sum"] + plain_product(
                probs.astype(jnp.bfloat16), g_ref[pl.ds(at, KCHUNK), : 2 * HD]
            )
            state["key_sum"] = state["key_sum"] + plain_product(
                back_scores.astype(jnp.bfloat16), q_ref[pl.ds(at, KCHUNK), : 2 * HD]
            )
            if j == WINDOW // KCHUNK - 1:
                rows = pl.ds(state["here"], CL)
                out_ref[rows, key_lanes] = (
                    unstacked(state["key_sum"]) * HD ** (-0.5)
                ).astype(jnp.bfloat16)
                out_ref[rows, value_lanes] = unstacked(state["value_sum"]).astype(jnp.bfloat16)

        ahead(
            [(slot, j) for slot in range(TILES_AT_ONCE) for j in range(WINDOW // KCHUNK)],
            produce,
            consume,
        )
        return carry

    lax.fori_loop(0, tiles // TILES_AT_ONCE, some_tiles, 0)


def lane_block(rows, first, heads=2):
    return pl.BlockSpec((rows, heads * HD), lambda pair, starts: (0, first + pair))


def fixed_lanes(rows, block):
    return pl.BlockSpec((rows, 2 * HD), lambda pair, starts: (0, block))


def row_block(columns, first, heads=2):
    return pl.BlockSpec((1, heads, columns), lambda pair, starts: (first + pair, 0, 0))


UNREAD = pl.BlockSpec(memory_space=pl.ANY)


VMEM_LIMIT = 60 * 1024 * 1024


def strip_call(kernel, pairs, in_specs, out_specs, out_shape, scratch, args, aliases=None):
    return pl.pallas_call(
        kernel,
        out_shape=out_shape,
        grid_spec=pltpu.PrefetchScalarGridSpec(
            num_scalar_prefetch=1,
            grid=(pairs,),
            in_specs=in_specs,
            out_specs=out_specs,
            scratch_shapes=scratch,
        ),
        input_output_aliases=aliases or {},
        compiler_params=pltpu.CompilerParams(vmem_limit_bytes=VMEM_LIMIT),
    )(*args)


def gelu_terms(value):
    t = 1.0 / (1.0 + (0.3275911 * 0.7071067811865476) * jnp.abs(value))
    bell = jnp.exp2(value * value * (-0.5 * 1.4426950408889634))
    tail = 0.5 * 1.061405429
    for term in (-0.5 * 1.453152027, 0.5 * 1.421413741, -0.5 * 0.284496736, 0.5 * 0.254829592):
        tail = tail * t + term
    tail = tail * t * bell
    cdf = jnp.where(value >= 0.0, 1.0 - tail, tail)
    return value * cdf, cdf + value * (0.3989422804014327 * bell)


def normalised(values):
    mean = jnp.mean(values, axis=-1, keepdims=True)
    centre = values - mean
    rate = lax.rsqrt(jnp.mean(centre * centre, axis=-1, keepdims=True) + EPSILON)
    return centre * rate, rate


def norm_back(scaled, unit, rate):
    first = jnp.mean(scaled, axis=-1, keepdims=True)
    second = jnp.mean(scaled * unit, axis=-1, keepdims=True)
    return rate * (scaled - first - unit * second)


def row_sums(values):
    rows, columns = values.shape
    return jnp.sum(values.reshape(rows // 8, 8, columns), axis=0)


def chain_kernel(
    att_ref,
    tok_ref,
    cot_ref,
    live_ref,
    lse_ref,
    mix_ref,
    up_ref,
    down_ref,
    vec_ref,
    bias_up_ref,
    spread_ref,
    out_ref,
    act_ref,
    upr_ref,
    hid_ref,
    pre_ref,
    mixr_ref,
    mixed_ref,
    back_ref,
    delta_ref,
    sum_ref,
    sum_up_ref,
    slope_ref,
):
    width = up_ref.shape[1]
    bias_mix, bias_down = vec_ref[0:1], vec_ref[1:2]
    gain_one, shift_one = vec_ref[2:3], vec_ref[3:4]
    gain_two, shift_two = vec_ref[4:5], vec_ref[5:6]

    @pl.when(pl.program_id(0) == 0)
    def _():
        sum_ref[...] = jnp.zeros_like(sum_ref)
        sum_up_ref[...] = jnp.zeros_like(sum_up_ref)

    attended = att_ref[...]
    mixed = plain_product(attended, mix_ref[...]) + bias_mix + tok_ref[...].astype(jnp.float32)
    unit_one, rate_one = normalised(mixed)
    hidden = unit_one * gain_one + shift_one
    hidden_rounded = hidden.astype(jnp.bfloat16)
    hid_ref[...] = hidden_rounded
    down_sum = bias_down + hidden
    for f in range(0, width, FCHUNK):
        up_sum = plain_product(hidden_rounded, up_ref[:, f : f + FCHUNK]) + (
            bias_up_ref[0:1, f : f + FCHUNK]
        )
        active, slope = gelu_terms(up_sum)
        active = active.astype(jnp.bfloat16)
        act_ref[:, f : f + FCHUNK] = active
        slope_ref[:, f : f + FCHUNK] = slope
        down_sum = down_sum + plain_product(active, down_ref[f : f + FCHUNK, :])
    unit_two, rate_two = normalised(down_sum)
    out_ref[...] = (unit_two * gain_two + shift_two).astype(jnp.bfloat16)
    cot = cot_ref[...].astype(jnp.float32)
    back_pre = norm_back(cot * gain_two, unit_two, rate_two)
    pre_rounded = back_pre.astype(jnp.bfloat16)
    pre_ref[...] = pre_rounded
    sum_ref[4] += row_sums(cot * unit_two)
    sum_ref[5] += row_sums(cot)
    sum_ref[1] += row_sums(back_pre)
    back_hidden = back_pre
    for f in range(0, width, FCHUNK):
        back_up = back_product(pre_rounded, down_ref[f : f + FCHUNK, :]) * (
            slope_ref[:, f : f + FCHUNK]
        )
        sum_up_ref[:, f : f + FCHUNK] += row_sums(back_up)
        up_rounded = back_up.astype(jnp.bfloat16)
        upr_ref[:, f : f + FCHUNK] = up_rounded
        back_hidden = back_hidden + back_product(up_rounded, up_ref[:, f : f + FCHUNK])
    sum_ref[2] += row_sums(back_hidden * unit_one)
    sum_ref[3] += row_sums(back_hidden)
    back_mixed = norm_back(back_hidden * gain_one, unit_one, rate_one)
    sum_ref[0] += row_sums(back_mixed)
    mixed_ref[...] = back_mixed
    mixed_rounded = back_mixed.astype(jnp.bfloat16)
    mixr_ref[...] = mixed_rounded
    back = back_product(mixed_rounded, mix_ref[...]).astype(jnp.bfloat16)
    back = jnp.where(live_ref[...] > 0.5, back, jnp.zeros_like(back))
    back_ref[:, : back.shape[1]] = back
    terms = back.astype(jnp.float32) * attended.astype(jnp.float32)
    high = terms.astype(jnp.bfloat16)
    low = (terms - high.astype(jnp.float32)).astype(jnp.bfloat16)
    delta = plain_product(high, spread_ref[...]) + plain_product(low, spread_ref[...])
    delta_ref[...] = delta
    lane = lax.broadcasted_iota(jnp.int32, delta.shape, 1)
    term = lane % TERMS
    whole = jnp.where(term < 3, lse_ref[...], delta)
    first = whole.astype(jnp.bfloat16)
    rest = whole - first.astype(jnp.float32)
    second = rest.astype(jnp.bfloat16)
    third = (rest - second.astype(jnp.float32)).astype(jnp.bfloat16)
    picked = jnp.where(
        (term == 0) | (term == 3),
        first.astype(jnp.float32),
        jnp.where((term == 2), third.astype(jnp.float32), second.astype(jnp.float32)),
    )
    picked = jnp.where(lane < TERMS * HEADS, picked, 0.0)
    back_ref[:, back.shape[1] :] = picked.astype(jnp.bfloat16)


def chain_call(att, tok, cot, live, lse, mix, up, down, vectors, bias_up):
    rows, width = tok.shape
    wide = up.shape[1]
    head_of = jnp.arange(width, dtype=jnp.int32)[:, None] // HD
    spread = (head_of == jnp.arange(2 * HD, dtype=jnp.int32)[None, :] // TERMS).astype(jnp.bfloat16)

    def tile(columns):
        return pl.BlockSpec((RTILE, columns), lambda i: (i, 0))

    def fixed(*shape):
        return pl.BlockSpec(shape, lambda i: (0,) * len(shape))

    bf16, f32 = jnp.bfloat16, jnp.float32
    return pl.pallas_call(
        chain_kernel,
        grid=(rows // RTILE,),
        in_specs=[
            tile(width),
            tile(width),
            tile(width),
            tile(1),
            tile(2 * HD),
            fixed(*mix.shape),
            fixed(*up.shape),
            fixed(*down.shape),
            fixed(*vectors.shape),
            fixed(*bias_up.shape),
            fixed(*spread.shape),
        ],
        out_specs=[
            tile(width),
            tile(wide),
            tile(wide),
            tile(width),
            tile(width),
            tile(width),
            tile(width),
            tile(width + 2 * HD),
            tile(2 * HD),
            fixed(6, 8, width),
            fixed(8, wide),
        ],
        out_shape=[
            jax.ShapeDtypeStruct((rows, width), bf16),
            jax.ShapeDtypeStruct((rows, wide), bf16),
            jax.ShapeDtypeStruct((rows, wide), bf16),
            jax.ShapeDtypeStruct((rows, width), bf16),
            jax.ShapeDtypeStruct((rows, width), bf16),
            jax.ShapeDtypeStruct((rows, width), bf16),
            jax.ShapeDtypeStruct((rows, width), f32),
            jax.ShapeDtypeStruct((rows, width + 2 * HD), bf16),
            jax.ShapeDtypeStruct((rows, 2 * HD), f32),
            jax.ShapeDtypeStruct((6, 8, width), f32),
            jax.ShapeDtypeStruct((8, wide), f32),
        ],
        scratch_shapes=[pltpu.VMEM((RTILE, wide), f32)],
        compiler_params=pltpu.CompilerParams(vmem_limit_bytes=VMEM_LIMIT),
    )(att, tok, cot, live, lse, mix, up, down, vectors, bias_up, spread)


def down_kernel(n_dp, core_ref, act, pre, *refs):
    send, keep, tmp = refs[-3:]
    step = pl.program_id(0)
    core = core_ref[0]
    down_rows = FF // n_dp
    tmp[...] = outer_sum(act[...], pre[...]).astype(jnp.bfloat16)
    per = D // down_rows
    for b in range(per):
        block = step * per + b
        x = block // 2
        rows = tmp[b * down_rows : (b + 1) * down_rows, :]

        @pl.when(lax.rem(block, 2) == core)
        def _():
            keep[pl.ds(x, 1)] = rows[None]

        @pl.when(lax.rem(block, 2) != core)
        def _():
            send[pl.ds(x, 1)] = rows[None]


def up_kernel(n_dp, core_ref, hid, upr, att, mixr, small, *refs):
    send, keep, tmp = refs[-3:]
    step = pl.program_id(0)
    core = core_ref[0]
    pieces = FF // D
    part_rows = D // n_dp

    def put(x, row, rows, begin):
        mine = pl.multiple_of(begin + core * rows, 16)
        other = pl.multiple_of(begin + (1 - core) * rows, 16)
        keep[x, pl.ds(row, rows), :] = tmp[pl.ds(mine, rows), :]
        send[x, pl.ds(row, rows), :] = tmp[pl.ds(other, rows), :]

    @pl.when(step < pieces)
    def _():
        tmp[...] = outer_sum(hid[...], upr[...]).astype(jnp.bfloat16)
        row = pl.multiple_of(step * part_rows, 16)
        for x in range(n_dp // 2):
            put(x, row, part_rows, 2 * x * part_rows)

    @pl.when(step == pieces)
    def _():
        tmp[...] = outer_sum(att[...], mixr[...]).astype(jnp.bfloat16)
        row = pieces * part_rows
        for x in range(n_dp // 2):
            put(x, row, part_rows, 2 * x * part_rows)
            last = row + part_rows
            keep[x, last:, :] = small[pl.ds(2 * x + core, 1), :, :][0]
            send[x, last:, :] = small[pl.ds(2 * x + 1 - core, 1), :, :][0]


def split_call(kernel, n_dp, steps, out_rows, in_specs, args, *needs):
    shape = (n_dp // 2, out_rows, D)
    return pl.pallas_call(
        functools.partial(kernel, n_dp),
        out_shape=[jax.ShapeDtypeStruct(shape, jnp.bfloat16)] * 2,
        grid_spec=pltpu.PrefetchScalarGridSpec(
            num_scalar_prefetch=1,
            grid=(steps,),
            in_specs=in_specs + [UNREAD] * len(needs),
            out_specs=[pl.BlockSpec(shape, lambda i, c: (0, 0, 0))] * 2,
            scratch_shapes=[pltpu.VMEM((D, D), jnp.bfloat16)],
        ),
        compiler_params=pltpu.CompilerParams(vmem_limit_bytes=VMEM_LIMIT),
    )(*args, *needs)


def whole_block(*shape):
    return pl.BlockSpec(shape, lambda i, c: (0,) * len(shape))


def down_call(n_dp, core, act, pre):
    rows = act.shape[0]
    specs = [pl.BlockSpec((rows, D), lambda i, c: (0, i)), whole_block(rows, D)]
    return split_call(down_kernel, n_dp, FF // D, FF // n_dp, specs, (core, act, pre))


def up_call(n_dp, core, hid, upr, att, mixr, small, *needs):
    rows = hid.shape[0]
    pieces = FF // D
    specs = [
        whole_block(rows, D),
        pl.BlockSpec((rows, D), lambda i, c: (0, jnp.minimum(i, pieces - 1))),
        whole_block(rows, D),
        whole_block(rows, D),
        whole_block(*small.shape),
    ]
    out_rows = (pieces + 1) * (D // n_dp) + small.shape[1]
    return split_call(
        up_kernel, n_dp, pieces + 1, out_rows, specs, (core, hid, upr, att, mixr, small), *needs
    )


def swap(value, axis, bit):
    devices = lax.axis_size(axis)
    return lax.ppermute(value, axis, [(i, i ^ bit) for i in range(devices)])


def dp_gather(shard, dp_rank):
    blocks = shard[None]
    bit = lax.axis_size("dp") // 2
    while bit >= 1:
        got = swap(blocks, "dp", bit)
        high = ((dp_rank // bit) % 2) == 1
        first = jnp.where(high, got, blocks)
        second = jnp.where(high, blocks, got)
        blocks = jnp.stack([first, second], axis=1).reshape((-1,) + shard.shape)
        bit //= 2
    return blocks.reshape((-1,) + shard.shape[1:])


def row_tile(rows, limit=256):
    for size in range(min(rows, limit), 15, -1):
        if rows % size == 0 and size % 16 == 0:
            return size
    return rows


def plain_params():
    return pltpu.CompilerParams(vmem_limit_bytes=VMEM_LIMIT)


def split_add_kernel(which, keep_mine, got_mine, keep_other, got_other, *refs):
    mine, other = refs[-2:]
    mine[...] = (keep_mine[...].astype(jnp.float32) + got_mine[...].astype(jnp.float32)).astype(
        mine.dtype
    )
    other[...] = (keep_other[...].astype(jnp.float32) + got_other[...].astype(jnp.float32)).astype(
        other.dtype
    )


def split_add(keep, got, which, *needs):
    blocks, rows, columns = keep.shape
    tile = row_tile(rows)

    def spec(flip):
        def place(b, i, w):
            bit = 1 - w[0] if flip else w[0]
            return 2 * b + bit, i, 0

        return pl.BlockSpec((1, tile, columns), place)

    out = pl.BlockSpec((1, tile, columns), lambda b, i, w: (b, i, 0))
    shape = jax.ShapeDtypeStruct((blocks // 2, rows, columns), keep.dtype)
    return pl.pallas_call(
        split_add_kernel,
        out_shape=[shape, shape],
        grid_spec=pltpu.PrefetchScalarGridSpec(
            num_scalar_prefetch=1,
            grid=(blocks // 2, rows // tile),
            in_specs=[spec(False), spec(False), spec(True), spec(True)] + [UNREAD] * len(needs),
            out_specs=[out, out],
        ),
        compiler_params=plain_params(),
    )(which, keep, got, keep, got, *needs)


def add_kernel(left, right, *refs):
    out = refs[-1]
    out[...] = (left[0].astype(jnp.float32) + right[0].astype(jnp.float32)).astype(out.dtype)


def add_blocks(left, right, *needs):
    _, rows, columns = left.shape
    tile = row_tile(rows)
    spec = pl.BlockSpec((1, tile, columns), lambda i: (0, i, 0))
    return pl.pallas_call(
        add_kernel,
        grid=(rows // tile,),
        in_specs=[spec, spec] + [UNREAD] * len(needs),
        out_specs=pl.BlockSpec((tile, columns), lambda i: (i, 0)),
        out_shape=jax.ShapeDtypeStruct((rows, columns), left.dtype),
        compiler_params=plain_params(),
    )(left, right, *needs)


def pieces_kernel(pieces, *refs):
    out = refs[-1]
    total = pieces[0].astype(jnp.float32)
    for i in range(1, pieces.shape[0]):
        total = total + pieces[i].astype(jnp.float32)
    total = total.astype(out.dtype)
    for i in range(out.shape[0]):
        out[i] = total


def summed_copies(pieces, copies, *needs):
    _, rows, columns = pieces.shape
    return pl.pallas_call(
        pieces_kernel,
        in_specs=[pl.BlockSpec(memory_space=pltpu.VMEM)] + [UNREAD] * len(needs),
        out_specs=pl.BlockSpec(memory_space=pltpu.VMEM),
        out_shape=jax.ShapeDtypeStruct((copies, rows, columns), pieces.dtype),
        compiler_params=plain_params(),
    )(pieces, *needs)


def pack_kernel(weight, *refs):
    vectors, out = refs[:7], refs[-1]
    rows = weight.shape[0]
    out[:rows, :] = weight[...]
    out[rows:, :] = jnp.zeros((out.shape[0] - rows, out.shape[1]), out.dtype)
    for i, vector in enumerate(vectors):
        out[rows + i : rows + i + 1, : vector.shape[1]] = vector[...]


def packed_vectors(weight, vectors, *needs):
    rows, columns = weight.shape
    return pl.pallas_call(
        pack_kernel,
        in_specs=[pl.BlockSpec(memory_space=pltpu.VMEM)] * 8 + [UNREAD] * len(needs),
        out_specs=pl.BlockSpec(memory_space=pltpu.VMEM),
        out_shape=jax.ShapeDtypeStruct((rows + 16, columns), weight.dtype),
        compiler_params=plain_params(),
    )(weight, *[vector[None] for vector in vectors], *needs)


def cluster_ids(group_order, own_start, span):
    padded = jnp.pad(group_order, ((0, 0), (HALO, HALO)), constant_values=-(1 << 24))
    wanted = lax.dynamic_slice_in_dim(padded, own_start, span, 1) - (own_start - HALO)
    tile_of = wanted >> 7
    lane_of_token = wanted & (CL - 1)
    cluster = (jnp.arange(span, dtype=jnp.int32) >> 7) + 1
    tile_hot = jnp.where(
        tile_of[:, :, None] == jnp.arange(span // CL, dtype=jnp.int32), cluster[None, :, None], 0
    ).astype(jnp.bfloat16)
    lane_hot = (lane_of_token[:, :, None] == jnp.arange(CL, dtype=jnp.int32)).astype(jnp.bfloat16)
    table = jnp.einsum("hpt,hpl->htl", tile_hot, lane_hot, preferred_element_type=jnp.float32)
    return table.reshape(HEADS, span) - 1.0


def on_device(
    tokens,
    input_weight,
    output_weight,
    up_weight,
    down_weight,
    output_bias,
    up_bias,
    down_bias,
    first_gain,
    first_shift,
    second_gain,
    second_shift,
    document_runs,
    document_trim,
    cluster_order,
    cotangent,
):
    bf16, f32 = jnp.bfloat16, jnp.float32
    n_dp = lax.axis_size("dp")
    n_seq = lax.axis_size("seq")
    dp_rank = lax.axis_index("dp")
    seq_rank = lax.axis_index("seq")
    inputs = tokens[0]
    tok_dev = inputs.shape[0]
    tiles = tok_dev // CL
    span = tok_dev + 2 * HALO
    own_start = seq_rank * tok_dev

    token_parts = halo_parts(inputs)
    n_parts = len(token_parts)

    weight_in = dp_gather(input_weight, dp_rank)
    weight_up = lax.all_gather(up_weight, "dp", axis=0, tiled=True)
    weight_down = lax.all_gather(down_weight, "dp", axis=0, tiled=True)

    runs = document_runs[0]
    first_cluster = jnp.cumsum(runs) - runs
    own_clusters = seq_rank * tiles + jnp.arange(tiles, dtype=jnp.int32)
    doc_start = jnp.max(
        jnp.where(first_cluster[None, :] <= own_clusters[:, None], first_cluster[None, :], 0), axis=1
    )
    starts = (doc_start - seq_rank * tiles + (MOSTB - 1)).astype(jnp.int32)

    cids = cluster_ids(cluster_order[0], own_start, span)
    positions = own_start - HALO + jnp.arange(span, dtype=jnp.int32)
    live = live_tokens(runs, document_trim[0], positions)
    usable = live[None, :] & (cids >= 0.0)
    key_ids = jnp.where(usable, cids, -1.0).reshape(PAIRS, 2, span)
    query_ids = jnp.where(usable, cids, -2.0).reshape(PAIRS, 2, span)
    own_live = live[HALO : HALO + tok_dev, None].astype(f32)

    projected = [plain_product(part, weight_in).astype(bf16) for part in token_parts]
    own = projected[n_parts // 2]
    vectors = [
        output_bias,
        down_bias,
        first_gain,
        first_shift,
        second_gain,
        second_shift,
        up_bias,
    ]
    mix_rows = output_weight.shape[0]
    mix_all = lax.all_gather(packed_vectors(output_weight, vectors), "dp", axis=0)
    weight_mix = mix_all[:, :mix_rows].reshape(D, D)
    small_all = mix_all[:, mix_rows:].astype(f32)
    vec = small_all[:, :6, :mix_rows].transpose(1, 0, 2).reshape(6, D)
    vec = jnp.pad(vec, ((0, 2), (0, 0)))
    bias_up = jnp.pad(small_all[:, 6, : up_bias.shape[0]].reshape(1, FF), ((0, 7), (0, 0)))
    heights = [part.shape[0] for part in token_parts]

    groups = HEADS // PACK
    group_lanes = PACK * HD
    group_key_ids = key_ids.reshape(groups, PACK, span)
    group_query_ids = query_ids.reshape(groups, PACK, span)
    group_scratch = pltpu.VMEM((span, group_lanes), bf16)

    def group_parts(third, first):
        return [lane_block(rows, third * groups + first, PACK) for rows in heights]

    attended, lse = strip_call(
        functools.partial(attend_kernel, tiles, n_parts),
        groups,
        [lane_block(tok_dev, 0, PACK)]
        + group_parts(1, 0)
        + group_parts(2, 0)
        + [row_block(span, 0, PACK), row_block(span, 0, PACK)],
        [lane_block(tok_dev, 0, PACK), fixed_lanes(tok_dev, 0)],
        [
            jax.ShapeDtypeStruct((tok_dev, D), bf16),
            jax.ShapeDtypeStruct((tok_dev, 2 * HD), f32),
        ],
        [group_scratch, group_scratch]
        + [pltpu.VMEM((PACK * CL, WINDOW), f32)] * 2
        + [pltpu.VMEM((PACK * CL, CL), f32)] * 2,
        (starts, own, *projected, *projected, group_query_ids, group_key_ids),
    )

    (
        result,
        active,
        up_rounded,
        hidden_rounded,
        pre_rounded,
        mixed_rounded,
        back_mixed,
        back_own,
        delta,
        sums,
        sums_up,
    ) = chain_call(
        attended,
        inputs,
        cotangent[0],
        own_live,
        lse,
        weight_mix,
        weight_up,
        weight_down,
        vec,
        bias_up,
    )
    back_parts = halo_parts(back_own)

    small = jnp.concatenate(
        [
            jnp.sum(sums, axis=1).reshape(6, n_dp, mix_rows).transpose(1, 0, 2).reshape(n_dp, -1),
            jnp.sum(sums_up, axis=0).reshape(n_dp, -1),
        ],
        axis=1,
    ).astype(bf16)
    unit = 8 * n_seq
    fixed_rows = (FF // D + 1) * (D // n_dp)
    small_rows = -(-(fixed_rows + -(-small.shape[1] // D)) // unit) * unit - fixed_rows
    small = jnp.pad(small, ((0, 0), (0, small_rows * D - small.shape[1])))
    small = small.reshape(n_dp, small_rows, D)
    core = (dp_rank % 2).astype(jnp.int32).reshape(1)
    down_send, down_keep = down_call(n_dp, core, active, pre_rounded)
    up_send, up_keep = up_call(
        n_dp, core, hidden_rounded, up_rounded, attended, mixed_rounded, small, down_send
    )
    down_got = swap(down_send, "dp", 1)
    up_got = swap(up_send, "dp", 1)

    def query_strip(first, *needs):
        buffer = needs[:1] if first > 0 else ()
        in_specs = (
            [lane_block(tok_dev, first, PACK)]
            + group_parts(1, first)
            + group_parts(2, first)
            + [
                lane_block(tok_dev, first, PACK),
                row_block(span, first, PACK),
                row_block(span, first, PACK),
                fixed_lanes(tok_dev, 0),
                fixed_lanes(tok_dev, 0),
            ]
            + [UNREAD] * len(needs)
        )
        return strip_call(
            functools.partial(query_kernel, tiles, n_parts, first * PACK),
            1,
            in_specs,
            lane_block(tok_dev, first, PACK),
            jax.ShapeDtypeStruct((tok_dev, D), bf16),
            [group_scratch, group_scratch],
            (
                starts,
                own,
                *projected,
                *projected,
                back_own,
                group_query_ids,
                group_key_ids,
                lse,
                delta,
                *needs,
            ),
            {len(in_specs) + 1 - len(needs): 0} if buffer else None,
        )

    key_pairs = PACK // 2
    pair_scratch = pltpu.VMEM((span, 4 * HD), bf16)

    def key_strip(first, *needs):
        buffer = needs[:1] if first > 0 else ()
        pair = first * key_pairs

        def parts(third):
            return [lane_block(rows, third * PAIRS + pair) for rows in heights]

        in_specs = (
            [lane_block(tok_dev, PAIRS + pair), lane_block(tok_dev, 2 * PAIRS + pair)]
            + parts(0)
            + parts(0)
            + [fixed_lanes(rows, PAIRS) for rows in heights]
            + [row_block(span, pair), row_block(span, pair)]
            + [UNREAD] * len(needs)
        )
        return strip_call(
            functools.partial(key_kernel, tiles, n_parts, pair),
            key_pairs,
            in_specs,
            pl.BlockSpec((tok_dev, 2 * group_lanes), lambda step, starts: (0, first)),
            jax.ShapeDtypeStruct((tok_dev, 2 * D), bf16),
            [pair_scratch, pair_scratch],
            (
                starts,
                own,
                own,
                *projected,
                *back_parts,
                *back_parts,
                query_ids,
                key_ids,
                *needs,
            ),
            {len(in_specs) + 1 - len(needs): 0} if buffer else None,
        )

    def scatter(share):
        rows, columns = share.shape
        return lax.all_to_all(
            share.reshape(n_seq, rows // n_seq, columns), "seq", split_axis=0, concat_axis=0
        )

    def everyone(copies):
        got = lax.all_to_all(copies, "seq", split_axis=0, concat_axis=0)
        return got.reshape(-1, copies.shape[-1])

    def first_split(keep, got, *needs):
        bit = 2
        while True:
            which = ((dp_rank // bit) % 2).astype(jnp.int32).reshape(1)
            mine, other = split_add(keep, got, which, *needs)
            got = swap(other, "dp", bit)
            if mine.shape[0] == 1:
                return mine, got
            keep, bit, needs = mine, bit * 2, ()

    def scatter_all(grad):
        rows, columns = grad.shape
        parts = n_dp * n_seq
        return lax.all_to_all(
            grad.astype(bf16).reshape(parts, rows // parts, columns),
            ("dp", "seq"),
            split_axis=0,
            concat_axis=0,
        )

    down_mine, down_got = first_split(down_keep, down_got, up_send)
    back_q = query_strip(0, down_mine)
    up_mine, up_got = first_split(up_keep, up_got, back_q)
    back_q = query_strip(1, back_q, up_mine)
    down_share = add_blocks(down_mine, down_got, back_q)
    down_pieces = scatter(down_share)
    back_q = query_strip(2, back_q, down_share, *back_parts)
    grad_q = outer_sum(inputs, back_q).astype(bf16)
    q_pieces = scatter_all(grad_q)
    up_share = add_blocks(up_mine, up_got, back_q)
    up_pieces = scatter(up_share)
    back_kv = key_strip(0, back_q, grad_q, up_share)
    down_copies = summed_copies(down_pieces, n_seq, back_kv)
    down_all = everyone(down_copies)
    back_kv = key_strip(1, back_kv, down_copies)
    cut = 2 * group_lanes * (groups - 1)
    grad_early = outer_sum(inputs, back_kv[:, :cut]).astype(bf16)
    early_pieces = scatter_all(grad_early)
    up_copies = summed_copies(up_pieces, n_seq, back_kv)
    up_all = everyone(up_copies)
    q_copies = summed_copies(q_pieces, n_seq, back_kv)
    q_all = everyone(q_copies)
    back_kv = key_strip(2, back_kv, grad_early, q_copies, up_copies)
    grad_late = outer_sum(inputs, back_kv[:, cut:]).astype(bf16)
    late_pieces = scatter_all(grad_late)
    early_all = everyone(summed_copies(early_pieces, n_seq, grad_late))
    late_all = everyone(summed_copies(late_pieces, n_seq))

    kv_weight = (
        weight_in[:, D:]
        .reshape(D, 2, groups, group_lanes)
        .transpose(0, 2, 1, 3)
        .reshape(D, 2 * D)
    )
    input_grad = (
        back_mixed + back_product(back_q, weight_in[:, :D]) + back_product(back_kv, kv_weight)
    )
    kv_all = jnp.concatenate([early_all, late_all], axis=1)
    kv_all = kv_all.reshape(-1, groups, 2, group_lanes).transpose(0, 2, 1, 3).reshape(-1, 2 * D)
    grad_in_total = jnp.concatenate([q_all, kv_all], axis=1).astype(f32)
    part_rows = D // n_dp
    up_rows = (FF // D) * part_rows
    grad_down = down_all.astype(f32)
    grad_up = (
        up_all[:up_rows]
        .reshape(FF // D, part_rows, D)
        .transpose(1, 0, 2)
        .reshape(part_rows, FF)
        .astype(f32)
    )
    grad_mix = up_all[up_rows : up_rows + part_rows].astype(f32)
    flat = up_all[up_rows + part_rows :].reshape(-1).astype(f32)
    vectors_out = [flat[i * part_rows : (i + 1) * part_rows] for i in range(6)]
    bias_up_out = flat[6 * part_rows : 6 * part_rows + FF // n_dp]
    return (
        result[None],
        input_grad[None],
        grad_in_total,
        grad_mix,
        grad_up,
        grad_down,
        vectors_out[0],
        bias_up_out,
        vectors_out[1],
        *vectors_out[2:],
    )


def solution(mesh):
    placed = (
        P("dp", "seq", None),
        P("dp", None),
        P("dp", None),
        P("dp", None),
        P("dp", None),
        P("dp"),
        P("dp"),
        P("dp"),
        P("dp"),
        P("dp"),
        P("dp"),
        P("dp"),
        P("dp", None),
        P("dp", None),
        P("dp", None, None),
        P("dp", "seq", None),
    )
    return jax.shard_map(
        on_device,
        mesh=mesh,
        in_specs=placed,
        out_specs=(
            P("dp", "seq", None),
            P("dp", "seq", None),
            P("dp", None),
            P("dp", None),
            P("dp", None),
            P("dp", None),
            P("dp"),
            P("dp"),
            P("dp"),
            P("dp"),
            P("dp"),
            P("dp"),
            P("dp"),
        ),
        check_vma=False,
    )
```

```python
import functools

import jax
import jax.numpy as jnp
from jax import lax
from jax.experimental import pallas as pl
from jax.experimental.pallas import tpu as pltpu
from jax.sharding import PartitionSpec as P

D = 768
HEADS = 12
HD = 64
CL = 128
MOSTB = 16
PAIRS = HEADS // 2
WINDOW = MOSTB * CL
HALO = (MOSTB - 1) * CL
CHUNK = 512
KCHUNK = 512
TILES_AT_ONCE = 2
PACK = 4
NEG = -1e30
TERMS = 5
FF = 3072
RTILE = 256
FCHUNK = 768
SCALE2 = HD ** (-0.5) * 1.4426950408889634

EPSILON = 1e-05


def shifted(value, axis, by):
    devices = lax.axis_size(axis)
    pairs = [(i, i + by) for i in range(devices) if 0 <= i + by < devices]
    return lax.ppermute(value, axis, pairs)


def halo_parts(value):
    own = value.shape[0]
    parts = [value]
    left = HALO
    distance = 1
    while left > 0:
        take = min(own, left)
        before = shifted(value[own - take :], "seq", distance)
        after = shifted(value[:take], "seq", -distance)
        parts = [before] + parts + [after]
        left -= take
        distance += 1
    return parts


def live_tokens(runs, trim, positions):
    ends = jnp.cumsum(runs) * CL
    starts = ends - runs * CL
    lengths = runs * CL - trim
    inside = (positions[..., None] >= starts) & (positions[..., None] < starts + lengths)
    return jnp.any(inside, axis=-1)


def outer_sum(left, right):
    return lax.dot_general(
        left, right, (((0,), (0,)), ((), ())), preferred_element_type=jnp.float32
    )


def back_product(left, right):
    return lax.dot_general(
        left, right, (((1,), (1,)), ((), ())), preferred_element_type=jnp.float32
    )


def plain_product(left, right):
    return jnp.dot(left, right, preferred_element_type=jnp.float32)


def stacked(tile):
    lane = lax.broadcasted_iota(jnp.int32, tile.shape, 1)
    zero = jnp.zeros_like(tile)
    heads = tile.shape[1] // HD
    return jnp.concatenate(
        [
            jnp.where((lane >= h * HD) & (lane < (h + 1) * HD), tile, zero)
            for h in range(heads)
        ],
        axis=0,
    )


def unstacked(stack):
    heads = stack.shape[1] // HD
    lane = lax.broadcasted_iota(jnp.int32, (CL, heads * HD), 1)
    result = stack[:CL]
    for h in range(1, heads):
        result = jnp.where(lane >= h * HD, stack[h * CL : (h + 1) * CL], result)
    return result


def as_column(row):
    return jnp.broadcast_to(row, (CL, CL)).T


def lane_of(tile, lane):
    lanes = lax.broadcasted_iota(jnp.int32, tile.shape, 1)
    return jnp.sum(jnp.where(lanes == lane, tile, 0.0), axis=1, keepdims=True)


def masked(scores, cols, row_ref, begin):
    parts = []
    wide = scores.shape[1]
    for half, one in enumerate(cols):
        row = row_ref[0, half : half + 1, pl.ds(begin, wide)]
        block = scores[half * CL : (half + 1) * CL]
        col = jnp.concatenate([one] * (wide // CL), axis=1)
        parts.append(jnp.where(col == row, block, NEG))
    return jnp.concatenate(parts, axis=0)


def assemble(parts, whole):
    at = 0
    for part in parts:
        rows = part.shape[0]
        whole[at : at + rows, :] = part[...]
        at += rows


def ahead(steps, produce, consume):
    held = produce(*steps[0])
    for i, step in enumerate(steps):
        following = produce(*steps[i + 1]) if i + 1 < len(steps) else None
        consume(*step, held)
        held = following


def attend_kernel(tiles, n_parts, starts, q_ref, *refs):
    k_parts, refs = refs[:n_parts], refs[n_parts:]
    v_parts, refs = refs[:n_parts], refs[n_parts:]
    qid_ref, kid_ref, out_ref, lse_ref, k_ref, v_ref, *slots = refs
    s_refs, top_refs = slots[:2], slots[2:]
    group = pl.program_id(0)
    heads = q_ref.shape[1] // HD
    chunks = WINDOW // CHUNK
    assemble(k_parts, k_ref)
    assemble(v_parts, v_ref)

    def first_half(tile):
        begin = pl.multiple_of(starts[tile] * CL, CL)
        own = pl.multiple_of(HALO + tile * CL, CL)
        here = pl.multiple_of(tile * CL, CL)
        query = stacked(q_ref[pl.ds(here, CL), :])
        cols = [as_column(qid_ref[0, half : half + 1, pl.ds(own, CL)]) for half in range(heads)]
        return begin, query, cols

    def score(state, slot, j):
        begin, query, cols = state
        at = pl.multiple_of(begin + j * CHUNK, CL)
        scores = masked(back_product(query, k_ref[pl.ds(at, CHUNK), :]), cols, kid_ref, at)
        s_refs[slot][:, j * CHUNK : (j + 1) * CHUNK] = scores
        top = scores[:, :CL]
        for i in range(1, CHUNK // CL):
            top = jnp.maximum(top, scores[:, i * CL : (i + 1) * CL])
        if j > 0:
            top = jnp.maximum(top, top_refs[slot][...])
        top_refs[slot][...] = top

    def both(tile, slot, next_tile):
        state = first_half(next_tile)
        begin = pl.multiple_of(starts[tile] * CL, CL)
        own = pl.multiple_of(HALO + tile * CL, CL)
        here = pl.multiple_of(tile * CL, CL)
        peak = jnp.max(top_refs[slot][...], axis=1, keepdims=True)
        total = jnp.zeros((heads * CL, CL), jnp.float32)
        result = jnp.zeros((heads * CL, heads * HD), jnp.float32)
        for j in range(chunks):
            score(state, 1 - slot, j)
            at = pl.multiple_of(begin + j * CHUNK, CL)
            weights = jnp.exp2((s_refs[slot][:, j * CHUNK : (j + 1) * CHUNK] - peak) * SCALE2)
            for i in range(CHUNK // CL):
                total = total + weights[:, i * CL : (i + 1) * CL]
            result = result + plain_product(
                weights.astype(jnp.bfloat16), v_ref[pl.ds(at, CHUNK), :]
            )
        total = jnp.sum(total, axis=1, keepdims=True)
        result = result / total
        lse = peak + jnp.log(total) * HD**0.5
        cols = [as_column(qid_ref[0, half : half + 1, pl.ds(own, CL)]) for half in range(heads)]
        live = (cols[0] >= 0.0).astype(jnp.float32)
        live = jnp.concatenate([live] * (heads * HD // CL), axis=1)
        out_ref[pl.ds(here, CL), :] = (unstacked(result) * live).astype(jnp.bfloat16)
        lane = lax.broadcasted_iota(jnp.int32, (CL, CL), 1)
        kept = lse_ref[pl.ds(here, CL), :]
        for half in range(heads):
            first = (heads * group + half) * TERMS
            kept = jnp.where(
                (lane >= first) & (lane < first + TERMS), lse[half * CL : (half + 1) * CL], kept
            )
        lse_ref[pl.ds(here, CL), :] = kept

    def two_tiles(step, carry):
        both(2 * step, 0, 2 * step + 1)
        both(2 * step + 1, 1, jnp.minimum(2 * step + 2, tiles - 1))
        return carry

    @pl.when(group == 0)
    def _():
        lse_ref[...] = jnp.zeros_like(lse_ref)

    state = first_half(0)
    for j in range(chunks):
        score(state, 0, j)
    lax.fori_loop(0, tiles // 2, two_tiles, 0)


def query_kernel(tiles, n_parts, first_head, starts, q_ref, *refs):
    k_parts, refs = refs[:n_parts], refs[n_parts:]
    v_parts, refs = refs[:n_parts], refs[n_parts:]
    g_ref, qid_ref, kid_ref, lse_ref, delta_ref = refs[:5]
    out_ref, k_ref, v_ref = refs[-3:]
    heads = q_ref.shape[1] // HD
    head = first_head + heads * pl.program_id(0)
    assemble(k_parts, k_ref)
    assemble(v_parts, v_ref)

    def some_tiles(step, carry):
        states = {}

        def state_of(slot):
            if slot not in states:
                tile = TILES_AT_ONCE * step + slot
                own = pl.multiple_of(HALO + tile * CL, CL)
                here = pl.multiple_of(tile * CL, CL)
                lse_tile = lse_ref[pl.ds(here, CL), :]
                delta_tile = delta_ref[pl.ds(here, CL), :]
                states[slot] = dict(
                    begin=pl.multiple_of(starts[tile] * CL, CL),
                    here=here,
                    query=stacked(q_ref[pl.ds(here, CL), :]),
                    back=stacked(g_ref[pl.ds(here, CL), :]),
                    cols=[
                        as_column(qid_ref[0, half : half + 1, pl.ds(own, CL)])
                        for half in range(heads)
                    ],
                    lse=jnp.concatenate(
                        [lane_of(lse_tile, (head + half) * TERMS) for half in range(heads)], axis=0
                    ),
                    delta=jnp.concatenate(
                        [lane_of(delta_tile, (head + half) * TERMS) for half in range(heads)],
                        axis=0,
                    ),
                    result=jnp.zeros((heads * CL, heads * HD), jnp.float32),
                )
            return states[slot]

        def produce(slot, j):
            state = state_of(slot)
            at = pl.multiple_of(state["begin"] + j * CHUNK, CL)
            scores = back_product(state["query"], k_ref[pl.ds(at, CHUNK), :])
            return scores, back_product(state["back"], v_ref[pl.ds(at, CHUNK), :])

        def consume(slot, j, held):
            state = state_of(slot)
            at = pl.multiple_of(state["begin"] + j * CHUNK, CL)
            scores, back_probs = held
            scores = masked((scores - state["lse"]) * SCALE2, state["cols"], kid_ref, at)
            back_scores = jnp.exp2(scores) * (back_probs - state["delta"])
            state["result"] = state["result"] + plain_product(
                back_scores.astype(jnp.bfloat16), k_ref[pl.ds(at, CHUNK), :]
            )
            if j == WINDOW // CHUNK - 1:
                out_ref[pl.ds(state["here"], CL), :] = (
                    unstacked(state["result"]) * HD ** (-0.5)
                ).astype(jnp.bfloat16)

        ahead(
            [(slot, j) for slot in range(TILES_AT_ONCE) for j in range(WINDOW // CHUNK)],
            produce,
            consume,
        )
        return carry

    lax.fori_loop(0, tiles // TILES_AT_ONCE, some_tiles, 0)


def key_kernel(tiles, n_parts, first_pair, starts, k_ref, v_ref, *refs):
    q_parts, refs = refs[:n_parts], refs[n_parts:]
    g_parts, refs = refs[:n_parts], refs[n_parts:]
    a_parts, refs = refs[:n_parts], refs[n_parts:]
    qid_ref, kid_ref = refs[:2]
    out_ref, q_ref, g_ref = refs[-3:]
    step_pair = pl.program_id(0)
    pair = first_pair + step_pair
    at = 0
    for q_part, g_part, a_part in zip(q_parts, g_parts, a_parts):
        rows = q_part.shape[0]
        q_ref[at : at + rows, : 2 * HD] = q_part[...]
        q_ref[at : at + rows, 2 * HD :] = a_part[...]
        g_ref[at : at + rows, : 2 * HD] = g_part[...]
        g_ref[at : at + rows, 2 * HD :] = a_part[...]
        at += rows

    lane = lax.broadcasted_iota(jnp.int32, (CL, CL), 1)
    lse_pick, delta_pick = [], []
    for half in range(2):
        first = (2 * pair + half) * TERMS
        lse_pick.append(jnp.where((lane >= first) & (lane < first + 3), -1.0, 0.0))
        delta_pick.append(jnp.where((lane >= first + 3) & (lane < first + TERMS), -1.0, 0.0))
    lse_pick = jnp.concatenate(lse_pick, axis=0).astype(jnp.bfloat16)
    delta_pick = jnp.concatenate(delta_pick, axis=0).astype(jnp.bfloat16)
    key_lanes = pl.ds(pl.multiple_of(step_pair * 2 * HD, 2 * HD), 2 * HD)
    value_lanes = pl.ds(
        pl.multiple_of(out_ref.shape[1] // 2 + step_pair * 2 * HD, 2 * HD), 2 * HD
    )

    def some_tiles(step, carry):
        states = {}

        def state_of(slot):
            if slot not in states:
                tile = TILES_AT_ONCE * step + slot
                own = pl.multiple_of(HALO + tile * CL, CL)
                here = pl.multiple_of(tile * CL, CL)
                states[slot] = dict(
                    begin=pl.multiple_of(starts[tile] * CL, CL),
                    here=here,
                    keys=jnp.concatenate([stacked(k_ref[pl.ds(here, CL), :]), lse_pick], axis=1),
                    values=jnp.concatenate(
                        [stacked(v_ref[pl.ds(here, CL), :]), delta_pick], axis=1
                    ),
                    cols=[
                        as_column(kid_ref[0, half : half + 1, pl.ds(own, CL)]) for half in range(2)
                    ],
                    key_sum=jnp.zeros((2 * CL, 2 * HD), jnp.float32),
                    value_sum=jnp.zeros((2 * CL, 2 * HD), jnp.float32),
                )
            return states[slot]

        def produce(slot, j):
            state = state_of(slot)
            at = pl.multiple_of(state["begin"] + j * KCHUNK, CL)
            scores = back_product(state["keys"], q_ref[pl.ds(at, KCHUNK), :])
            return scores, back_product(state["values"], g_ref[pl.ds(at, KCHUNK), :])

        def consume(slot, j, held):
            state = state_of(slot)
            at = pl.multiple_of(state["begin"] + j * KCHUNK, CL)
            scores, back_probs = held
            probs = jnp.exp2(masked(scores * SCALE2, state["cols"], qid_ref, at))
            back_scores = probs * back_probs
            state["value_sum"] = state["value_sum"] + plain_product(
                probs.astype(jnp.bfloat16), g_ref[pl.ds(at, KCHUNK), : 2 * HD]
            )
            state["key_sum"] = state["key_sum"] + plain_product(
                back_scores.astype(jnp.bfloat16), q_ref[pl.ds(at, KCHUNK), : 2 * HD]
            )
            if j == WINDOW // KCHUNK - 1:
                rows = pl.ds(state["here"], CL)
                out_ref[rows, key_lanes] = (
                    unstacked(state["key_sum"]) * HD ** (-0.5)
                ).astype(jnp.bfloat16)
                out_ref[rows, value_lanes] = unstacked(state["value_sum"]).astype(jnp.bfloat16)

        ahead(
            [(slot, j) for slot in range(TILES_AT_ONCE) for j in range(WINDOW // KCHUNK)],
            produce,
            consume,
        )
        return carry

    lax.fori_loop(0, tiles // TILES_AT_ONCE, some_tiles, 0)


def lane_block(rows, first, heads=2):
    return pl.BlockSpec((rows, heads * HD), lambda pair, starts: (0, first + pair))


def fixed_lanes(rows, block):
    return pl.BlockSpec((rows, 2 * HD), lambda pair, starts: (0, block))


def row_block(columns, first, heads=2):
    return pl.BlockSpec((1, heads, columns), lambda pair, starts: (first + pair, 0, 0))


UNREAD = pl.BlockSpec(memory_space=pl.ANY)


VMEM_LIMIT = 60 * 1024 * 1024


def strip_call(kernel, pairs, in_specs, out_specs, out_shape, scratch, args, aliases=None):
    return pl.pallas_call(
        kernel,
        out_shape=out_shape,
        grid_spec=pltpu.PrefetchScalarGridSpec(
            num_scalar_prefetch=1,
            grid=(pairs,),
            in_specs=in_specs,
            out_specs=out_specs,
            scratch_shapes=scratch,
        ),
        input_output_aliases=aliases or {},
        compiler_params=pltpu.CompilerParams(vmem_limit_bytes=VMEM_LIMIT),
    )(*args)


def gelu_terms(value):
    t = 1.0 / (1.0 + (0.3275911 * 0.7071067811865476) * jnp.abs(value))
    bell = jnp.exp2(value * value * (-0.5 * 1.4426950408889634))
    tail = 0.5 * 1.061405429
    for term in (-0.5 * 1.453152027, 0.5 * 1.421413741, -0.5 * 0.284496736, 0.5 * 0.254829592):
        tail = tail * t + term
    tail = tail * t * bell
    cdf = jnp.where(value >= 0.0, 1.0 - tail, tail)
    return value * cdf, cdf + value * (0.3989422804014327 * bell)


def normalised(values):
    mean = jnp.mean(values, axis=-1, keepdims=True)
    centre = values - mean
    rate = lax.rsqrt(jnp.mean(centre * centre, axis=-1, keepdims=True) + EPSILON)
    return centre * rate, rate


def norm_back(scaled, unit, rate):
    first = jnp.mean(scaled, axis=-1, keepdims=True)
    second = jnp.mean(scaled * unit, axis=-1, keepdims=True)
    return rate * (scaled - first - unit * second)


def row_sums(values):
    rows, columns = values.shape
    return jnp.sum(values.reshape(rows // 8, 8, columns), axis=0)


def chain_kernel(
    att_ref,
    tok_ref,
    cot_ref,
    live_ref,
    lse_ref,
    mix_ref,
    up_ref,
    down_ref,
    vec_ref,
    bias_up_ref,
    spread_ref,
    out_ref,
    act_ref,
    upr_ref,
    hid_ref,
    pre_ref,
    mixr_ref,
    mixed_ref,
    back_ref,
    delta_ref,
    sum_ref,
    sum_up_ref,
    slope_ref,
):
    width = up_ref.shape[1]
    bias_mix, bias_down = vec_ref[0:1], vec_ref[1:2]
    gain_one, shift_one = vec_ref[2:3], vec_ref[3:4]
    gain_two, shift_two = vec_ref[4:5], vec_ref[5:6]

    @pl.when(pl.program_id(0) == 0)
    def _():
        sum_ref[...] = jnp.zeros_like(sum_ref)
        sum_up_ref[...] = jnp.zeros_like(sum_up_ref)

    attended = att_ref[...]
    mixed = plain_product(attended, mix_ref[...]) + bias_mix + tok_ref[...].astype(jnp.float32)
    unit_one, rate_one = normalised(mixed)
    hidden = unit_one * gain_one + shift_one
    hidden_rounded = hidden.astype(jnp.bfloat16)
    hid_ref[...] = hidden_rounded
    down_sum = bias_down + hidden
    for f in range(0, width, FCHUNK):
        up_sum = plain_product(hidden_rounded, up_ref[:, f : f + FCHUNK]) + (
            bias_up_ref[0:1, f : f + FCHUNK]
        )
        active, slope = gelu_terms(up_sum)
        active = active.astype(jnp.bfloat16)
        act_ref[:, f : f + FCHUNK] = active
        slope_ref[:, f : f + FCHUNK] = slope
        down_sum = down_sum + plain_product(active, down_ref[f : f + FCHUNK, :])
    unit_two, rate_two = normalised(down_sum)
    out_ref[...] = (unit_two * gain_two + shift_two).astype(jnp.bfloat16)
    cot = cot_ref[...].astype(jnp.float32)
    back_pre = norm_back(cot * gain_two, unit_two, rate_two)
    pre_rounded = back_pre.astype(jnp.bfloat16)
    pre_ref[...] = pre_rounded
    sum_ref[4] += row_sums(cot * unit_two)
    sum_ref[5] += row_sums(cot)
    sum_ref[1] += row_sums(back_pre)
    back_hidden = back_pre
    for f in range(0, width, FCHUNK):
        back_up = back_product(pre_rounded, down_ref[f : f + FCHUNK, :]) * (
            slope_ref[:, f : f + FCHUNK]
        )
        sum_up_ref[:, f : f + FCHUNK] += row_sums(back_up)
        up_rounded = back_up.astype(jnp.bfloat16)
        upr_ref[:, f : f + FCHUNK] = up_rounded
        back_hidden = back_hidden + back_product(up_rounded, up_ref[:, f : f + FCHUNK])
    sum_ref[2] += row_sums(back_hidden * unit_one)
    sum_ref[3] += row_sums(back_hidden)
    back_mixed = norm_back(back_hidden * gain_one, unit_one, rate_one)
    sum_ref[0] += row_sums(back_mixed)
    mixed_ref[...] = back_mixed
    mixed_rounded = back_mixed.astype(jnp.bfloat16)
    mixr_ref[...] = mixed_rounded
    back = back_product(mixed_rounded, mix_ref[...]).astype(jnp.bfloat16)
    back = jnp.where(live_ref[...] > 0.5, back, jnp.zeros_like(back))
    back_ref[:, : back.shape[1]] = back
    terms = back.astype(jnp.float32) * attended.astype(jnp.float32)
    high = terms.astype(jnp.bfloat16)
    low = (terms - high.astype(jnp.float32)).astype(jnp.bfloat16)
    delta = plain_product(high, spread_ref[...]) + plain_product(low, spread_ref[...])
    delta_ref[...] = delta
    lane = lax.broadcasted_iota(jnp.int32, delta.shape, 1)
    term = lane % TERMS
    whole = jnp.where(term < 3, lse_ref[...], delta)
    first = whole.astype(jnp.bfloat16)
    rest = whole - first.astype(jnp.float32)
    second = rest.astype(jnp.bfloat16)
    third = (rest - second.astype(jnp.float32)).astype(jnp.bfloat16)
    picked = jnp.where(
        (term == 0) | (term == 3),
        first.astype(jnp.float32),
        jnp.where((term == 2), third.astype(jnp.float32), second.astype(jnp.float32)),
    )
    picked = jnp.where(lane < TERMS * HEADS, picked, 0.0)
    back_ref[:, back.shape[1] :] = picked.astype(jnp.bfloat16)


def chain_call(att, tok, cot, live, lse, mix, up, down, vectors, bias_up):
    rows, width = tok.shape
    wide = up.shape[1]
    head_of = jnp.arange(width, dtype=jnp.int32)[:, None] // HD
    spread = (head_of == jnp.arange(2 * HD, dtype=jnp.int32)[None, :] // TERMS).astype(jnp.bfloat16)

    def tile(columns):
        return pl.BlockSpec((RTILE, columns), lambda i: (i, 0))

    def fixed(*shape):
        return pl.BlockSpec(shape, lambda i: (0,) * len(shape))

    bf16, f32 = jnp.bfloat16, jnp.float32
    return pl.pallas_call(
        chain_kernel,
        grid=(rows // RTILE,),
        in_specs=[
            tile(width),
            tile(width),
            tile(width),
            tile(1),
            tile(2 * HD),
            fixed(*mix.shape),
            fixed(*up.shape),
            fixed(*down.shape),
            fixed(*vectors.shape),
            fixed(*bias_up.shape),
            fixed(*spread.shape),
        ],
        out_specs=[
            tile(width),
            tile(wide),
            tile(wide),
            tile(width),
            tile(width),
            tile(width),
            tile(width),
            tile(width + 2 * HD),
            tile(2 * HD),
            fixed(6, 8, width),
            fixed(8, wide),
        ],
        out_shape=[
            jax.ShapeDtypeStruct((rows, width), bf16),
            jax.ShapeDtypeStruct((rows, wide), bf16),
            jax.ShapeDtypeStruct((rows, wide), bf16),
            jax.ShapeDtypeStruct((rows, width), bf16),
            jax.ShapeDtypeStruct((rows, width), bf16),
            jax.ShapeDtypeStruct((rows, width), bf16),
            jax.ShapeDtypeStruct((rows, width), f32),
            jax.ShapeDtypeStruct((rows, width + 2 * HD), bf16),
            jax.ShapeDtypeStruct((rows, 2 * HD), f32),
            jax.ShapeDtypeStruct((6, 8, width), f32),
            jax.ShapeDtypeStruct((8, wide), f32),
        ],
        scratch_shapes=[pltpu.VMEM((RTILE, wide), f32)],
        compiler_params=pltpu.CompilerParams(vmem_limit_bytes=VMEM_LIMIT),
    )(att, tok, cot, live, lse, mix, up, down, vectors, bias_up, spread)


def weight_kernel(n_dp, core_ref, act, pre, hid, upr, att, mixr, small, send, keep, tmp):
    step = pl.program_id(0)
    core = core_ref[0]
    pieces = FF // D
    down_rows = FF // n_dp
    part_rows = D // n_dp

    def put(x, row, rows, begin):
        mine = pl.multiple_of(begin + core * rows, 16)
        other = pl.multiple_of(begin + (1 - core) * rows, 16)
        keep[pl.ds(x, 1), pl.ds(row, rows), :] = tmp[pl.ds(mine, rows), :][None]
        send[pl.ds(x, 1), pl.ds(row, rows), :] = tmp[pl.ds(other, rows), :][None]

    @pl.when(step < pieces)
    def _():
        tmp[...] = outer_sum(act[...], pre[...]).astype(jnp.bfloat16)
        per = D // down_rows
        for b in range(per):
            block = step * per + b
            x = block // 2
            rows = tmp[b * down_rows : (b + 1) * down_rows, :]

            @pl.when(lax.rem(block, 2) == core)
            def _():
                keep[pl.ds(x, 1), 0:down_rows, :] = rows[None]

            @pl.when(lax.rem(block, 2) != core)
            def _():
                send[pl.ds(x, 1), 0:down_rows, :] = rows[None]

    @pl.when((step >= pieces) & (step < 2 * pieces))
    def _():
        tmp[...] = outer_sum(hid[...], upr[...]).astype(jnp.bfloat16)
        row = pl.multiple_of(down_rows + (step - pieces) * part_rows, 16)
        for x in range(n_dp // 2):
            put(x, row, part_rows, 2 * x * part_rows)

    @pl.when(step == 2 * pieces)
    def _():
        tmp[...] = outer_sum(att[...], mixr[...]).astype(jnp.bfloat16)
        row = down_rows + pieces * part_rows
        for x in range(n_dp // 2):
            put(x, row, part_rows, 2 * x * part_rows)
            last = row + part_rows
            rows = keep.shape[1] - last
            keep[x, last:, :] = small[pl.ds(2 * x + core, 1), :, :][0]
            send[x, last:, :] = small[pl.ds(2 * x + 1 - core, 1), :, :][0]


def weight_call(n_dp, core, act, pre, hid, upr, att, mixr, small):
    rows = act.shape[0]
    pieces = FF // D
    out_rows = FF // n_dp + (pieces + 1) * (D // n_dp) + small.shape[1]

    def fixed(*shape):
        return pl.BlockSpec(shape, lambda i, c: (0,) * len(shape))

    def stepped(first):
        return pl.BlockSpec((rows, D), lambda i, c: (0, jnp.clip(i - first, 0, pieces - 1)))

    shape = (n_dp // 2, out_rows, D)
    return pl.pallas_call(
        functools.partial(weight_kernel, n_dp),
        out_shape=[jax.ShapeDtypeStruct(shape, jnp.bfloat16)] * 2,
        grid_spec=pltpu.PrefetchScalarGridSpec(
            num_scalar_prefetch=1,
            grid=(2 * pieces + 1,),
            in_specs=[
                stepped(0),
                fixed(rows, D),
                fixed(rows, D),
                stepped(pieces),
                fixed(rows, D),
                fixed(rows, D),
                fixed(*small.shape),
            ],
            out_specs=[fixed(*shape)] * 2,
            scratch_shapes=[pltpu.VMEM((D, D), jnp.bfloat16)],
        ),
        compiler_params=pltpu.CompilerParams(vmem_limit_bytes=VMEM_LIMIT),
    )(core, act, pre, hid, upr, att, mixr, small)


def swap(value, axis, bit):
    devices = lax.axis_size(axis)
    return lax.ppermute(value, axis, [(i, i ^ bit) for i in range(devices)])


def dp_gather(shard, dp_rank):
    blocks = shard[None]
    bit = lax.axis_size("dp") // 2
    while bit >= 1:
        got = swap(blocks, "dp", bit)
        high = ((dp_rank // bit) % 2) == 1
        first = jnp.where(high, got, blocks)
        second = jnp.where(high, blocks, got)
        blocks = jnp.stack([first, second], axis=1).reshape((-1,) + shard.shape)
        bit //= 2
    return blocks.reshape((-1,) + shard.shape[1:])


def row_tile(rows, limit=256):
    for size in range(min(rows, limit), 15, -1):
        if rows % size == 0 and size % 16 == 0:
            return size
    return rows


def plain_params():
    return pltpu.CompilerParams(vmem_limit_bytes=VMEM_LIMIT)


def split_add_kernel(which, keep_mine, got_mine, keep_other, got_other, *refs):
    mine, other = refs[-2:]
    mine[...] = (keep_mine[...].astype(jnp.float32) + got_mine[...].astype(jnp.float32)).astype(
        mine.dtype
    )
    other[...] = (keep_other[...].astype(jnp.float32) + got_other[...].astype(jnp.float32)).astype(
        other.dtype
    )


def split_add(keep, got, which, *needs):
    blocks, rows, columns = keep.shape
    tile = row_tile(rows)

    def spec(flip):
        def place(b, i, w):
            bit = 1 - w[0] if flip else w[0]
            return 2 * b + bit, i, 0

        return pl.BlockSpec((1, tile, columns), place)

    out = pl.BlockSpec((1, tile, columns), lambda b, i, w: (b, i, 0))
    shape = jax.ShapeDtypeStruct((blocks // 2, rows, columns), keep.dtype)
    return pl.pallas_call(
        split_add_kernel,
        out_shape=[shape, shape],
        grid_spec=pltpu.PrefetchScalarGridSpec(
            num_scalar_prefetch=1,
            grid=(blocks // 2, rows // tile),
            in_specs=[spec(False), spec(False), spec(True), spec(True)] + [UNREAD] * len(needs),
            out_specs=[out, out],
        ),
        compiler_params=plain_params(),
    )(which, keep, got, keep, got, *needs)


def add_kernel(left, right, *refs):
    out = refs[-1]
    out[...] = (left[0].astype(jnp.float32) + right[0].astype(jnp.float32)).astype(out.dtype)


def add_blocks(left, right, *needs):
    _, rows, columns = left.shape
    tile = row_tile(rows)
    spec = pl.BlockSpec((1, tile, columns), lambda i: (0, i, 0))
    return pl.pallas_call(
        add_kernel,
        grid=(rows // tile,),
        in_specs=[spec, spec] + [UNREAD] * len(needs),
        out_specs=pl.BlockSpec((tile, columns), lambda i: (i, 0)),
        out_shape=jax.ShapeDtypeStruct((rows, columns), left.dtype),
        compiler_params=plain_params(),
    )(left, right, *needs)


def pieces_kernel(pieces, *refs):
    out = refs[-1]
    total = pieces[0].astype(jnp.float32)
    for i in range(1, pieces.shape[0]):
        total = total + pieces[i].astype(jnp.float32)
    total = total.astype(out.dtype)
    for i in range(out.shape[0]):
        out[i] = total


def summed_copies(pieces, copies, *needs):
    _, rows, columns = pieces.shape
    return pl.pallas_call(
        pieces_kernel,
        in_specs=[pl.BlockSpec(memory_space=pltpu.VMEM)] + [UNREAD] * len(needs),
        out_specs=pl.BlockSpec(memory_space=pltpu.VMEM),
        out_shape=jax.ShapeDtypeStruct((copies, rows, columns), pieces.dtype),
        compiler_params=plain_params(),
    )(pieces, *needs)


def gate_kernel(value, *refs):
    refs[-1][...] = value[...]


def gated(value, *needs):
    return pl.pallas_call(
        gate_kernel,
        in_specs=[pl.BlockSpec(memory_space=pltpu.VMEM)] + [UNREAD] * len(needs),
        out_specs=pl.BlockSpec(memory_space=pltpu.VMEM),
        out_shape=jax.ShapeDtypeStruct(value.shape, value.dtype),
        compiler_params=plain_params(),
    )(value, *needs)


def cluster_ids(group_order, own_start, span):
    padded = jnp.pad(group_order, ((0, 0), (HALO, HALO)), constant_values=-(1 << 24))
    wanted = lax.dynamic_slice_in_dim(padded, own_start, span, 1) - (own_start - HALO)
    tile_of = wanted >> 7
    lane_of_token = wanted & (CL - 1)
    cluster = (jnp.arange(span, dtype=jnp.int32) >> 7) + 1
    tile_hot = jnp.where(
        tile_of[:, :, None] == jnp.arange(span // CL, dtype=jnp.int32), cluster[None, :, None], 0
    ).astype(jnp.bfloat16)
    lane_hot = (lane_of_token[:, :, None] == jnp.arange(CL, dtype=jnp.int32)).astype(jnp.bfloat16)
    table = jnp.einsum("hpt,hpl->htl", tile_hot, lane_hot, preferred_element_type=jnp.float32)
    return table.reshape(HEADS, span) - 1.0


def on_device(
    tokens,
    input_weight,
    output_weight,
    up_weight,
    down_weight,
    output_bias,
    up_bias,
    down_bias,
    first_gain,
    first_shift,
    second_gain,
    second_shift,
    document_runs,
    document_trim,
    cluster_order,
    cotangent,
):
    bf16, f32 = jnp.bfloat16, jnp.float32
    n_dp = lax.axis_size("dp")
    n_seq = lax.axis_size("seq")
    dp_rank = lax.axis_index("dp")
    seq_rank = lax.axis_index("seq")
    inputs = tokens[0]
    tok_dev = inputs.shape[0]
    tiles = tok_dev // CL
    span = tok_dev + 2 * HALO
    own_start = seq_rank * tok_dev

    token_parts = halo_parts(inputs)
    n_parts = len(token_parts)

    weight_in = dp_gather(input_weight, dp_rank)
    weight_up = lax.all_gather(up_weight, "dp", axis=0, tiled=True)
    weight_down = lax.all_gather(down_weight, "dp", axis=0, tiled=True)

    runs = document_runs[0]
    first_cluster = jnp.cumsum(runs) - runs
    own_clusters = seq_rank * tiles + jnp.arange(tiles, dtype=jnp.int32)
    doc_start = jnp.max(
        jnp.where(first_cluster[None, :] <= own_clusters[:, None], first_cluster[None, :], 0), axis=1
    )
    starts = (doc_start - seq_rank * tiles + (MOSTB - 1)).astype(jnp.int32)

    cids = cluster_ids(cluster_order[0], own_start, span)
    positions = own_start - HALO + jnp.arange(span, dtype=jnp.int32)
    live = live_tokens(runs, document_trim[0], positions)
    usable = live[None, :] & (cids >= 0.0)
    key_ids = jnp.where(usable, cids, -1.0).reshape(PAIRS, 2, span)
    query_ids = jnp.where(usable, cids, -2.0).reshape(PAIRS, 2, span)
    own_live = live[HALO : HALO + tok_dev, None].astype(f32)

    projected = [plain_product(part, weight_in).astype(bf16) for part in token_parts]
    own = projected[n_parts // 2]
    vectors = [
        output_bias,
        down_bias,
        first_gain,
        first_shift,
        second_gain,
        second_shift,
        up_bias,
    ]
    mix_rows = output_weight.shape[0]
    packed = jnp.concatenate(vectors)
    pad_rows = -(-packed.shape[0] // (16 * D)) * 16
    packed = jnp.pad(packed, (0, pad_rows * D - packed.shape[0])).reshape(pad_rows, D)
    mix_shard = gated(jnp.concatenate([output_weight, packed], 0), projected[0], projected[-1])
    mix_all = dp_gather(mix_shard, dp_rank)
    mix_all = mix_all.reshape(n_dp, mix_rows + pad_rows, D)
    weight_mix = mix_all[:, :mix_rows].reshape(D, D)
    small_all = mix_all[:, mix_rows:].reshape(n_dp, -1).astype(f32)
    vec = small_all[:, : 6 * mix_rows].reshape(n_dp, 6, mix_rows).transpose(1, 0, 2).reshape(6, D)
    vec = jnp.pad(vec, ((0, 2), (0, 0)))
    up_part = up_bias.shape[0]
    bias_up = small_all[:, 6 * mix_rows : 6 * mix_rows + up_part].reshape(1, FF)
    bias_up = jnp.pad(bias_up, ((0, 7), (0, 0)))
    heights = [part.shape[0] for part in token_parts]

    groups = HEADS // PACK
    group_lanes = PACK * HD
    group_key_ids = key_ids.reshape(groups, PACK, span)
    group_query_ids = query_ids.reshape(groups, PACK, span)
    group_scratch = pltpu.VMEM((span, group_lanes), bf16)

    def group_parts(third, first):
        return [lane_block(rows, third * groups + first, PACK) for rows in heights]

    attended, lse = strip_call(
        functools.partial(attend_kernel, tiles, n_parts),
        groups,
        [lane_block(tok_dev, 0, PACK)]
        + group_parts(1, 0)
        + group_parts(2, 0)
        + [row_block(span, 0, PACK), row_block(span, 0, PACK)],
        [lane_block(tok_dev, 0, PACK), fixed_lanes(tok_dev, 0)],
        [
            jax.ShapeDtypeStruct((tok_dev, D), bf16),
            jax.ShapeDtypeStruct((tok_dev, 2 * HD), f32),
        ],
        [group_scratch, group_scratch]
        + [pltpu.VMEM((PACK * CL, WINDOW), f32)] * 2
        + [pltpu.VMEM((PACK * CL, CL), f32)] * 2,
        (starts, own, *projected, *projected, group_query_ids, group_key_ids),
    )

    (
        result,
        active,
        up_rounded,
        hidden_rounded,
        pre_rounded,
        mixed_rounded,
        back_mixed,
        back_own,
        delta,
        sums,
        sums_up,
    ) = chain_call(
        attended,
        inputs,
        cotangent[0],
        own_live,
        lse,
        weight_mix,
        weight_up,
        weight_down,
        vec,
        bias_up,
    )
    back_parts = halo_parts(back_own)

    small = jnp.concatenate(
        [
            jnp.sum(sums, axis=1).reshape(6, n_dp, mix_rows).transpose(1, 0, 2).reshape(n_dp, -1),
            jnp.sum(sums_up, axis=0).reshape(n_dp, -1),
        ],
        axis=1,
    ).astype(bf16)
    unit = 8 * n_seq
    fixed_rows = FF // n_dp + (FF // D + 1) * (D // n_dp)
    small_rows = -(-(fixed_rows + -(-small.shape[1] // D)) // unit) * unit - fixed_rows
    small = jnp.pad(small, ((0, 0), (0, small_rows * D - small.shape[1])))
    small = small.reshape(n_dp, small_rows, D)
    core = (dp_rank % 2).astype(jnp.int32)
    send, keep = weight_call(
        n_dp,
        core.reshape(1),
        active,
        pre_rounded,
        hidden_rounded,
        up_rounded,
        attended,
        mixed_rounded,
        small,
    )
    core_got = swap(send, "dp", 1)

    def query_strip(first, *needs):
        buffer = needs[:1] if first > 0 else ()
        in_specs = (
            [lane_block(tok_dev, first, PACK)]
            + group_parts(1, first)
            + group_parts(2, first)
            + [
                lane_block(tok_dev, first, PACK),
                row_block(span, first, PACK),
                row_block(span, first, PACK),
                fixed_lanes(tok_dev, 0),
                fixed_lanes(tok_dev, 0),
            ]
            + [UNREAD] * len(needs)
        )
        return strip_call(
            functools.partial(query_kernel, tiles, n_parts, first * PACK),
            1,
            in_specs,
            lane_block(tok_dev, first, PACK),
            jax.ShapeDtypeStruct((tok_dev, D), bf16),
            [group_scratch, group_scratch],
            (
                starts,
                own,
                *projected,
                *projected,
                back_own,
                group_query_ids,
                group_key_ids,
                lse,
                delta,
                *needs,
            ),
            {len(in_specs) + 1 - len(needs): 0} if buffer else None,
        )

    key_pairs = PACK // 2
    pair_scratch = pltpu.VMEM((span, 4 * HD), bf16)

    def key_strip(first, *needs):
        buffer = needs[:1] if first > 0 else ()
        pair = first * key_pairs

        def parts(third):
            return [lane_block(rows, third * PAIRS + pair) for rows in heights]

        in_specs = (
            [lane_block(tok_dev, PAIRS + pair), lane_block(tok_dev, 2 * PAIRS + pair)]
            + parts(0)
            + parts(0)
            + [fixed_lanes(rows, PAIRS) for rows in heights]
            + [row_block(span, pair), row_block(span, pair)]
            + [UNREAD] * len(needs)
        )
        return strip_call(
            functools.partial(key_kernel, tiles, n_parts, pair),
            key_pairs,
            in_specs,
            pl.BlockSpec((tok_dev, 2 * group_lanes), lambda step, starts: (0, first)),
            jax.ShapeDtypeStruct((tok_dev, 2 * D), bf16),
            [pair_scratch, pair_scratch],
            (
                starts,
                own,
                own,
                *projected,
                *back_parts,
                *back_parts,
                query_ids,
                key_ids,
                *needs,
            ),
            {len(in_specs) + 1 - len(needs): 0} if buffer else None,
        )

    def scatter(share):
        rows, columns = share.shape
        return lax.all_to_all(
            share.reshape(n_seq, rows // n_seq, columns), "seq", split_axis=0, concat_axis=0
        )

    def everyone(copies):
        got = lax.all_to_all(copies, "seq", split_axis=0, concat_axis=0)
        return got.reshape(-1, copies.shape[-1])

    def first_split(keep, got, *needs):
        bit = 2
        while True:
            which = ((dp_rank // bit) % 2).astype(jnp.int32).reshape(1)
            mine, other = split_add(keep, got, which, *needs)
            got = swap(other, "dp", bit)
            if mine.shape[0] == 1:
                return mine, got
            keep, bit, needs = mine, bit * 2, ()

    def core_split(grad):
        rows, columns = grad.shape
        blocks = grad.astype(bf16).reshape(n_dp // 2, 2, rows // n_dp, columns)
        return (
            lax.dynamic_index_in_dim(blocks, 1 - core, 1, keepdims=False),
            lax.dynamic_index_in_dim(blocks, core, 1, keepdims=False),
        )

    mine, x_got = first_split(keep, core_got)
    back_q = query_strip(0)
    back_q = query_strip(1, back_q, mine)
    back_q = query_strip(2, back_q, *back_parts)
    share = add_blocks(mine, x_got, back_q)
    pieces = scatter(share)
    back_kv = key_strip(0, back_q, share)
    back_kv = key_strip(1, back_kv)
    copies = summed_copies(pieces, 1, back_kv)
    all_sums = lax.all_gather(copies[0], "seq", axis=0, tiled=True)
    cut = 2 * group_lanes * (groups - 1)
    early_cols = jnp.concatenate([back_q, back_kv[:, :cut]], axis=1)
    early_send, early_keep = core_split(outer_sum(inputs, early_cols))
    early_core = swap(early_send, "dp", 1)
    back_kv = key_strip(2, back_kv, early_send, copies)
    early_mine, early_got = first_split(early_keep, early_core, back_kv)
    late_send, late_keep = core_split(outer_sum(inputs, back_kv[:, cut:]))
    late_mine, late_got = first_split(late_keep, swap(late_send, "dp", 1), early_mine)
    in_share = jnp.concatenate(
        [add_blocks(early_mine, early_got, all_sums), add_blocks(late_mine, late_got)], axis=1
    )
    in_all = everyone(summed_copies(scatter(in_share), n_seq))

    kv_weight = (
        weight_in[:, D:]
        .reshape(D, 2, groups, group_lanes)
        .transpose(0, 2, 1, 3)
        .reshape(D, 2 * D)
    )
    input_grad = (
        back_mixed + back_product(back_q, weight_in[:, :D]) + back_product(back_kv, kv_weight)
    )
    kv_all = in_all[:, D:].reshape(-1, groups, 2, group_lanes).transpose(0, 2, 1, 3)
    grad_in_total = jnp.concatenate([in_all[:, :D], kv_all.reshape(-1, 2 * D)], axis=1).astype(f32)
    down_rows = FF // n_dp
    part_rows = D // n_dp
    grad_down = all_sums[:down_rows].astype(f32)
    grad_up = (
        all_sums[down_rows : down_rows + (FF // D) * part_rows]
        .reshape(FF // D, part_rows, D)
        .transpose(1, 0, 2)
        .reshape(part_rows, FF)
        .astype(f32)
    )
    at = down_rows + (FF // D) * part_rows
    grad_mix = all_sums[at : at + part_rows].astype(f32)
    flat = all_sums[at + part_rows :].reshape(-1).astype(f32)
    vectors_out = [flat[i * part_rows : (i + 1) * part_rows] for i in range(6)]
    bias_up_out = flat[6 * part_rows : 6 * part_rows + down_rows]
    return (
        result[None],
        input_grad[None],
        grad_in_total,
        grad_mix,
        grad_up,
        grad_down,
        vectors_out[0],
        bias_up_out,
        vectors_out[1],
        *vectors_out[2:],
    )


def solution(mesh):
    placed = (
        P("dp", "seq", None),
        P("dp", None),
        P("dp", None),
        P("dp", None),
        P("dp", None),
        P("dp"),
        P("dp"),
        P("dp"),
        P("dp"),
        P("dp"),
        P("dp"),
        P("dp"),
        P("dp", None),
        P("dp", None),
        P("dp", None, None),
        P("dp", "seq", None),
    )
    return jax.shard_map(
        on_device,
        mesh=mesh,
        in_specs=placed,
        out_specs=(
            P("dp", "seq", None),
            P("dp", "seq", None),
            P("dp", None),
            P("dp", None),
            P("dp", None),
            P("dp", None),
            P("dp"),
            P("dp"),
            P("dp"),
            P("dp"),
            P("dp"),
            P("dp"),
            P("dp"),
        ),
        check_vma=False,
    )
```

```python
import functools

import jax
import jax.numpy as jnp
from jax import lax
from jax.experimental import pallas as pl
from jax.experimental.pallas import tpu as pltpu
from jax.sharding import PartitionSpec as P

D = 768
HEADS = 12
HD = 64
CL = 128
MOSTB = 16
PAIRS = HEADS // 2
WINDOW = MOSTB * CL
HALO = (MOSTB - 1) * CL
CHUNK = 512
KCHUNK = 512
TILES_AT_ONCE = 2
PACK = 4
NEG = -1e30
TERMS = 5
FF = 3072
RTILE = 512
FCHUNK = 768
SCALE2 = HD ** (-0.5) * 1.4426950408889634

EPSILON = 1e-05


def shifted(value, axis, by):
    devices = lax.axis_size(axis)
    pairs = [(i, i + by) for i in range(devices) if 0 <= i + by < devices]
    return lax.ppermute(value, axis, pairs)


def halo_parts(value):
    own = value.shape[0]
    parts = [value]
    left = HALO
    distance = 1
    while left > 0:
        take = min(own, left)
        before = shifted(value[own - take :], "seq", distance)
        after = shifted(value[:take], "seq", -distance)
        parts = [before] + parts + [after]
        left -= take
        distance += 1
    return parts


def live_tokens(runs, trim, positions):
    ends = jnp.cumsum(runs) * CL
    starts = ends - runs * CL
    lengths = runs * CL - trim
    inside = (positions[..., None] >= starts) & (positions[..., None] < starts + lengths)
    return jnp.any(inside, axis=-1)


def outer_sum(left, right):
    return lax.dot_general(
        left, right, (((0,), (0,)), ((), ())), preferred_element_type=jnp.float32
    )


def back_product(left, right):
    return lax.dot_general(
        left, right, (((1,), (1,)), ((), ())), preferred_element_type=jnp.float32
    )


def plain_product(left, right):
    return jnp.dot(left, right, preferred_element_type=jnp.float32)


def stacked(tile):
    lane = lax.broadcasted_iota(jnp.int32, tile.shape, 1)
    zero = jnp.zeros_like(tile)
    heads = tile.shape[1] // HD
    return jnp.concatenate(
        [
            jnp.where((lane >= h * HD) & (lane < (h + 1) * HD), tile, zero)
            for h in range(heads)
        ],
        axis=0,
    )


def unstacked(stack):
    heads = stack.shape[1] // HD
    lane = lax.broadcasted_iota(jnp.int32, (CL, heads * HD), 1)
    result = stack[:CL]
    for h in range(1, heads):
        result = jnp.where(lane >= h * HD, stack[h * CL : (h + 1) * CL], result)
    return result


def as_column(row):
    return jnp.broadcast_to(row, (CL, CL)).T


def lane_of(tile, lane):
    lanes = lax.broadcasted_iota(jnp.int32, tile.shape, 1)
    return jnp.sum(jnp.where(lanes == lane, tile, 0.0), axis=1, keepdims=True)


def masked(scores, cols, row_ref, begin):
    parts = []
    wide = scores.shape[1]
    for half, one in enumerate(cols):
        row = row_ref[0, half : half + 1, pl.ds(begin, wide)]
        block = scores[half * CL : (half + 1) * CL]
        col = jnp.concatenate([one] * (wide // CL), axis=1)
        parts.append(jnp.where(col == row, block, NEG))
    return jnp.concatenate(parts, axis=0)


def assemble(parts, whole):
    at = 0
    for part in parts:
        rows = part.shape[0]
        whole[at : at + rows, :] = part[...]
        at += rows


def ahead(steps, produce, consume):
    held = produce(*steps[0])
    for i, step in enumerate(steps):
        following = produce(*steps[i + 1]) if i + 1 < len(steps) else None
        consume(*step, held)
        held = following


def attend_kernel(n_parts, starts, q_ref, *refs):
    k_parts, refs = refs[:n_parts], refs[n_parts:]
    v_parts, refs = refs[:n_parts], refs[n_parts:]
    qid_ref, kid_ref, out_ref, lse_ref, rate_ref, p_ref, k_ref, v_ref, *slots = refs
    s_refs, top_refs = slots[:TILES_AT_ONCE], slots[TILES_AT_ONCE:]
    group, step = pl.program_id(0), pl.program_id(1)
    heads = q_ref.shape[1] // HD
    chunks = WINDOW // CHUNK

    @pl.when(step == 0)
    def _():
        assemble(k_parts, k_ref)
        assemble(v_parts, v_ref)

    @pl.when((group == 0) & (step == 0))
    def _():
        lse_ref[...] = jnp.zeros_like(lse_ref)
        rate_ref[...] = jnp.zeros_like(rate_ref)

    def first_half(slot):
        tile = TILES_AT_ONCE * step + slot
        own = pl.multiple_of(HALO + tile * CL, CL)
        return dict(
            begin=pl.multiple_of(starts[tile] * CL, CL),
            query=stacked(q_ref[slot * CL : (slot + 1) * CL, :]),
            cols=[
                as_column(qid_ref[0, half : half + 1, pl.ds(own, CL)]) for half in range(heads)
            ],
        )

    def score(state, slot, j):
        at = pl.multiple_of(state["begin"] + j * CHUNK, CL)
        scores = back_product(state["query"], k_ref[pl.ds(at, CHUNK), :])
        scores = masked(scores, state["cols"], kid_ref, at)
        s_refs[slot][:, j * CHUNK : (j + 1) * CHUNK] = scores
        top = scores[:, :CL]
        for i in range(1, CHUNK // CL):
            top = jnp.maximum(top, scores[:, i * CL : (i + 1) * CL])
        if j > 0:
            top = jnp.maximum(top, top_refs[slot][...])
        top_refs[slot][...] = top

    states = [first_half(0)]
    for j in range(chunks):
        score(states[0], 0, j)
    for slot in range(TILES_AT_ONCE):
        if slot + 1 < TILES_AT_ONCE:
            states.append(first_half(slot + 1))
        state = states[slot]
        peak = jnp.max(top_refs[slot][...], axis=1, keepdims=True)
        total = jnp.zeros((heads * CL, CL), jnp.float32)
        result = jnp.zeros((heads * CL, heads * HD), jnp.float32)
        for j in range(chunks):
            if slot + 1 < TILES_AT_ONCE:
                score(states[slot + 1], slot + 1, j)
            at = pl.multiple_of(state["begin"] + j * CHUNK, CL)
            columns = slice(j * CHUNK, (j + 1) * CHUNK)
            weights = jnp.exp2((s_refs[slot][:, columns] - peak) * SCALE2)
            for i in range(CHUNK // CL):
                total = total + weights[:, i * CL : (i + 1) * CL]
            weights = weights.astype(jnp.bfloat16)
            p_ref[0, slot, :, columns] = weights
            result = result + plain_product(weights, v_ref[pl.ds(at, CHUNK), :])
        total = jnp.sum(total, axis=1, keepdims=True)
        rate = 1.0 / total
        result = result * rate
        lse = peak + jnp.log(total) * HD**0.5
        live = (state["cols"][0] >= 0.0).astype(jnp.float32)
        live = jnp.concatenate([live] * (heads * HD // CL), axis=1)
        rows = slice(slot * CL, (slot + 1) * CL)
        out_ref[rows, :] = (unstacked(result) * live).astype(jnp.bfloat16)
        here = pl.ds(pl.multiple_of((TILES_AT_ONCE * step + slot) * CL, CL), CL)
        lane = lax.broadcasted_iota(jnp.int32, (CL, CL), 1)
        kept, kept_rate = lse_ref[here, :], rate_ref[here, :]
        for half in range(heads):
            first = (heads * group + half) * TERMS
            inside = (lane >= first) & (lane < first + TERMS)
            part = slice(half * CL, (half + 1) * CL)
            kept = jnp.where(inside, lse[part], kept)
            kept_rate = jnp.where(inside, rate[part], kept_rate)
        lse_ref[here, :] = kept
        rate_ref[here, :] = kept_rate


def query_kernel(n_parts, first_head, starts, *refs):
    k_parts, refs = refs[:n_parts], refs[n_parts:]
    v_parts, refs = refs[:n_parts], refs[n_parts:]
    g_ref, p_ref, rate_ref, delta_ref = refs[:4]
    out_ref, k_ref, v_ref = refs[-3:]
    step = pl.program_id(0)
    heads = g_ref.shape[1] // HD
    chunks = WINDOW // CHUNK

    @pl.when(step == 0)
    def _():
        assemble(k_parts, k_ref)
        assemble(v_parts, v_ref)

    states = {}

    def state_of(slot):
        if slot not in states:
            rows = slice(slot * CL, (slot + 1) * CL)
            columns = [
                jnp.concatenate(
                    [lane_of(ref[rows, :], (first_head + half) * TERMS) for half in range(heads)],
                    axis=0,
                )
                for ref in (delta_ref, rate_ref)
            ]
            states[slot] = dict(
                begin=pl.multiple_of(starts[TILES_AT_ONCE * step + slot] * CL, CL),
                back=stacked(g_ref[rows, :]),
                delta=columns[0],
                rate=columns[1],
                result=jnp.zeros((heads * CL, heads * HD), jnp.float32),
            )
        return states[slot]

    def produce(slot, j):
        state = state_of(slot)
        at = pl.multiple_of(state["begin"] + j * CHUNK, CL)
        return back_product(state["back"], v_ref[pl.ds(at, CHUNK), :])

    def consume(slot, j, back_probs):
        state = state_of(slot)
        at = pl.multiple_of(state["begin"] + j * CHUNK, CL)
        weights = p_ref[0, slot, :, j * CHUNK : (j + 1) * CHUNK].astype(jnp.float32)
        back_scores = weights * (back_probs - state["delta"])
        state["result"] = state["result"] + plain_product(
            back_scores.astype(jnp.bfloat16), k_ref[pl.ds(at, CHUNK), :]
        )
        if j == chunks - 1:
            out_ref[slot * CL : (slot + 1) * CL, :] = unstacked(
                state["result"] * (state["rate"] * HD ** (-0.5))
            ).astype(jnp.bfloat16)

    ahead(
        [(slot, j) for slot in range(TILES_AT_ONCE) for j in range(chunks)], produce, consume
    )


def key_kernel(tiles, n_parts, first_pair, starts, k_ref, v_ref, *refs):
    q_parts, refs = refs[:n_parts], refs[n_parts:]
    g_parts, refs = refs[:n_parts], refs[n_parts:]
    a_parts, refs = refs[:n_parts], refs[n_parts:]
    qid_ref, kid_ref = refs[:2]
    out_ref, q_ref, g_ref = refs[-3:]
    step_pair = pl.program_id(0)
    pair = first_pair + step_pair
    at = 0
    for q_part, g_part, a_part in zip(q_parts, g_parts, a_parts):
        rows = q_part.shape[0]
        q_ref[at : at + rows, : 2 * HD] = q_part[...]
        q_ref[at : at + rows, 2 * HD :] = a_part[...]
        g_ref[at : at + rows, : 2 * HD] = g_part[...]
        g_ref[at : at + rows, 2 * HD :] = a_part[...]
        at += rows

    lane = lax.broadcasted_iota(jnp.int32, (CL, CL), 1)
    lse_pick, delta_pick = [], []
    for half in range(2):
        first = (2 * pair + half) * TERMS
        lse_pick.append(jnp.where((lane >= first) & (lane < first + 3), -1.0, 0.0))
        delta_pick.append(jnp.where((lane >= first + 3) & (lane < first + TERMS), -1.0, 0.0))
    lse_pick = jnp.concatenate(lse_pick, axis=0).astype(jnp.bfloat16)
    delta_pick = jnp.concatenate(delta_pick, axis=0).astype(jnp.bfloat16)
    key_lanes = pl.ds(pl.multiple_of(step_pair * 2 * HD, 2 * HD), 2 * HD)
    value_lanes = pl.ds(
        pl.multiple_of(out_ref.shape[1] // 2 + step_pair * 2 * HD, 2 * HD), 2 * HD
    )

    def some_tiles(step, carry):
        states = {}

        def state_of(slot):
            if slot not in states:
                tile = TILES_AT_ONCE * step + slot
                own = pl.multiple_of(HALO + tile * CL, CL)
                here = pl.multiple_of(tile * CL, CL)
                states[slot] = dict(
                    begin=pl.multiple_of(starts[tile] * CL, CL),
                    here=here,
                    keys=jnp.concatenate([stacked(k_ref[pl.ds(here, CL), :]), lse_pick], axis=1),
                    values=jnp.concatenate(
                        [stacked(v_ref[pl.ds(here, CL), :]), delta_pick], axis=1
                    ),
                    cols=[
                        as_column(kid_ref[0, half : half + 1, pl.ds(own, CL)]) for half in range(2)
                    ],
                    key_sum=jnp.zeros((2 * CL, 2 * HD), jnp.float32),
                    value_sum=jnp.zeros((2 * CL, 2 * HD), jnp.float32),
                )
            return states[slot]

        def produce(slot, j):
            state = state_of(slot)
            at = pl.multiple_of(state["begin"] + j * KCHUNK, CL)
            scores = back_product(state["keys"], q_ref[pl.ds(at, KCHUNK), :])
            return scores, back_product(state["values"], g_ref[pl.ds(at, KCHUNK), :])

        def consume(slot, j, held):
            state = state_of(slot)
            at = pl.multiple_of(state["begin"] + j * KCHUNK, CL)
            scores, back_probs = held
            probs = jnp.exp2(masked(scores * SCALE2, state["cols"], qid_ref, at))
            back_scores = probs * back_probs
            state["value_sum"] = state["value_sum"] + plain_product(
                probs.astype(jnp.bfloat16), g_ref[pl.ds(at, KCHUNK), : 2 * HD]
            )
            state["key_sum"] = state["key_sum"] + plain_product(
                back_scores.astype(jnp.bfloat16), q_ref[pl.ds(at, KCHUNK), : 2 * HD]
            )
            if j == WINDOW // KCHUNK - 1:
                rows = pl.ds(state["here"], CL)
                out_ref[rows, key_lanes] = (
                    unstacked(state["key_sum"]) * HD ** (-0.5)
                ).astype(jnp.bfloat16)
                out_ref[rows, value_lanes] = unstacked(state["value_sum"]).astype(jnp.bfloat16)

        ahead(
            [(slot, j) for slot in range(TILES_AT_ONCE) for j in range(WINDOW // KCHUNK)],
            produce,
            consume,
        )
        return carry

    lax.fori_loop(0, tiles // TILES_AT_ONCE, some_tiles, 0)


def lane_block(rows, first, heads=2):
    return pl.BlockSpec((rows, heads * HD), lambda pair, starts: (0, first + pair))


def fixed_lanes(rows, block):
    return pl.BlockSpec((rows, 2 * HD), lambda pair, starts: (0, block))


def row_block(columns, first, heads=2):
    return pl.BlockSpec((1, heads, columns), lambda pair, starts: (first + pair, 0, 0))


UNREAD = pl.BlockSpec(memory_space=pl.ANY)


VMEM_LIMIT = 60 * 1024 * 1024


def strip_call(
    kernel, length, grid, in_specs, out_specs, out_shape, scratch, args, aliases=None
):
    return pl.pallas_call(
        kernel,
        out_shape=out_shape,
        grid_spec=pltpu.PrefetchScalarGridSpec(
            num_scalar_prefetch=1,
            grid=grid,
            in_specs=in_specs,
            out_specs=out_specs,
            scratch_shapes=scratch,
        ),
        input_output_aliases=aliases or {},
        cost_estimate=work(length),
        compiler_params=pltpu.CompilerParams(vmem_limit_bytes=VMEM_LIMIT),
    )(*args)


def project_kernel(weight, *refs):
    half = len(refs) // 2
    for source, target in zip(refs[:half], refs[half:]):
        target[...] = plain_product(source[...], weight[...]).astype(target.dtype)


def project_call(parts, weight):
    depth, columns = weight.shape
    block = PACK * HD
    return pl.pallas_call(
        project_kernel,
        grid=(columns // block,),
        in_specs=[pl.BlockSpec((depth, block), lambda i: (0, i))]
        + [pl.BlockSpec(part.shape, lambda i: (0, 0)) for part in parts],
        out_specs=[pl.BlockSpec((part.shape[0], block), lambda i: (0, i)) for part in parts],
        out_shape=[jax.ShapeDtypeStruct((part.shape[0], columns), part.dtype) for part in parts],
        cost_estimate=work(22),
        compiler_params=pltpu.CompilerParams(vmem_limit_bytes=VMEM_LIMIT),
    )(weight, *parts)


def gelu_terms(value):
    t = 1.0 / (1.0 + (0.3275911 * 0.7071067811865476) * jnp.abs(value))
    bell = jnp.exp2(value * value * (-0.5 * 1.4426950408889634))
    tail = 0.5 * 1.061405429
    for term in (-0.5 * 1.453152027, 0.5 * 1.421413741, -0.5 * 0.284496736, 0.5 * 0.254829592):
        tail = tail * t + term
    tail = tail * t * bell
    cdf = jnp.where(value >= 0.0, 1.0 - tail, tail)
    return value * cdf, cdf + value * (0.3989422804014327 * bell)


def normalised(values):
    mean = jnp.mean(values, axis=-1, keepdims=True)
    centre = values - mean
    rate = lax.rsqrt(jnp.mean(centre * centre, axis=-1, keepdims=True) + EPSILON)
    return centre * rate, rate


def norm_back(scaled, unit, rate):
    first = jnp.mean(scaled, axis=-1, keepdims=True)
    second = jnp.mean(scaled * unit, axis=-1, keepdims=True)
    return rate * (scaled - first - unit * second)


def row_sums(values):
    rows, columns = values.shape
    return jnp.sum(values.reshape(rows // 8, 8, columns), axis=0)


def chain_kernel(
    att_ref,
    tok_ref,
    cot_ref,
    live_ref,
    lse_ref,
    mix_ref,
    up_ref,
    down_ref,
    vec_ref,
    bias_up_ref,
    spread_ref,
    out_ref,
    act_ref,
    upr_ref,
    hid_ref,
    pre_ref,
    mixr_ref,
    mixed_ref,
    back_ref,
    delta_ref,
    sum_ref,
    sum_up_ref,
    slope_ref,
):
    width = up_ref.shape[1]
    bias_mix, bias_down = vec_ref[0:1], vec_ref[1:2]
    gain_one, shift_one = vec_ref[2:3], vec_ref[3:4]
    gain_two, shift_two = vec_ref[4:5], vec_ref[5:6]

    @pl.when(pl.program_id(0) == 0)
    def _():
        sum_ref[...] = jnp.zeros_like(sum_ref)
        sum_up_ref[...] = jnp.zeros_like(sum_up_ref)

    attended = att_ref[...]
    mixed = plain_product(attended, mix_ref[...]) + bias_mix + tok_ref[...].astype(jnp.float32)
    unit_one, rate_one = normalised(mixed)
    hidden = unit_one * gain_one + shift_one
    hidden_rounded = hidden.astype(jnp.bfloat16)
    hid_ref[...] = hidden_rounded
    down_sum = bias_down + hidden
    for f in range(0, width, FCHUNK):
        up_sum = plain_product(hidden_rounded, up_ref[:, f : f + FCHUNK]) + (
            bias_up_ref[0:1, f : f + FCHUNK]
        )
        active, slope = gelu_terms(up_sum)
        active = active.astype(jnp.bfloat16)
        act_ref[:, f : f + FCHUNK] = active
        slope_ref[:, f : f + FCHUNK] = slope
        down_sum = down_sum + plain_product(active, down_ref[f : f + FCHUNK, :])
    unit_two, rate_two = normalised(down_sum)
    out_ref[...] = (unit_two * gain_two + shift_two).astype(jnp.bfloat16)
    cot = cot_ref[...].astype(jnp.float32)
    back_pre = norm_back(cot * gain_two, unit_two, rate_two)
    pre_rounded = back_pre.astype(jnp.bfloat16)
    pre_ref[...] = pre_rounded
    sum_ref[4] += row_sums(cot * unit_two)
    sum_ref[5] += row_sums(cot)
    sum_ref[1] += row_sums(back_pre)
    back_hidden = back_pre
    for f in range(0, width, FCHUNK):
        back_up = back_product(pre_rounded, down_ref[f : f + FCHUNK, :]) * (
            slope_ref[:, f : f + FCHUNK]
        )
        sum_up_ref[:, f : f + FCHUNK] += row_sums(back_up)
        up_rounded = back_up.astype(jnp.bfloat16)
        upr_ref[:, f : f + FCHUNK] = up_rounded
        back_hidden = back_hidden + back_product(up_rounded, up_ref[:, f : f + FCHUNK])
    sum_ref[2] += row_sums(back_hidden * unit_one)
    sum_ref[3] += row_sums(back_hidden)
    back_mixed = norm_back(back_hidden * gain_one, unit_one, rate_one)
    sum_ref[0] += row_sums(back_mixed)
    mixed_ref[...] = back_mixed
    mixed_rounded = back_mixed.astype(jnp.bfloat16)
    mixr_ref[...] = mixed_rounded
    back = back_product(mixed_rounded, mix_ref[...]).astype(jnp.bfloat16)
    back = jnp.where(live_ref[...] > 0.5, back, jnp.zeros_like(back))
    back_ref[:, : back.shape[1]] = back
    terms = back.astype(jnp.float32) * attended.astype(jnp.float32)
    high = terms.astype(jnp.bfloat16)
    low = (terms - high.astype(jnp.float32)).astype(jnp.bfloat16)
    delta = plain_product(high, spread_ref[...]) + plain_product(low, spread_ref[...])
    delta_ref[...] = delta
    lane = lax.broadcasted_iota(jnp.int32, delta.shape, 1)
    term = lane % TERMS
    whole = jnp.where(term < 3, lse_ref[...], delta)
    first = whole.astype(jnp.bfloat16)
    rest = whole - first.astype(jnp.float32)
    second = rest.astype(jnp.bfloat16)
    third = (rest - second.astype(jnp.float32)).astype(jnp.bfloat16)
    picked = jnp.where(
        (term == 0) | (term == 3),
        first.astype(jnp.float32),
        jnp.where((term == 2), third.astype(jnp.float32), second.astype(jnp.float32)),
    )
    picked = jnp.where(lane < TERMS * HEADS, picked, 0.0)
    back_ref[:, back.shape[1] :] = picked.astype(jnp.bfloat16)


def chain_call(att, tok, cot, live, lse, mix, up, down, vectors, bias_up):
    rows, width = tok.shape
    wide = up.shape[1]
    head_of = jnp.arange(width, dtype=jnp.int32)[:, None] // HD
    spread = (head_of == jnp.arange(2 * HD, dtype=jnp.int32)[None, :] // TERMS).astype(jnp.bfloat16)

    def tile(columns):
        return pl.BlockSpec((RTILE, columns), lambda i: (i, 0))

    def fixed(*shape):
        return pl.BlockSpec(shape, lambda i: (0,) * len(shape))

    bf16, f32 = jnp.bfloat16, jnp.float32
    return pl.pallas_call(
        chain_kernel,
        grid=(rows // RTILE,),
        in_specs=[
            tile(width),
            tile(width),
            tile(width),
            tile(1),
            tile(2 * HD),
            fixed(*mix.shape),
            fixed(*up.shape),
            fixed(*down.shape),
            fixed(*vectors.shape),
            fixed(*bias_up.shape),
            fixed(*spread.shape),
        ],
        out_specs=[
            tile(width),
            tile(wide),
            tile(wide),
            tile(width),
            tile(width),
            tile(width),
            tile(width),
            tile(width + 2 * HD),
            tile(2 * HD),
            fixed(6, 8, width),
            fixed(8, wide),
        ],
        out_shape=[
            jax.ShapeDtypeStruct((rows, width), bf16),
            jax.ShapeDtypeStruct((rows, wide), bf16),
            jax.ShapeDtypeStruct((rows, wide), bf16),
            jax.ShapeDtypeStruct((rows, width), bf16),
            jax.ShapeDtypeStruct((rows, width), bf16),
            jax.ShapeDtypeStruct((rows, width), bf16),
            jax.ShapeDtypeStruct((rows, width), f32),
            jax.ShapeDtypeStruct((rows, width + 2 * HD), bf16),
            jax.ShapeDtypeStruct((rows, 2 * HD), f32),
            jax.ShapeDtypeStruct((6, 8, width), f32),
            jax.ShapeDtypeStruct((8, wide), f32),
        ],
        scratch_shapes=[pltpu.VMEM((RTILE, wide), f32)],
        cost_estimate=work(44),
        compiler_params=pltpu.CompilerParams(vmem_limit_bytes=VMEM_LIMIT),
    )(att, tok, cot, live, lse, mix, up, down, vectors, bias_up, spread)


def weight_kernel(n_dp, core_ref, act, pre, hid, upr, att, mixr, small, *refs):
    send, keep, tmp = refs[-3:]
    step = pl.program_id(0)
    core = core_ref[0]
    pieces = FF // D
    down_rows = FF // n_dp
    part_rows = D // n_dp

    def put(x, row, rows, begin):
        mine = pl.multiple_of(begin + core * rows, 16)
        other = pl.multiple_of(begin + (1 - core) * rows, 16)
        keep[pl.ds(x, 1), pl.ds(row, rows), :] = tmp[pl.ds(mine, rows), :][None]
        send[pl.ds(x, 1), pl.ds(row, rows), :] = tmp[pl.ds(other, rows), :][None]

    @pl.when(step < pieces)
    def _():
        tmp[...] = outer_sum(act[...], pre[...]).astype(jnp.bfloat16)
        per = D // down_rows
        for b in range(per):
            block = step * per + b
            x = block // 2
            rows = tmp[b * down_rows : (b + 1) * down_rows, :]

            @pl.when(lax.rem(block, 2) == core)
            def _():
                keep[pl.ds(x, 1), 0:down_rows, :] = rows[None]

            @pl.when(lax.rem(block, 2) != core)
            def _():
                send[pl.ds(x, 1), 0:down_rows, :] = rows[None]

    @pl.when((step >= pieces) & (step < 2 * pieces))
    def _():
        tmp[...] = outer_sum(hid[...], upr[...]).astype(jnp.bfloat16)
        row = pl.multiple_of(down_rows + (step - pieces) * part_rows, 16)
        for x in range(n_dp // 2):
            put(x, row, part_rows, 2 * x * part_rows)

    @pl.when(step == 2 * pieces)
    def _():
        tmp[...] = outer_sum(att[...], mixr[...]).astype(jnp.bfloat16)
        row = down_rows + pieces * part_rows
        for x in range(n_dp // 2):
            put(x, row, part_rows, 2 * x * part_rows)
            last = row + part_rows
            rows = keep.shape[1] - last
            keep[x, last:, :] = small[pl.ds(2 * x + core, 1), :, :][0]
            send[x, last:, :] = small[pl.ds(2 * x + 1 - core, 1), :, :][0]


def weight_call(n_dp, core, act, pre, hid, upr, att, mixr, small, *needs):
    rows = act.shape[0]
    pieces = FF // D
    out_rows = FF // n_dp + (pieces + 1) * (D // n_dp) + small.shape[1]

    def fixed(*shape):
        return pl.BlockSpec(shape, lambda i, c: (0,) * len(shape))

    def stepped(first):
        return pl.BlockSpec((rows, D), lambda i, c: (0, jnp.clip(i - first, 0, pieces - 1)))

    shape = (n_dp // 2, out_rows, D)
    return pl.pallas_call(
        functools.partial(weight_kernel, n_dp),
        out_shape=[jax.ShapeDtypeStruct(shape, jnp.bfloat16)] * 2,
        grid_spec=pltpu.PrefetchScalarGridSpec(
            num_scalar_prefetch=1,
            grid=(2 * pieces + 1,),
            in_specs=[
                stepped(0),
                fixed(rows, D),
                fixed(rows, D),
                stepped(pieces),
                fixed(rows, D),
                fixed(rows, D),
                fixed(*small.shape),
            ]
            + [UNREAD] * len(needs),
            out_specs=[fixed(*shape)] * 2,
            scratch_shapes=[pltpu.VMEM((D, D), jnp.bfloat16)],
        ),
        cost_estimate=work(22),
        compiler_params=pltpu.CompilerParams(vmem_limit_bytes=VMEM_LIMIT),
    )(core, act, pre, hid, upr, att, mixr, small, *needs)


def swap(value, axis, bit):
    devices = lax.axis_size(axis)
    return lax.ppermute(value, axis, [(i, i ^ bit) for i in range(devices)])


def dp_gather(shard, dp_rank):
    blocks = shard[None]
    bit = lax.axis_size("dp") // 2
    while bit >= 1:
        got = swap(blocks, "dp", bit)
        high = ((dp_rank // bit) % 2) == 1
        first = jnp.where(high, got, blocks)
        second = jnp.where(high, blocks, got)
        blocks = jnp.stack([first, second], axis=1).reshape((-1,) + shard.shape)
        bit //= 2
    return blocks.reshape((-1,) + shard.shape[1:])


def work(microseconds):
    return pl.CostEstimate(
        flops=int(microseconds * 0.4e9), transcendentals=0, bytes_accessed=1 << 20
    )


def row_tile(rows, limit=512):
    for size in range(min(rows, limit), 15, -1):
        if rows % size == 0 and size % 16 == 0:
            return size
    return rows


def plain_params():
    return pltpu.CompilerParams(vmem_limit_bytes=VMEM_LIMIT)


def split_add_kernel(which, keep_mine, got_mine, keep_other, got_other, *refs):
    mine, other = refs[-2:]
    mine[...] = (keep_mine[...].astype(jnp.float32) + got_mine[...].astype(jnp.float32)).astype(
        mine.dtype
    )
    other[...] = (keep_other[...].astype(jnp.float32) + got_other[...].astype(jnp.float32)).astype(
        other.dtype
    )


def split_add(keep, got, which, *needs):
    blocks, rows, columns = keep.shape
    tile = row_tile(rows)

    def spec(flip):
        def place(b, i, w):
            bit = 1 - w[0] if flip else w[0]
            return 2 * b + bit, i, 0

        return pl.BlockSpec((1, tile, columns), place)

    out = pl.BlockSpec((1, tile, columns), lambda b, i, w: (b, i, 0))
    shape = jax.ShapeDtypeStruct((blocks // 2, rows, columns), keep.dtype)
    return pl.pallas_call(
        split_add_kernel,
        out_shape=[shape, shape],
        grid_spec=pltpu.PrefetchScalarGridSpec(
            num_scalar_prefetch=1,
            grid=(blocks // 2, rows // tile),
            in_specs=[spec(False), spec(False), spec(True), spec(True)] + [UNREAD] * len(needs),
            out_specs=[out, out],
        ),
        cost_estimate=work(4),
        compiler_params=plain_params(),
    )(which, keep, got, keep, got, *needs)


def add_kernel(left, right, *refs):
    out = refs[-1]
    out[...] = (left[0].astype(jnp.float32) + right[0].astype(jnp.float32)).astype(out.dtype)


def add_blocks(left, right, *needs):
    _, rows, columns = left.shape
    tile = row_tile(rows)
    spec = pl.BlockSpec((1, tile, columns), lambda i: (0, i, 0))
    return pl.pallas_call(
        add_kernel,
        grid=(rows // tile,),
        in_specs=[spec, spec] + [UNREAD] * len(needs),
        out_specs=pl.BlockSpec((tile, columns), lambda i: (i, 0)),
        cost_estimate=work(3),
        out_shape=jax.ShapeDtypeStruct((rows, columns), left.dtype),
        compiler_params=plain_params(),
    )(left, right, *needs)


def pieces_kernel(pieces, *refs):
    out = refs[-1]
    total = pieces[0].astype(jnp.float32)
    for i in range(1, pieces.shape[0]):
        total = total + pieces[i].astype(jnp.float32)
    total = total.astype(out.dtype)
    for i in range(out.shape[0]):
        out[i] = total


def summed_copies(pieces, copies, *needs):
    _, rows, columns = pieces.shape
    return pl.pallas_call(
        pieces_kernel,
        in_specs=[pl.BlockSpec(memory_space=pltpu.VMEM)] + [UNREAD] * len(needs),
        out_specs=pl.BlockSpec(memory_space=pltpu.VMEM),
        out_shape=jax.ShapeDtypeStruct((copies, rows, columns), pieces.dtype),
        cost_estimate=work(2),
        compiler_params=plain_params(),
    )(pieces, *needs)


def gate_kernel(value, *refs):
    refs[-1][...] = value[...]


def gated(value, *needs):
    return pl.pallas_call(
        gate_kernel,
        in_specs=[pl.BlockSpec(memory_space=pltpu.VMEM)] + [UNREAD] * len(needs),
        out_specs=pl.BlockSpec(memory_space=pltpu.VMEM),
        out_shape=jax.ShapeDtypeStruct(value.shape, value.dtype),
        cost_estimate=work(1),
        compiler_params=plain_params(),
    )(value, *needs)


def cluster_ids(group_order, own_start, span):
    padded = jnp.pad(group_order, ((0, 0), (HALO, HALO)), constant_values=-(1 << 24))
    wanted = lax.dynamic_slice_in_dim(padded, own_start, span, 1) - (own_start - HALO)
    tile_of = wanted >> 7
    lane_of_token = wanted & (CL - 1)
    cluster = (jnp.arange(span, dtype=jnp.int32) >> 7) + 1
    tile_hot = jnp.where(
        tile_of[:, :, None] == jnp.arange(span // CL, dtype=jnp.int32), cluster[None, :, None], 0
    ).astype(jnp.bfloat16)
    lane_hot = (lane_of_token[:, :, None] == jnp.arange(CL, dtype=jnp.int32)).astype(jnp.bfloat16)
    table = jnp.einsum("hpt,hpl->htl", tile_hot, lane_hot, preferred_element_type=jnp.float32)
    return table.reshape(HEADS, span) - 1.0


def on_device(
    tokens,
    input_weight,
    output_weight,
    up_weight,
    down_weight,
    output_bias,
    up_bias,
    down_bias,
    first_gain,
    first_shift,
    second_gain,
    second_shift,
    document_runs,
    document_trim,
    cluster_order,
    cotangent,
):
    bf16, f32 = jnp.bfloat16, jnp.float32
    n_dp = lax.axis_size("dp")
    n_seq = lax.axis_size("seq")
    dp_rank = lax.axis_index("dp")
    seq_rank = lax.axis_index("seq")
    inputs = tokens[0]
    tok_dev = inputs.shape[0]
    tiles = tok_dev // CL
    span = tok_dev + 2 * HALO
    own_start = seq_rank * tok_dev

    token_parts = halo_parts(inputs)
    n_parts = len(token_parts)

    weight_in = dp_gather(input_weight, dp_rank)
    weight_up = lax.all_gather(up_weight, "dp", axis=0, tiled=True)
    weight_down = lax.all_gather(down_weight, "dp", axis=0, tiled=True)

    runs = document_runs[0]
    first_cluster = jnp.cumsum(runs) - runs
    own_clusters = seq_rank * tiles + jnp.arange(tiles, dtype=jnp.int32)
    doc_start = jnp.max(
        jnp.where(first_cluster[None, :] <= own_clusters[:, None], first_cluster[None, :], 0), axis=1
    )
    starts = (doc_start - seq_rank * tiles + (MOSTB - 1)).astype(jnp.int32)

    cids = cluster_ids(cluster_order[0], own_start, span)
    positions = own_start - HALO + jnp.arange(span, dtype=jnp.int32)
    live = live_tokens(runs, document_trim[0], positions)
    usable = live[None, :] & (cids >= 0.0)
    key_ids = jnp.where(usable, cids, -1.0).reshape(PAIRS, 2, span)
    query_ids = jnp.where(usable, cids, -2.0).reshape(PAIRS, 2, span)
    own_live = live[HALO : HALO + tok_dev, None].astype(f32)

    own = plain_product(inputs, weight_in).astype(bf16)
    middle = n_parts // 2
    around = project_call(token_parts[:middle] + token_parts[middle + 1 :], weight_in)
    projected = [*around[:middle], own, *around[middle:]]
    vectors = [
        output_bias,
        down_bias,
        first_gain,
        first_shift,
        second_gain,
        second_shift,
        up_bias,
    ]
    mix_rows = output_weight.shape[0]
    packed = jnp.concatenate(vectors)
    pad_rows = -(-packed.shape[0] // (16 * D)) * 16
    packed = jnp.pad(packed, (0, pad_rows * D - packed.shape[0])).reshape(pad_rows, D)
    mix_shard = gated(jnp.concatenate([output_weight, packed], 0), own)
    mix_all = dp_gather(mix_shard, dp_rank)
    mix_all = mix_all.reshape(n_dp, mix_rows + pad_rows, D)
    weight_mix = mix_all[:, :mix_rows].reshape(D, D)
    small_all = mix_all[:, mix_rows:].reshape(n_dp, -1).astype(f32)
    vec = small_all[:, : 6 * mix_rows].reshape(n_dp, 6, mix_rows).transpose(1, 0, 2).reshape(6, D)
    vec = jnp.pad(vec, ((0, 2), (0, 0)))
    up_part = up_bias.shape[0]
    bias_up = small_all[:, 6 * mix_rows : 6 * mix_rows + up_part].reshape(1, FF)
    bias_up = jnp.pad(bias_up, ((0, 7), (0, 0)))
    heights = [part.shape[0] for part in token_parts]

    groups = HEADS // PACK
    group_lanes = PACK * HD
    group_key_ids = key_ids.reshape(groups, PACK, span)
    group_query_ids = query_ids.reshape(groups, PACK, span)
    group_scratch = pltpu.VMEM((span, group_lanes), bf16)

    def group_parts(third, first):
        return [lane_block(rows, third * groups + first, PACK) for rows in heights]

    steps = tiles // TILES_AT_ONCE
    step_rows = TILES_AT_ONCE * CL

    def of_group(rows, first):
        return pl.BlockSpec((rows, group_lanes), lambda g, t, starts: (0, first + g))

    def ids_of_group():
        return pl.BlockSpec((1, PACK, span), lambda g, t, starts: (g, 0, 0))

    step_block = pl.BlockSpec((step_rows, group_lanes), lambda g, t, starts: (t, g))
    whole_lanes = pl.BlockSpec((tok_dev, 2 * HD), lambda g, t, starts: (0, 0))
    attended, lse, rate, probs = strip_call(
        functools.partial(attend_kernel, n_parts),
        52,
        (groups, steps),
        [step_block]
        + [of_group(rows, groups) for rows in heights]
        + [of_group(rows, 2 * groups) for rows in heights]
        + [ids_of_group(), ids_of_group()],
        [
            step_block,
            whole_lanes,
            whole_lanes,
            pl.BlockSpec(
                (1, TILES_AT_ONCE, PACK * CL, WINDOW), lambda g, t, starts: (g, t, 0, 0)
            ),
        ],
        [
            jax.ShapeDtypeStruct((tok_dev, D), bf16),
            jax.ShapeDtypeStruct((tok_dev, 2 * HD), f32),
            jax.ShapeDtypeStruct((tok_dev, 2 * HD), f32),
            jax.ShapeDtypeStruct((groups, tiles, PACK * CL, WINDOW), bf16),
        ],
        [group_scratch, group_scratch]
        + [pltpu.VMEM((PACK * CL, WINDOW), f32)] * TILES_AT_ONCE
        + [pltpu.VMEM((PACK * CL, CL), f32)] * TILES_AT_ONCE,
        (starts, own, *projected, *projected, group_query_ids, group_key_ids),
    )

    (
        result,
        active,
        up_rounded,
        hidden_rounded,
        pre_rounded,
        mixed_rounded,
        back_mixed,
        back_own,
        delta,
        sums,
        sums_up,
    ) = chain_call(
        attended,
        inputs,
        cotangent[0],
        own_live,
        lse,
        weight_mix,
        weight_up,
        weight_down,
        vec,
        bias_up,
    )
    back_parts = halo_parts(back_own)

    small = jnp.concatenate(
        [
            jnp.sum(sums, axis=1).reshape(6, n_dp, mix_rows).transpose(1, 0, 2).reshape(n_dp, -1),
            jnp.sum(sums_up, axis=0).reshape(n_dp, -1),
        ],
        axis=1,
    ).astype(bf16)
    unit = 8 * n_seq
    fixed_rows = FF // n_dp + (FF // D + 1) * (D // n_dp)
    small_rows = -(-(fixed_rows + -(-small.shape[1] // D)) // unit) * unit - fixed_rows
    small = jnp.pad(small, ((0, 0), (0, small_rows * D - small.shape[1])))
    small = small.reshape(n_dp, small_rows, D)
    core = (dp_rank % 2).astype(jnp.int32)
    def query_strip(first, *needs):
        buffer = needs[:1] if first > 0 else ()

        def parts(third):
            return [
                pl.BlockSpec(
                    (rows, group_lanes), lambda t, starts: (0, third * groups + first)
                )
                for rows in heights
            ]

        block = pl.BlockSpec((step_rows, group_lanes), lambda t, starts: (t, first))
        lanes = pl.BlockSpec((step_rows, 2 * HD), lambda t, starts: (t, 0))
        in_specs = (
            parts(1)
            + parts(2)
            + [
                block,
                pl.BlockSpec(
                    (1, TILES_AT_ONCE, PACK * CL, WINDOW), lambda t, starts: (first, t, 0, 0)
                ),
                lanes,
                lanes,
            ]
            + [UNREAD] * len(needs)
        )
        return strip_call(
            functools.partial(query_kernel, n_parts, first * PACK),
            16,
            (steps,),
            in_specs,
            block,
            jax.ShapeDtypeStruct((tok_dev, D), bf16),
            [group_scratch, group_scratch],
            (starts, *projected, *projected, back_own, probs, rate, delta, *needs),
            {len(in_specs) + 1 - len(needs): 0} if buffer else None,
        )

    key_pairs = PACK // 2
    pair_scratch = pltpu.VMEM((span, 4 * HD), bf16)

    def key_strip(first, *needs):
        buffer = needs[:1] if first > 0 else ()
        pair = first * key_pairs

        def parts(third):
            return [lane_block(rows, third * PAIRS + pair) for rows in heights]

        in_specs = (
            [lane_block(tok_dev, PAIRS + pair), lane_block(tok_dev, 2 * PAIRS + pair)]
            + parts(0)
            + parts(0)
            + [fixed_lanes(rows, PAIRS) for rows in heights]
            + [row_block(span, pair), row_block(span, pair)]
            + [UNREAD] * len(needs)
        )
        return strip_call(
            functools.partial(key_kernel, tiles, n_parts, pair),
            27,
            (key_pairs,),
            in_specs,
            pl.BlockSpec((tok_dev, 2 * group_lanes), lambda step, starts: (0, first)),
            jax.ShapeDtypeStruct((tok_dev, 2 * D), bf16),
            [pair_scratch, pair_scratch],
            (
                starts,
                own,
                own,
                *projected,
                *back_parts,
                *back_parts,
                query_ids,
                key_ids,
                *needs,
            ),
            {len(in_specs) + 1 - len(needs): 0} if buffer else None,
        )

    def scatter(share):
        rows, columns = share.shape
        return lax.all_to_all(
            share.reshape(n_seq, rows // n_seq, columns), "seq", split_axis=0, concat_axis=0
        )

    def everyone(copies):
        got = lax.all_to_all(copies, "seq", split_axis=0, concat_axis=0)
        return got.reshape(-1, copies.shape[-1])

    def first_split(keep, got, *needs):
        bit = 2
        while True:
            which = ((dp_rank // bit) % 2).astype(jnp.int32).reshape(1)
            mine, other = split_add(keep, got, which, *needs)
            got = swap(other, "dp", bit)
            if mine.shape[0] == 1:
                return mine, got
            keep, bit, needs = mine, bit * 2, ()

    def core_split(grad):
        rows, columns = grad.shape
        blocks = grad.astype(bf16).reshape(n_dp // 2, 2, rows // n_dp, columns)
        return (
            lax.dynamic_index_in_dim(blocks, 1 - core, 1, keepdims=False),
            lax.dynamic_index_in_dim(blocks, core, 1, keepdims=False),
        )

    send, keep = weight_call(
        n_dp,
        core.reshape(1),
        active,
        pre_rounded,
        hidden_rounded,
        up_rounded,
        attended,
        mixed_rounded,
        small,
    )
    core_got = swap(send, "dp", 1)
    back_q = query_strip(0, send)
    mine, x_got = first_split(keep, core_got, back_q)
    back_q = query_strip(1, back_q, mine)
    back_q = query_strip(2, back_q)
    back_kv = key_strip(0, back_q)
    share = add_blocks(mine, x_got, back_kv)
    pieces = scatter(share)
    cut = 2 * group_lanes
    early_cols = jnp.concatenate([back_q, back_kv[:, :cut]], axis=1)
    early_send, early_keep = core_split(outer_sum(inputs, early_cols))
    early_core = swap(early_send, "dp", 1)
    back_kv = key_strip(1, back_kv, early_send, share)
    early_mine, early_got = first_split(early_keep, early_core, back_kv)
    back_kv = key_strip(2, back_kv, early_mine)
    copies = summed_copies(pieces, 1, back_kv)
    all_sums = lax.all_gather(copies[0], "seq", axis=0, tiled=True)
    late_send, late_keep = core_split(outer_sum(inputs, back_kv[:, cut:]))
    late_mine, late_got = first_split(late_keep, swap(late_send, "dp", 1))
    early_pieces = scatter(add_blocks(early_mine, early_got, late_send))
    late_pieces = scatter(add_blocks(late_mine, late_got))
    early_all = everyone(summed_copies(early_pieces, n_seq))
    late_all = everyone(summed_copies(late_pieces, n_seq, all_sums))

    kv_weight = (
        weight_in[:, D:]
        .reshape(D, 2, groups, group_lanes)
        .transpose(0, 2, 1, 3)
        .reshape(D, 2 * D)
    )
    input_grad = (
        back_mixed + back_product(back_q, weight_in[:, :D]) + back_product(back_kv, kv_weight)
    )
    kv_all = jnp.concatenate([early_all[:, D:], late_all], axis=1)
    kv_all = kv_all.reshape(-1, groups, 2, group_lanes).transpose(0, 2, 1, 3)
    grad_in_total = jnp.concatenate(
        [early_all[:, :D], kv_all.reshape(-1, 2 * D)], axis=1
    ).astype(f32)
    down_rows = FF // n_dp
    part_rows = D // n_dp
    grad_down = all_sums[:down_rows].astype(f32)
    grad_up = (
        all_sums[down_rows : down_rows + (FF // D) * part_rows]
        .reshape(FF // D, part_rows, D)
        .transpose(1, 0, 2)
        .reshape(part_rows, FF)
        .astype(f32)
    )
    at = down_rows + (FF // D) * part_rows
    grad_mix = all_sums[at : at + part_rows].astype(f32)
    flat = all_sums[at + part_rows :].reshape(-1).astype(f32)
    vectors_out = [flat[i * part_rows : (i + 1) * part_rows] for i in range(6)]
    bias_up_out = flat[6 * part_rows : 6 * part_rows + down_rows]
    return (
        result[None],
        input_grad[None],
        grad_in_total,
        grad_mix,
        grad_up,
        grad_down,
        vectors_out[0],
        bias_up_out,
        vectors_out[1],
        *vectors_out[2:],
    )


def solution(mesh):
    placed = (
        P("dp", "seq", None),
        P("dp", None),
        P("dp", None),
        P("dp", None),
        P("dp", None),
        P("dp"),
        P("dp"),
        P("dp"),
        P("dp"),
        P("dp"),
        P("dp"),
        P("dp"),
        P("dp", None),
        P("dp", None),
        P("dp", None, None),
        P("dp", "seq", None),
    )
    return jax.shard_map(
        on_device,
        mesh=mesh,
        in_specs=placed,
        out_specs=(
            P("dp", "seq", None),
            P("dp", "seq", None),
            P("dp", None),
            P("dp", None),
            P("dp", None),
            P("dp", None),
            P("dp"),
            P("dp"),
            P("dp"),
            P("dp"),
            P("dp"),
            P("dp"),
            P("dp"),
        ),
        check_vma=False,
    )
```

```python
import functools

import jax
import jax.numpy as jnp
from jax import lax
from jax.experimental import pallas as pl
from jax.experimental.pallas import tpu as pltpu
from jax.sharding import PartitionSpec as P

D = 768
HEADS = 12
HD = 64
CL = 128
MOSTB = 16
PAIRS = HEADS // 2
WINDOW = MOSTB * CL
HALO = (MOSTB - 1) * CL
CHUNK = 512
KCHUNK = 512
TILES_AT_ONCE = 2
PACK = 4
NEG = -1e30
TERMS = 5
FF = 3072
RTILE = 512
FCHUNK = 768
SCALE2 = HD ** (-0.5) * 1.4426950408889634

EPSILON = 1e-05


def shifted(value, axis, by):
    devices = lax.axis_size(axis)
    pairs = [(i, i + by) for i in range(devices) if 0 <= i + by < devices]
    return lax.ppermute(value, axis, pairs)


def halo_parts(value):
    own = value.shape[0]
    far = HALO - own
    devices = lax.axis_size("seq")
    assert 0 < far <= own and devices % 2 == 0
    partner = lax.ppermute(value, "seq", [(i, i ^ 1) for i in range(devices)])
    pairs = [(i, i - 1 if i % 2 == 0 else i + 1) for i in range(devices)]
    other = lax.ppermute(value, "seq", [(i, k) for i, k in pairs if 0 <= k < devices])
    before = shifted(value[own - far :], "seq", 2)
    following = shifted(value[:far], "seq", -2)
    return [before, partner, value, other, following]


def places(starts, tiles, parts):
    far, own = parts[0].shape[0], parts[2].shape[0]
    return [
        0,
        pl.multiple_of(starts[tiles] * CL, CL),
        far + own,
        pl.multiple_of(starts[tiles + 1] * CL, CL),
        far + 3 * own,
    ]


def live_tokens(runs, trim, positions):
    ends = jnp.cumsum(runs) * CL
    starts = ends - runs * CL
    lengths = runs * CL - trim
    inside = (positions[..., None] >= starts) & (positions[..., None] < starts + lengths)
    return jnp.any(inside, axis=-1)


def outer_sum(left, right):
    return lax.dot_general(
        left, right, (((0,), (0,)), ((), ())), preferred_element_type=jnp.float32
    )


def back_product(left, right):
    return lax.dot_general(
        left, right, (((1,), (1,)), ((), ())), preferred_element_type=jnp.float32
    )


def plain_product(left, right):
    return jnp.dot(left, right, preferred_element_type=jnp.float32)


def stacked(tile):
    lane = lax.broadcasted_iota(jnp.int32, tile.shape, 1)
    zero = jnp.zeros_like(tile)
    heads = tile.shape[1] // HD
    return jnp.concatenate(
        [
            jnp.where((lane >= h * HD) & (lane < (h + 1) * HD), tile, zero)
            for h in range(heads)
        ],
        axis=0,
    )


def unstacked(stack):
    heads = stack.shape[1] // HD
    lane = lax.broadcasted_iota(jnp.int32, (CL, heads * HD), 1)
    result = stack[:CL]
    for h in range(1, heads):
        result = jnp.where(lane >= h * HD, stack[h * CL : (h + 1) * CL], result)
    return result


def as_column(row):
    return jnp.broadcast_to(row, (CL, CL)).T


def lane_of(tile, lane):
    lanes = lax.broadcasted_iota(jnp.int32, tile.shape, 1)
    return jnp.sum(jnp.where(lanes == lane, tile, 0.0), axis=1, keepdims=True)


def masked(scores, cols, row_ref, begin):
    parts = []
    wide = scores.shape[1]
    for half, one in enumerate(cols):
        row = row_ref[0, half : half + 1, pl.ds(begin, wide)]
        block = scores[half * CL : (half + 1) * CL]
        col = jnp.concatenate([one] * (wide // CL), axis=1)
        parts.append(jnp.where(col == row, block, NEG))
    return jnp.concatenate(parts, axis=0)


def assemble(parts, offsets, whole):
    for part, at in zip(parts, offsets):
        whole[pl.ds(at, part.shape[0]), :] = part[...]


def ahead(steps, produce, consume):
    held = produce(*steps[0])
    for i, step in enumerate(steps):
        following = produce(*steps[i + 1]) if i + 1 < len(steps) else None
        consume(*step, held)
        held = following


def attend_kernel(tiles, n_parts, starts, q_ref, *refs):
    k_parts, refs = refs[:n_parts], refs[n_parts:]
    v_parts, refs = refs[:n_parts], refs[n_parts:]
    qid_ref, kid_ref, out_ref, lse_ref, rate_ref, p_ref, k_ref, v_ref, *slots = refs
    s_refs, top_refs = slots[:TILES_AT_ONCE], slots[TILES_AT_ONCE:]
    group, step = pl.program_id(0), pl.program_id(1)
    heads = q_ref.shape[1] // HD
    chunks = WINDOW // CHUNK

    @pl.when(step == 0)
    def _():
        offsets = places(starts, tiles, k_parts)
        assemble(k_parts, offsets, k_ref)
        assemble(v_parts, offsets, v_ref)

    @pl.when((group == 0) & (step == 0))
    def _():
        lse_ref[...] = jnp.zeros_like(lse_ref)
        rate_ref[...] = jnp.zeros_like(rate_ref)

    def first_half(slot):
        tile = TILES_AT_ONCE * step + slot
        own = pl.multiple_of(HALO + tile * CL, CL)
        return dict(
            begin=pl.multiple_of(starts[tile] * CL, CL),
            query=stacked(q_ref[slot * CL : (slot + 1) * CL, :]),
            cols=[
                as_column(qid_ref[0, half : half + 1, pl.ds(own, CL)]) for half in range(heads)
            ],
        )

    def score(state, slot, j):
        at = pl.multiple_of(state["begin"] + j * CHUNK, CL)
        scores = back_product(state["query"], k_ref[pl.ds(at, CHUNK), :])
        scores = masked(scores, state["cols"], kid_ref, at)
        s_refs[slot][:, j * CHUNK : (j + 1) * CHUNK] = scores
        top = scores[:, :CL]
        for i in range(1, CHUNK // CL):
            top = jnp.maximum(top, scores[:, i * CL : (i + 1) * CL])
        if j > 0:
            top = jnp.maximum(top, top_refs[slot][...])
        top_refs[slot][...] = top

    states = [first_half(0)]
    for j in range(chunks):
        score(states[0], 0, j)
    for slot in range(TILES_AT_ONCE):
        if slot + 1 < TILES_AT_ONCE:
            states.append(first_half(slot + 1))
        state = states[slot]
        peak = jnp.max(top_refs[slot][...], axis=1, keepdims=True)
        total = jnp.zeros((heads * CL, CL), jnp.float32)
        result = jnp.zeros((heads * CL, heads * HD), jnp.float32)
        for j in range(chunks):
            if slot + 1 < TILES_AT_ONCE:
                score(states[slot + 1], slot + 1, j)
            at = pl.multiple_of(state["begin"] + j * CHUNK, CL)
            columns = slice(j * CHUNK, (j + 1) * CHUNK)
            weights = jnp.exp2((s_refs[slot][:, columns] - peak) * SCALE2)
            for i in range(CHUNK // CL):
                total = total + weights[:, i * CL : (i + 1) * CL]
            p_ref[0, slot, :, columns] = weights.astype(jnp.bfloat16)
            result = result + plain_product(
                p_ref[0, slot, :, columns], v_ref[pl.ds(at, CHUNK), :]
            )
        total = jnp.sum(total, axis=1, keepdims=True)
        rate = 1.0 / total
        result = result * rate
        lse = peak + jnp.log(total) * HD**0.5
        live = (state["cols"][0] >= 0.0).astype(jnp.float32)
        live = jnp.concatenate([live] * (heads * HD // CL), axis=1)
        rows = slice(slot * CL, (slot + 1) * CL)
        out_ref[rows, :] = (unstacked(result) * live).astype(jnp.bfloat16)
        here = pl.ds(pl.multiple_of((TILES_AT_ONCE * step + slot) * CL, CL), CL)
        lane = lax.broadcasted_iota(jnp.int32, (CL, CL), 1)
        kept, kept_rate = lse_ref[here, :], rate_ref[here, :]
        for half in range(heads):
            first = (heads * group + half) * TERMS
            inside = (lane >= first) & (lane < first + TERMS)
            part = slice(half * CL, (half + 1) * CL)
            kept = jnp.where(inside, lse[part], kept)
            kept_rate = jnp.where(inside, rate[part], kept_rate)
        lse_ref[here, :] = kept
        rate_ref[here, :] = kept_rate


def query_kernel(tiles, n_parts, first_head, starts, *refs):
    k_parts, refs = refs[:n_parts], refs[n_parts:]
    v_parts, refs = refs[:n_parts], refs[n_parts:]
    g_ref, p_ref, rate_ref, delta_ref = refs[:4]
    out_ref, k_ref, v_ref = refs[-3:]
    step = pl.program_id(0)
    heads = g_ref.shape[1] // HD
    chunks = WINDOW // CHUNK

    @pl.when(step == 0)
    def _():
        offsets = places(starts, tiles, k_parts)
        assemble(k_parts, offsets, k_ref)
        assemble(v_parts, offsets, v_ref)

    states = {}

    def state_of(slot):
        if slot not in states:
            rows = slice(slot * CL, (slot + 1) * CL)
            columns = [
                jnp.concatenate(
                    [lane_of(ref[rows, :], (first_head + half) * TERMS) for half in range(heads)],
                    axis=0,
                )
                for ref in (delta_ref, rate_ref)
            ]
            states[slot] = dict(
                begin=pl.multiple_of(starts[TILES_AT_ONCE * step + slot] * CL, CL),
                back=stacked(g_ref[rows, :]),
                delta=columns[0],
                rate=columns[1],
                result=jnp.zeros((heads * CL, heads * HD), jnp.float32),
            )
        return states[slot]

    def produce(slot, j):
        state = state_of(slot)
        at = pl.multiple_of(state["begin"] + j * CHUNK, CL)
        return back_product(state["back"], v_ref[pl.ds(at, CHUNK), :])

    def consume(slot, j, back_probs):
        state = state_of(slot)
        at = pl.multiple_of(state["begin"] + j * CHUNK, CL)
        weights = p_ref[0, slot, :, j * CHUNK : (j + 1) * CHUNK].astype(jnp.float32)
        back_scores = weights * (back_probs - state["delta"])
        state["result"] = state["result"] + plain_product(
            back_scores.astype(jnp.bfloat16), k_ref[pl.ds(at, CHUNK), :]
        )
        if j == chunks - 1:
            out_ref[slot * CL : (slot + 1) * CL, :] = unstacked(
                state["result"] * (state["rate"] * HD ** (-0.5))
            ).astype(jnp.bfloat16)

    ahead(
        [(slot, j) for slot in range(TILES_AT_ONCE) for j in range(chunks)], produce, consume
    )


def key_kernel(tiles, n_parts, first_pair, starts, k_ref, v_ref, *refs):
    q_parts, refs = refs[:n_parts], refs[n_parts:]
    g_parts, refs = refs[:n_parts], refs[n_parts:]
    a_parts, refs = refs[:n_parts], refs[n_parts:]
    qid_ref, kid_ref = refs[:2]
    out_ref, q_ref, g_ref = refs[-3:]
    step_pair = pl.program_id(0)
    pair = first_pair + step_pair
    offsets = places(starts, tiles, q_parts)
    for at, q_part, g_part, a_part in zip(offsets, q_parts, g_parts, a_parts):
        rows = pl.ds(at, q_part.shape[0])
        q_ref[rows, : 2 * HD] = q_part[...]
        q_ref[rows, 2 * HD :] = a_part[...]
        g_ref[rows, : 2 * HD] = g_part[...]
        g_ref[rows, 2 * HD :] = a_part[...]

    lane = lax.broadcasted_iota(jnp.int32, (CL, CL), 1)
    lse_pick, delta_pick = [], []
    for half in range(2):
        first = (2 * pair + half) * TERMS
        lse_pick.append(jnp.where((lane >= first) & (lane < first + 3), -1.0, 0.0))
        delta_pick.append(jnp.where((lane >= first + 3) & (lane < first + TERMS), -1.0, 0.0))
    lse_pick = jnp.concatenate(lse_pick, axis=0).astype(jnp.bfloat16)
    delta_pick = jnp.concatenate(delta_pick, axis=0).astype(jnp.bfloat16)
    key_lanes = pl.ds(pl.multiple_of(step_pair * 2 * HD, 2 * HD), 2 * HD)
    value_lanes = pl.ds(
        pl.multiple_of(out_ref.shape[1] // 2 + step_pair * 2 * HD, 2 * HD), 2 * HD
    )

    def some_tiles(step, carry):
        states = {}

        def state_of(slot):
            if slot not in states:
                tile = TILES_AT_ONCE * step + slot
                own = pl.multiple_of(HALO + tile * CL, CL)
                here = pl.multiple_of(tile * CL, CL)
                states[slot] = dict(
                    begin=pl.multiple_of(starts[tile] * CL, CL),
                    here=here,
                    keys=jnp.concatenate([stacked(k_ref[pl.ds(here, CL), :]), lse_pick], axis=1),
                    values=jnp.concatenate(
                        [stacked(v_ref[pl.ds(here, CL), :]), delta_pick], axis=1
                    ),
                    cols=[
                        as_column(kid_ref[0, half : half + 1, pl.ds(own, CL)]) for half in range(2)
                    ],
                    key_sum=jnp.zeros((2 * CL, 2 * HD), jnp.float32),
                    value_sum=jnp.zeros((2 * CL, 2 * HD), jnp.float32),
                )
            return states[slot]

        def produce(slot, j):
            state = state_of(slot)
            at = pl.multiple_of(state["begin"] + j * KCHUNK, CL)
            scores = back_product(state["keys"], q_ref[pl.ds(at, KCHUNK), :])
            return scores, back_product(state["values"], g_ref[pl.ds(at, KCHUNK), :])

        def consume(slot, j, held):
            state = state_of(slot)
            at = pl.multiple_of(state["begin"] + j * KCHUNK, CL)
            scores, back_probs = held
            probs = jnp.exp2(masked(scores * SCALE2, state["cols"], qid_ref, at))
            back_scores = probs * back_probs
            state["value_sum"] = state["value_sum"] + plain_product(
                probs.astype(jnp.bfloat16), g_ref[pl.ds(at, KCHUNK), : 2 * HD]
            )
            state["key_sum"] = state["key_sum"] + plain_product(
                back_scores.astype(jnp.bfloat16), q_ref[pl.ds(at, KCHUNK), : 2 * HD]
            )
            if j == WINDOW // KCHUNK - 1:
                rows = pl.ds(state["here"], CL)
                out_ref[rows, key_lanes] = (
                    unstacked(state["key_sum"]) * HD ** (-0.5)
                ).astype(jnp.bfloat16)
                out_ref[rows, value_lanes] = unstacked(state["value_sum"]).astype(jnp.bfloat16)

        ahead(
            [(slot, j) for slot in range(TILES_AT_ONCE) for j in range(WINDOW // KCHUNK)],
            produce,
            consume,
        )
        return carry

    lax.fori_loop(0, tiles // TILES_AT_ONCE, some_tiles, 0)


def lane_block(rows, first, heads=2):
    return pl.BlockSpec((rows, heads * HD), lambda pair, starts: (0, first + pair))


def fixed_lanes(rows, block):
    return pl.BlockSpec((rows, 2 * HD), lambda pair, starts: (0, block))


def row_block(columns, first, heads=2):
    return pl.BlockSpec((1, heads, columns), lambda pair, starts: (first + pair, 0, 0))


UNREAD = pl.BlockSpec(memory_space=pl.ANY)


VMEM_LIMIT = 60 * 1024 * 1024


def strip_call(
    kernel, length, grid, in_specs, out_specs, out_shape, scratch, args, aliases=None
):
    return pl.pallas_call(
        kernel,
        out_shape=out_shape,
        grid_spec=pltpu.PrefetchScalarGridSpec(
            num_scalar_prefetch=1,
            grid=grid,
            in_specs=in_specs,
            out_specs=out_specs,
            scratch_shapes=scratch,
        ),
        input_output_aliases=aliases or {},
        cost_estimate=work(length),
        compiler_params=pltpu.CompilerParams(vmem_limit_bytes=VMEM_LIMIT),
    )(*args)


def project_kernel(weight, *refs):
    half = len(refs) // 2
    for source, target in zip(refs[:half], refs[half:]):
        target[...] = plain_product(source[...], weight[...]).astype(target.dtype)


def project_call(parts, weight):
    depth, columns = weight.shape
    block = PACK * HD
    return pl.pallas_call(
        project_kernel,
        grid=(columns // block,),
        in_specs=[pl.BlockSpec((depth, block), lambda i: (0, i))]
        + [pl.BlockSpec(part.shape, lambda i: (0, 0)) for part in parts],
        out_specs=[pl.BlockSpec((part.shape[0], block), lambda i: (0, i)) for part in parts],
        out_shape=[jax.ShapeDtypeStruct((part.shape[0], columns), part.dtype) for part in parts],
        cost_estimate=work(15),
        compiler_params=pltpu.CompilerParams(vmem_limit_bytes=VMEM_LIMIT),
    )(weight, *parts)


def gelu_terms(value):
    t = 1.0 / (1.0 + (0.3275911 * 0.7071067811865476) * jnp.abs(value))
    bell = jnp.exp2(value * value * (-0.5 * 1.4426950408889634))
    tail = 0.5 * 1.061405429
    for term in (-0.5 * 1.453152027, 0.5 * 1.421413741, -0.5 * 0.284496736, 0.5 * 0.254829592):
        tail = tail * t + term
    tail = tail * t * bell
    cdf = jnp.where(value >= 0.0, 1.0 - tail, tail)
    return value * cdf, cdf + value * (0.3989422804014327 * bell)


def normalised(values):
    mean = jnp.mean(values, axis=-1, keepdims=True)
    centre = values - mean
    rate = lax.rsqrt(jnp.mean(centre * centre, axis=-1, keepdims=True) + EPSILON)
    return centre * rate, rate


def norm_back(scaled, unit, rate):
    first = jnp.mean(scaled, axis=-1, keepdims=True)
    second = jnp.mean(scaled * unit, axis=-1, keepdims=True)
    return rate * (scaled - first - unit * second)


def row_sums(values):
    rows, columns = values.shape
    return jnp.sum(values.reshape(rows // 8, 8, columns), axis=0)


def chain_kernel(
    att_ref,
    tok_ref,
    cot_ref,
    live_ref,
    lse_ref,
    mix_ref,
    up_ref,
    down_ref,
    vec_ref,
    bias_up_ref,
    spread_ref,
    out_ref,
    act_ref,
    upr_ref,
    hid_ref,
    pre_ref,
    mixr_ref,
    mixed_ref,
    back_ref,
    delta_ref,
    sum_ref,
    sum_up_ref,
    slope_ref,
):
    width = up_ref.shape[1]
    bias_mix, bias_down = vec_ref[0:1], vec_ref[1:2]
    gain_one, shift_one = vec_ref[2:3], vec_ref[3:4]
    gain_two, shift_two = vec_ref[4:5], vec_ref[5:6]

    @pl.when(pl.program_id(0) == 0)
    def _():
        sum_ref[...] = jnp.zeros_like(sum_ref)
        sum_up_ref[...] = jnp.zeros_like(sum_up_ref)

    attended = att_ref[...]
    mixed = plain_product(attended, mix_ref[...]) + bias_mix + tok_ref[...].astype(jnp.float32)
    unit_one, rate_one = normalised(mixed)
    hidden = unit_one * gain_one + shift_one
    hidden_rounded = hidden.astype(jnp.bfloat16)
    hid_ref[...] = hidden_rounded
    down_sum = bias_down + hidden
    for f in range(0, width, FCHUNK):
        up_sum = plain_product(hidden_rounded, up_ref[:, f : f + FCHUNK]) + (
            bias_up_ref[0:1, f : f + FCHUNK]
        )
        active, slope = gelu_terms(up_sum)
        active = active.astype(jnp.bfloat16)
        act_ref[:, f : f + FCHUNK] = active
        slope_ref[:, f : f + FCHUNK] = slope
        down_sum = down_sum + plain_product(active, down_ref[f : f + FCHUNK, :])
    unit_two, rate_two = normalised(down_sum)
    out_ref[...] = (unit_two * gain_two + shift_two).astype(jnp.bfloat16)
    cot = cot_ref[...].astype(jnp.float32)
    back_pre = norm_back(cot * gain_two, unit_two, rate_two)
    pre_rounded = back_pre.astype(jnp.bfloat16)
    pre_ref[...] = pre_rounded
    sum_ref[4] += row_sums(cot * unit_two)
    sum_ref[5] += row_sums(cot)
    sum_ref[1] += row_sums(back_pre)
    back_hidden = back_pre
    for f in range(0, width, FCHUNK):
        back_up = back_product(pre_rounded, down_ref[f : f + FCHUNK, :]) * (
            slope_ref[:, f : f + FCHUNK]
        )
        sum_up_ref[:, f : f + FCHUNK] += row_sums(back_up)
        up_rounded = back_up.astype(jnp.bfloat16)
        upr_ref[:, f : f + FCHUNK] = up_rounded
        back_hidden = back_hidden + back_product(up_rounded, up_ref[:, f : f + FCHUNK])
    sum_ref[2] += row_sums(back_hidden * unit_one)
    sum_ref[3] += row_sums(back_hidden)
    back_mixed = norm_back(back_hidden * gain_one, unit_one, rate_one)
    sum_ref[0] += row_sums(back_mixed)
    mixed_ref[...] = back_mixed
    mixed_rounded = back_mixed.astype(jnp.bfloat16)
    mixr_ref[...] = mixed_rounded
    back = back_product(mixed_rounded, mix_ref[...]).astype(jnp.bfloat16)
    back = jnp.where(live_ref[...] > 0.5, back, jnp.zeros_like(back))
    back_ref[:, : back.shape[1]] = back
    terms = back.astype(jnp.float32) * attended.astype(jnp.float32)
    high = terms.astype(jnp.bfloat16)
    low = (terms - high.astype(jnp.float32)).astype(jnp.bfloat16)
    delta = plain_product(high, spread_ref[...]) + plain_product(low, spread_ref[...])
    delta_ref[...] = delta
    lane = lax.broadcasted_iota(jnp.int32, delta.shape, 1)
    term = lane % TERMS
    whole = jnp.where(term < 3, lse_ref[...], delta)
    first = whole.astype(jnp.bfloat16)
    rest = whole - first.astype(jnp.float32)
    second = rest.astype(jnp.bfloat16)
    third = (rest - second.astype(jnp.float32)).astype(jnp.bfloat16)
    picked = jnp.where(
        (term == 0) | (term == 3),
        first.astype(jnp.float32),
        jnp.where((term == 2), third.astype(jnp.float32), second.astype(jnp.float32)),
    )
    picked = jnp.where(lane < TERMS * HEADS, picked, 0.0)
    back_ref[:, back.shape[1] :] = picked.astype(jnp.bfloat16)


def chain_call(att, tok, cot, live, lse, mix, up, down, vectors, bias_up):
    rows, width = tok.shape
    wide = up.shape[1]
    head_of = jnp.arange(width, dtype=jnp.int32)[:, None] // HD
    spread = (head_of == jnp.arange(2 * HD, dtype=jnp.int32)[None, :] // TERMS).astype(jnp.bfloat16)

    def tile(columns):
        return pl.BlockSpec((RTILE, columns), lambda i: (i, 0))

    def fixed(*shape):
        return pl.BlockSpec(shape, lambda i: (0,) * len(shape))

    bf16, f32 = jnp.bfloat16, jnp.float32
    return pl.pallas_call(
        chain_kernel,
        grid=(rows // RTILE,),
        in_specs=[
            tile(width),
            tile(width),
            tile(width),
            tile(1),
            tile(2 * HD),
            fixed(*mix.shape),
            fixed(*up.shape),
            fixed(*down.shape),
            fixed(*vectors.shape),
            fixed(*bias_up.shape),
            fixed(*spread.shape),
        ],
        out_specs=[
            tile(width),
            tile(wide),
            tile(wide),
            tile(width),
            tile(width),
            tile(width),
            tile(width),
            tile(width + 2 * HD),
            tile(2 * HD),
            fixed(6, 8, width),
            fixed(8, wide),
        ],
        out_shape=[
            jax.ShapeDtypeStruct((rows, width), bf16),
            jax.ShapeDtypeStruct((rows, wide), bf16),
            jax.ShapeDtypeStruct((rows, wide), bf16),
            jax.ShapeDtypeStruct((rows, width), bf16),
            jax.ShapeDtypeStruct((rows, width), bf16),
            jax.ShapeDtypeStruct((rows, width), bf16),
            jax.ShapeDtypeStruct((rows, width), f32),
            jax.ShapeDtypeStruct((rows, width + 2 * HD), bf16),
            jax.ShapeDtypeStruct((rows, 2 * HD), f32),
            jax.ShapeDtypeStruct((6, 8, width), f32),
            jax.ShapeDtypeStruct((8, wide), f32),
        ],
        scratch_shapes=[pltpu.VMEM((RTILE, wide), f32)],
        cost_estimate=work(44),
        compiler_params=pltpu.CompilerParams(vmem_limit_bytes=VMEM_LIMIT),
    )(att, tok, cot, live, lse, mix, up, down, vectors, bias_up, spread)


def weight_kernel(n_dp, core_ref, act, pre, hid, upr, att, mixr, small, *refs):
    send, keep, tmp = refs[-3:]
    step = pl.program_id(0)
    core = core_ref[0]
    pieces = FF // D
    down_rows = FF // n_dp
    part_rows = D // n_dp

    def put(x, row, rows, begin):
        mine = pl.multiple_of(begin + core * rows, 16)
        other = pl.multiple_of(begin + (1 - core) * rows, 16)
        keep[pl.ds(x, 1), pl.ds(row, rows), :] = tmp[pl.ds(mine, rows), :][None]
        send[pl.ds(x, 1), pl.ds(row, rows), :] = tmp[pl.ds(other, rows), :][None]

    @pl.when(step < pieces)
    def _():
        tmp[...] = outer_sum(act[...], pre[...]).astype(jnp.bfloat16)
        per = D // down_rows
        for b in range(per):
            block = step * per + b
            x = block // 2
            rows = tmp[b * down_rows : (b + 1) * down_rows, :]

            @pl.when(lax.rem(block, 2) == core)
            def _():
                keep[pl.ds(x, 1), 0:down_rows, :] = rows[None]

            @pl.when(lax.rem(block, 2) != core)
            def _():
                send[pl.ds(x, 1), 0:down_rows, :] = rows[None]

    @pl.when((step >= pieces) & (step < 2 * pieces))
    def _():
        tmp[...] = outer_sum(hid[...], upr[...]).astype(jnp.bfloat16)
        row = pl.multiple_of(down_rows + (step - pieces) * part_rows, 16)
        for x in range(n_dp // 2):
            put(x, row, part_rows, 2 * x * part_rows)

    @pl.when(step == 2 * pieces)
    def _():
        tmp[...] = outer_sum(att[...], mixr[...]).astype(jnp.bfloat16)
        row = down_rows + pieces * part_rows
        for x in range(n_dp // 2):
            put(x, row, part_rows, 2 * x * part_rows)
            last = row + part_rows
            rows = keep.shape[1] - last
            keep[x, last:, :] = small[pl.ds(2 * x + core, 1), :, :][0]
            send[x, last:, :] = small[pl.ds(2 * x + 1 - core, 1), :, :][0]


def weight_call(n_dp, core, act, pre, hid, upr, att, mixr, small, *needs):
    rows = act.shape[0]
    pieces = FF // D
    out_rows = FF // n_dp + (pieces + 1) * (D // n_dp) + small.shape[1]

    def fixed(*shape):
        return pl.BlockSpec(shape, lambda i, c: (0,) * len(shape))

    def stepped(first):
        return pl.BlockSpec((rows, D), lambda i, c: (0, jnp.clip(i - first, 0, pieces - 1)))

    shape = (n_dp // 2, out_rows, D)
    return pl.pallas_call(
        functools.partial(weight_kernel, n_dp),
        out_shape=[jax.ShapeDtypeStruct(shape, jnp.bfloat16)] * 2,
        grid_spec=pltpu.PrefetchScalarGridSpec(
            num_scalar_prefetch=1,
            grid=(2 * pieces + 1,),
            in_specs=[
                stepped(0),
                fixed(rows, D),
                fixed(rows, D),
                stepped(pieces),
                fixed(rows, D),
                fixed(rows, D),
                fixed(*small.shape),
            ]
            + [UNREAD] * len(needs),
            out_specs=[fixed(*shape)] * 2,
            scratch_shapes=[pltpu.VMEM((D, D), jnp.bfloat16)],
        ),
        cost_estimate=work(22),
        compiler_params=pltpu.CompilerParams(vmem_limit_bytes=VMEM_LIMIT),
    )(core, act, pre, hid, upr, att, mixr, small, *needs)


def swap(value, axis, bit):
    devices = lax.axis_size(axis)
    return lax.ppermute(value, axis, [(i, i ^ bit) for i in range(devices)])


def dp_gather(shard, dp_rank):
    blocks = shard[None]
    bit = lax.axis_size("dp") // 2
    while bit >= 1:
        got = swap(blocks, "dp", bit)
        high = ((dp_rank // bit) % 2) == 1
        first = jnp.where(high, got, blocks)
        second = jnp.where(high, blocks, got)
        blocks = jnp.stack([first, second], axis=1).reshape((-1,) + shard.shape)
        bit //= 2
    return blocks.reshape((-1,) + shard.shape[1:])


def work(microseconds):
    return pl.CostEstimate(
        flops=int(microseconds * 0.4e9), transcendentals=0, bytes_accessed=1 << 20
    )


def row_tile(rows, limit=512):
    for size in range(min(rows, limit), 15, -1):
        if rows % size == 0 and size % 16 == 0:
            return size
    return rows


def plain_params():
    return pltpu.CompilerParams(vmem_limit_bytes=VMEM_LIMIT)


def split_add_kernel(which, keep_mine, got_mine, keep_other, got_other, *refs):
    mine, other = refs[-2:]
    mine[...] = (keep_mine[...].astype(jnp.float32) + got_mine[...].astype(jnp.float32)).astype(
        mine.dtype
    )
    other[...] = (keep_other[...].astype(jnp.float32) + got_other[...].astype(jnp.float32)).astype(
        other.dtype
    )


def split_add(keep, got, which, *needs):
    blocks, rows, columns = keep.shape
    tile = row_tile(rows)

    def spec(flip):
        def place(b, i, w):
            bit = 1 - w[0] if flip else w[0]
            return 2 * b + bit, i, 0

        return pl.BlockSpec((1, tile, columns), place)

    out = pl.BlockSpec((1, tile, columns), lambda b, i, w: (b, i, 0))
    shape = jax.ShapeDtypeStruct((blocks // 2, rows, columns), keep.dtype)
    return pl.pallas_call(
        split_add_kernel,
        out_shape=[shape, shape],
        grid_spec=pltpu.PrefetchScalarGridSpec(
            num_scalar_prefetch=1,
            grid=(blocks // 2, rows // tile),
            in_specs=[spec(False), spec(False), spec(True), spec(True)] + [UNREAD] * len(needs),
            out_specs=[out, out],
        ),
        cost_estimate=work(4),
        compiler_params=plain_params(),
    )(which, keep, got, keep, got, *needs)


def add_kernel(left, right, *refs):
    out = refs[-1]
    out[...] = (left[0].astype(jnp.float32) + right[0].astype(jnp.float32)).astype(out.dtype)


def add_blocks(left, right, *needs):
    _, rows, columns = left.shape
    tile = row_tile(rows)
    spec = pl.BlockSpec((1, tile, columns), lambda i: (0, i, 0))
    return pl.pallas_call(
        add_kernel,
        grid=(rows // tile,),
        in_specs=[spec, spec] + [UNREAD] * len(needs),
        out_specs=pl.BlockSpec((tile, columns), lambda i: (i, 0)),
        cost_estimate=work(3),
        out_shape=jax.ShapeDtypeStruct((rows, columns), left.dtype),
        compiler_params=plain_params(),
    )(left, right, *needs)


def pieces_kernel(pieces, *refs):
    out = refs[-1]
    total = pieces[0].astype(jnp.float32)
    for i in range(1, pieces.shape[0]):
        total = total + pieces[i].astype(jnp.float32)
    total = total.astype(out.dtype)
    for i in range(out.shape[0]):
        out[i] = total


def summed_copies(pieces, copies, *needs):
    _, rows, columns = pieces.shape
    return pl.pallas_call(
        pieces_kernel,
        in_specs=[pl.BlockSpec(memory_space=pltpu.VMEM)] + [UNREAD] * len(needs),
        out_specs=pl.BlockSpec(memory_space=pltpu.VMEM),
        out_shape=jax.ShapeDtypeStruct((copies, rows, columns), pieces.dtype),
        cost_estimate=work(2),
        compiler_params=plain_params(),
    )(pieces, *needs)


def gate_kernel(value, *refs):
    refs[-1][...] = value[...]


def gated(value, *needs):
    return pl.pallas_call(
        gate_kernel,
        in_specs=[pl.BlockSpec(memory_space=pltpu.VMEM)] + [UNREAD] * len(needs),
        out_specs=pl.BlockSpec(memory_space=pltpu.VMEM),
        out_shape=jax.ShapeDtypeStruct(value.shape, value.dtype),
        cost_estimate=work(1),
        compiler_params=plain_params(),
    )(value, *needs)


def cluster_ids(group_order, own_start, span):
    padded = jnp.pad(group_order, ((0, 0), (HALO, HALO)), constant_values=-(1 << 24))
    wanted = lax.dynamic_slice_in_dim(padded, own_start, span, 1) - (own_start - HALO)
    tile_of = wanted >> 7
    lane_of_token = wanted & (CL - 1)
    cluster = (jnp.arange(span, dtype=jnp.int32) >> 7) + 1
    tile_hot = jnp.where(
        tile_of[:, :, None] == jnp.arange(span // CL, dtype=jnp.int32), cluster[None, :, None], 0
    ).astype(jnp.bfloat16)
    lane_hot = (lane_of_token[:, :, None] == jnp.arange(CL, dtype=jnp.int32)).astype(jnp.bfloat16)
    table = jnp.einsum("hpt,hpl->htl", tile_hot, lane_hot, preferred_element_type=jnp.float32)
    return table.reshape(HEADS, span) - 1.0


def on_device(
    tokens,
    input_weight,
    output_weight,
    up_weight,
    down_weight,
    output_bias,
    up_bias,
    down_bias,
    first_gain,
    first_shift,
    second_gain,
    second_shift,
    document_runs,
    document_trim,
    cluster_order,
    cotangent,
):
    bf16, f32 = jnp.bfloat16, jnp.float32
    n_dp = lax.axis_size("dp")
    n_seq = lax.axis_size("seq")
    dp_rank = lax.axis_index("dp")
    seq_rank = lax.axis_index("seq")
    inputs = tokens[0]
    tok_dev = inputs.shape[0]
    tiles = tok_dev // CL
    span = tok_dev + 2 * HALO
    own_start = seq_rank * tok_dev

    token_parts = halo_parts(inputs)
    n_parts = len(token_parts)

    weight_in = lax.all_gather(input_weight, "dp", axis=0, tiled=True)
    weight_up = lax.all_gather(up_weight, "dp", axis=0, tiled=True)
    weight_down = lax.all_gather(down_weight, "dp", axis=0, tiled=True)

    runs = document_runs[0]
    first_cluster = jnp.cumsum(runs) - runs
    own_clusters = seq_rank * tiles + jnp.arange(tiles, dtype=jnp.int32)
    doc_start = jnp.max(
        jnp.where(first_cluster[None, :] <= own_clusters[:, None], first_cluster[None, :], 0), axis=1
    )
    starts = (doc_start - seq_rank * tiles + (MOSTB - 1)).astype(jnp.int32)
    near_left = HALO // CL - tiles
    near = near_left + 2 * tiles * jnp.stack([1 - seq_rank % 2, seq_rank % 2])
    starts = jnp.concatenate([starts, near.astype(jnp.int32)])

    cids = cluster_ids(cluster_order[0], own_start, span)
    positions = own_start - HALO + jnp.arange(span, dtype=jnp.int32)
    live = live_tokens(runs, document_trim[0], positions)
    usable = live[None, :] & (cids >= 0.0)
    key_ids = jnp.where(usable, cids, -1.0).reshape(PAIRS, 2, span)
    query_ids = jnp.where(usable, cids, -2.0).reshape(PAIRS, 2, span)
    own_live = live[HALO : HALO + tok_dev, None].astype(f32)

    own = plain_product(inputs, weight_in).astype(bf16)
    partner = plain_product(token_parts[1], weight_in).astype(bf16)
    around = project_call([token_parts[0], token_parts[3], token_parts[4]], weight_in)
    projected = [around[0], partner, own, around[1], around[2]]
    vectors = [
        output_bias,
        down_bias,
        first_gain,
        first_shift,
        second_gain,
        second_shift,
        up_bias,
    ]
    mix_rows = output_weight.shape[0]
    packed = jnp.concatenate(vectors)
    pad_rows = -(-packed.shape[0] // (16 * D)) * 16
    packed = jnp.pad(packed, (0, pad_rows * D - packed.shape[0])).reshape(pad_rows, D)
    mix_shard = gated(jnp.concatenate([output_weight, packed], 0), own)
    mix_all = dp_gather(mix_shard, dp_rank)
    mix_all = mix_all.reshape(n_dp, mix_rows + pad_rows, D)
    weight_mix = mix_all[:, :mix_rows].reshape(D, D)
    small_all = mix_all[:, mix_rows:].reshape(n_dp, -1).astype(f32)
    vec = small_all[:, : 6 * mix_rows].reshape(n_dp, 6, mix_rows).transpose(1, 0, 2).reshape(6, D)
    vec = jnp.pad(vec, ((0, 2), (0, 0)))
    up_part = up_bias.shape[0]
    bias_up = small_all[:, 6 * mix_rows : 6 * mix_rows + up_part].reshape(1, FF)
    bias_up = jnp.pad(bias_up, ((0, 7), (0, 0)))
    heights = [part.shape[0] for part in token_parts]

    groups = HEADS // PACK
    group_lanes = PACK * HD
    group_key_ids = key_ids.reshape(groups, PACK, span)
    group_query_ids = query_ids.reshape(groups, PACK, span)
    group_scratch = pltpu.VMEM((span, group_lanes), bf16)

    def group_parts(third, first):
        return [lane_block(rows, third * groups + first, PACK) for rows in heights]

    steps = tiles // TILES_AT_ONCE
    step_rows = TILES_AT_ONCE * CL

    def of_group(rows, first):
        return pl.BlockSpec((rows, group_lanes), lambda g, t, starts: (0, first + g))

    def ids_of_group():
        return pl.BlockSpec((1, PACK, span), lambda g, t, starts: (g, 0, 0))

    step_block = pl.BlockSpec((step_rows, group_lanes), lambda g, t, starts: (t, g))
    whole_lanes = pl.BlockSpec((tok_dev, 2 * HD), lambda g, t, starts: (0, 0))
    attended, lse, rate, probs = strip_call(
        functools.partial(attend_kernel, tiles, n_parts),
        52,
        (groups, steps),
        [step_block]
        + [of_group(rows, groups) for rows in heights]
        + [of_group(rows, 2 * groups) for rows in heights]
        + [ids_of_group(), ids_of_group()],
        [
            step_block,
            whole_lanes,
            whole_lanes,
            pl.BlockSpec(
                (1, TILES_AT_ONCE, PACK * CL, WINDOW), lambda g, t, starts: (g, t, 0, 0)
            ),
        ],
        [
            jax.ShapeDtypeStruct((tok_dev, D), bf16),
            jax.ShapeDtypeStruct((tok_dev, 2 * HD), f32),
            jax.ShapeDtypeStruct((tok_dev, 2 * HD), f32),
            jax.ShapeDtypeStruct((groups, tiles, PACK * CL, WINDOW), bf16),
        ],
        [group_scratch, group_scratch]
        + [pltpu.VMEM((PACK * CL, WINDOW), f32)] * TILES_AT_ONCE
        + [pltpu.VMEM((PACK * CL, CL), f32)] * TILES_AT_ONCE,
        (starts, own, *projected, *projected, group_query_ids, group_key_ids),
    )

    (
        result,
        active,
        up_rounded,
        hidden_rounded,
        pre_rounded,
        mixed_rounded,
        back_mixed,
        back_own,
        delta,
        sums,
        sums_up,
    ) = chain_call(
        attended,
        inputs,
        cotangent[0],
        own_live,
        lse,
        weight_mix,
        weight_up,
        weight_down,
        vec,
        bias_up,
    )
    back_parts = halo_parts(back_own)

    small = jnp.concatenate(
        [
            jnp.sum(sums, axis=1).reshape(6, n_dp, mix_rows).transpose(1, 0, 2).reshape(n_dp, -1),
            jnp.sum(sums_up, axis=0).reshape(n_dp, -1),
        ],
        axis=1,
    ).astype(bf16)
    unit = 8 * n_seq
    fixed_rows = FF // n_dp + (FF // D + 1) * (D // n_dp)
    small_rows = -(-(fixed_rows + -(-small.shape[1] // D)) // unit) * unit - fixed_rows
    small = jnp.pad(small, ((0, 0), (0, small_rows * D - small.shape[1])))
    small = small.reshape(n_dp, small_rows, D)
    core = (dp_rank % 2).astype(jnp.int32)
    def query_strip(first, *needs):
        buffer = needs[:1] if first > 0 else ()

        def parts(third):
            return [
                pl.BlockSpec(
                    (rows, group_lanes), lambda t, starts: (0, third * groups + first)
                )
                for rows in heights
            ]

        block = pl.BlockSpec((step_rows, group_lanes), lambda t, starts: (t, first))
        lanes = pl.BlockSpec((step_rows, 2 * HD), lambda t, starts: (t, 0))
        in_specs = (
            parts(1)
            + parts(2)
            + [
                block,
                pl.BlockSpec(
                    (1, TILES_AT_ONCE, PACK * CL, WINDOW), lambda t, starts: (first, t, 0, 0)
                ),
                lanes,
                lanes,
            ]
            + [UNREAD] * len(needs)
        )
        return strip_call(
            functools.partial(query_kernel, tiles, n_parts, first * PACK),
            16,
            (steps,),
            in_specs,
            block,
            jax.ShapeDtypeStruct((tok_dev, D), bf16),
            [group_scratch, group_scratch],
            (starts, *projected, *projected, back_own, probs, rate, delta, *needs),
            {len(in_specs) + 1 - len(needs): 0} if buffer else None,
        )

    key_pairs = PACK // 2
    pair_scratch = pltpu.VMEM((span, 4 * HD), bf16)

    def key_strip(first, length, *needs):
        buffer = needs[:1] if first > 0 else ()
        pair = first * key_pairs

        def parts(third):
            return [lane_block(rows, third * PAIRS + pair) for rows in heights]

        in_specs = (
            [lane_block(tok_dev, PAIRS + pair), lane_block(tok_dev, 2 * PAIRS + pair)]
            + parts(0)
            + parts(0)
            + [fixed_lanes(rows, PAIRS) for rows in heights]
            + [row_block(span, pair), row_block(span, pair)]
            + [UNREAD] * len(needs)
        )
        return strip_call(
            functools.partial(key_kernel, tiles, n_parts, pair),
            length,
            (key_pairs,),
            in_specs,
            pl.BlockSpec((tok_dev, 2 * group_lanes), lambda step, starts: (0, first)),
            jax.ShapeDtypeStruct((tok_dev, 2 * D), bf16),
            [pair_scratch, pair_scratch],
            (
                starts,
                own,
                own,
                *projected,
                *back_parts,
                *back_parts,
                query_ids,
                key_ids,
                *needs,
            ),
            {len(in_specs) + 1 - len(needs): 0} if buffer else None,
        )

    def scatter(share):
        rows, columns = share.shape
        return lax.all_to_all(
            share.reshape(n_seq, rows // n_seq, columns), "seq", split_axis=0, concat_axis=0
        )

    def everyone(copies):
        got = lax.all_to_all(copies, "seq", split_axis=0, concat_axis=0)
        return got.reshape(-1, copies.shape[-1])

    def first_split(keep, got, *needs):
        bit = 2
        while True:
            which = ((dp_rank // bit) % 2).astype(jnp.int32).reshape(1)
            mine, other = split_add(keep, got, which, *needs)
            got = swap(other, "dp", bit)
            if mine.shape[0] == 1:
                return mine, got
            keep, bit, needs = mine, bit * 2, ()

    def core_split(grad):
        rows, columns = grad.shape
        blocks = grad.astype(bf16).reshape(n_dp // 2, 2, rows // n_dp, columns)
        return (
            lax.dynamic_index_in_dim(blocks, 1 - core, 1, keepdims=False),
            lax.dynamic_index_in_dim(blocks, core, 1, keepdims=False),
        )

    send, keep = weight_call(
        n_dp,
        core.reshape(1),
        active,
        pre_rounded,
        hidden_rounded,
        up_rounded,
        attended,
        mixed_rounded,
        small,
    )
    core_got = swap(send, "dp", 1)
    back_q = query_strip(0, send)
    mine, x_got = first_split(keep, core_got, back_q)
    back_q = query_strip(1, back_q, mine)
    back_q = query_strip(2, back_q)
    back_kv = key_strip(0, 27, back_q)
    share = add_blocks(mine, x_got, back_kv)
    pieces = scatter(share)
    cut = 2 * group_lanes
    early_cols = jnp.concatenate([back_q, back_kv[:, :cut]], axis=1)
    early_send, early_keep = core_split(outer_sum(inputs, early_cols))
    early_core = swap(early_send, "dp", 1)
    back_kv = key_strip(1, 27, back_kv, early_send, share)
    early_mine, early_got = first_split(early_keep, early_core, back_kv)
    back_kv = key_strip(2, 2, back_kv, early_mine)
    early_share = add_blocks(early_mine, early_got, back_kv)
    copies = summed_copies(pieces, 1, early_share)
    all_sums = lax.all_gather(copies[0], "seq", axis=0, tiled=True)
    late_send, late_keep = core_split(outer_sum(inputs, back_kv[:, cut:]))
    late_mine, late_got = first_split(late_keep, swap(late_send, "dp", 1))
    in_share = jnp.concatenate([early_share, add_blocks(late_mine, late_got)], axis=1)
    in_all = everyone(summed_copies(scatter(in_share), n_seq, all_sums))

    kv_weight = (
        weight_in[:, D:]
        .reshape(D, 2, groups, group_lanes)
        .transpose(0, 2, 1, 3)
        .reshape(D, 2 * D)
    )
    input_grad = (
        back_mixed + back_product(back_q, weight_in[:, :D]) + back_product(back_kv, kv_weight)
    )
    kv_all = in_all[:, D:].reshape(-1, groups, 2, group_lanes).transpose(0, 2, 1, 3)
    grad_in_total = jnp.concatenate([in_all[:, :D], kv_all.reshape(-1, 2 * D)], axis=1).astype(f32)
    down_rows = FF // n_dp
    part_rows = D // n_dp
    grad_down = all_sums[:down_rows].astype(f32)
    grad_up = (
        all_sums[down_rows : down_rows + (FF // D) * part_rows]
        .reshape(FF // D, part_rows, D)
        .transpose(1, 0, 2)
        .reshape(part_rows, FF)
        .astype(f32)
    )
    at = down_rows + (FF // D) * part_rows
    grad_mix = all_sums[at : at + part_rows].astype(f32)
    flat = all_sums[at + part_rows :].reshape(-1).astype(f32)
    vectors_out = [flat[i * part_rows : (i + 1) * part_rows] for i in range(6)]
    bias_up_out = flat[6 * part_rows : 6 * part_rows + down_rows]
    return (
        result[None],
        input_grad[None],
        grad_in_total,
        grad_mix,
        grad_up,
        grad_down,
        vectors_out[0],
        bias_up_out,
        vectors_out[1],
        *vectors_out[2:],
    )


def solution(mesh):
    placed = (
        P("dp", "seq", None),
        P("dp", None),
        P("dp", None),
        P("dp", None),
        P("dp", None),
        P("dp"),
        P("dp"),
        P("dp"),
        P("dp"),
        P("dp"),
        P("dp"),
        P("dp"),
        P("dp", None),
        P("dp", None),
        P("dp", None, None),
        P("dp", "seq", None),
    )
    return jax.shard_map(
        on_device,
        mesh=mesh,
        in_specs=placed,
        out_specs=(
            P("dp", "seq", None),
            P("dp", "seq", None),
            P("dp", None),
            P("dp", None),
            P("dp", None),
            P("dp", None),
            P("dp"),
            P("dp"),
            P("dp"),
            P("dp"),
            P("dp"),
            P("dp"),
            P("dp"),
        ),
        check_vma=False,
    )
```

```python
import functools

import jax
import jax.numpy as jnp
from jax import lax
from jax.experimental import pallas as pl
from jax.experimental.pallas import tpu as pltpu
from jax.sharding import PartitionSpec as P

D = 768
HEADS = 12
HD = 64
CL = 128
MOSTB = 16
PAIRS = HEADS // 2
WINDOW = MOSTB * CL
HALO = (MOSTB - 1) * CL
CHUNK = 512
KCHUNK = 512
TILES_AT_ONCE = 2
PACK = 4
NEG = -1e30
TERMS = 5
FF = 3072
RTILE = 256
FCHUNK = 768
SCALE2 = HD ** (-0.5) * 1.4426950408889634

EPSILON = 1e-05


def shifted(value, axis, by):
    devices = lax.axis_size(axis)
    pairs = [(i, i + by) for i in range(devices) if 0 <= i + by < devices]
    return lax.ppermute(value, axis, pairs)


def halo_parts(value):
    own = value.shape[0]
    far = HALO - own
    devices = lax.axis_size("seq")
    assert 0 < far <= own and devices % 2 == 0
    partner = lax.ppermute(value, "seq", [(i, i ^ 1) for i in range(devices)])
    pairs = [(i, i - 1 if i % 2 == 0 else i + 1) for i in range(devices)]
    other = lax.ppermute(value, "seq", [(i, k) for i, k in pairs if 0 <= k < devices])
    before = shifted(value[own - far :], "seq", 2)
    following = shifted(value[:far], "seq", -2)
    return [before, partner, value, other, following]


def places(starts, tiles, parts):
    far, own = parts[0].shape[0], parts[2].shape[0]
    return [
        0,
        pl.multiple_of(starts[tiles] * CL, CL),
        far + own,
        pl.multiple_of(starts[tiles + 1] * CL, CL),
        far + 3 * own,
    ]


def live_tokens(runs, trim, positions):
    ends = jnp.cumsum(runs) * CL
    starts = ends - runs * CL
    lengths = runs * CL - trim
    inside = (positions[..., None] >= starts) & (positions[..., None] < starts + lengths)
    return jnp.any(inside, axis=-1)


def outer_sum(left, right):
    return lax.dot_general(
        left, right, (((0,), (0,)), ((), ())), preferred_element_type=jnp.float32
    )


def back_product(left, right):
    return lax.dot_general(
        left, right, (((1,), (1,)), ((), ())), preferred_element_type=jnp.float32
    )


def plain_product(left, right):
    return jnp.dot(left, right, preferred_element_type=jnp.float32)


def stacked(tile):
    lane = lax.broadcasted_iota(jnp.int32, tile.shape, 1)
    zero = jnp.zeros_like(tile)
    heads = tile.shape[1] // HD
    return jnp.concatenate(
        [
            jnp.where((lane >= h * HD) & (lane < (h + 1) * HD), tile, zero)
            for h in range(heads)
        ],
        axis=0,
    )


def unstacked(stack):
    heads = stack.shape[1] // HD
    lane = lax.broadcasted_iota(jnp.int32, (CL, heads * HD), 1)
    result = stack[:CL]
    for h in range(1, heads):
        result = jnp.where(lane >= h * HD, stack[h * CL : (h + 1) * CL], result)
    return result


def as_column(row):
    return jnp.broadcast_to(row, (CL, CL)).T


def lane_of(tile, lane):
    lanes = lax.broadcasted_iota(jnp.int32, tile.shape, 1)
    return jnp.sum(jnp.where(lanes == lane, tile, 0.0), axis=1, keepdims=True)


def masked(scores, cols, row_ref, begin):
    parts = []
    wide = scores.shape[1]
    for half, one in enumerate(cols):
        row = row_ref[0, half : half + 1, pl.ds(begin, wide)]
        block = scores[half * CL : (half + 1) * CL]
        col = jnp.concatenate([one] * (wide // CL), axis=1)
        parts.append(jnp.where(col == row, block, NEG))
    return jnp.concatenate(parts, axis=0)


def assemble(parts, offsets, whole):
    for part, at in zip(parts, offsets):
        whole[pl.ds(at, part.shape[0]), :] = part[...]


def ahead(steps, produce, consume):
    held = produce(*steps[0])
    for i, step in enumerate(steps):
        following = produce(*steps[i + 1]) if i + 1 < len(steps) else None
        consume(*step, held)
        held = following


def attend_kernel(tiles, n_parts, starts, q_ref, *refs):
    k_parts, refs = refs[:n_parts], refs[n_parts:]
    v_parts, refs = refs[:n_parts], refs[n_parts:]
    qid_ref, kid_ref, out_ref, lse_ref, rate_ref, p_ref, k_ref, v_ref, *slots = refs
    s_refs, top_refs = slots[:TILES_AT_ONCE], slots[TILES_AT_ONCE:]
    group, step = pl.program_id(0), pl.program_id(1)
    heads = q_ref.shape[1] // HD
    chunks = WINDOW // CHUNK

    @pl.when(step == 0)
    def _():
        offsets = places(starts, tiles, k_parts)
        assemble(k_parts, offsets, k_ref)
        assemble(v_parts, offsets, v_ref)

    @pl.when((group == 0) & (step == 0))
    def _():
        lse_ref[...] = jnp.zeros_like(lse_ref)
        rate_ref[...] = jnp.zeros_like(rate_ref)

    def first_half(slot):
        tile = TILES_AT_ONCE * step + slot
        own = pl.multiple_of(HALO + tile * CL, CL)
        return dict(
            begin=pl.multiple_of(starts[tile] * CL, CL),
            query=stacked(q_ref[slot * CL : (slot + 1) * CL, :]),
            cols=[
                as_column(qid_ref[0, half : half + 1, pl.ds(own, CL)]) for half in range(heads)
            ],
        )

    def score(state, slot, j):
        at = pl.multiple_of(state["begin"] + j * CHUNK, CL)
        scores = back_product(state["query"], k_ref[pl.ds(at, CHUNK), :])
        scores = masked(scores, state["cols"], kid_ref, at)
        s_refs[slot][:, j * CHUNK : (j + 1) * CHUNK] = scores
        top = scores[:, :CL]
        for i in range(1, CHUNK // CL):
            top = jnp.maximum(top, scores[:, i * CL : (i + 1) * CL])
        if j > 0:
            top = jnp.maximum(top, top_refs[slot][...])
        top_refs[slot][...] = top

    states = [first_half(0)]
    for j in range(chunks):
        score(states[0], 0, j)
    for slot in range(TILES_AT_ONCE):
        if slot + 1 < TILES_AT_ONCE:
            states.append(first_half(slot + 1))
        state = states[slot]
        peak = jnp.max(top_refs[slot][...], axis=1, keepdims=True)
        total = jnp.zeros((heads * CL, CL), jnp.float32)
        result = jnp.zeros((heads * CL, heads * HD), jnp.float32)
        for j in range(chunks):
            if slot + 1 < TILES_AT_ONCE:
                score(states[slot + 1], slot + 1, j)
            at = pl.multiple_of(state["begin"] + j * CHUNK, CL)
            columns = slice(j * CHUNK, (j + 1) * CHUNK)
            weights = jnp.exp2((s_refs[slot][:, columns] - peak) * SCALE2)
            for i in range(CHUNK // CL):
                total = total + weights[:, i * CL : (i + 1) * CL]
            p_ref[0, slot, :, columns] = weights.astype(jnp.bfloat16)
            result = result + plain_product(
                p_ref[0, slot, :, columns], v_ref[pl.ds(at, CHUNK), :]
            )
        total = jnp.sum(total, axis=1, keepdims=True)
        rate = 1.0 / total
        result = result * rate
        lse = peak + jnp.log(total) * HD**0.5
        live = (state["cols"][0] >= 0.0).astype(jnp.float32)
        live = jnp.concatenate([live] * (heads * HD // CL), axis=1)
        rows = slice(slot * CL, (slot + 1) * CL)
        out_ref[rows, :] = (unstacked(result) * live).astype(jnp.bfloat16)
        here = pl.ds(pl.multiple_of((TILES_AT_ONCE * step + slot) * CL, CL), CL)
        lane = lax.broadcasted_iota(jnp.int32, (CL, CL), 1)
        kept, kept_rate = lse_ref[here, :], rate_ref[here, :]
        for half in range(heads):
            first = (heads * group + half) * TERMS
            inside = (lane >= first) & (lane < first + TERMS)
            part = slice(half * CL, (half + 1) * CL)
            kept = jnp.where(inside, lse[part], kept)
            kept_rate = jnp.where(inside, rate[part], kept_rate)
        lse_ref[here, :] = kept
        rate_ref[here, :] = kept_rate


def query_kernel(tiles, n_parts, first_head, starts, *refs):
    k_parts, refs = refs[:n_parts], refs[n_parts:]
    v_parts, refs = refs[:n_parts], refs[n_parts:]
    g_ref, p_ref, rate_ref, delta_ref = refs[:4]
    out_ref, k_ref, v_ref = refs[-3:]
    step = pl.program_id(0)
    heads = g_ref.shape[1] // HD
    chunks = WINDOW // CHUNK

    @pl.when(step == 0)
    def _():
        offsets = places(starts, tiles, k_parts)
        assemble(k_parts, offsets, k_ref)
        assemble(v_parts, offsets, v_ref)

    states = {}

    def state_of(slot):
        if slot not in states:
            rows = slice(slot * CL, (slot + 1) * CL)
            columns = [
                jnp.concatenate(
                    [lane_of(ref[rows, :], (first_head + half) * TERMS) for half in range(heads)],
                    axis=0,
                )
                for ref in (delta_ref, rate_ref)
            ]
            states[slot] = dict(
                begin=pl.multiple_of(starts[TILES_AT_ONCE * step + slot] * CL, CL),
                back=stacked(g_ref[rows, :]),
                delta=columns[0],
                rate=columns[1],
                result=jnp.zeros((heads * CL, heads * HD), jnp.float32),
            )
        return states[slot]

    def produce(slot, j):
        state = state_of(slot)
        at = pl.multiple_of(state["begin"] + j * CHUNK, CL)
        return back_product(state["back"], v_ref[pl.ds(at, CHUNK), :])

    def consume(slot, j, back_probs):
        state = state_of(slot)
        at = pl.multiple_of(state["begin"] + j * CHUNK, CL)
        weights = p_ref[0, slot, :, j * CHUNK : (j + 1) * CHUNK].astype(jnp.float32)
        back_scores = weights * (back_probs - state["delta"])
        state["result"] = state["result"] + plain_product(
            back_scores.astype(jnp.bfloat16), k_ref[pl.ds(at, CHUNK), :]
        )
        if j == chunks - 1:
            out_ref[slot * CL : (slot + 1) * CL, :] = unstacked(
                state["result"] * (state["rate"] * HD ** (-0.5))
            ).astype(jnp.bfloat16)

    ahead(
        [(slot, j) for slot in range(TILES_AT_ONCE) for j in range(chunks)], produce, consume
    )


def key_kernel(tiles, n_parts, first_pair, starts, k_ref, v_ref, *refs):
    q_parts, refs = refs[:n_parts], refs[n_parts:]
    g_parts, refs = refs[:n_parts], refs[n_parts:]
    a_parts, refs = refs[:n_parts], refs[n_parts:]
    qid_ref, kid_ref = refs[:2]
    out_ref, q_ref, g_ref = refs[-3:]
    step_pair = pl.program_id(0)
    pair = first_pair + step_pair
    offsets = places(starts, tiles, q_parts)
    for at, q_part, g_part, a_part in zip(offsets, q_parts, g_parts, a_parts):
        rows = pl.ds(at, q_part.shape[0])
        q_ref[rows, : 2 * HD] = q_part[...]
        q_ref[rows, 2 * HD :] = a_part[...]
        g_ref[rows, : 2 * HD] = g_part[...]
        g_ref[rows, 2 * HD :] = a_part[...]

    lane = lax.broadcasted_iota(jnp.int32, (CL, CL), 1)
    lse_pick, delta_pick = [], []
    for half in range(2):
        first = (2 * pair + half) * TERMS
        lse_pick.append(jnp.where((lane >= first) & (lane < first + 3), -1.0, 0.0))
        delta_pick.append(jnp.where((lane >= first + 3) & (lane < first + TERMS), -1.0, 0.0))
    lse_pick = jnp.concatenate(lse_pick, axis=0).astype(jnp.bfloat16)
    delta_pick = jnp.concatenate(delta_pick, axis=0).astype(jnp.bfloat16)
    key_lanes = pl.ds(pl.multiple_of(step_pair * 2 * HD, 2 * HD), 2 * HD)
    value_lanes = pl.ds(
        pl.multiple_of(out_ref.shape[1] // 2 + step_pair * 2 * HD, 2 * HD), 2 * HD
    )

    def some_tiles(step, carry):
        states = {}

        def state_of(slot):
            if slot not in states:
                tile = TILES_AT_ONCE * step + slot
                own = pl.multiple_of(HALO + tile * CL, CL)
                here = pl.multiple_of(tile * CL, CL)
                states[slot] = dict(
                    begin=pl.multiple_of(starts[tile] * CL, CL),
                    here=here,
                    keys=jnp.concatenate([stacked(k_ref[pl.ds(here, CL), :]), lse_pick], axis=1),
                    values=jnp.concatenate(
                        [stacked(v_ref[pl.ds(here, CL), :]), delta_pick], axis=1
                    ),
                    cols=[
                        as_column(kid_ref[0, half : half + 1, pl.ds(own, CL)]) for half in range(2)
                    ],
                    key_sum=jnp.zeros((2 * CL, 2 * HD), jnp.float32),
                    value_sum=jnp.zeros((2 * CL, 2 * HD), jnp.float32),
                )
            return states[slot]

        def produce(slot, j):
            state = state_of(slot)
            at = pl.multiple_of(state["begin"] + j * KCHUNK, CL)
            scores = back_product(state["keys"], q_ref[pl.ds(at, KCHUNK), :])
            return scores, back_product(state["values"], g_ref[pl.ds(at, KCHUNK), :])

        def consume(slot, j, held):
            state = state_of(slot)
            at = pl.multiple_of(state["begin"] + j * KCHUNK, CL)
            scores, back_probs = held
            probs = jnp.exp2(masked(scores * SCALE2, state["cols"], qid_ref, at))
            back_scores = probs * back_probs
            state["value_sum"] = state["value_sum"] + plain_product(
                probs.astype(jnp.bfloat16), g_ref[pl.ds(at, KCHUNK), : 2 * HD]
            )
            state["key_sum"] = state["key_sum"] + plain_product(
                back_scores.astype(jnp.bfloat16), q_ref[pl.ds(at, KCHUNK), : 2 * HD]
            )
            if j == WINDOW // KCHUNK - 1:
                rows = pl.ds(state["here"], CL)
                out_ref[rows, key_lanes] = (
                    unstacked(state["key_sum"]) * HD ** (-0.5)
                ).astype(jnp.bfloat16)
                out_ref[rows, value_lanes] = unstacked(state["value_sum"]).astype(jnp.bfloat16)

        ahead(
            [(slot, j) for slot in range(TILES_AT_ONCE) for j in range(WINDOW // KCHUNK)],
            produce,
            consume,
        )
        return carry

    lax.fori_loop(0, tiles // TILES_AT_ONCE, some_tiles, 0)


def lane_block(rows, first, heads=2):
    return pl.BlockSpec((rows, heads * HD), lambda pair, starts: (0, first + pair))


def fixed_lanes(rows, block):
    return pl.BlockSpec((rows, 2 * HD), lambda pair, starts: (0, block))


def row_block(columns, first, heads=2):
    return pl.BlockSpec((1, heads, columns), lambda pair, starts: (first + pair, 0, 0))


UNREAD = pl.BlockSpec(memory_space=pl.ANY)


VMEM_LIMIT = 60 * 1024 * 1024


def strip_call(
    kernel, length, grid, in_specs, out_specs, out_shape, scratch, args, aliases=None
):
    return pl.pallas_call(
        kernel,
        out_shape=out_shape,
        grid_spec=pltpu.PrefetchScalarGridSpec(
            num_scalar_prefetch=1,
            grid=grid,
            in_specs=in_specs,
            out_specs=out_specs,
            scratch_shapes=scratch,
        ),
        input_output_aliases=aliases or {},
        cost_estimate=work(length),
        compiler_params=pltpu.CompilerParams(vmem_limit_bytes=VMEM_LIMIT),
    )(*args)


def project_kernel(parts, weight, *refs):
    for source, target in zip(refs[:parts], refs[-parts:]):
        target[...] = plain_product(source[...], weight[...]).astype(target.dtype)


def project_call(parts, weight, *needs):
    depth, columns = weight.shape
    block = PACK * HD
    return pl.pallas_call(
        functools.partial(project_kernel, len(parts)),
        grid=(columns // block,),
        in_specs=[pl.BlockSpec((depth, block), lambda i: (0, i))]
        + [pl.BlockSpec(part.shape, lambda i: (0, 0)) for part in parts]
        + [UNREAD] * len(needs),
        out_specs=[pl.BlockSpec((part.shape[0], block), lambda i: (0, i)) for part in parts],
        out_shape=[jax.ShapeDtypeStruct((part.shape[0], columns), part.dtype) for part in parts],
        cost_estimate=work(10),
        compiler_params=pltpu.CompilerParams(vmem_limit_bytes=VMEM_LIMIT),
    )(weight, *parts, *needs)


def gelu_terms(value):
    t = 1.0 / (1.0 + (0.3275911 * 0.7071067811865476) * jnp.abs(value))
    bell = jnp.exp2(value * value * (-0.5 * 1.4426950408889634))
    tail = 0.5 * 1.061405429
    for term in (-0.5 * 1.453152027, 0.5 * 1.421413741, -0.5 * 0.284496736, 0.5 * 0.254829592):
        tail = tail * t + term
    tail = tail * t * bell
    cdf = jnp.where(value >= 0.0, 1.0 - tail, tail)
    return value * cdf, cdf + value * (0.3989422804014327 * bell)


def normalised(values):
    mean = jnp.mean(values, axis=-1, keepdims=True)
    centre = values - mean
    rate = lax.rsqrt(jnp.mean(centre * centre, axis=-1, keepdims=True) + EPSILON)
    return centre * rate, rate


def norm_back(scaled, unit, rate):
    first = jnp.mean(scaled, axis=-1, keepdims=True)
    second = jnp.mean(scaled * unit, axis=-1, keepdims=True)
    return rate * (scaled - first - unit * second)


def row_sums(values):
    rows, columns = values.shape
    return jnp.sum(values.reshape(rows // 8, 8, columns), axis=0)


def chain_kernel(
    att_ref,
    tok_ref,
    cot_ref,
    live_ref,
    lse_ref,
    mix_ref,
    up_ref,
    down_ref,
    vec_ref,
    bias_up_ref,
    spread_ref,
    out_ref,
    act_ref,
    upr_ref,
    hid_ref,
    pre_ref,
    mixr_ref,
    mixed_ref,
    back_ref,
    delta_ref,
    sum_ref,
    sum_up_ref,
    slope_ref,
):
    width = up_ref.shape[1]
    bias_mix, bias_down = vec_ref[0:1], vec_ref[1:2]
    gain_one, shift_one = vec_ref[2:3], vec_ref[3:4]
    gain_two, shift_two = vec_ref[4:5], vec_ref[5:6]

    @pl.when(pl.program_id(0) == 0)
    def _():
        sum_ref[...] = jnp.zeros_like(sum_ref)
        sum_up_ref[...] = jnp.zeros_like(sum_up_ref)

    attended = att_ref[...]
    mixed = plain_product(attended, mix_ref[...]) + bias_mix + tok_ref[...].astype(jnp.float32)
    unit_one, rate_one = normalised(mixed)
    hidden = unit_one * gain_one + shift_one
    hidden_rounded = hidden.astype(jnp.bfloat16)
    hid_ref[...] = hidden_rounded
    down_sum = bias_down + hidden
    for f in range(0, width, FCHUNK):
        up_sum = plain_product(hidden_rounded, up_ref[:, f : f + FCHUNK]) + (
            bias_up_ref[0:1, f : f + FCHUNK]
        )
        active, slope = gelu_terms(up_sum)
        active = active.astype(jnp.bfloat16)
        act_ref[:, f : f + FCHUNK] = active
        slope_ref[:, f : f + FCHUNK] = slope
        down_sum = down_sum + plain_product(active, down_ref[f : f + FCHUNK, :])
    unit_two, rate_two = normalised(down_sum)
    out_ref[...] = (unit_two * gain_two + shift_two).astype(jnp.bfloat16)
    cot = cot_ref[...].astype(jnp.float32)
    back_pre = norm_back(cot * gain_two, unit_two, rate_two)
    pre_rounded = back_pre.astype(jnp.bfloat16)
    pre_ref[...] = pre_rounded
    sum_ref[4] += row_sums(cot * unit_two)
    sum_ref[5] += row_sums(cot)
    sum_ref[1] += row_sums(back_pre)
    back_hidden = back_pre
    for f in range(0, width, FCHUNK):
        back_up = back_product(pre_rounded, down_ref[f : f + FCHUNK, :]) * (
            slope_ref[:, f : f + FCHUNK]
        )
        sum_up_ref[:, f : f + FCHUNK] += row_sums(back_up)
        up_rounded = back_up.astype(jnp.bfloat16)
        upr_ref[:, f : f + FCHUNK] = up_rounded
        back_hidden = back_hidden + back_product(up_rounded, up_ref[:, f : f + FCHUNK])
    sum_ref[2] += row_sums(back_hidden * unit_one)
    sum_ref[3] += row_sums(back_hidden)
    back_mixed = norm_back(back_hidden * gain_one, unit_one, rate_one)
    sum_ref[0] += row_sums(back_mixed)
    mixed_ref[...] = back_mixed
    mixed_rounded = back_mixed.astype(jnp.bfloat16)
    mixr_ref[...] = mixed_rounded
    back = back_product(mixed_rounded, mix_ref[...]).astype(jnp.bfloat16)
    back = jnp.where(live_ref[...] > 0.5, back, jnp.zeros_like(back))
    back_ref[:, : back.shape[1]] = back
    terms = back.astype(jnp.float32) * attended.astype(jnp.float32)
    high = terms.astype(jnp.bfloat16)
    low = (terms - high.astype(jnp.float32)).astype(jnp.bfloat16)
    delta = plain_product(high, spread_ref[...]) + plain_product(low, spread_ref[...])
    delta_ref[...] = delta
    lane = lax.broadcasted_iota(jnp.int32, delta.shape, 1)
    term = lane % TERMS
    whole = jnp.where(term < 3, lse_ref[...], delta)
    first = whole.astype(jnp.bfloat16)
    rest = whole - first.astype(jnp.float32)
    second = rest.astype(jnp.bfloat16)
    third = (rest - second.astype(jnp.float32)).astype(jnp.bfloat16)
    picked = jnp.where(
        (term == 0) | (term == 3),
        first.astype(jnp.float32),
        jnp.where((term == 2), third.astype(jnp.float32), second.astype(jnp.float32)),
    )
    picked = jnp.where(lane < TERMS * HEADS, picked, 0.0)
    back_ref[:, back.shape[1] :] = picked.astype(jnp.bfloat16)


def chain_call(att, tok, cot, live, lse, mix, up, down, vectors, bias_up):
    rows, width = tok.shape
    wide = up.shape[1]
    head_of = jnp.arange(width, dtype=jnp.int32)[:, None] // HD
    spread = (head_of == jnp.arange(2 * HD, dtype=jnp.int32)[None, :] // TERMS).astype(jnp.bfloat16)

    def tile(columns):
        return pl.BlockSpec((RTILE, columns), lambda i: (i, 0))

    def fixed(*shape):
        return pl.BlockSpec(shape, lambda i: (0,) * len(shape))

    bf16, f32 = jnp.bfloat16, jnp.float32
    return pl.pallas_call(
        chain_kernel,
        grid=(rows // RTILE,),
        in_specs=[
            tile(width),
            tile(width),
            tile(width),
            tile(1),
            tile(2 * HD),
            fixed(*mix.shape),
            fixed(*up.shape),
            fixed(*down.shape),
            fixed(*vectors.shape),
            fixed(*bias_up.shape),
            fixed(*spread.shape),
        ],
        out_specs=[
            tile(width),
            tile(wide),
            tile(wide),
            tile(width),
            tile(width),
            tile(width),
            tile(width),
            tile(width + 2 * HD),
            tile(2 * HD),
            fixed(6, 8, width),
            fixed(8, wide),
        ],
        out_shape=[
            jax.ShapeDtypeStruct((rows, width), bf16),
            jax.ShapeDtypeStruct((rows, wide), bf16),
            jax.ShapeDtypeStruct((rows, wide), bf16),
            jax.ShapeDtypeStruct((rows, width), bf16),
            jax.ShapeDtypeStruct((rows, width), bf16),
            jax.ShapeDtypeStruct((rows, width), bf16),
            jax.ShapeDtypeStruct((rows, width), f32),
            jax.ShapeDtypeStruct((rows, width + 2 * HD), bf16),
            jax.ShapeDtypeStruct((rows, 2 * HD), f32),
            jax.ShapeDtypeStruct((6, 8, width), f32),
            jax.ShapeDtypeStruct((8, wide), f32),
        ],
        scratch_shapes=[pltpu.VMEM((RTILE, wide), f32)],
        cost_estimate=work(44),
        compiler_params=pltpu.CompilerParams(vmem_limit_bytes=VMEM_LIMIT),
    )(att, tok, cot, live, lse, mix, up, down, vectors, bias_up, spread)


def weight_kernel(n_dp, core_ref, act, pre, hid, upr, att, mixr, small, *refs):
    send, keep, tmp = refs[-3:]
    step = pl.program_id(0)
    core = core_ref[0]
    pieces = FF // D
    down_rows = FF // n_dp
    part_rows = D // n_dp

    def put(x, row, rows, begin):
        mine = pl.multiple_of(begin + core * rows, 16)
        other = pl.multiple_of(begin + (1 - core) * rows, 16)
        keep[pl.ds(x, 1), pl.ds(row, rows), :] = tmp[pl.ds(mine, rows), :][None]
        send[pl.ds(x, 1), pl.ds(row, rows), :] = tmp[pl.ds(other, rows), :][None]

    @pl.when(step < pieces)
    def _():
        tmp[...] = outer_sum(act[...], pre[...]).astype(jnp.bfloat16)
        per = D // down_rows
        for b in range(per):
            block = step * per + b
            x = block // 2
            rows = tmp[b * down_rows : (b + 1) * down_rows, :]

            @pl.when(lax.rem(block, 2) == core)
            def _():
                keep[pl.ds(x, 1), 0:down_rows, :] = rows[None]

            @pl.when(lax.rem(block, 2) != core)
            def _():
                send[pl.ds(x, 1), 0:down_rows, :] = rows[None]

    @pl.when((step >= pieces) & (step < 2 * pieces))
    def _():
        tmp[...] = outer_sum(hid[...], upr[...]).astype(jnp.bfloat16)
        row = pl.multiple_of(down_rows + (step - pieces) * part_rows, 16)
        for x in range(n_dp // 2):
            put(x, row, part_rows, 2 * x * part_rows)

    @pl.when(step == 2 * pieces)
    def _():
        tmp[...] = outer_sum(att[...], mixr[...]).astype(jnp.bfloat16)
        row = down_rows + pieces * part_rows
        for x in range(n_dp // 2):
            put(x, row, part_rows, 2 * x * part_rows)
            last = row + part_rows
            rows = keep.shape[1] - last
            keep[x, last:, :] = small[pl.ds(2 * x + core, 1), :, :][0]
            send[x, last:, :] = small[pl.ds(2 * x + 1 - core, 1), :, :][0]


def weight_call(n_dp, core, act, pre, hid, upr, att, mixr, small, *needs):
    rows = act.shape[0]
    pieces = FF // D
    out_rows = FF // n_dp + (pieces + 1) * (D // n_dp) + small.shape[1]

    def fixed(*shape):
        return pl.BlockSpec(shape, lambda i, c: (0,) * len(shape))

    def stepped(first):
        return pl.BlockSpec((rows, D), lambda i, c: (0, jnp.clip(i - first, 0, pieces - 1)))

    shape = (n_dp // 2, out_rows, D)
    return pl.pallas_call(
        functools.partial(weight_kernel, n_dp),
        out_shape=[jax.ShapeDtypeStruct(shape, jnp.bfloat16)] * 2,
        grid_spec=pltpu.PrefetchScalarGridSpec(
            num_scalar_prefetch=1,
            grid=(2 * pieces + 1,),
            in_specs=[
                stepped(0),
                fixed(rows, D),
                fixed(rows, D),
                stepped(pieces),
                fixed(rows, D),
                fixed(rows, D),
                fixed(*small.shape),
            ]
            + [UNREAD] * len(needs),
            out_specs=[fixed(*shape)] * 2,
            scratch_shapes=[pltpu.VMEM((D, D), jnp.bfloat16)],
        ),
        cost_estimate=work(22),
        compiler_params=pltpu.CompilerParams(vmem_limit_bytes=VMEM_LIMIT),
    )(core, act, pre, hid, upr, att, mixr, small, *needs)


def outer_kernel(n_dp, core_ref, tokens, columns, *refs):
    send, keep, tmp = refs[-3:]
    core = core_ref[0]
    rows = tokens.shape[1] // n_dp
    tmp[...] = outer_sum(tokens[...], columns[...]).astype(tmp.dtype)
    for x in range(n_dp // 2):
        mine = pl.multiple_of((2 * x + core) * rows, 16)
        other = pl.multiple_of((2 * x + 1 - core) * rows, 16)
        keep[x] = tmp[pl.ds(mine, rows), :]
        send[x] = tmp[pl.ds(other, rows), :]


def outer_split(n_dp, core, tokens, columns, first, block, *needs):
    rows, depth = tokens.shape
    steps = columns.shape[1] // block - first
    shape = (n_dp // 2, depth // n_dp, block * steps)
    out = pl.BlockSpec(shape[:2] + (block,), lambda i, c: (0, 0, i))
    return pl.pallas_call(
        functools.partial(outer_kernel, n_dp),
        out_shape=[jax.ShapeDtypeStruct(shape, jnp.bfloat16)] * 2,
        grid_spec=pltpu.PrefetchScalarGridSpec(
            num_scalar_prefetch=1,
            grid=(steps,),
            in_specs=[
                pl.BlockSpec((rows, depth), lambda i, c: (0, 0)),
                pl.BlockSpec((rows, block), lambda i, c: (0, first + i)),
            ]
            + [UNREAD] * len(needs),
            out_specs=[out, out],
            scratch_shapes=[pltpu.VMEM((depth, block), jnp.bfloat16)],
        ),
        cost_estimate=work(4),
        compiler_params=plain_params(),
    )(core, tokens, columns, *needs)


def swap(value, axis, bit):
    devices = lax.axis_size(axis)
    return lax.ppermute(value, axis, [(i, i ^ bit) for i in range(devices)])


def dp_gather(shard, dp_rank):
    blocks = shard[None]
    bit = lax.axis_size("dp") // 2
    while bit >= 1:
        got = swap(blocks, "dp", bit)
        high = ((dp_rank // bit) % 2) == 1
        first = jnp.where(high, got, blocks)
        second = jnp.where(high, blocks, got)
        blocks = jnp.stack([first, second], axis=1).reshape((-1,) + shard.shape)
        bit //= 2
    return blocks.reshape((-1,) + shard.shape[1:])


def work(microseconds):
    return pl.CostEstimate(
        flops=int(microseconds * 0.4e9), transcendentals=0, bytes_accessed=1 << 20
    )


def row_tile(rows, limit=512):
    for size in range(min(rows, limit), 15, -1):
        if rows % size == 0 and size % 16 == 0:
            return size
    return rows


def plain_params():
    return pltpu.CompilerParams(vmem_limit_bytes=VMEM_LIMIT)


def split_add_kernel(which, keep_mine, got_mine, keep_other, got_other, *refs):
    mine, other = refs[-2:]
    mine[...] = (keep_mine[...].astype(jnp.float32) + got_mine[...].astype(jnp.float32)).astype(
        mine.dtype
    )
    other[...] = (keep_other[...].astype(jnp.float32) + got_other[...].astype(jnp.float32)).astype(
        other.dtype
    )


def split_add(keep, got, which, *needs):
    blocks, rows, columns = keep.shape
    tile = row_tile(rows)

    def spec(flip):
        def place(b, i, w):
            bit = 1 - w[0] if flip else w[0]
            return 2 * b + bit, i, 0

        return pl.BlockSpec((1, tile, columns), place)

    out = pl.BlockSpec((1, tile, columns), lambda b, i, w: (b, i, 0))
    shape = jax.ShapeDtypeStruct((blocks // 2, rows, columns), keep.dtype)
    return pl.pallas_call(
        split_add_kernel,
        out_shape=[shape, shape],
        grid_spec=pltpu.PrefetchScalarGridSpec(
            num_scalar_prefetch=1,
            grid=(blocks // 2, rows // tile),
            in_specs=[spec(False), spec(False), spec(True), spec(True)] + [UNREAD] * len(needs),
            out_specs=[out, out],
        ),
        cost_estimate=work(4),
        compiler_params=plain_params(),
    )(which, keep, got, keep, got, *needs)


def add_kernel(left, right, *refs):
    out = refs[-1]
    out[...] = (left[0].astype(jnp.float32) + right[0].astype(jnp.float32)).astype(out.dtype)


def add_blocks(left, right, *needs):
    _, rows, columns = left.shape
    tile = row_tile(rows)
    spec = pl.BlockSpec((1, tile, columns), lambda i: (0, i, 0))
    return pl.pallas_call(
        add_kernel,
        grid=(rows // tile,),
        in_specs=[spec, spec] + [UNREAD] * len(needs),
        out_specs=pl.BlockSpec((tile, columns), lambda i: (i, 0)),
        cost_estimate=work(3),
        out_shape=jax.ShapeDtypeStruct((rows, columns), left.dtype),
        compiler_params=plain_params(),
    )(left, right, *needs)


def pieces_kernel(pieces, *refs):
    out = refs[-1]
    total = pieces[0].astype(jnp.float32)
    for i in range(1, pieces.shape[0]):
        total = total + pieces[i].astype(jnp.float32)
    total = total.astype(out.dtype)
    for i in range(out.shape[0]):
        out[i] = total


def summed_copies(pieces, copies, *needs):
    _, rows, columns = pieces.shape
    return pl.pallas_call(
        pieces_kernel,
        in_specs=[pl.BlockSpec(memory_space=pltpu.VMEM)] + [UNREAD] * len(needs),
        out_specs=pl.BlockSpec(memory_space=pltpu.VMEM),
        out_shape=jax.ShapeDtypeStruct((copies, rows, columns), pieces.dtype),
        cost_estimate=work(2),
        compiler_params=plain_params(),
    )(pieces, *needs)


def gate_kernel(value, *refs):
    refs[-1][...] = value[...]


def gated(value, *needs):
    return pl.pallas_call(
        gate_kernel,
        in_specs=[pl.BlockSpec(memory_space=pltpu.VMEM)] + [UNREAD] * len(needs),
        out_specs=pl.BlockSpec(memory_space=pltpu.VMEM),
        out_shape=jax.ShapeDtypeStruct(value.shape, value.dtype),
        cost_estimate=work(1),
        compiler_params=plain_params(),
    )(value, *needs)


def cluster_ids(group_order, own_start, span):
    padded = jnp.pad(group_order, ((0, 0), (HALO, HALO)), constant_values=-(1 << 24))
    wanted = lax.dynamic_slice_in_dim(padded, own_start, span, 1) - (own_start - HALO)
    tile_of = wanted >> 7
    lane_of_token = wanted & (CL - 1)
    cluster = (jnp.arange(span, dtype=jnp.int32) >> 7) + 1
    tile_hot = jnp.where(
        tile_of[:, :, None] == jnp.arange(span // CL, dtype=jnp.int32), cluster[None, :, None], 0
    ).astype(jnp.bfloat16)
    lane_hot = (lane_of_token[:, :, None] == jnp.arange(CL, dtype=jnp.int32)).astype(jnp.bfloat16)
    table = jnp.einsum("hpt,hpl->htl", tile_hot, lane_hot, preferred_element_type=jnp.float32)
    return table.reshape(HEADS, span) - 1.0


def on_device(
    tokens,
    input_weight,
    output_weight,
    up_weight,
    down_weight,
    output_bias,
    up_bias,
    down_bias,
    first_gain,
    first_shift,
    second_gain,
    second_shift,
    document_runs,
    document_trim,
    cluster_order,
    cotangent,
):
    bf16, f32 = jnp.bfloat16, jnp.float32
    n_dp = lax.axis_size("dp")
    n_seq = lax.axis_size("seq")
    dp_rank = lax.axis_index("dp")
    seq_rank = lax.axis_index("seq")
    inputs = tokens[0]
    tok_dev = inputs.shape[0]
    tiles = tok_dev // CL
    span = tok_dev + 2 * HALO
    own_start = seq_rank * tok_dev

    token_parts = halo_parts(inputs)
    n_parts = len(token_parts)

    weight_in = lax.all_gather(input_weight, "dp", axis=0, tiled=True)
    weight_up = lax.all_gather(up_weight, "dp", axis=0, tiled=True)
    weight_down = lax.all_gather(down_weight, "dp", axis=0, tiled=True)

    runs = document_runs[0]
    first_cluster = jnp.cumsum(runs) - runs
    own_clusters = seq_rank * tiles + jnp.arange(tiles, dtype=jnp.int32)
    doc_start = jnp.max(
        jnp.where(first_cluster[None, :] <= own_clusters[:, None], first_cluster[None, :], 0), axis=1
    )
    starts = (doc_start - seq_rank * tiles + (MOSTB - 1)).astype(jnp.int32)
    near_left = HALO // CL - tiles
    near = near_left + 2 * tiles * jnp.stack([1 - seq_rank % 2, seq_rank % 2])
    starts = jnp.concatenate([starts, near.astype(jnp.int32)])

    cids = cluster_ids(cluster_order[0], own_start, span)
    positions = own_start - HALO + jnp.arange(span, dtype=jnp.int32)
    live = live_tokens(runs, document_trim[0], positions)
    usable = live[None, :] & (cids >= 0.0)
    key_ids = jnp.where(usable, cids, -1.0).reshape(PAIRS, 2, span)
    query_ids = jnp.where(usable, cids, -2.0).reshape(PAIRS, 2, span)
    own_live = live[HALO : HALO + tok_dev, None].astype(f32)

    own = plain_product(inputs, weight_in).astype(bf16)
    far = project_call([token_parts[0], token_parts[4]], weight_in, own)
    groups = HEADS // PACK
    group_lanes = PACK * HD
    kv_weight = (
        weight_in[:, D:]
        .reshape(D, 2, groups, group_lanes)
        .transpose(0, 2, 1, 3)
        .reshape(D, 2 * D)
    )
    near_parts = project_call([token_parts[1], token_parts[3]], weight_in, *far, kv_weight)
    projected = [far[0], near_parts[0], own, near_parts[1], far[1]]
    vectors = [
        output_bias,
        down_bias,
        first_gain,
        first_shift,
        second_gain,
        second_shift,
        up_bias,
    ]
    mix_rows = output_weight.shape[0]
    packed = jnp.concatenate(vectors)
    pad_rows = -(-packed.shape[0] // (16 * D)) * 16
    packed = jnp.pad(packed, (0, pad_rows * D - packed.shape[0])).reshape(pad_rows, D)
    mix_shard = gated(jnp.concatenate([output_weight, packed], 0), own)
    mix_all = dp_gather(mix_shard, dp_rank)
    mix_all = mix_all.reshape(n_dp, mix_rows + pad_rows, D)
    weight_mix = mix_all[:, :mix_rows].reshape(D, D)
    small_all = mix_all[:, mix_rows:].reshape(n_dp, -1).astype(f32)
    vec = small_all[:, : 6 * mix_rows].reshape(n_dp, 6, mix_rows).transpose(1, 0, 2).reshape(6, D)
    vec = jnp.pad(vec, ((0, 2), (0, 0)))
    up_part = up_bias.shape[0]
    bias_up = small_all[:, 6 * mix_rows : 6 * mix_rows + up_part].reshape(1, FF)
    bias_up = jnp.pad(bias_up, ((0, 7), (0, 0)))
    heights = [part.shape[0] for part in token_parts]

    groups = HEADS // PACK
    group_lanes = PACK * HD
    group_key_ids = key_ids.reshape(groups, PACK, span)
    group_query_ids = query_ids.reshape(groups, PACK, span)
    group_scratch = pltpu.VMEM((span, group_lanes), bf16)

    def group_parts(third, first):
        return [lane_block(rows, third * groups + first, PACK) for rows in heights]

    steps = tiles // TILES_AT_ONCE
    step_rows = TILES_AT_ONCE * CL

    def of_group(rows, first):
        return pl.BlockSpec((rows, group_lanes), lambda g, t, starts: (0, first + g))

    def ids_of_group():
        return pl.BlockSpec((1, PACK, span), lambda g, t, starts: (g, 0, 0))

    step_block = pl.BlockSpec((step_rows, group_lanes), lambda g, t, starts: (t, g))
    whole_lanes = pl.BlockSpec((tok_dev, 2 * HD), lambda g, t, starts: (0, 0))
    attended, lse, rate, probs = strip_call(
        functools.partial(attend_kernel, tiles, n_parts),
        52,
        (groups, steps),
        [step_block]
        + [of_group(rows, groups) for rows in heights]
        + [of_group(rows, 2 * groups) for rows in heights]
        + [ids_of_group(), ids_of_group()],
        [
            step_block,
            whole_lanes,
            whole_lanes,
            pl.BlockSpec(
                (1, TILES_AT_ONCE, PACK * CL, WINDOW), lambda g, t, starts: (g, t, 0, 0)
            ),
        ],
        [
            jax.ShapeDtypeStruct((tok_dev, D), bf16),
            jax.ShapeDtypeStruct((tok_dev, 2 * HD), f32),
            jax.ShapeDtypeStruct((tok_dev, 2 * HD), f32),
            jax.ShapeDtypeStruct((groups, tiles, PACK * CL, WINDOW), bf16),
        ],
        [group_scratch, group_scratch]
        + [pltpu.VMEM((PACK * CL, WINDOW), f32)] * TILES_AT_ONCE
        + [pltpu.VMEM((PACK * CL, CL), f32)] * TILES_AT_ONCE,
        (starts, own, *projected, *projected, group_query_ids, group_key_ids),
    )

    (
        result,
        active,
        up_rounded,
        hidden_rounded,
        pre_rounded,
        mixed_rounded,
        back_mixed,
        back_own,
        delta,
        sums,
        sums_up,
    ) = chain_call(
        attended,
        inputs,
        cotangent[0],
        own_live,
        lse,
        weight_mix,
        weight_up,
        weight_down,
        vec,
        bias_up,
    )
    back_parts = halo_parts(back_own)

    small = jnp.concatenate(
        [
            jnp.sum(sums, axis=1).reshape(6, n_dp, mix_rows).transpose(1, 0, 2).reshape(n_dp, -1),
            jnp.sum(sums_up, axis=0).reshape(n_dp, -1),
        ],
        axis=1,
    ).astype(bf16)
    unit = 8 * n_seq
    fixed_rows = FF // n_dp + (FF // D + 1) * (D // n_dp)
    small_rows = -(-(fixed_rows + -(-small.shape[1] // D)) // unit) * unit - fixed_rows
    small = jnp.pad(small, ((0, 0), (0, small_rows * D - small.shape[1])))
    small = small.reshape(n_dp, small_rows, D)
    core = (dp_rank % 2).astype(jnp.int32)
    def query_strip(first, *needs):
        buffer = needs[:1] if first > 0 else ()

        def parts(third):
            return [
                pl.BlockSpec(
                    (rows, group_lanes), lambda t, starts: (0, third * groups + first)
                )
                for rows in heights
            ]

        block = pl.BlockSpec((step_rows, group_lanes), lambda t, starts: (t, first))
        lanes = pl.BlockSpec((step_rows, 2 * HD), lambda t, starts: (t, 0))
        in_specs = (
            parts(1)
            + parts(2)
            + [
                block,
                pl.BlockSpec(
                    (1, TILES_AT_ONCE, PACK * CL, WINDOW), lambda t, starts: (first, t, 0, 0)
                ),
                lanes,
                lanes,
            ]
            + [UNREAD] * len(needs)
        )
        return strip_call(
            functools.partial(query_kernel, tiles, n_parts, first * PACK),
            16,
            (steps,),
            in_specs,
            block,
            jax.ShapeDtypeStruct((tok_dev, D), bf16),
            [group_scratch, group_scratch],
            (starts, *projected, *projected, back_own, probs, rate, delta, *needs),
            {len(in_specs) + 1 - len(needs): 0} if buffer else None,
        )

    key_pairs = PACK // 2
    pair_scratch = pltpu.VMEM((span, 4 * HD), bf16)

    def key_strip(first, length, *needs):
        buffer = needs[:1] if first > 0 else ()
        pair = first * key_pairs

        def parts(third):
            return [lane_block(rows, third * PAIRS + pair) for rows in heights]

        in_specs = (
            [lane_block(tok_dev, PAIRS + pair), lane_block(tok_dev, 2 * PAIRS + pair)]
            + parts(0)
            + parts(0)
            + [fixed_lanes(rows, PAIRS) for rows in heights]
            + [row_block(span, pair), row_block(span, pair)]
            + [UNREAD] * len(needs)
        )
        return strip_call(
            functools.partial(key_kernel, tiles, n_parts, pair),
            length,
            (key_pairs,),
            in_specs,
            pl.BlockSpec((tok_dev, 2 * group_lanes), lambda step, starts: (0, first)),
            jax.ShapeDtypeStruct((tok_dev, 2 * D), bf16),
            [pair_scratch, pair_scratch],
            (
                starts,
                own,
                own,
                *projected,
                *back_parts,
                *back_parts,
                query_ids,
                key_ids,
                *needs,
            ),
            {len(in_specs) + 1 - len(needs): 0} if buffer else None,
        )

    def scatter(share):
        rows, columns = share.shape
        return lax.all_to_all(
            share.reshape(n_seq, rows // n_seq, columns), "seq", split_axis=0, concat_axis=0
        )

    def everyone(copies):
        got = lax.all_to_all(copies, "seq", split_axis=0, concat_axis=0)
        return got.reshape(-1, copies.shape[-1])

    def first_split(keep, got, *needs):
        bit = 2
        while True:
            which = ((dp_rank // bit) % 2).astype(jnp.int32).reshape(1)
            mine, other = split_add(keep, got, which, *needs)
            got = swap(other, "dp", bit)
            if mine.shape[0] == 1:
                return mine, got
            keep, bit, needs = mine, bit * 2, ()

    def core_split(grad):
        rows, columns = grad.shape
        blocks = grad.astype(bf16).reshape(n_dp // 2, 2, rows // n_dp, columns)
        return (
            lax.dynamic_index_in_dim(blocks, 1 - core, 1, keepdims=False),
            lax.dynamic_index_in_dim(blocks, core, 1, keepdims=False),
        )

    send, keep = weight_call(
        n_dp,
        core.reshape(1),
        active,
        pre_rounded,
        hidden_rounded,
        up_rounded,
        attended,
        mixed_rounded,
        small,
    )
    core_got = swap(send, "dp", 1)
    mine, x_got = first_split(keep, core_got)
    back_q = query_strip(0, mine)
    back_q = query_strip(1, back_q)
    back_q = query_strip(2, back_q)
    share = add_blocks(mine, x_got, back_q)
    back_kv = key_strip(0, 27, back_q, share)
    pieces = scatter(share)
    cut = 2 * group_lanes
    early_cols = jnp.concatenate([back_q, back_kv[:, :cut]], axis=1)
    early_send, early_keep = core_split(outer_sum(inputs, early_cols))
    early_core = swap(early_send, "dp", 1)
    back_kv = key_strip(1, 27, back_kv, early_send)
    early_mine, early_got = first_split(early_keep, early_core, back_kv)
    copies = summed_copies(pieces, 1, back_kv)
    back_kv = key_strip(2, 2, back_kv, early_mine, copies)
    early_share = add_blocks(early_mine, early_got, back_kv)
    all_sums = lax.all_gather(copies[0], "seq", axis=0, tiled=True)
    late_send, late_keep = outer_split(
        n_dp, core.reshape(1), inputs, back_kv, 1, cut, early_share
    )
    late_mine, late_got = first_split(late_keep, swap(late_send, "dp", 1))
    late_share = add_blocks(late_mine, late_got, all_sums)
    in_share = jnp.concatenate([early_share, late_share], axis=1)
    in_all = everyone(summed_copies(scatter(in_share), n_seq))

    input_grad = (
        back_mixed + back_product(back_q, weight_in[:, :D]) + back_product(back_kv, kv_weight)
    )
    kv_all = in_all[:, D:].reshape(-1, groups, 2, group_lanes).transpose(0, 2, 1, 3)
    grad_in_total = jnp.concatenate([in_all[:, :D], kv_all.reshape(-1, 2 * D)], axis=1).astype(f32)
    down_rows = FF // n_dp
    part_rows = D // n_dp
    grad_down = all_sums[:down_rows].astype(f32)
    grad_up = (
        all_sums[down_rows : down_rows + (FF // D) * part_rows]
        .reshape(FF // D, part_rows, D)
        .transpose(1, 0, 2)
        .reshape(part_rows, FF)
        .astype(f32)
    )
    at = down_rows + (FF // D) * part_rows
    grad_mix = all_sums[at : at + part_rows].astype(f32)
    flat = all_sums[at + part_rows :].reshape(-1).astype(f32)
    vectors_out = [flat[i * part_rows : (i + 1) * part_rows] for i in range(6)]
    bias_up_out = flat[6 * part_rows : 6 * part_rows + down_rows]
    return (
        result[None],
        input_grad[None],
        grad_in_total,
        grad_mix,
        grad_up,
        grad_down,
        vectors_out[0],
        bias_up_out,
        vectors_out[1],
        *vectors_out[2:],
    )


def solution(mesh):
    placed = (
        P("dp", "seq", None),
        P("dp", None),
        P("dp", None),
        P("dp", None),
        P("dp", None),
        P("dp"),
        P("dp"),
        P("dp"),
        P("dp"),
        P("dp"),
        P("dp"),
        P("dp"),
        P("dp", None),
        P("dp", None),
        P("dp", None, None),
        P("dp", "seq", None),
    )
    return jax.shard_map(
        on_device,
        mesh=mesh,
        in_specs=placed,
        out_specs=(
            P("dp", "seq", None),
            P("dp", "seq", None),
            P("dp", None),
            P("dp", None),
            P("dp", None),
            P("dp", None),
            P("dp"),
            P("dp"),
            P("dp"),
            P("dp"),
            P("dp"),
            P("dp"),
            P("dp"),
        ),
        check_vma=False,
    )
```

```python
import functools

import jax
import jax.numpy as jnp
from jax import lax
from jax.experimental import pallas as pl
from jax.experimental.pallas import tpu as pltpu
from jax.sharding import PartitionSpec as P

D = 768
HEADS = 12
HD = 64
CL = 128
MOSTB = 16
PAIRS = HEADS // 2
WINDOW = MOSTB * CL
HALO = (MOSTB - 1) * CL
CHUNK = 512
KCHUNK = 512
TILES_AT_ONCE = 2
PACK = 4
NEG = -1e30
TERMS = 5
FF = 3072
RTILE = 256
FCHUNK = 768
SCALE2 = HD ** (-0.5) * 1.4426950408889634

EPSILON = 1e-05


def shifted(value, axis, by):
    devices = lax.axis_size(axis)
    pairs = [(i, i + by) for i in range(devices) if 0 <= i + by < devices]
    return lax.ppermute(value, axis, pairs)


def halo_parts(value):
    own = value.shape[0]
    far = HALO - own
    devices = lax.axis_size("seq")
    assert 0 < far <= own and devices % 2 == 0
    partner = lax.ppermute(value, "seq", [(i, i ^ 1) for i in range(devices)])
    pairs = [(i, i - 1 if i % 2 == 0 else i + 1) for i in range(devices)]
    other = lax.ppermute(value, "seq", [(i, k) for i, k in pairs if 0 <= k < devices])
    before = shifted(value[own - far :], "seq", 2)
    following = shifted(value[:far], "seq", -2)
    return [before, partner, value, other, following]


def places(starts, tiles, parts):
    far, own = parts[0].shape[0], parts[2].shape[0]
    return [
        0,
        pl.multiple_of(starts[tiles] * CL, CL),
        far + own,
        pl.multiple_of(starts[tiles + 1] * CL, CL),
        far + 3 * own,
    ]


def live_tokens(runs, trim, positions):
    ends = jnp.cumsum(runs) * CL
    starts = ends - runs * CL
    lengths = runs * CL - trim
    inside = (positions[..., None] >= starts) & (positions[..., None] < starts + lengths)
    return jnp.any(inside, axis=-1)


def outer_sum(left, right):
    return lax.dot_general(
        left, right, (((0,), (0,)), ((), ())), preferred_element_type=jnp.float32
    )


def back_product(left, right):
    return lax.dot_general(
        left, right, (((1,), (1,)), ((), ())), preferred_element_type=jnp.float32
    )


def plain_product(left, right):
    return jnp.dot(left, right, preferred_element_type=jnp.float32)


def stacked(tile):
    lane = lax.broadcasted_iota(jnp.int32, tile.shape, 1)
    zero = jnp.zeros_like(tile)
    heads = tile.shape[1] // HD
    return jnp.concatenate(
        [
            jnp.where((lane >= h * HD) & (lane < (h + 1) * HD), tile, zero)
            for h in range(heads)
        ],
        axis=0,
    )


def unstacked(stack):
    heads = stack.shape[1] // HD
    lane = lax.broadcasted_iota(jnp.int32, (CL, heads * HD), 1)
    result = stack[:CL]
    for h in range(1, heads):
        result = jnp.where(lane >= h * HD, stack[h * CL : (h + 1) * CL], result)
    return result


def as_column(row):
    return jnp.broadcast_to(row, (CL, CL)).T


def lane_of(tile, lane):
    lanes = lax.broadcasted_iota(jnp.int32, tile.shape, 1)
    return jnp.sum(jnp.where(lanes == lane, tile, 0.0), axis=1, keepdims=True)


def masked(scores, cols, row_ref, begin):
    parts = []
    wide = scores.shape[1]
    for half, one in enumerate(cols):
        row = row_ref[0, half : half + 1, pl.ds(begin, wide)]
        block = scores[half * CL : (half + 1) * CL]
        col = jnp.concatenate([one] * (wide // CL), axis=1)
        parts.append(jnp.where(col == row, block, NEG))
    return jnp.concatenate(parts, axis=0)


def assemble(parts, offsets, whole):
    for part, at in zip(parts, offsets):
        whole[pl.ds(at, part.shape[0]), :] = part[...]


def ahead(steps, produce, consume):
    held = produce(*steps[0])
    for i, step in enumerate(steps):
        following = produce(*steps[i + 1]) if i + 1 < len(steps) else None
        consume(*step, held)
        held = following


def attend_kernel(tiles, n_parts, starts, q_ref, *refs):
    k_parts, refs = refs[:n_parts], refs[n_parts:]
    v_parts, refs = refs[:n_parts], refs[n_parts:]
    qid_ref, kid_ref, out_ref, lse_ref, rate_ref, p_ref, k_ref, v_ref, *slots = refs
    s_refs, top_refs = slots[:TILES_AT_ONCE], slots[TILES_AT_ONCE:]
    group, step = pl.program_id(0), pl.program_id(1)
    heads = q_ref.shape[1] // HD
    chunks = WINDOW // CHUNK

    @pl.when(step == 0)
    def _():
        offsets = places(starts, tiles, k_parts)
        assemble(k_parts, offsets, k_ref)
        assemble(v_parts, offsets, v_ref)

    @pl.when((group == 0) & (step == 0))
    def _():
        lse_ref[...] = jnp.zeros_like(lse_ref)
        rate_ref[...] = jnp.zeros_like(rate_ref)

    def first_half(slot):
        tile = TILES_AT_ONCE * step + slot
        own = pl.multiple_of(HALO + tile * CL, CL)
        return dict(
            begin=pl.multiple_of(starts[tile] * CL, CL),
            query=stacked(q_ref[slot * CL : (slot + 1) * CL, :]),
            cols=[
                as_column(qid_ref[0, half : half + 1, pl.ds(own, CL)]) for half in range(heads)
            ],
        )

    def score(state, slot, j):
        at = pl.multiple_of(state["begin"] + j * CHUNK, CL)
        scores = back_product(state["query"], k_ref[pl.ds(at, CHUNK), :])
        scores = masked(scores, state["cols"], kid_ref, at)
        s_refs[slot][:, j * CHUNK : (j + 1) * CHUNK] = scores
        top = scores[:, :CL]
        for i in range(1, CHUNK // CL):
            top = jnp.maximum(top, scores[:, i * CL : (i + 1) * CL])
        if j > 0:
            top = jnp.maximum(top, top_refs[slot][...])
        top_refs[slot][...] = top

    states = [first_half(0)]
    for j in range(chunks):
        score(states[0], 0, j)
    for slot in range(TILES_AT_ONCE):
        if slot + 1 < TILES_AT_ONCE:
            states.append(first_half(slot + 1))
        state = states[slot]
        peak = jnp.max(top_refs[slot][...], axis=1, keepdims=True)
        total = jnp.zeros((heads * CL, CL), jnp.float32)
        result = jnp.zeros((heads * CL, heads * HD), jnp.float32)
        for j in range(chunks):
            if slot + 1 < TILES_AT_ONCE:
                score(states[slot + 1], slot + 1, j)
            at = pl.multiple_of(state["begin"] + j * CHUNK, CL)
            columns = slice(j * CHUNK, (j + 1) * CHUNK)
            weights = jnp.exp2((s_refs[slot][:, columns] - peak) * SCALE2)
            for i in range(CHUNK // CL):
                total = total + weights[:, i * CL : (i + 1) * CL]
            p_ref[0, slot, :, columns] = weights.astype(jnp.bfloat16)
            result = result + plain_product(
                p_ref[0, slot, :, columns], v_ref[pl.ds(at, CHUNK), :]
            )
        total = jnp.sum(total, axis=1, keepdims=True)
        rate = 1.0 / total
        result = result * rate
        lse = peak + jnp.log(total) * HD**0.5
        live = (state["cols"][0] >= 0.0).astype(jnp.float32)
        live = jnp.concatenate([live] * (heads * HD // CL), axis=1)
        rows = slice(slot * CL, (slot + 1) * CL)
        out_ref[rows, :] = (unstacked(result) * live).astype(jnp.bfloat16)
        here = pl.ds(pl.multiple_of((TILES_AT_ONCE * step + slot) * CL, CL), CL)
        lane = lax.broadcasted_iota(jnp.int32, (CL, CL), 1)
        kept, kept_rate = lse_ref[here, :], rate_ref[here, :]
        for half in range(heads):
            first = (heads * group + half) * TERMS
            inside = (lane >= first) & (lane < first + TERMS)
            part = slice(half * CL, (half + 1) * CL)
            kept = jnp.where(inside, lse[part], kept)
            kept_rate = jnp.where(inside, rate[part], kept_rate)
        lse_ref[here, :] = kept
        rate_ref[here, :] = kept_rate


def query_kernel(tiles, n_parts, first_head, starts, *refs):
    k_parts, refs = refs[:n_parts], refs[n_parts:]
    v_parts, refs = refs[:n_parts], refs[n_parts:]
    g_ref, p_ref, rate_ref, delta_ref = refs[:4]
    out_ref, k_ref, v_ref = refs[-3:]
    step = pl.program_id(0)
    heads = g_ref.shape[1] // HD
    chunks = WINDOW // CHUNK

    @pl.when(step == 0)
    def _():
        offsets = places(starts, tiles, k_parts)
        assemble(k_parts, offsets, k_ref)
        assemble(v_parts, offsets, v_ref)

    states = {}

    def state_of(slot):
        if slot not in states:
            rows = slice(slot * CL, (slot + 1) * CL)
            columns = [
                jnp.concatenate(
                    [lane_of(ref[rows, :], (first_head + half) * TERMS) for half in range(heads)],
                    axis=0,
                )
                for ref in (delta_ref, rate_ref)
            ]
            states[slot] = dict(
                begin=pl.multiple_of(starts[TILES_AT_ONCE * step + slot] * CL, CL),
                back=stacked(g_ref[rows, :]),
                delta=columns[0],
                rate=columns[1],
                result=jnp.zeros((heads * CL, heads * HD), jnp.float32),
            )
        return states[slot]

    def produce(slot, j):
        state = state_of(slot)
        at = pl.multiple_of(state["begin"] + j * CHUNK, CL)
        return back_product(state["back"], v_ref[pl.ds(at, CHUNK), :])

    def consume(slot, j, back_probs):
        state = state_of(slot)
        at = pl.multiple_of(state["begin"] + j * CHUNK, CL)
        weights = p_ref[0, slot, :, j * CHUNK : (j + 1) * CHUNK].astype(jnp.float32)
        back_scores = weights * (back_probs - state["delta"])
        state["result"] = state["result"] + plain_product(
            back_scores.astype(jnp.bfloat16), k_ref[pl.ds(at, CHUNK), :]
        )
        if j == chunks - 1:
            out_ref[slot * CL : (slot + 1) * CL, :] = unstacked(
                state["result"] * (state["rate"] * HD ** (-0.5))
            ).astype(jnp.bfloat16)

    ahead(
        [(slot, j) for slot in range(TILES_AT_ONCE) for j in range(chunks)], produce, consume
    )


def key_kernel(tiles, n_parts, first_pair, starts, k_ref, v_ref, *refs):
    q_parts, refs = refs[:n_parts], refs[n_parts:]
    g_parts, refs = refs[:n_parts], refs[n_parts:]
    a_parts, refs = refs[:n_parts], refs[n_parts:]
    qid_ref, kid_ref = refs[:2]
    out_ref, q_ref, g_ref = refs[-3:]
    step_pair = pl.program_id(0)
    pair = first_pair + step_pair
    offsets = places(starts, tiles, q_parts)
    for at, q_part, g_part, a_part in zip(offsets, q_parts, g_parts, a_parts):
        rows = pl.ds(at, q_part.shape[0])
        q_ref[rows, : 2 * HD] = q_part[...]
        q_ref[rows, 2 * HD :] = a_part[...]
        g_ref[rows, : 2 * HD] = g_part[...]
        g_ref[rows, 2 * HD :] = a_part[...]

    lane = lax.broadcasted_iota(jnp.int32, (CL, CL), 1)
    lse_pick, delta_pick = [], []
    for half in range(2):
        first = (2 * pair + half) * TERMS
        lse_pick.append(jnp.where((lane >= first) & (lane < first + 3), -1.0, 0.0))
        delta_pick.append(jnp.where((lane >= first + 3) & (lane < first + TERMS), -1.0, 0.0))
    lse_pick = jnp.concatenate(lse_pick, axis=0).astype(jnp.bfloat16)
    delta_pick = jnp.concatenate(delta_pick, axis=0).astype(jnp.bfloat16)
    key_lanes = pl.ds(pl.multiple_of(step_pair * 2 * HD, 2 * HD), 2 * HD)
    value_lanes = pl.ds(
        pl.multiple_of(out_ref.shape[1] // 2 + step_pair * 2 * HD, 2 * HD), 2 * HD
    )

    def some_tiles(step, carry):
        states = {}

        def state_of(slot):
            if slot not in states:
                tile = TILES_AT_ONCE * step + slot
                own = pl.multiple_of(HALO + tile * CL, CL)
                here = pl.multiple_of(tile * CL, CL)
                states[slot] = dict(
                    begin=pl.multiple_of(starts[tile] * CL, CL),
                    here=here,
                    keys=jnp.concatenate([stacked(k_ref[pl.ds(here, CL), :]), lse_pick], axis=1),
                    values=jnp.concatenate(
                        [stacked(v_ref[pl.ds(here, CL), :]), delta_pick], axis=1
                    ),
                    cols=[
                        as_column(kid_ref[0, half : half + 1, pl.ds(own, CL)]) for half in range(2)
                    ],
                    key_sum=jnp.zeros((2 * CL, 2 * HD), jnp.float32),
                    value_sum=jnp.zeros((2 * CL, 2 * HD), jnp.float32),
                )
            return states[slot]

        def produce(slot, j):
            state = state_of(slot)
            at = pl.multiple_of(state["begin"] + j * KCHUNK, CL)
            scores = back_product(state["keys"], q_ref[pl.ds(at, KCHUNK), :])
            return scores, back_product(state["values"], g_ref[pl.ds(at, KCHUNK), :])

        def consume(slot, j, held):
            state = state_of(slot)
            at = pl.multiple_of(state["begin"] + j * KCHUNK, CL)
            scores, back_probs = held
            probs = jnp.exp2(masked(scores * SCALE2, state["cols"], qid_ref, at))
            back_scores = probs * back_probs
            state["value_sum"] = state["value_sum"] + plain_product(
                probs.astype(jnp.bfloat16), g_ref[pl.ds(at, KCHUNK), : 2 * HD]
            )
            state["key_sum"] = state["key_sum"] + plain_product(
                back_scores.astype(jnp.bfloat16), q_ref[pl.ds(at, KCHUNK), : 2 * HD]
            )
            if j == WINDOW // KCHUNK - 1:
                rows = pl.ds(state["here"], CL)
                out_ref[rows, key_lanes] = (
                    unstacked(state["key_sum"]) * HD ** (-0.5)
                ).astype(jnp.bfloat16)
                out_ref[rows, value_lanes] = unstacked(state["value_sum"]).astype(jnp.bfloat16)

        ahead(
            [(slot, j) for slot in range(TILES_AT_ONCE) for j in range(WINDOW // KCHUNK)],
            produce,
            consume,
        )
        return carry

    lax.fori_loop(0, tiles // TILES_AT_ONCE, some_tiles, 0)


def lane_block(rows, first, heads=2):
    return pl.BlockSpec((rows, heads * HD), lambda pair, starts: (0, first + pair))


def fixed_lanes(rows, block):
    return pl.BlockSpec((rows, 2 * HD), lambda pair, starts: (0, block))


def row_block(columns, first, heads=2):
    return pl.BlockSpec((1, heads, columns), lambda pair, starts: (first + pair, 0, 0))


UNREAD = pl.BlockSpec(memory_space=pl.ANY)


VMEM_LIMIT = 60 * 1024 * 1024


def strip_call(
    kernel, length, grid, in_specs, out_specs, out_shape, scratch, args, aliases=None
):
    return pl.pallas_call(
        kernel,
        out_shape=out_shape,
        grid_spec=pltpu.PrefetchScalarGridSpec(
            num_scalar_prefetch=1,
            grid=grid,
            in_specs=in_specs,
            out_specs=out_specs,
            scratch_shapes=scratch,
        ),
        input_output_aliases=aliases or {},
        cost_estimate=work(length),
        compiler_params=pltpu.CompilerParams(vmem_limit_bytes=VMEM_LIMIT),
    )(*args)


def project_kernel(parts, weight, *refs):
    for source, target in zip(refs[:parts], refs[-parts:]):
        target[...] = plain_product(source[...], weight[...]).astype(target.dtype)


def project_call(parts, weight, *needs):
    depth, columns = weight.shape
    block = PACK * HD
    return pl.pallas_call(
        functools.partial(project_kernel, len(parts)),
        grid=(columns // block,),
        in_specs=[pl.BlockSpec((depth, block), lambda i: (0, i))]
        + [pl.BlockSpec(part.shape, lambda i: (0, 0)) for part in parts]
        + [UNREAD] * len(needs),
        out_specs=[pl.BlockSpec((part.shape[0], block), lambda i: (0, i)) for part in parts],
        out_shape=[jax.ShapeDtypeStruct((part.shape[0], columns), part.dtype) for part in parts],
        cost_estimate=work(10),
        compiler_params=pltpu.CompilerParams(vmem_limit_bytes=VMEM_LIMIT),
    )(weight, *parts, *needs)


def gelu_terms(value):
    t = 1.0 / (1.0 + (0.3275911 * 0.7071067811865476) * jnp.abs(value))
    bell = jnp.exp2(value * value * (-0.5 * 1.4426950408889634))
    tail = 0.5 * 1.061405429
    for term in (-0.5 * 1.453152027, 0.5 * 1.421413741, -0.5 * 0.284496736, 0.5 * 0.254829592):
        tail = tail * t + term
    tail = tail * t * bell
    cdf = jnp.where(value >= 0.0, 1.0 - tail, tail)
    return value * cdf, cdf + value * (0.3989422804014327 * bell)


def normalised(values):
    mean = jnp.mean(values, axis=-1, keepdims=True)
    centre = values - mean
    rate = lax.rsqrt(jnp.mean(centre * centre, axis=-1, keepdims=True) + EPSILON)
    return centre * rate, rate


def norm_back(scaled, unit, rate):
    first = jnp.mean(scaled, axis=-1, keepdims=True)
    second = jnp.mean(scaled * unit, axis=-1, keepdims=True)
    return rate * (scaled - first - unit * second)


def row_sums(values):
    rows, columns = values.shape
    return jnp.sum(values.reshape(rows // 8, 8, columns), axis=0)


def chain_kernel(
    att_ref,
    tok_ref,
    cot_ref,
    live_ref,
    lse_ref,
    mix_ref,
    up_ref,
    down_ref,
    vec_ref,
    bias_up_ref,
    spread_ref,
    out_ref,
    act_ref,
    upr_ref,
    hid_ref,
    pre_ref,
    mixr_ref,
    mixed_ref,
    back_ref,
    delta_ref,
    sum_ref,
    sum_up_ref,
    slope_ref,
):
    width = up_ref.shape[1]
    bias_mix, bias_down = vec_ref[0:1], vec_ref[1:2]
    gain_one, shift_one = vec_ref[2:3], vec_ref[3:4]
    gain_two, shift_two = vec_ref[4:5], vec_ref[5:6]

    @pl.when(pl.program_id(0) == 0)
    def _():
        sum_ref[...] = jnp.zeros_like(sum_ref)
        sum_up_ref[...] = jnp.zeros_like(sum_up_ref)

    attended = att_ref[...]
    mixed = plain_product(attended, mix_ref[...]) + bias_mix + tok_ref[...].astype(jnp.float32)
    unit_one, rate_one = normalised(mixed)
    hidden = unit_one * gain_one + shift_one
    hidden_rounded = hidden.astype(jnp.bfloat16)
    hid_ref[...] = hidden_rounded
    down_sum = bias_down + hidden
    for f in range(0, width, FCHUNK):
        up_sum = plain_product(hidden_rounded, up_ref[:, f : f + FCHUNK]) + (
            bias_up_ref[0:1, f : f + FCHUNK]
        )
        active, slope = gelu_terms(up_sum)
        active = active.astype(jnp.bfloat16)
        act_ref[:, f : f + FCHUNK] = active
        slope_ref[:, f : f + FCHUNK] = slope
        down_sum = down_sum + plain_product(active, down_ref[f : f + FCHUNK, :])
    unit_two, rate_two = normalised(down_sum)
    out_ref[...] = (unit_two * gain_two + shift_two).astype(jnp.bfloat16)
    cot = cot_ref[...].astype(jnp.float32)
    back_pre = norm_back(cot * gain_two, unit_two, rate_two)
    pre_rounded = back_pre.astype(jnp.bfloat16)
    pre_ref[...] = pre_rounded
    sum_ref[4] += row_sums(cot * unit_two)
    sum_ref[5] += row_sums(cot)
    sum_ref[1] += row_sums(back_pre)
    back_hidden = back_pre
    for f in range(0, width, FCHUNK):
        back_up = back_product(pre_rounded, down_ref[f : f + FCHUNK, :]) * (
            slope_ref[:, f : f + FCHUNK]
        )
        sum_up_ref[:, f : f + FCHUNK] += row_sums(back_up)
        up_rounded = back_up.astype(jnp.bfloat16)
        upr_ref[:, f : f + FCHUNK] = up_rounded
        back_hidden = back_hidden + back_product(up_rounded, up_ref[:, f : f + FCHUNK])
    sum_ref[2] += row_sums(back_hidden * unit_one)
    sum_ref[3] += row_sums(back_hidden)
    back_mixed = norm_back(back_hidden * gain_one, unit_one, rate_one)
    sum_ref[0] += row_sums(back_mixed)
    mixed_ref[...] = back_mixed
    mixed_rounded = back_mixed.astype(jnp.bfloat16)
    mixr_ref[...] = mixed_rounded
    back = back_product(mixed_rounded, mix_ref[...]).astype(jnp.bfloat16)
    back = jnp.where(live_ref[...] > 0.5, back, jnp.zeros_like(back))
    back_ref[:, : back.shape[1]] = back
    terms = back.astype(jnp.float32) * attended.astype(jnp.float32)
    high = terms.astype(jnp.bfloat16)
    low = (terms - high.astype(jnp.float32)).astype(jnp.bfloat16)
    delta = plain_product(high, spread_ref[...]) + plain_product(low, spread_ref[...])
    delta_ref[...] = delta
    lane = lax.broadcasted_iota(jnp.int32, delta.shape, 1)
    term = lane % TERMS
    whole = jnp.where(term < 3, lse_ref[...], delta)
    first = whole.astype(jnp.bfloat16)
    rest = whole - first.astype(jnp.float32)
    second = rest.astype(jnp.bfloat16)
    third = (rest - second.astype(jnp.float32)).astype(jnp.bfloat16)
    picked = jnp.where(
        (term == 0) | (term == 3),
        first.astype(jnp.float32),
        jnp.where((term == 2), third.astype(jnp.float32), second.astype(jnp.float32)),
    )
    picked = jnp.where(lane < TERMS * HEADS, picked, 0.0)
    back_ref[:, back.shape[1] :] = picked.astype(jnp.bfloat16)


def chain_call(att, tok, cot, live, lse, mix, up, down, vectors, bias_up):
    rows, width = tok.shape
    wide = up.shape[1]
    head_of = jnp.arange(width, dtype=jnp.int32)[:, None] // HD
    spread = (head_of == jnp.arange(2 * HD, dtype=jnp.int32)[None, :] // TERMS).astype(jnp.bfloat16)

    def tile(columns):
        return pl.BlockSpec((RTILE, columns), lambda i: (i, 0))

    def fixed(*shape):
        return pl.BlockSpec(shape, lambda i: (0,) * len(shape))

    bf16, f32 = jnp.bfloat16, jnp.float32
    return pl.pallas_call(
        chain_kernel,
        grid=(rows // RTILE,),
        in_specs=[
            tile(width),
            tile(width),
            tile(width),
            tile(1),
            tile(2 * HD),
            fixed(*mix.shape),
            fixed(*up.shape),
            fixed(*down.shape),
            fixed(*vectors.shape),
            fixed(*bias_up.shape),
            fixed(*spread.shape),
        ],
        out_specs=[
            tile(width),
            tile(wide),
            tile(wide),
            tile(width),
            tile(width),
            tile(width),
            tile(width),
            tile(width + 2 * HD),
            tile(2 * HD),
            fixed(6, 8, width),
            fixed(8, wide),
        ],
        out_shape=[
            jax.ShapeDtypeStruct((rows, width), bf16),
            jax.ShapeDtypeStruct((rows, wide), bf16),
            jax.ShapeDtypeStruct((rows, wide), bf16),
            jax.ShapeDtypeStruct((rows, width), bf16),
            jax.ShapeDtypeStruct((rows, width), bf16),
            jax.ShapeDtypeStruct((rows, width), bf16),
            jax.ShapeDtypeStruct((rows, width), f32),
            jax.ShapeDtypeStruct((rows, width + 2 * HD), bf16),
            jax.ShapeDtypeStruct((rows, 2 * HD), f32),
            jax.ShapeDtypeStruct((6, 8, width), f32),
            jax.ShapeDtypeStruct((8, wide), f32),
        ],
        scratch_shapes=[pltpu.VMEM((RTILE, wide), f32)],
        cost_estimate=work(44),
        compiler_params=pltpu.CompilerParams(vmem_limit_bytes=VMEM_LIMIT),
    )(att, tok, cot, live, lse, mix, up, down, vectors, bias_up, spread)


def weight_kernel(n_dp, core_ref, act, pre, hid, upr, att, mixr, small, *refs):
    send, keep, tmp = refs[-3:]
    step = pl.program_id(0)
    core = core_ref[0]
    pieces = FF // D
    down_rows = FF // n_dp
    part_rows = D // n_dp

    def put(x, row, rows, begin):
        mine = pl.multiple_of(begin + core * rows, 16)
        other = pl.multiple_of(begin + (1 - core) * rows, 16)
        keep[pl.ds(x, 1), pl.ds(row, rows), :] = tmp[pl.ds(mine, rows), :][None]
        send[pl.ds(x, 1), pl.ds(row, rows), :] = tmp[pl.ds(other, rows), :][None]

    @pl.when(step < pieces)
    def _():
        tmp[...] = outer_sum(act[...], pre[...]).astype(jnp.bfloat16)
        per = D // down_rows
        for b in range(per):
            block = step * per + b
            x = block // 2
            rows = tmp[b * down_rows : (b + 1) * down_rows, :]

            @pl.when(lax.rem(block, 2) == core)
            def _():
                keep[pl.ds(x, 1), 0:down_rows, :] = rows[None]

            @pl.when(lax.rem(block, 2) != core)
            def _():
                send[pl.ds(x, 1), 0:down_rows, :] = rows[None]

    @pl.when((step >= pieces) & (step < 2 * pieces))
    def _():
        tmp[...] = outer_sum(hid[...], upr[...]).astype(jnp.bfloat16)
        row = pl.multiple_of(down_rows + (step - pieces) * part_rows, 16)
        for x in range(n_dp // 2):
            put(x, row, part_rows, 2 * x * part_rows)

    @pl.when(step == 2 * pieces)
    def _():
        tmp[...] = outer_sum(att[...], mixr[...]).astype(jnp.bfloat16)
        row = down_rows + pieces * part_rows
        for x in range(n_dp // 2):
            put(x, row, part_rows, 2 * x * part_rows)
            last = row + part_rows
            rows = keep.shape[1] - last
            keep[x, last:, :] = small[pl.ds(2 * x + core, 1), :, :][0]
            send[x, last:, :] = small[pl.ds(2 * x + 1 - core, 1), :, :][0]


def weight_call(n_dp, core, act, pre, hid, upr, att, mixr, small, *needs):
    rows = act.shape[0]
    pieces = FF // D
    out_rows = FF // n_dp + (pieces + 1) * (D // n_dp) + small.shape[1]

    def fixed(*shape):
        return pl.BlockSpec(shape, lambda i, c: (0,) * len(shape))

    def stepped(first):
        return pl.BlockSpec((rows, D), lambda i, c: (0, jnp.clip(i - first, 0, pieces - 1)))

    shape = (n_dp // 2, out_rows, D)
    return pl.pallas_call(
        functools.partial(weight_kernel, n_dp),
        out_shape=[jax.ShapeDtypeStruct(shape, jnp.bfloat16)] * 2,
        grid_spec=pltpu.PrefetchScalarGridSpec(
            num_scalar_prefetch=1,
            grid=(2 * pieces + 1,),
            in_specs=[
                stepped(0),
                fixed(rows, D),
                fixed(rows, D),
                stepped(pieces),
                fixed(rows, D),
                fixed(rows, D),
                fixed(*small.shape),
            ]
            + [UNREAD] * len(needs),
            out_specs=[fixed(*shape)] * 2,
            scratch_shapes=[pltpu.VMEM((D, D), jnp.bfloat16)],
        ),
        cost_estimate=work(22),
        compiler_params=pltpu.CompilerParams(vmem_limit_bytes=VMEM_LIMIT),
    )(core, act, pre, hid, upr, att, mixr, small, *needs)


def outer_kernel(n_dp, core_ref, tokens, columns, *refs):
    send, keep, tmp = refs[-3:]
    core = core_ref[0]
    rows = tokens.shape[1] // n_dp
    tmp[...] = outer_sum(tokens[...], columns[...]).astype(tmp.dtype)
    for x in range(n_dp // 2):
        mine = pl.multiple_of((2 * x + core) * rows, 16)
        other = pl.multiple_of((2 * x + 1 - core) * rows, 16)
        keep[x] = tmp[pl.ds(mine, rows), :]
        send[x] = tmp[pl.ds(other, rows), :]


def outer_split(n_dp, core, tokens, columns, first, block, *needs):
    rows, depth = tokens.shape
    steps = columns.shape[1] // block - first
    shape = (n_dp // 2, depth // n_dp, block * steps)
    out = pl.BlockSpec(shape[:2] + (block,), lambda i, c: (0, 0, i))
    return pl.pallas_call(
        functools.partial(outer_kernel, n_dp),
        out_shape=[jax.ShapeDtypeStruct(shape, jnp.bfloat16)] * 2,
        grid_spec=pltpu.PrefetchScalarGridSpec(
            num_scalar_prefetch=1,
            grid=(steps,),
            in_specs=[
                pl.BlockSpec((rows, depth), lambda i, c: (0, 0)),
                pl.BlockSpec((rows, block), lambda i, c: (0, first + i)),
            ]
            + [UNREAD] * len(needs),
            out_specs=[out, out],
            scratch_shapes=[pltpu.VMEM((depth, block), jnp.bfloat16)],
        ),
        cost_estimate=work(4),
        compiler_params=plain_params(),
    )(core, tokens, columns, *needs)


def swap(value, axis, bit):
    devices = lax.axis_size(axis)
    return lax.ppermute(value, axis, [(i, i ^ bit) for i in range(devices)])


def dp_gather(shard, dp_rank):
    blocks = shard[None]
    bit = lax.axis_size("dp") // 2
    while bit >= 1:
        got = swap(blocks, "dp", bit)
        high = ((dp_rank // bit) % 2) == 1
        first = jnp.where(high, got, blocks)
        second = jnp.where(high, blocks, got)
        blocks = jnp.stack([first, second], axis=1).reshape((-1,) + shard.shape)
        bit //= 2
    return blocks.reshape((-1,) + shard.shape[1:])


def work(microseconds):
    return pl.CostEstimate(
        flops=int(microseconds * 0.4e9), transcendentals=0, bytes_accessed=1 << 20
    )


def row_tile(rows, limit=512):
    for size in range(min(rows, limit), 15, -1):
        if rows % size == 0 and size % 16 == 0:
            return size
    return rows


def plain_params():
    return pltpu.CompilerParams(vmem_limit_bytes=VMEM_LIMIT)


def split_add_kernel(which, keep_mine, got_mine, keep_other, got_other, *refs):
    mine, other = refs[-2:]
    mine[...] = (keep_mine[...].astype(jnp.float32) + got_mine[...].astype(jnp.float32)).astype(
        mine.dtype
    )
    other[...] = (keep_other[...].astype(jnp.float32) + got_other[...].astype(jnp.float32)).astype(
        other.dtype
    )


def split_add(keep, got, which, *needs):
    blocks, rows, columns = keep.shape
    tile = row_tile(rows)

    def spec(flip):
        def place(b, i, w):
            bit = 1 - w[0] if flip else w[0]
            return 2 * b + bit, i, 0

        return pl.BlockSpec((1, tile, columns), place)

    out = pl.BlockSpec((1, tile, columns), lambda b, i, w: (b, i, 0))
    shape = jax.ShapeDtypeStruct((blocks // 2, rows, columns), keep.dtype)
    return pl.pallas_call(
        split_add_kernel,
        out_shape=[shape, shape],
        grid_spec=pltpu.PrefetchScalarGridSpec(
            num_scalar_prefetch=1,
            grid=(blocks // 2, rows // tile),
            in_specs=[spec(False), spec(False), spec(True), spec(True)] + [UNREAD] * len(needs),
            out_specs=[out, out],
        ),
        cost_estimate=work(4),
        compiler_params=plain_params(),
    )(which, keep, got, keep, got, *needs)


def add_kernel(left, right, *refs):
    out = refs[-1]
    out[...] = (left[0].astype(jnp.float32) + right[0].astype(jnp.float32)).astype(out.dtype)


def add_blocks(left, right, *needs):
    _, rows, columns = left.shape
    tile = row_tile(rows)
    spec = pl.BlockSpec((1, tile, columns), lambda i: (0, i, 0))
    return pl.pallas_call(
        add_kernel,
        grid=(rows // tile,),
        in_specs=[spec, spec] + [UNREAD] * len(needs),
        out_specs=pl.BlockSpec((tile, columns), lambda i: (i, 0)),
        cost_estimate=work(3),
        out_shape=jax.ShapeDtypeStruct((rows, columns), left.dtype),
        compiler_params=plain_params(),
    )(left, right, *needs)


def pieces_kernel(pieces, *refs):
    out = refs[-1]
    total = pieces[0].astype(jnp.float32)
    for i in range(1, pieces.shape[0]):
        total = total + pieces[i].astype(jnp.float32)
    total = total.astype(out.dtype)
    for i in range(out.shape[0]):
        out[i] = total


def summed_copies(pieces, copies, *needs):
    _, rows, columns = pieces.shape
    return pl.pallas_call(
        pieces_kernel,
        in_specs=[pl.BlockSpec(memory_space=pltpu.VMEM)] + [UNREAD] * len(needs),
        out_specs=pl.BlockSpec(memory_space=pltpu.VMEM),
        out_shape=jax.ShapeDtypeStruct((copies, rows, columns), pieces.dtype),
        cost_estimate=work(2),
        compiler_params=plain_params(),
    )(pieces, *needs)


def gate_kernel(value, *refs):
    refs[-1][...] = value[...]


def gated(value, *needs):
    return pl.pallas_call(
        gate_kernel,
        in_specs=[pl.BlockSpec(memory_space=pltpu.VMEM)] + [UNREAD] * len(needs),
        out_specs=pl.BlockSpec(memory_space=pltpu.VMEM),
        out_shape=jax.ShapeDtypeStruct(value.shape, value.dtype),
        cost_estimate=work(1),
        compiler_params=plain_params(),
    )(value, *needs)


def cluster_ids(group_order, own_start, span):
    padded = jnp.pad(group_order, ((0, 0), (HALO, HALO)), constant_values=-(1 << 24))
    wanted = lax.dynamic_slice_in_dim(padded, own_start, span, 1) - (own_start - HALO)
    tile_of = wanted >> 7
    lane_of_token = wanted & (CL - 1)
    cluster = (jnp.arange(span, dtype=jnp.int32) >> 7) + 1
    tile_hot = jnp.where(
        tile_of[:, :, None] == jnp.arange(span // CL, dtype=jnp.int32), cluster[None, :, None], 0
    ).astype(jnp.bfloat16)
    lane_hot = (lane_of_token[:, :, None] == jnp.arange(CL, dtype=jnp.int32)).astype(jnp.bfloat16)
    table = jnp.einsum("hpt,hpl->htl", tile_hot, lane_hot, preferred_element_type=jnp.float32)
    return table.reshape(HEADS, span) - 1.0


def on_device(
    tokens,
    input_weight,
    output_weight,
    up_weight,
    down_weight,
    output_bias,
    up_bias,
    down_bias,
    first_gain,
    first_shift,
    second_gain,
    second_shift,
    document_runs,
    document_trim,
    cluster_order,
    cotangent,
):
    bf16, f32 = jnp.bfloat16, jnp.float32
    n_dp = lax.axis_size("dp")
    n_seq = lax.axis_size("seq")
    dp_rank = lax.axis_index("dp")
    seq_rank = lax.axis_index("seq")
    inputs = tokens[0]
    tok_dev = inputs.shape[0]
    tiles = tok_dev // CL
    span = tok_dev + 2 * HALO
    own_start = seq_rank * tok_dev

    token_parts = halo_parts(inputs)
    n_parts = len(token_parts)

    weight_in = lax.all_gather(input_weight, "dp", axis=0, tiled=True)
    weight_up = lax.all_gather(up_weight, "dp", axis=0, tiled=True)
    weight_down = lax.all_gather(down_weight, "dp", axis=0, tiled=True)

    runs = document_runs[0]
    first_cluster = jnp.cumsum(runs) - runs
    own_clusters = seq_rank * tiles + jnp.arange(tiles, dtype=jnp.int32)
    doc_start = jnp.max(
        jnp.where(first_cluster[None, :] <= own_clusters[:, None], first_cluster[None, :], 0), axis=1
    )
    starts = (doc_start - seq_rank * tiles + (MOSTB - 1)).astype(jnp.int32)
    near_left = HALO // CL - tiles
    near = near_left + 2 * tiles * jnp.stack([1 - seq_rank % 2, seq_rank % 2])
    starts = jnp.concatenate([starts, near.astype(jnp.int32)])

    cids = cluster_ids(cluster_order[0], own_start, span)
    positions = own_start - HALO + jnp.arange(span, dtype=jnp.int32)
    live = live_tokens(runs, document_trim[0], positions)
    usable = live[None, :] & (cids >= 0.0)
    key_ids = jnp.where(usable, cids, -1.0).reshape(PAIRS, 2, span)
    query_ids = jnp.where(usable, cids, -2.0).reshape(PAIRS, 2, span)
    own_live = live[HALO : HALO + tok_dev, None].astype(f32)

    own = plain_product(inputs, weight_in).astype(bf16)
    far = project_call([token_parts[0], token_parts[4]], weight_in, own)
    groups = HEADS // PACK
    group_lanes = PACK * HD
    kv_weight = (
        weight_in[:, D:]
        .reshape(D, 2, groups, group_lanes)
        .transpose(0, 2, 1, 3)
        .reshape(D, 2 * D)
    )
    near_parts = project_call([token_parts[1], token_parts[3]], weight_in, *far, kv_weight)
    projected = [far[0], near_parts[0], own, near_parts[1], far[1]]
    vectors = [
        output_bias,
        down_bias,
        first_gain,
        first_shift,
        second_gain,
        second_shift,
        up_bias,
    ]
    mix_rows = output_weight.shape[0]
    packed = jnp.concatenate(vectors)
    pad_rows = -(-packed.shape[0] // (16 * D)) * 16
    packed = jnp.pad(packed, (0, pad_rows * D - packed.shape[0])).reshape(pad_rows, D)
    mix_shard = gated(jnp.concatenate([output_weight, packed], 0), own)
    mix_all = dp_gather(mix_shard, dp_rank)
    mix_all = mix_all.reshape(n_dp, mix_rows + pad_rows, D)
    weight_mix = mix_all[:, :mix_rows].reshape(D, D)
    small_all = mix_all[:, mix_rows:].reshape(n_dp, -1).astype(f32)
    vec = small_all[:, : 6 * mix_rows].reshape(n_dp, 6, mix_rows).transpose(1, 0, 2).reshape(6, D)
    vec = jnp.pad(vec, ((0, 2), (0, 0)))
    up_part = up_bias.shape[0]
    bias_up = small_all[:, 6 * mix_rows : 6 * mix_rows + up_part].reshape(1, FF)
    bias_up = jnp.pad(bias_up, ((0, 7), (0, 0)))
    heights = [part.shape[0] for part in token_parts]

    groups = HEADS // PACK
    group_lanes = PACK * HD
    group_key_ids = key_ids.reshape(groups, PACK, span)
    group_query_ids = query_ids.reshape(groups, PACK, span)
    group_scratch = pltpu.VMEM((span, group_lanes), bf16)

    def group_parts(third, first):
        return [lane_block(rows, third * groups + first, PACK) for rows in heights]

    steps = tiles // TILES_AT_ONCE
    step_rows = TILES_AT_ONCE * CL

    def of_group(rows, first):
        return pl.BlockSpec((rows, group_lanes), lambda g, t, starts: (0, first + g))

    def ids_of_group():
        return pl.BlockSpec((1, PACK, span), lambda g, t, starts: (g, 0, 0))

    step_block = pl.BlockSpec((step_rows, group_lanes), lambda g, t, starts: (t, g))
    whole_lanes = pl.BlockSpec((tok_dev, 2 * HD), lambda g, t, starts: (0, 0))
    attended, lse, rate, probs = strip_call(
        functools.partial(attend_kernel, tiles, n_parts),
        52,
        (groups, steps),
        [step_block]
        + [of_group(rows, groups) for rows in heights]
        + [of_group(rows, 2 * groups) for rows in heights]
        + [ids_of_group(), ids_of_group()],
        [
            step_block,
            whole_lanes,
            whole_lanes,
            pl.BlockSpec(
                (1, TILES_AT_ONCE, PACK * CL, WINDOW), lambda g, t, starts: (g, t, 0, 0)
            ),
        ],
        [
            jax.ShapeDtypeStruct((tok_dev, D), bf16),
            jax.ShapeDtypeStruct((tok_dev, 2 * HD), f32),
            jax.ShapeDtypeStruct((tok_dev, 2 * HD), f32),
            jax.ShapeDtypeStruct((groups, tiles, PACK * CL, WINDOW), bf16),
        ],
        [group_scratch, group_scratch]
        + [pltpu.VMEM((PACK * CL, WINDOW), f32)] * TILES_AT_ONCE
        + [pltpu.VMEM((PACK * CL, CL), f32)] * TILES_AT_ONCE,
        (starts, own, *projected, *projected, group_query_ids, group_key_ids),
    )

    (
        result,
        active,
        up_rounded,
        hidden_rounded,
        pre_rounded,
        mixed_rounded,
        back_mixed,
        back_own,
        delta,
        sums,
        sums_up,
    ) = chain_call(
        attended,
        inputs,
        cotangent[0],
        own_live,
        lse,
        weight_mix,
        weight_up,
        weight_down,
        vec,
        bias_up,
    )
    back_parts = halo_parts(back_own)

    small = jnp.concatenate(
        [
            jnp.sum(sums, axis=1).reshape(6, n_dp, mix_rows).transpose(1, 0, 2).reshape(n_dp, -1),
            jnp.sum(sums_up, axis=0).reshape(n_dp, -1),
        ],
        axis=1,
    ).astype(bf16)
    unit = 8 * n_seq
    fixed_rows = FF // n_dp + (FF // D + 1) * (D // n_dp)
    small_rows = -(-(fixed_rows + -(-small.shape[1] // D)) // unit) * unit - fixed_rows
    small = jnp.pad(small, ((0, 0), (0, small_rows * D - small.shape[1])))
    small = small.reshape(n_dp, small_rows, D)
    core = (dp_rank % 2).astype(jnp.int32)
    def query_strip(first, *needs):
        buffer = needs[:1] if first > 0 else ()

        def parts(third):
            return [
                pl.BlockSpec(
                    (rows, group_lanes), lambda t, starts: (0, third * groups + first)
                )
                for rows in heights
            ]

        block = pl.BlockSpec((step_rows, group_lanes), lambda t, starts: (t, first))
        lanes = pl.BlockSpec((step_rows, 2 * HD), lambda t, starts: (t, 0))
        in_specs = (
            parts(1)
            + parts(2)
            + [
                block,
                pl.BlockSpec(
                    (1, TILES_AT_ONCE, PACK * CL, WINDOW), lambda t, starts: (first, t, 0, 0)
                ),
                lanes,
                lanes,
            ]
            + [UNREAD] * len(needs)
        )
        return strip_call(
            functools.partial(query_kernel, tiles, n_parts, first * PACK),
            16,
            (steps,),
            in_specs,
            block,
            jax.ShapeDtypeStruct((tok_dev, D), bf16),
            [group_scratch, group_scratch],
            (starts, *projected, *projected, back_own, probs, rate, delta, *needs),
            {len(in_specs) + 1 - len(needs): 0} if buffer else None,
        )

    key_pairs = PACK // 2
    pair_scratch = pltpu.VMEM((span, 4 * HD), bf16)

    def key_strip(first, length, *needs):
        buffer = needs[:1] if first > 0 else ()
        pair = first * key_pairs

        def parts(third):
            return [lane_block(rows, third * PAIRS + pair) for rows in heights]

        in_specs = (
            [lane_block(tok_dev, PAIRS + pair), lane_block(tok_dev, 2 * PAIRS + pair)]
            + parts(0)
            + parts(0)
            + [fixed_lanes(rows, PAIRS) for rows in heights]
            + [row_block(span, pair), row_block(span, pair)]
            + [UNREAD] * len(needs)
        )
        return strip_call(
            functools.partial(key_kernel, tiles, n_parts, pair),
            length,
            (key_pairs,),
            in_specs,
            pl.BlockSpec((tok_dev, 2 * group_lanes), lambda step, starts: (0, first)),
            jax.ShapeDtypeStruct((tok_dev, 2 * D), bf16),
            [pair_scratch, pair_scratch],
            (
                starts,
                own,
                own,
                *projected,
                *back_parts,
                *back_parts,
                query_ids,
                key_ids,
                *needs,
            ),
            {len(in_specs) + 1 - len(needs): 0} if buffer else None,
        )

    def scatter(share):
        rows, columns = share.shape
        return lax.all_to_all(
            share.reshape(n_seq, rows // n_seq, columns), "seq", split_axis=0, concat_axis=0
        )

    def everyone(copies):
        got = lax.all_to_all(copies, "seq", split_axis=0, concat_axis=0)
        return got.reshape(-1, copies.shape[-1])

    def first_split(keep, got, *needs):
        bit = 2
        while True:
            which = ((dp_rank // bit) % 2).astype(jnp.int32).reshape(1)
            mine, other = split_add(keep, got, which, *needs)
            got = swap(other, "dp", bit)
            if mine.shape[0] == 1:
                return mine, got
            keep, bit, needs = mine, bit * 2, ()

    def core_split(grad):
        rows, columns = grad.shape
        blocks = grad.astype(bf16).reshape(n_dp // 2, 2, rows // n_dp, columns)
        return (
            lax.dynamic_index_in_dim(blocks, 1 - core, 1, keepdims=False),
            lax.dynamic_index_in_dim(blocks, core, 1, keepdims=False),
        )

    send, keep = weight_call(
        n_dp,
        core.reshape(1),
        active,
        pre_rounded,
        hidden_rounded,
        up_rounded,
        attended,
        mixed_rounded,
        small,
    )
    core_got = swap(send, "dp", 1)
    mine, x_got = first_split(keep, core_got)
    back_q = query_strip(0, mine)
    back_q = query_strip(1, back_q, back_parts[0], back_parts[4])
    back_q = query_strip(2, back_q)
    share = add_blocks(mine, x_got, back_q, *back_parts)
    back_kv = key_strip(0, 27, back_q, share)
    pieces = scatter(share)
    cut = 2 * group_lanes
    early_cols = jnp.concatenate([back_q, back_kv[:, :cut]], axis=1)
    early_send, early_keep = core_split(outer_sum(inputs, early_cols))
    early_core = swap(early_send, "dp", 1)
    back_kv = key_strip(1, 27, back_kv, early_send)
    early_mine, early_got = first_split(early_keep, early_core, back_kv)
    copies = summed_copies(pieces, 1, back_kv)
    back_kv = key_strip(2, 2, back_kv, early_mine, copies)
    early_share = add_blocks(early_mine, early_got, back_kv)
    all_sums = lax.all_gather(copies[0], "seq", axis=0, tiled=True)
    late_send, late_keep = outer_split(
        n_dp, core.reshape(1), inputs, back_kv, 1, cut, early_share
    )
    late_mine, late_got = first_split(late_keep, swap(late_send, "dp", 1))
    late_share = add_blocks(late_mine, late_got, all_sums)
    in_share = jnp.concatenate([early_share, late_share], axis=1)
    in_all = everyone(summed_copies(scatter(in_share), n_seq))

    input_grad = (
        back_mixed + back_product(back_q, weight_in[:, :D]) + back_product(back_kv, kv_weight)
    )
    kv_all = in_all[:, D:].reshape(-1, groups, 2, group_lanes).transpose(0, 2, 1, 3)
    grad_in_total = jnp.concatenate([in_all[:, :D], kv_all.reshape(-1, 2 * D)], axis=1).astype(f32)
    down_rows = FF // n_dp
    part_rows = D // n_dp
    grad_down = all_sums[:down_rows].astype(f32)
    grad_up = (
        all_sums[down_rows : down_rows + (FF // D) * part_rows]
        .reshape(FF // D, part_rows, D)
        .transpose(1, 0, 2)
        .reshape(part_rows, FF)
        .astype(f32)
    )
    at = down_rows + (FF // D) * part_rows
    grad_mix = all_sums[at : at + part_rows].astype(f32)
    flat = all_sums[at + part_rows :].reshape(-1).astype(f32)
    vectors_out = [flat[i * part_rows : (i + 1) * part_rows] for i in range(6)]
    bias_up_out = flat[6 * part_rows : 6 * part_rows + down_rows]
    return (
        result[None],
        input_grad[None],
        grad_in_total,
        grad_mix,
        grad_up,
        grad_down,
        vectors_out[0],
        bias_up_out,
        vectors_out[1],
        *vectors_out[2:],
    )


def solution(mesh):
    placed = (
        P("dp", "seq", None),
        P("dp", None),
        P("dp", None),
        P("dp", None),
        P("dp", None),
        P("dp"),
        P("dp"),
        P("dp"),
        P("dp"),
        P("dp"),
        P("dp"),
        P("dp"),
        P("dp", None),
        P("dp", None),
        P("dp", None, None),
        P("dp", "seq", None),
    )
    return jax.shard_map(
        on_device,
        mesh=mesh,
        in_specs=placed,
        out_specs=(
            P("dp", "seq", None),
            P("dp", "seq", None),
            P("dp", None),
            P("dp", None),
            P("dp", None),
            P("dp", None),
            P("dp"),
            P("dp"),
            P("dp"),
            P("dp"),
            P("dp"),
            P("dp"),
            P("dp"),
        ),
        check_vma=False,
    )
```

```python
import functools

import jax
import jax.numpy as jnp
from jax import lax
from jax.experimental import pallas as pl
from jax.experimental.pallas import tpu as pltpu
from jax.sharding import PartitionSpec as P

D = 768
HEADS = 12
HD = 64
CL = 128
MOSTB = 16
PAIRS = HEADS // 2
WINDOW = MOSTB * CL
HALO = (MOSTB - 1) * CL
CHUNK = 512
KCHUNK = 512
TILES_AT_ONCE = 2
PACK = 4
NEG = -1e30
TERMS = 5
FF = 3072
RTILE = 256
FCHUNK = 768
SCALE2 = HD ** (-0.5) * 1.4426950408889634

EPSILON = 1e-05


def shifted(value, axis, by):
    devices = lax.axis_size(axis)
    pairs = [(i, i + by) for i in range(devices) if 0 <= i + by < devices]
    return lax.ppermute(value, axis, pairs)


def halo_parts(value):
    own = value.shape[0]
    far = HALO - own
    devices = lax.axis_size("seq")
    assert 0 < far <= own and devices % 2 == 0
    partner = lax.ppermute(value, "seq", [(i, i ^ 1) for i in range(devices)])
    pairs = [(i, i - 1 if i % 2 == 0 else i + 1) for i in range(devices)]
    other = lax.ppermute(value, "seq", [(i, k) for i, k in pairs if 0 <= k < devices])
    before = shifted(value[own - far :], "seq", 2)
    following = shifted(value[:far], "seq", -2)
    return [before, partner, value, other, following]


def places(starts, tiles, parts):
    far, own = parts[0].shape[0], parts[2].shape[0]
    return [
        0,
        pl.multiple_of(starts[tiles] * CL, CL),
        far + own,
        pl.multiple_of(starts[tiles + 1] * CL, CL),
        far + 3 * own,
    ]


def live_tokens(runs, trim, positions):
    ends = jnp.cumsum(runs) * CL
    starts = ends - runs * CL
    lengths = runs * CL - trim
    inside = (positions[..., None] >= starts) & (positions[..., None] < starts + lengths)
    return jnp.any(inside, axis=-1)


def outer_sum(left, right):
    return lax.dot_general(
        left, right, (((0,), (0,)), ((), ())), preferred_element_type=jnp.float32
    )


def back_product(left, right):
    return lax.dot_general(
        left, right, (((1,), (1,)), ((), ())), preferred_element_type=jnp.float32
    )


def plain_product(left, right):
    return jnp.dot(left, right, preferred_element_type=jnp.float32)


def stacked(tile):
    lane = lax.broadcasted_iota(jnp.int32, tile.shape, 1)
    zero = jnp.zeros_like(tile)
    heads = tile.shape[1] // HD
    return jnp.concatenate(
        [
            jnp.where((lane >= h * HD) & (lane < (h + 1) * HD), tile, zero)
            for h in range(heads)
        ],
        axis=0,
    )


def unstacked(stack):
    heads = stack.shape[1] // HD
    lane = lax.broadcasted_iota(jnp.int32, (CL, heads * HD), 1)
    result = stack[:CL]
    for h in range(1, heads):
        result = jnp.where(lane >= h * HD, stack[h * CL : (h + 1) * CL], result)
    return result


def as_column(row):
    return jnp.broadcast_to(row, (CL, CL)).T


def lane_of(tile, lane):
    lanes = lax.broadcasted_iota(jnp.int32, tile.shape, 1)
    return jnp.sum(jnp.where(lanes == lane, tile, 0.0), axis=1, keepdims=True)


def masked(scores, cols, row_ref, begin):
    parts = []
    wide = scores.shape[1]
    for half, one in enumerate(cols):
        row = row_ref[0, half : half + 1, pl.ds(begin, wide)]
        block = scores[half * CL : (half + 1) * CL]
        col = jnp.concatenate([one] * (wide // CL), axis=1)
        parts.append(jnp.where(col == row, block, NEG))
    return jnp.concatenate(parts, axis=0)


def assemble(parts, offsets, whole):
    for part, at in zip(parts, offsets):
        whole[pl.ds(at, part.shape[0]), :] = part[...]


def ahead(steps, produce, consume):
    held = produce(*steps[0])
    for i, step in enumerate(steps):
        following = produce(*steps[i + 1]) if i + 1 < len(steps) else None
        consume(*step, held)
        held = following


def attend_kernel(tiles, n_parts, starts, q_ref, *refs):
    k_parts, refs = refs[:n_parts], refs[n_parts:]
    v_parts, refs = refs[:n_parts], refs[n_parts:]
    qid_ref, kid_ref, out_ref, lse_ref, rate_ref, p_ref, k_ref, v_ref, *slots = refs
    s_refs, top_refs = slots[:TILES_AT_ONCE], slots[TILES_AT_ONCE:]
    group, step = pl.program_id(0), pl.program_id(1)
    heads = q_ref.shape[1] // HD
    chunks = WINDOW // CHUNK

    @pl.when(step == 0)
    def _():
        offsets = places(starts, tiles, k_parts)
        assemble(k_parts, offsets, k_ref)
        assemble(v_parts, offsets, v_ref)

    @pl.when((group == 0) & (step == 0))
    def _():
        lse_ref[...] = jnp.zeros_like(lse_ref)
        rate_ref[...] = jnp.zeros_like(rate_ref)

    def first_half(slot):
        tile = TILES_AT_ONCE * step + slot
        own = pl.multiple_of(HALO + tile * CL, CL)
        return dict(
            begin=pl.multiple_of(starts[tile] * CL, CL),
            query=stacked(q_ref[slot * CL : (slot + 1) * CL, :]),
            cols=[
                as_column(qid_ref[0, half : half + 1, pl.ds(own, CL)]) for half in range(heads)
            ],
        )

    def score(state, slot, j):
        at = pl.multiple_of(state["begin"] + j * CHUNK, CL)
        scores = back_product(state["query"], k_ref[pl.ds(at, CHUNK), :])
        scores = masked(scores, state["cols"], kid_ref, at)
        s_refs[slot][:, j * CHUNK : (j + 1) * CHUNK] = scores
        top = scores[:, :CL]
        for i in range(1, CHUNK // CL):
            top = jnp.maximum(top, scores[:, i * CL : (i + 1) * CL])
        if j > 0:
            top = jnp.maximum(top, top_refs[slot][...])
        top_refs[slot][...] = top

    states = [first_half(0)]
    for j in range(chunks):
        score(states[0], 0, j)
    for slot in range(TILES_AT_ONCE):
        if slot + 1 < TILES_AT_ONCE:
            states.append(first_half(slot + 1))
        state = states[slot]
        peak = jnp.max(top_refs[slot][...], axis=1, keepdims=True)
        total = jnp.zeros((heads * CL, CL), jnp.float32)
        result = jnp.zeros((heads * CL, heads * HD), jnp.float32)
        for j in range(chunks):
            if slot + 1 < TILES_AT_ONCE:
                score(states[slot + 1], slot + 1, j)
            at = pl.multiple_of(state["begin"] + j * CHUNK, CL)
            columns = slice(j * CHUNK, (j + 1) * CHUNK)
            weights = jnp.exp2((s_refs[slot][:, columns] - peak) * SCALE2)
            for i in range(CHUNK // CL):
                total = total + weights[:, i * CL : (i + 1) * CL]
            p_ref[0, slot, :, columns] = weights.astype(jnp.bfloat16)
            result = result + plain_product(
                p_ref[0, slot, :, columns], v_ref[pl.ds(at, CHUNK), :]
            )
        total = jnp.sum(total, axis=1, keepdims=True)
        rate = 1.0 / total
        result = result * rate
        lse = peak + jnp.log(total) * HD**0.5
        live = (state["cols"][0] >= 0.0).astype(jnp.float32)
        live = jnp.concatenate([live] * (heads * HD // CL), axis=1)
        rows = slice(slot * CL, (slot + 1) * CL)
        out_ref[rows, :] = (unstacked(result) * live).astype(jnp.bfloat16)
        here = pl.ds(pl.multiple_of((TILES_AT_ONCE * step + slot) * CL, CL), CL)
        lane = lax.broadcasted_iota(jnp.int32, (CL, CL), 1)
        kept, kept_rate = lse_ref[here, :], rate_ref[here, :]
        for half in range(heads):
            first = (heads * group + half) * TERMS
            inside = (lane >= first) & (lane < first + TERMS)
            part = slice(half * CL, (half + 1) * CL)
            kept = jnp.where(inside, lse[part], kept)
            kept_rate = jnp.where(inside, rate[part], kept_rate)
        lse_ref[here, :] = kept
        rate_ref[here, :] = kept_rate


def query_kernel(tiles, n_parts, first_head, starts, *refs):
    k_parts, refs = refs[:n_parts], refs[n_parts:]
    v_parts, refs = refs[:n_parts], refs[n_parts:]
    g_ref, p_ref, rate_ref, delta_ref = refs[:4]
    out_ref, k_ref, v_ref = refs[-3:]
    step = pl.program_id(0)
    heads = g_ref.shape[1] // HD
    chunks = WINDOW // CHUNK

    @pl.when(step == 0)
    def _():
        offsets = places(starts, tiles, k_parts)
        assemble(k_parts, offsets, k_ref)
        assemble(v_parts, offsets, v_ref)

    states = {}

    def state_of(slot):
        if slot not in states:
            rows = slice(slot * CL, (slot + 1) * CL)
            columns = [
                jnp.concatenate(
                    [lane_of(ref[rows, :], (first_head + half) * TERMS) for half in range(heads)],
                    axis=0,
                )
                for ref in (delta_ref, rate_ref)
            ]
            states[slot] = dict(
                begin=pl.multiple_of(starts[TILES_AT_ONCE * step + slot] * CL, CL),
                back=stacked(g_ref[rows, :]),
                delta=columns[0],
                rate=columns[1],
                result=jnp.zeros((heads * CL, heads * HD), jnp.float32),
            )
        return states[slot]

    def produce(slot, j):
        state = state_of(slot)
        at = pl.multiple_of(state["begin"] + j * CHUNK, CL)
        return back_product(state["back"], v_ref[pl.ds(at, CHUNK), :])

    def consume(slot, j, back_probs):
        state = state_of(slot)
        at = pl.multiple_of(state["begin"] + j * CHUNK, CL)
        weights = p_ref[0, slot, :, j * CHUNK : (j + 1) * CHUNK].astype(jnp.float32)
        back_scores = weights * (back_probs - state["delta"])
        state["result"] = state["result"] + plain_product(
            back_scores.astype(jnp.bfloat16), k_ref[pl.ds(at, CHUNK), :]
        )
        if j == chunks - 1:
            out_ref[slot * CL : (slot + 1) * CL, :] = unstacked(
                state["result"] * (state["rate"] * HD ** (-0.5))
            ).astype(jnp.bfloat16)

    ahead(
        [(slot, j) for slot in range(TILES_AT_ONCE) for j in range(chunks)], produce, consume
    )


def key_kernel(tiles, n_parts, first_pair, starts, k_ref, v_ref, *refs):
    q_parts, refs = refs[:n_parts], refs[n_parts:]
    g_parts, refs = refs[:n_parts], refs[n_parts:]
    a_parts, refs = refs[:n_parts], refs[n_parts:]
    qid_ref, kid_ref = refs[:2]
    out_ref, q_ref, g_ref = refs[-3:]
    step_pair = pl.program_id(0)
    pair = first_pair + step_pair
    offsets = places(starts, tiles, q_parts)
    for at, q_part, g_part, a_part in zip(offsets, q_parts, g_parts, a_parts):
        rows = pl.ds(at, q_part.shape[0])
        q_ref[rows, : 2 * HD] = q_part[...]
        q_ref[rows, 2 * HD :] = a_part[...]
        g_ref[rows, : 2 * HD] = g_part[...]
        g_ref[rows, 2 * HD :] = a_part[...]

    lane = lax.broadcasted_iota(jnp.int32, (CL, CL), 1)
    lse_pick, delta_pick = [], []
    for half in range(2):
        first = (2 * pair + half) * TERMS
        lse_pick.append(jnp.where((lane >= first) & (lane < first + 3), -1.0, 0.0))
        delta_pick.append(jnp.where((lane >= first + 3) & (lane < first + TERMS), -1.0, 0.0))
    lse_pick = jnp.concatenate(lse_pick, axis=0).astype(jnp.bfloat16)
    delta_pick = jnp.concatenate(delta_pick, axis=0).astype(jnp.bfloat16)
    key_lanes = pl.ds(pl.multiple_of(step_pair * 2 * HD, 2 * HD), 2 * HD)
    value_lanes = pl.ds(
        pl.multiple_of(out_ref.shape[1] // 2 + step_pair * 2 * HD, 2 * HD), 2 * HD
    )

    def some_tiles(step, carry):
        states = {}

        def state_of(slot):
            if slot not in states:
                tile = TILES_AT_ONCE * step + slot
                own = pl.multiple_of(HALO + tile * CL, CL)
                here = pl.multiple_of(tile * CL, CL)
                states[slot] = dict(
                    begin=pl.multiple_of(starts[tile] * CL, CL),
                    here=here,
                    keys=jnp.concatenate([stacked(k_ref[pl.ds(here, CL), :]), lse_pick], axis=1),
                    values=jnp.concatenate(
                        [stacked(v_ref[pl.ds(here, CL), :]), delta_pick], axis=1
                    ),
                    cols=[
                        as_column(kid_ref[0, half : half + 1, pl.ds(own, CL)]) for half in range(2)
                    ],
                    key_sum=jnp.zeros((2 * CL, 2 * HD), jnp.float32),
                    value_sum=jnp.zeros((2 * CL, 2 * HD), jnp.float32),
                )
            return states[slot]

        def produce(slot, j):
            state = state_of(slot)
            at = pl.multiple_of(state["begin"] + j * KCHUNK, CL)
            scores = back_product(state["keys"], q_ref[pl.ds(at, KCHUNK), :])
            return scores, back_product(state["values"], g_ref[pl.ds(at, KCHUNK), :])

        def consume(slot, j, held):
            state = state_of(slot)
            at = pl.multiple_of(state["begin"] + j * KCHUNK, CL)
            scores, back_probs = held
            probs = jnp.exp2(masked(scores * SCALE2, state["cols"], qid_ref, at))
            back_scores = probs * back_probs
            state["value_sum"] = state["value_sum"] + plain_product(
                probs.astype(jnp.bfloat16), g_ref[pl.ds(at, KCHUNK), : 2 * HD]
            )
            state["key_sum"] = state["key_sum"] + plain_product(
                back_scores.astype(jnp.bfloat16), q_ref[pl.ds(at, KCHUNK), : 2 * HD]
            )
            if j == WINDOW // KCHUNK - 1:
                rows = pl.ds(state["here"], CL)
                out_ref[rows, key_lanes] = (
                    unstacked(state["key_sum"]) * HD ** (-0.5)
                ).astype(jnp.bfloat16)
                out_ref[rows, value_lanes] = unstacked(state["value_sum"]).astype(jnp.bfloat16)

        ahead(
            [(slot, j) for slot in range(TILES_AT_ONCE) for j in range(WINDOW // KCHUNK)],
            produce,
            consume,
        )
        return carry

    lax.fori_loop(0, tiles // TILES_AT_ONCE, some_tiles, 0)


def lane_block(rows, first, heads=2):
    return pl.BlockSpec((rows, heads * HD), lambda pair, starts: (0, first + pair))


def fixed_lanes(rows, block):
    return pl.BlockSpec((rows, 2 * HD), lambda pair, starts: (0, block))


def row_block(columns, first, heads=2):
    return pl.BlockSpec((1, heads, columns), lambda pair, starts: (first + pair, 0, 0))


UNREAD = pl.BlockSpec(memory_space=pl.ANY)


VMEM_LIMIT = 60 * 1024 * 1024


def strip_call(
    kernel, length, grid, in_specs, out_specs, out_shape, scratch, args, aliases=None
):
    return pl.pallas_call(
        kernel,
        out_shape=out_shape,
        grid_spec=pltpu.PrefetchScalarGridSpec(
            num_scalar_prefetch=1,
            grid=grid,
            in_specs=in_specs,
            out_specs=out_specs,
            scratch_shapes=scratch,
        ),
        input_output_aliases=aliases or {},
        cost_estimate=work(length),
        compiler_params=pltpu.CompilerParams(vmem_limit_bytes=VMEM_LIMIT),
    )(*args)


def project_kernel(parts, weight, *refs):
    for source, target in zip(refs[:parts], refs[-parts:]):
        target[...] = plain_product(source[...], weight[...]).astype(target.dtype)


def project_call(parts, weight, *needs):
    depth, columns = weight.shape
    block = PACK * HD
    return pl.pallas_call(
        functools.partial(project_kernel, len(parts)),
        grid=(columns // block,),
        in_specs=[pl.BlockSpec((depth, block), lambda i: (0, i))]
        + [pl.BlockSpec(part.shape, lambda i: (0, 0)) for part in parts]
        + [UNREAD] * len(needs),
        out_specs=[pl.BlockSpec((part.shape[0], block), lambda i: (0, i)) for part in parts],
        out_shape=[jax.ShapeDtypeStruct((part.shape[0], columns), part.dtype) for part in parts],
        cost_estimate=work(20),
        compiler_params=pltpu.CompilerParams(vmem_limit_bytes=VMEM_LIMIT),
    )(weight, *parts, *needs)


def gelu_terms(value):
    t = 1.0 / (1.0 + (0.3275911 * 0.7071067811865476) * jnp.abs(value))
    bell = jnp.exp2(value * value * (-0.5 * 1.4426950408889634))
    tail = 0.5 * 1.061405429
    for term in (-0.5 * 1.453152027, 0.5 * 1.421413741, -0.5 * 0.284496736, 0.5 * 0.254829592):
        tail = tail * t + term
    tail = tail * t * bell
    cdf = jnp.where(value >= 0.0, 1.0 - tail, tail)
    return value * cdf, cdf + value * (0.3989422804014327 * bell)


def normalised(values):
    mean = jnp.mean(values, axis=-1, keepdims=True)
    centre = values - mean
    rate = lax.rsqrt(jnp.mean(centre * centre, axis=-1, keepdims=True) + EPSILON)
    return centre * rate, rate


def norm_back(scaled, unit, rate):
    first = jnp.mean(scaled, axis=-1, keepdims=True)
    second = jnp.mean(scaled * unit, axis=-1, keepdims=True)
    return rate * (scaled - first - unit * second)


def row_sums(values):
    rows, columns = values.shape
    return jnp.sum(values.reshape(rows // 8, 8, columns), axis=0)


def chain_kernel(
    att_ref,
    tok_ref,
    cot_ref,
    live_ref,
    lse_ref,
    mix_ref,
    up_ref,
    down_ref,
    vec_ref,
    bias_up_ref,
    spread_ref,
    out_ref,
    act_ref,
    upr_ref,
    hid_ref,
    pre_ref,
    mixr_ref,
    mixed_ref,
    back_ref,
    delta_ref,
    sum_ref,
    sum_up_ref,
    slope_ref,
):
    width = up_ref.shape[1]
    bias_mix, bias_down = vec_ref[0:1], vec_ref[1:2]
    gain_one, shift_one = vec_ref[2:3], vec_ref[3:4]
    gain_two, shift_two = vec_ref[4:5], vec_ref[5:6]

    @pl.when(pl.program_id(0) == 0)
    def _():
        sum_ref[...] = jnp.zeros_like(sum_ref)
        sum_up_ref[...] = jnp.zeros_like(sum_up_ref)

    attended = att_ref[...]
    mixed = plain_product(attended, mix_ref[...]) + bias_mix + tok_ref[...].astype(jnp.float32)
    unit_one, rate_one = normalised(mixed)
    hidden = unit_one * gain_one + shift_one
    hidden_rounded = hidden.astype(jnp.bfloat16)
    hid_ref[...] = hidden_rounded
    down_sum = bias_down + hidden
    for f in range(0, width, FCHUNK):
        up_sum = plain_product(hidden_rounded, up_ref[:, f : f + FCHUNK]) + (
            bias_up_ref[0:1, f : f + FCHUNK]
        )
        active, slope = gelu_terms(up_sum)
        active = active.astype(jnp.bfloat16)
        act_ref[:, f : f + FCHUNK] = active
        slope_ref[:, f : f + FCHUNK] = slope
        down_sum = down_sum + plain_product(active, down_ref[f : f + FCHUNK, :])
    unit_two, rate_two = normalised(down_sum)
    out_ref[...] = (unit_two * gain_two + shift_two).astype(jnp.bfloat16)
    cot = cot_ref[...].astype(jnp.float32)
    back_pre = norm_back(cot * gain_two, unit_two, rate_two)
    pre_rounded = back_pre.astype(jnp.bfloat16)
    pre_ref[...] = pre_rounded
    sum_ref[4] += row_sums(cot * unit_two)
    sum_ref[5] += row_sums(cot)
    sum_ref[1] += row_sums(back_pre)
    back_hidden = back_pre
    for f in range(0, width, FCHUNK):
        back_up = back_product(pre_rounded, down_ref[f : f + FCHUNK, :]) * (
            slope_ref[:, f : f + FCHUNK]
        )
        sum_up_ref[:, f : f + FCHUNK] += row_sums(back_up)
        up_rounded = back_up.astype(jnp.bfloat16)
        upr_ref[:, f : f + FCHUNK] = up_rounded
        back_hidden = back_hidden + back_product(up_rounded, up_ref[:, f : f + FCHUNK])
    sum_ref[2] += row_sums(back_hidden * unit_one)
    sum_ref[3] += row_sums(back_hidden)
    back_mixed = norm_back(back_hidden * gain_one, unit_one, rate_one)
    sum_ref[0] += row_sums(back_mixed)
    mixed_ref[...] = back_mixed
    mixed_rounded = back_mixed.astype(jnp.bfloat16)
    mixr_ref[...] = mixed_rounded
    back = back_product(mixed_rounded, mix_ref[...]).astype(jnp.bfloat16)
    back = jnp.where(live_ref[...] > 0.5, back, jnp.zeros_like(back))
    back_ref[:, : back.shape[1]] = back
    terms = back.astype(jnp.float32) * attended.astype(jnp.float32)
    high = terms.astype(jnp.bfloat16)
    low = (terms - high.astype(jnp.float32)).astype(jnp.bfloat16)
    delta = plain_product(high, spread_ref[...]) + plain_product(low, spread_ref[...])
    delta_ref[...] = delta
    lane = lax.broadcasted_iota(jnp.int32, delta.shape, 1)
    term = lane % TERMS
    whole = jnp.where(term < 3, lse_ref[...], delta)
    first = whole.astype(jnp.bfloat16)
    rest = whole - first.astype(jnp.float32)
    second = rest.astype(jnp.bfloat16)
    third = (rest - second.astype(jnp.float32)).astype(jnp.bfloat16)
    picked = jnp.where(
        (term == 0) | (term == 3),
        first.astype(jnp.float32),
        jnp.where((term == 2), third.astype(jnp.float32), second.astype(jnp.float32)),
    )
    picked = jnp.where(lane < TERMS * HEADS, picked, 0.0)
    back_ref[:, back.shape[1] :] = picked.astype(jnp.bfloat16)


def chain_call(att, tok, cot, live, lse, mix, up, down, vectors, bias_up):
    rows, width = tok.shape
    wide = up.shape[1]
    head_of = jnp.arange(width, dtype=jnp.int32)[:, None] // HD
    spread = (head_of == jnp.arange(2 * HD, dtype=jnp.int32)[None, :] // TERMS).astype(jnp.bfloat16)

    def tile(columns):
        return pl.BlockSpec((RTILE, columns), lambda i: (i, 0))

    def fixed(*shape):
        return pl.BlockSpec(shape, lambda i: (0,) * len(shape))

    bf16, f32 = jnp.bfloat16, jnp.float32
    return pl.pallas_call(
        chain_kernel,
        grid=(rows // RTILE,),
        in_specs=[
            tile(width),
            tile(width),
            tile(width),
            tile(1),
            tile(2 * HD),
            fixed(*mix.shape),
            fixed(*up.shape),
            fixed(*down.shape),
            fixed(*vectors.shape),
            fixed(*bias_up.shape),
            fixed(*spread.shape),
        ],
        out_specs=[
            tile(width),
            tile(wide),
            tile(wide),
            tile(width),
            tile(width),
            tile(width),
            tile(width),
            tile(width + 2 * HD),
            tile(2 * HD),
            fixed(6, 8, width),
            fixed(8, wide),
        ],
        out_shape=[
            jax.ShapeDtypeStruct((rows, width), bf16),
            jax.ShapeDtypeStruct((rows, wide), bf16),
            jax.ShapeDtypeStruct((rows, wide), bf16),
            jax.ShapeDtypeStruct((rows, width), bf16),
            jax.ShapeDtypeStruct((rows, width), bf16),
            jax.ShapeDtypeStruct((rows, width), bf16),
            jax.ShapeDtypeStruct((rows, width), f32),
            jax.ShapeDtypeStruct((rows, width + 2 * HD), bf16),
            jax.ShapeDtypeStruct((rows, 2 * HD), f32),
            jax.ShapeDtypeStruct((6, 8, width), f32),
            jax.ShapeDtypeStruct((8, wide), f32),
        ],
        scratch_shapes=[pltpu.VMEM((RTILE, wide), f32)],
        cost_estimate=work(44),
        compiler_params=pltpu.CompilerParams(vmem_limit_bytes=VMEM_LIMIT),
    )(att, tok, cot, live, lse, mix, up, down, vectors, bias_up, spread)


def weight_kernel(n_dp, core_ref, act, pre, hid, upr, att, mixr, small, *refs):
    send, keep, tmp = refs[-3:]
    step = pl.program_id(0)
    core = core_ref[0]
    pieces = FF // D
    down_rows = FF // n_dp
    part_rows = D // n_dp

    def put(x, row, rows, begin):
        mine = pl.multiple_of(begin + core * rows, 16)
        other = pl.multiple_of(begin + (1 - core) * rows, 16)
        keep[pl.ds(x, 1), pl.ds(row, rows), :] = tmp[pl.ds(mine, rows), :][None]
        send[pl.ds(x, 1), pl.ds(row, rows), :] = tmp[pl.ds(other, rows), :][None]

    @pl.when(step < pieces)
    def _():
        tmp[...] = outer_sum(act[...], pre[...]).astype(jnp.bfloat16)
        per = D // down_rows
        for b in range(per):
            block = step * per + b
            x = block // 2
            rows = tmp[b * down_rows : (b + 1) * down_rows, :]

            @pl.when(lax.rem(block, 2) == core)
            def _():
                keep[pl.ds(x, 1), 0:down_rows, :] = rows[None]

            @pl.when(lax.rem(block, 2) != core)
            def _():
                send[pl.ds(x, 1), 0:down_rows, :] = rows[None]

    @pl.when((step >= pieces) & (step < 2 * pieces))
    def _():
        tmp[...] = outer_sum(hid[...], upr[...]).astype(jnp.bfloat16)
        row = pl.multiple_of(down_rows + (step - pieces) * part_rows, 16)
        for x in range(n_dp // 2):
            put(x, row, part_rows, 2 * x * part_rows)

    @pl.when(step == 2 * pieces)
    def _():
        tmp[...] = outer_sum(att[...], mixr[...]).astype(jnp.bfloat16)
        row = down_rows + pieces * part_rows
        for x in range(n_dp // 2):
            put(x, row, part_rows, 2 * x * part_rows)
            last = row + part_rows
            rows = keep.shape[1] - last
            keep[x, last:, :] = small[pl.ds(2 * x + core, 1), :, :][0]
            send[x, last:, :] = small[pl.ds(2 * x + 1 - core, 1), :, :][0]


def weight_call(n_dp, core, act, pre, hid, upr, att, mixr, small, *needs):
    rows = act.shape[0]
    pieces = FF // D
    out_rows = FF // n_dp + (pieces + 1) * (D // n_dp) + small.shape[1]

    def fixed(*shape):
        return pl.BlockSpec(shape, lambda i, c: (0,) * len(shape))

    def stepped(first):
        return pl.BlockSpec((rows, D), lambda i, c: (0, jnp.clip(i - first, 0, pieces - 1)))

    shape = (n_dp // 2, out_rows, D)
    return pl.pallas_call(
        functools.partial(weight_kernel, n_dp),
        out_shape=[jax.ShapeDtypeStruct(shape, jnp.bfloat16)] * 2,
        grid_spec=pltpu.PrefetchScalarGridSpec(
            num_scalar_prefetch=1,
            grid=(2 * pieces + 1,),
            in_specs=[
                stepped(0),
                fixed(rows, D),
                fixed(rows, D),
                stepped(pieces),
                fixed(rows, D),
                fixed(rows, D),
                fixed(*small.shape),
            ]
            + [UNREAD] * len(needs),
            out_specs=[fixed(*shape)] * 2,
            scratch_shapes=[pltpu.VMEM((D, D), jnp.bfloat16)],
        ),
        cost_estimate=work(22),
        compiler_params=pltpu.CompilerParams(vmem_limit_bytes=VMEM_LIMIT),
    )(core, act, pre, hid, upr, att, mixr, small, *needs)


def outer_kernel(n_dp, core_ref, tokens, columns, *refs):
    send, keep, tmp = refs[-3:]
    core = core_ref[0]
    rows = tokens.shape[1] // n_dp
    tmp[...] = outer_sum(tokens[...], columns[...]).astype(tmp.dtype)
    for x in range(n_dp // 2):
        mine = pl.multiple_of((2 * x + core) * rows, 16)
        other = pl.multiple_of((2 * x + 1 - core) * rows, 16)
        keep[x] = tmp[pl.ds(mine, rows), :]
        send[x] = tmp[pl.ds(other, rows), :]


def outer_split(n_dp, core, tokens, columns, first, block, *needs):
    rows, depth = tokens.shape
    steps = columns.shape[1] // block - first
    shape = (n_dp // 2, depth // n_dp, block * steps)
    out = pl.BlockSpec(shape[:2] + (block,), lambda i, c: (0, 0, i))
    return pl.pallas_call(
        functools.partial(outer_kernel, n_dp),
        out_shape=[jax.ShapeDtypeStruct(shape, jnp.bfloat16)] * 2,
        grid_spec=pltpu.PrefetchScalarGridSpec(
            num_scalar_prefetch=1,
            grid=(steps,),
            in_specs=[
                pl.BlockSpec((rows, depth), lambda i, c: (0, 0)),
                pl.BlockSpec((rows, block), lambda i, c: (0, first + i)),
            ]
            + [UNREAD] * len(needs),
            out_specs=[out, out],
            scratch_shapes=[pltpu.VMEM((depth, block), jnp.bfloat16)],
        ),
        cost_estimate=work(4),
        compiler_params=plain_params(),
    )(core, tokens, columns, *needs)


def swap(value, axis, bit):
    devices = lax.axis_size(axis)
    return lax.ppermute(value, axis, [(i, i ^ bit) for i in range(devices)])


def dp_gather(shard, dp_rank):
    blocks = shard[None]
    bit = lax.axis_size("dp") // 2
    while bit >= 1:
        got = swap(blocks, "dp", bit)
        high = ((dp_rank // bit) % 2) == 1
        first = jnp.where(high, got, blocks)
        second = jnp.where(high, blocks, got)
        blocks = jnp.stack([first, second], axis=1).reshape((-1,) + shard.shape)
        bit //= 2
    return blocks.reshape((-1,) + shard.shape[1:])


def work(microseconds):
    return pl.CostEstimate(
        flops=int(microseconds * 0.4e9), transcendentals=0, bytes_accessed=1 << 20
    )


def row_tile(rows, limit=512):
    for size in range(min(rows, limit), 15, -1):
        if rows % size == 0 and size % 16 == 0:
            return size
    return rows


def plain_params():
    return pltpu.CompilerParams(vmem_limit_bytes=VMEM_LIMIT)


def split_add_kernel(which, keep_mine, got_mine, keep_other, got_other, *refs):
    mine, other = refs[-2:]
    mine[...] = (keep_mine[...].astype(jnp.float32) + got_mine[...].astype(jnp.float32)).astype(
        mine.dtype
    )
    other[...] = (keep_other[...].astype(jnp.float32) + got_other[...].astype(jnp.float32)).astype(
        other.dtype
    )


def split_add(keep, got, which, *needs):
    blocks, rows, columns = keep.shape
    tile = row_tile(rows)

    def spec(flip):
        def place(b, i, w):
            bit = 1 - w[0] if flip else w[0]
            return 2 * b + bit, i, 0

        return pl.BlockSpec((1, tile, columns), place)

    out = pl.BlockSpec((1, tile, columns), lambda b, i, w: (b, i, 0))
    shape = jax.ShapeDtypeStruct((blocks // 2, rows, columns), keep.dtype)
    return pl.pallas_call(
        split_add_kernel,
        out_shape=[shape, shape],
        grid_spec=pltpu.PrefetchScalarGridSpec(
            num_scalar_prefetch=1,
            grid=(blocks // 2, rows // tile),
            in_specs=[spec(False), spec(False), spec(True), spec(True)] + [UNREAD] * len(needs),
            out_specs=[out, out],
        ),
        cost_estimate=work(4),
        compiler_params=plain_params(),
    )(which, keep, got, keep, got, *needs)


def add_kernel(left, right, *refs):
    out = refs[-1]
    out[...] = (left[0].astype(jnp.float32) + right[0].astype(jnp.float32)).astype(out.dtype)


def add_blocks(left, right, *needs):
    _, rows, columns = left.shape
    tile = row_tile(rows)
    spec = pl.BlockSpec((1, tile, columns), lambda i: (0, i, 0))
    return pl.pallas_call(
        add_kernel,
        grid=(rows // tile,),
        in_specs=[spec, spec] + [UNREAD] * len(needs),
        out_specs=pl.BlockSpec((tile, columns), lambda i: (i, 0)),
        cost_estimate=work(3),
        out_shape=jax.ShapeDtypeStruct((rows, columns), left.dtype),
        compiler_params=plain_params(),
    )(left, right, *needs)


def pieces_kernel(pieces, *refs):
    out = refs[-1]
    total = pieces[0].astype(jnp.float32)
    for i in range(1, pieces.shape[0]):
        total = total + pieces[i].astype(jnp.float32)
    total = total.astype(out.dtype)
    for i in range(out.shape[0]):
        out[i] = total


def summed_copies(pieces, copies, *needs):
    _, rows, columns = pieces.shape
    return pl.pallas_call(
        pieces_kernel,
        in_specs=[pl.BlockSpec(memory_space=pltpu.VMEM)] + [UNREAD] * len(needs),
        out_specs=pl.BlockSpec(memory_space=pltpu.VMEM),
        out_shape=jax.ShapeDtypeStruct((copies, rows, columns), pieces.dtype),
        cost_estimate=work(2),
        compiler_params=plain_params(),
    )(pieces, *needs)


def gate_kernel(value, *refs):
    refs[-1][...] = value[...]


def gated(value, *needs):
    return pl.pallas_call(
        gate_kernel,
        in_specs=[pl.BlockSpec(memory_space=pltpu.VMEM)] + [UNREAD] * len(needs),
        out_specs=pl.BlockSpec(memory_space=pltpu.VMEM),
        out_shape=jax.ShapeDtypeStruct(value.shape, value.dtype),
        cost_estimate=work(1),
        compiler_params=plain_params(),
    )(value, *needs)


def cluster_ids(group_order, own_start, span):
    padded = jnp.pad(group_order, ((0, 0), (HALO, HALO)), constant_values=-(1 << 24))
    wanted = lax.dynamic_slice_in_dim(padded, own_start, span, 1) - (own_start - HALO)
    tile_of = wanted >> 7
    lane_of_token = wanted & (CL - 1)
    cluster = (jnp.arange(span, dtype=jnp.int32) >> 7) + 1
    tile_hot = jnp.where(
        tile_of[:, :, None] == jnp.arange(span // CL, dtype=jnp.int32), cluster[None, :, None], 0
    ).astype(jnp.bfloat16)
    lane_hot = (lane_of_token[:, :, None] == jnp.arange(CL, dtype=jnp.int32)).astype(jnp.bfloat16)
    table = jnp.einsum("hpt,hpl->htl", tile_hot, lane_hot, preferred_element_type=jnp.float32)
    return table.reshape(HEADS, span) - 1.0


def on_device(
    tokens,
    input_weight,
    output_weight,
    up_weight,
    down_weight,
    output_bias,
    up_bias,
    down_bias,
    first_gain,
    first_shift,
    second_gain,
    second_shift,
    document_runs,
    document_trim,
    cluster_order,
    cotangent,
):
    bf16, f32 = jnp.bfloat16, jnp.float32
    n_dp = lax.axis_size("dp")
    n_seq = lax.axis_size("seq")
    dp_rank = lax.axis_index("dp")
    seq_rank = lax.axis_index("seq")
    inputs = tokens[0]
    tok_dev = inputs.shape[0]
    tiles = tok_dev // CL
    span = tok_dev + 2 * HALO
    own_start = seq_rank * tok_dev

    token_parts = halo_parts(inputs)
    n_parts = len(token_parts)

    weight_in = lax.all_gather(input_weight, "dp", axis=0, tiled=True)
    weight_up = lax.all_gather(up_weight, "dp", axis=0, tiled=True)
    weight_down = lax.all_gather(down_weight, "dp", axis=0, tiled=True)

    runs = document_runs[0]
    first_cluster = jnp.cumsum(runs) - runs
    own_clusters = seq_rank * tiles + jnp.arange(tiles, dtype=jnp.int32)
    doc_start = jnp.max(
        jnp.where(first_cluster[None, :] <= own_clusters[:, None], first_cluster[None, :], 0), axis=1
    )
    starts = (doc_start - seq_rank * tiles + (MOSTB - 1)).astype(jnp.int32)
    near_left = HALO // CL - tiles
    near = near_left + 2 * tiles * jnp.stack([1 - seq_rank % 2, seq_rank % 2])
    starts = jnp.concatenate([starts, near.astype(jnp.int32)])

    cids = cluster_ids(cluster_order[0], own_start, span)
    positions = own_start - HALO + jnp.arange(span, dtype=jnp.int32)
    live = live_tokens(runs, document_trim[0], positions)
    usable = live[None, :] & (cids >= 0.0)
    key_ids = jnp.where(usable, cids, -1.0).reshape(PAIRS, 2, span)
    query_ids = jnp.where(usable, cids, -2.0).reshape(PAIRS, 2, span)
    own_live = live[HALO : HALO + tok_dev, None].astype(f32)

    own = plain_product(inputs, weight_in).astype(bf16)
    groups = HEADS // PACK
    group_lanes = PACK * HD
    kv_weight = (
        weight_in[:, D:]
        .reshape(D, 2, groups, group_lanes)
        .transpose(0, 2, 1, 3)
        .reshape(D, 2 * D)
    )
    around = project_call(token_parts[:2] + token_parts[3:], weight_in, kv_weight)
    projected = [*around[:2], own, *around[2:]]
    vectors = [
        output_bias,
        down_bias,
        first_gain,
        first_shift,
        second_gain,
        second_shift,
        up_bias,
    ]
    mix_rows = output_weight.shape[0]
    packed = jnp.concatenate(vectors)
    pad_rows = -(-packed.shape[0] // (16 * D)) * 16
    packed = jnp.pad(packed, (0, pad_rows * D - packed.shape[0])).reshape(pad_rows, D)
    mix_shard = gated(jnp.concatenate([output_weight, packed], 0), own)
    mix_all = dp_gather(mix_shard, dp_rank)
    mix_all = mix_all.reshape(n_dp, mix_rows + pad_rows, D)
    weight_mix = mix_all[:, :mix_rows].reshape(D, D)
    small_all = mix_all[:, mix_rows:].reshape(n_dp, -1).astype(f32)
    vec = small_all[:, : 6 * mix_rows].reshape(n_dp, 6, mix_rows).transpose(1, 0, 2).reshape(6, D)
    vec = jnp.pad(vec, ((0, 2), (0, 0)))
    up_part = up_bias.shape[0]
    bias_up = small_all[:, 6 * mix_rows : 6 * mix_rows + up_part].reshape(1, FF)
    bias_up = jnp.pad(bias_up, ((0, 7), (0, 0)))
    heights = [part.shape[0] for part in token_parts]

    groups = HEADS // PACK
    group_lanes = PACK * HD
    group_key_ids = key_ids.reshape(groups, PACK, span)
    group_query_ids = query_ids.reshape(groups, PACK, span)
    group_scratch = pltpu.VMEM((span, group_lanes), bf16)

    def group_parts(third, first):
        return [lane_block(rows, third * groups + first, PACK) for rows in heights]

    steps = tiles // TILES_AT_ONCE
    step_rows = TILES_AT_ONCE * CL

    def of_group(rows, first):
        return pl.BlockSpec((rows, group_lanes), lambda g, t, starts: (0, first + g))

    def ids_of_group():
        return pl.BlockSpec((1, PACK, span), lambda g, t, starts: (g, 0, 0))

    step_block = pl.BlockSpec((step_rows, group_lanes), lambda g, t, starts: (t, g))
    whole_lanes = pl.BlockSpec((tok_dev, 2 * HD), lambda g, t, starts: (0, 0))
    attended, lse, rate, probs = strip_call(
        functools.partial(attend_kernel, tiles, n_parts),
        52,
        (groups, steps),
        [step_block]
        + [of_group(rows, groups) for rows in heights]
        + [of_group(rows, 2 * groups) for rows in heights]
        + [ids_of_group(), ids_of_group()],
        [
            step_block,
            whole_lanes,
            whole_lanes,
            pl.BlockSpec(
                (1, TILES_AT_ONCE, PACK * CL, WINDOW), lambda g, t, starts: (g, t, 0, 0)
            ),
        ],
        [
            jax.ShapeDtypeStruct((tok_dev, D), bf16),
            jax.ShapeDtypeStruct((tok_dev, 2 * HD), f32),
            jax.ShapeDtypeStruct((tok_dev, 2 * HD), f32),
            jax.ShapeDtypeStruct((groups, tiles, PACK * CL, WINDOW), bf16),
        ],
        [group_scratch, group_scratch]
        + [pltpu.VMEM((PACK * CL, WINDOW), f32)] * TILES_AT_ONCE
        + [pltpu.VMEM((PACK * CL, CL), f32)] * TILES_AT_ONCE,
        (starts, own, *projected, *projected, group_query_ids, group_key_ids),
    )

    (
        result,
        active,
        up_rounded,
        hidden_rounded,
        pre_rounded,
        mixed_rounded,
        back_mixed,
        back_own,
        delta,
        sums,
        sums_up,
    ) = chain_call(
        attended,
        inputs,
        cotangent[0],
        own_live,
        lse,
        weight_mix,
        weight_up,
        weight_down,
        vec,
        bias_up,
    )
    back_parts = halo_parts(back_own)

    small = jnp.concatenate(
        [
            jnp.sum(sums, axis=1).reshape(6, n_dp, mix_rows).transpose(1, 0, 2).reshape(n_dp, -1),
            jnp.sum(sums_up, axis=0).reshape(n_dp, -1),
        ],
        axis=1,
    ).astype(bf16)
    unit = 8 * n_seq
    fixed_rows = FF // n_dp + (FF // D + 1) * (D // n_dp)
    small_rows = -(-(fixed_rows + -(-small.shape[1] // D)) // unit) * unit - fixed_rows
    small = jnp.pad(small, ((0, 0), (0, small_rows * D - small.shape[1])))
    small = small.reshape(n_dp, small_rows, D)
    core = (dp_rank % 2).astype(jnp.int32)
    def query_strip(first, *needs):
        buffer = needs[:1] if first > 0 else ()

        def parts(third):
            return [
                pl.BlockSpec(
                    (rows, group_lanes), lambda t, starts: (0, third * groups + first)
                )
                for rows in heights
            ]

        block = pl.BlockSpec((step_rows, group_lanes), lambda t, starts: (t, first))
        lanes = pl.BlockSpec((step_rows, 2 * HD), lambda t, starts: (t, 0))
        in_specs = (
            parts(1)
            + parts(2)
            + [
                block,
                pl.BlockSpec(
                    (1, TILES_AT_ONCE, PACK * CL, WINDOW), lambda t, starts: (first, t, 0, 0)
                ),
                lanes,
                lanes,
            ]
            + [UNREAD] * len(needs)
        )
        return strip_call(
            functools.partial(query_kernel, tiles, n_parts, first * PACK),
            16,
            (steps,),
            in_specs,
            block,
            jax.ShapeDtypeStruct((tok_dev, D), bf16),
            [group_scratch, group_scratch],
            (starts, *projected, *projected, back_own, probs, rate, delta, *needs),
            {len(in_specs) + 1 - len(needs): 0} if buffer else None,
        )

    key_pairs = PACK // 2
    pair_scratch = pltpu.VMEM((span, 4 * HD), bf16)

    def key_strip(first, length, *needs):
        buffer = needs[:1] if first > 0 else ()
        pair = first * key_pairs

        def parts(third):
            return [lane_block(rows, third * PAIRS + pair) for rows in heights]

        in_specs = (
            [lane_block(tok_dev, PAIRS + pair), lane_block(tok_dev, 2 * PAIRS + pair)]
            + parts(0)
            + parts(0)
            + [fixed_lanes(rows, PAIRS) for rows in heights]
            + [row_block(span, pair), row_block(span, pair)]
            + [UNREAD] * len(needs)
        )
        return strip_call(
            functools.partial(key_kernel, tiles, n_parts, pair),
            length,
            (key_pairs,),
            in_specs,
            pl.BlockSpec((tok_dev, 2 * group_lanes), lambda step, starts: (0, first)),
            jax.ShapeDtypeStruct((tok_dev, 2 * D), bf16),
            [pair_scratch, pair_scratch],
            (
                starts,
                own,
                own,
                *projected,
                *back_parts,
                *back_parts,
                query_ids,
                key_ids,
                *needs,
            ),
            {len(in_specs) + 1 - len(needs): 0} if buffer else None,
        )

    def scatter(share):
        rows, columns = share.shape
        return lax.all_to_all(
            share.reshape(n_seq, rows // n_seq, columns), "seq", split_axis=0, concat_axis=0
        )

    def everyone(copies):
        got = lax.all_to_all(copies, "seq", split_axis=0, concat_axis=0)
        return got.reshape(-1, copies.shape[-1])

    def first_split(keep, got, *needs):
        bit = 2
        while True:
            which = ((dp_rank // bit) % 2).astype(jnp.int32).reshape(1)
            mine, other = split_add(keep, got, which, *needs)
            got = swap(other, "dp", bit)
            if mine.shape[0] == 1:
                return mine, got
            keep, bit, needs = mine, bit * 2, ()

    def core_split(grad):
        rows, columns = grad.shape
        blocks = grad.astype(bf16).reshape(n_dp // 2, 2, rows // n_dp, columns)
        return (
            lax.dynamic_index_in_dim(blocks, 1 - core, 1, keepdims=False),
            lax.dynamic_index_in_dim(blocks, core, 1, keepdims=False),
        )

    send, keep = weight_call(
        n_dp,
        core.reshape(1),
        active,
        pre_rounded,
        hidden_rounded,
        up_rounded,
        attended,
        mixed_rounded,
        small,
    )
    core_got = swap(send, "dp", 1)
    mine, x_got = first_split(keep, core_got)
    back_q = query_strip(0, mine)
    back_q = query_strip(1, back_q)
    back_q = query_strip(2, back_q, back_parts[1], back_parts[3])
    share = add_blocks(mine, x_got, back_q)
    back_kv = key_strip(0, 27, back_q, share)
    pieces = scatter(share)
    cut = 2 * group_lanes
    early_cols = jnp.concatenate([back_q, back_kv[:, :cut]], axis=1)
    early_send, early_keep = core_split(outer_sum(inputs, early_cols))
    early_core = swap(early_send, "dp", 1)
    back_kv = key_strip(1, 27, back_kv, early_send)
    early_mine, early_got = first_split(early_keep, early_core, back_kv)
    copies = summed_copies(pieces, 1, back_kv)
    back_kv = key_strip(2, 2, back_kv, early_mine, copies)
    early_share = add_blocks(early_mine, early_got, back_kv)
    all_sums = lax.all_gather(copies[0], "seq", axis=0, tiled=True)
    late_send, late_keep = outer_split(
        n_dp, core.reshape(1), inputs, back_kv, 1, cut, early_share
    )
    late_mine, late_got = first_split(late_keep, swap(late_send, "dp", 1))
    late_share = add_blocks(late_mine, late_got, all_sums)
    in_share = jnp.concatenate([early_share, late_share], axis=1)
    in_all = everyone(summed_copies(scatter(in_share), n_seq))

    input_grad = (
        back_mixed + back_product(back_q, weight_in[:, :D]) + back_product(back_kv, kv_weight)
    )
    kv_all = in_all[:, D:].reshape(-1, groups, 2, group_lanes).transpose(0, 2, 1, 3)
    grad_in_total = jnp.concatenate([in_all[:, :D], kv_all.reshape(-1, 2 * D)], axis=1).astype(f32)
    down_rows = FF // n_dp
    part_rows = D // n_dp
    grad_down = all_sums[:down_rows].astype(f32)
    grad_up = (
        all_sums[down_rows : down_rows + (FF // D) * part_rows]
        .reshape(FF // D, part_rows, D)
        .transpose(1, 0, 2)
        .reshape(part_rows, FF)
        .astype(f32)
    )
    at = down_rows + (FF // D) * part_rows
    grad_mix = all_sums[at : at + part_rows].astype(f32)
    flat = all_sums[at + part_rows :].reshape(-1).astype(f32)
    vectors_out = [flat[i * part_rows : (i + 1) * part_rows] for i in range(6)]
    bias_up_out = flat[6 * part_rows : 6 * part_rows + down_rows]
    return (
        result[None],
        input_grad[None],
        grad_in_total,
        grad_mix,
        grad_up,
        grad_down,
        vectors_out[0],
        bias_up_out,
        vectors_out[1],
        *vectors_out[2:],
    )


def solution(mesh):
    placed = (
        P("dp", "seq", None),
        P("dp", None),
        P("dp", None),
        P("dp", None),
        P("dp", None),
        P("dp"),
        P("dp"),
        P("dp"),
        P("dp"),
        P("dp"),
        P("dp"),
        P("dp"),
        P("dp", None),
        P("dp", None),
        P("dp", None, None),
        P("dp", "seq", None),
    )
    return jax.shard_map(
        on_device,
        mesh=mesh,
        in_specs=placed,
        out_specs=(
            P("dp", "seq", None),
            P("dp", "seq", None),
            P("dp", None),
            P("dp", None),
            P("dp", None),
            P("dp", None),
            P("dp"),
            P("dp"),
            P("dp"),
            P("dp"),
            P("dp"),
            P("dp"),
            P("dp"),
        ),
        check_vma=False,
    )
```

```python
import functools

import jax
import jax.numpy as jnp
from jax import lax
from jax.experimental import pallas as pl
from jax.experimental.pallas import tpu as pltpu
from jax.sharding import PartitionSpec as P

D = 768
HEADS = 12
HD = 64
CL = 128
MOSTB = 16
PAIRS = HEADS // 2
WINDOW = MOSTB * CL
HALO = (MOSTB - 1) * CL
CHUNK = 512
KCHUNK = 512
TILES_AT_ONCE = 2
PACK = 4
NEG = -1e30
TERMS = 5
FF = 3072
RTILE = 256
FCHUNK = 768
SCALE2 = HD ** (-0.5) * 1.4426950408889634

EPSILON = 1e-05


def shifted(value, axis, by):
    devices = lax.axis_size(axis)
    pairs = [(i, i + by) for i in range(devices) if 0 <= i + by < devices]
    return lax.ppermute(value, axis, pairs)


def halo_parts(value):
    own = value.shape[0]
    far = HALO - own
    devices = lax.axis_size("seq")
    assert 0 < far <= own and devices % 2 == 0
    partner = lax.ppermute(value, "seq", [(i, i ^ 1) for i in range(devices)])
    pairs = [(i, i - 1 if i % 2 == 0 else i + 1) for i in range(devices)]
    other = lax.ppermute(value, "seq", [(i, k) for i, k in pairs if 0 <= k < devices])
    before = shifted(value[own - far :], "seq", 2)
    following = shifted(value[:far], "seq", -2)
    return [before, partner, value, other, following]


def places(starts, tiles, parts):
    far, own = parts[0].shape[0], parts[2].shape[0]
    return [
        0,
        pl.multiple_of(starts[tiles] * CL, CL),
        far + own,
        pl.multiple_of(starts[tiles + 1] * CL, CL),
        far + 3 * own,
    ]


def live_tokens(runs, trim, positions):
    ends = jnp.cumsum(runs) * CL
    starts = ends - runs * CL
    lengths = runs * CL - trim
    inside = (positions[..., None] >= starts) & (positions[..., None] < starts + lengths)
    return jnp.any(inside, axis=-1)


def outer_sum(left, right):
    return lax.dot_general(
        left, right, (((0,), (0,)), ((), ())), preferred_element_type=jnp.float32
    )


def back_product(left, right):
    return lax.dot_general(
        left, right, (((1,), (1,)), ((), ())), preferred_element_type=jnp.float32
    )


def plain_product(left, right):
    return jnp.dot(left, right, preferred_element_type=jnp.float32)


def stacked(tile):
    lane = lax.broadcasted_iota(jnp.int32, tile.shape, 1)
    zero = jnp.zeros_like(tile)
    heads = tile.shape[1] // HD
    return jnp.concatenate(
        [
            jnp.where((lane >= h * HD) & (lane < (h + 1) * HD), tile, zero)
            for h in range(heads)
        ],
        axis=0,
    )


def unstacked(stack):
    heads = stack.shape[1] // HD
    lane = lax.broadcasted_iota(jnp.int32, (CL, heads * HD), 1)
    result = stack[:CL]
    for h in range(1, heads):
        result = jnp.where(lane >= h * HD, stack[h * CL : (h + 1) * CL], result)
    return result


def as_column(row):
    return jnp.broadcast_to(row, (CL, CL)).T


def lane_of(tile, lane):
    lanes = lax.broadcasted_iota(jnp.int32, tile.shape, 1)
    return jnp.sum(jnp.where(lanes == lane, tile, 0.0), axis=1, keepdims=True)


def masked(scores, cols, row_ref, begin):
    parts = []
    wide = scores.shape[1]
    for half, one in enumerate(cols):
        row = row_ref[0, half : half + 1, pl.ds(begin, wide)]
        block = scores[half * CL : (half + 1) * CL]
        col = jnp.concatenate([one] * (wide // CL), axis=1)
        parts.append(jnp.where(col == row, block, NEG))
    return jnp.concatenate(parts, axis=0)


def assemble(parts, offsets, whole):
    for part, at in zip(parts, offsets):
        whole[pl.ds(at, part.shape[0]), :] = part[...]


def ahead(steps, produce, consume):
    held = produce(*steps[0])
    for i, step in enumerate(steps):
        following = produce(*steps[i + 1]) if i + 1 < len(steps) else None
        consume(*step, held)
        held = following


def attend_kernel(tiles, n_parts, starts, q_ref, *refs):
    k_parts, refs = refs[:n_parts], refs[n_parts:]
    v_parts, refs = refs[:n_parts], refs[n_parts:]
    qid_ref, kid_ref, out_ref, lse_ref, rate_ref, p_ref, k_ref, v_ref, *slots = refs
    s_refs, top_refs = slots[:TILES_AT_ONCE], slots[TILES_AT_ONCE:]
    group, step = pl.program_id(0), pl.program_id(1)
    heads = q_ref.shape[1] // HD
    chunks = WINDOW // CHUNK

    @pl.when(step == 0)
    def _():
        offsets = places(starts, tiles, k_parts)
        assemble(k_parts, offsets, k_ref)
        assemble(v_parts, offsets, v_ref)

    @pl.when((group == 0) & (step == 0))
    def _():
        lse_ref[...] = jnp.zeros_like(lse_ref)
        rate_ref[...] = jnp.zeros_like(rate_ref)

    def first_half(slot):
        tile = TILES_AT_ONCE * step + slot
        own = pl.multiple_of(HALO + tile * CL, CL)
        return dict(
            begin=pl.multiple_of(starts[tile] * CL, CL),
            query=stacked(q_ref[slot * CL : (slot + 1) * CL, :]),
            cols=[
                as_column(qid_ref[0, half : half + 1, pl.ds(own, CL)]) for half in range(heads)
            ],
        )

    def score(state, slot, j):
        at = pl.multiple_of(state["begin"] + j * CHUNK, CL)
        scores = back_product(state["query"], k_ref[pl.ds(at, CHUNK), :])
        scores = masked(scores, state["cols"], kid_ref, at)
        s_refs[slot][:, j * CHUNK : (j + 1) * CHUNK] = scores
        top = scores[:, :CL]
        for i in range(1, CHUNK // CL):
            top = jnp.maximum(top, scores[:, i * CL : (i + 1) * CL])
        if j > 0:
            top = jnp.maximum(top, top_refs[slot][...])
        top_refs[slot][...] = top

    states = [first_half(0)]
    for j in range(chunks):
        score(states[0], 0, j)
    for slot in range(TILES_AT_ONCE):
        if slot + 1 < TILES_AT_ONCE:
            states.append(first_half(slot + 1))
        state = states[slot]
        peak = jnp.max(top_refs[slot][...], axis=1, keepdims=True)
        total = jnp.zeros((heads * CL, CL), jnp.float32)
        result = jnp.zeros((heads * CL, heads * HD), jnp.float32)
        for j in range(chunks):
            if slot + 1 < TILES_AT_ONCE:
                score(states[slot + 1], slot + 1, j)
            at = pl.multiple_of(state["begin"] + j * CHUNK, CL)
            columns = slice(j * CHUNK, (j + 1) * CHUNK)
            weights = jnp.exp2((s_refs[slot][:, columns] - peak) * SCALE2)
            for i in range(CHUNK // CL):
                total = total + weights[:, i * CL : (i + 1) * CL]
            p_ref[0, slot, :, columns] = weights.astype(jnp.bfloat16)
            result = result + plain_product(
                p_ref[0, slot, :, columns], v_ref[pl.ds(at, CHUNK), :]
            )
        total = jnp.sum(total, axis=1, keepdims=True)
        rate = 1.0 / total
        result = result * rate
        lse = peak + jnp.log(total) * HD**0.5
        live = (state["cols"][0] >= 0.0).astype(jnp.float32)
        live = jnp.concatenate([live] * (heads * HD // CL), axis=1)
        rows = slice(slot * CL, (slot + 1) * CL)
        out_ref[rows, :] = (unstacked(result) * live).astype(jnp.bfloat16)
        here = pl.ds(pl.multiple_of((TILES_AT_ONCE * step + slot) * CL, CL), CL)
        lane = lax.broadcasted_iota(jnp.int32, (CL, CL), 1)
        kept, kept_rate = lse_ref[here, :], rate_ref[here, :]
        for half in range(heads):
            first = (heads * group + half) * TERMS
            inside = (lane >= first) & (lane < first + TERMS)
            part = slice(half * CL, (half + 1) * CL)
            kept = jnp.where(inside, lse[part], kept)
            kept_rate = jnp.where(inside, rate[part], kept_rate)
        lse_ref[here, :] = kept
        rate_ref[here, :] = kept_rate


def query_kernel(tiles, n_parts, first_head, starts, *refs):
    k_parts, refs = refs[:n_parts], refs[n_parts:]
    v_parts, refs = refs[:n_parts], refs[n_parts:]
    g_ref, p_ref, rate_ref, delta_ref = refs[:4]
    out_ref, k_ref, v_ref = refs[-3:]
    step = pl.program_id(0)
    heads = g_ref.shape[1] // HD
    chunks = WINDOW // CHUNK

    @pl.when(step == 0)
    def _():
        offsets = places(starts, tiles, k_parts)
        assemble(k_parts, offsets, k_ref)
        assemble(v_parts, offsets, v_ref)

    states = {}

    def state_of(slot):
        if slot not in states:
            rows = slice(slot * CL, (slot + 1) * CL)
            columns = [
                jnp.concatenate(
                    [lane_of(ref[rows, :], (first_head + half) * TERMS) for half in range(heads)],
                    axis=0,
                )
                for ref in (delta_ref, rate_ref)
            ]
            states[slot] = dict(
                begin=pl.multiple_of(starts[TILES_AT_ONCE * step + slot] * CL, CL),
                back=stacked(g_ref[rows, :]),
                delta=columns[0],
                rate=columns[1],
                result=jnp.zeros((heads * CL, heads * HD), jnp.float32),
            )
        return states[slot]

    def produce(slot, j):
        state = state_of(slot)
        at = pl.multiple_of(state["begin"] + j * CHUNK, CL)
        return back_product(state["back"], v_ref[pl.ds(at, CHUNK), :])

    def consume(slot, j, back_probs):
        state = state_of(slot)
        at = pl.multiple_of(state["begin"] + j * CHUNK, CL)
        weights = p_ref[0, slot, :, j * CHUNK : (j + 1) * CHUNK].astype(jnp.float32)
        back_scores = weights * (back_probs - state["delta"])
        state["result"] = state["result"] + plain_product(
            back_scores.astype(jnp.bfloat16), k_ref[pl.ds(at, CHUNK), :]
        )
        if j == chunks - 1:
            out_ref[slot * CL : (slot + 1) * CL, :] = unstacked(
                state["result"] * (state["rate"] * HD ** (-0.5))
            ).astype(jnp.bfloat16)

    ahead(
        [(slot, j) for slot in range(TILES_AT_ONCE) for j in range(chunks)], produce, consume
    )


def key_kernel(tiles, n_parts, first_pair, starts, k_ref, v_ref, *refs):
    q_parts, refs = refs[:n_parts], refs[n_parts:]
    g_parts, refs = refs[:n_parts], refs[n_parts:]
    a_parts, refs = refs[:n_parts], refs[n_parts:]
    qid_ref, kid_ref = refs[:2]
    out_ref, q_ref, g_ref = refs[-3:]
    pair = first_pair + pl.program_id(0)
    offsets = places(starts, tiles, q_parts)
    for at, q_part, g_part, a_part in zip(offsets, q_parts, g_parts, a_parts):
        rows = pl.ds(at, q_part.shape[0])
        q_ref[rows, : 2 * HD] = q_part[...]
        q_ref[rows, 2 * HD :] = a_part[...]
        g_ref[rows, : 2 * HD] = g_part[...]
        g_ref[rows, 2 * HD :] = a_part[...]

    lane = lax.broadcasted_iota(jnp.int32, (CL, CL), 1)
    lse_pick, delta_pick = [], []
    for half in range(2):
        first = (2 * pair + half) * TERMS
        lse_pick.append(jnp.where((lane >= first) & (lane < first + 3), -1.0, 0.0))
        delta_pick.append(jnp.where((lane >= first + 3) & (lane < first + TERMS), -1.0, 0.0))
    lse_pick = jnp.concatenate(lse_pick, axis=0).astype(jnp.bfloat16)
    delta_pick = jnp.concatenate(delta_pick, axis=0).astype(jnp.bfloat16)

    def some_tiles(step, carry):
        states = {}

        def state_of(slot):
            if slot not in states:
                tile = TILES_AT_ONCE * step + slot
                own = pl.multiple_of(HALO + tile * CL, CL)
                here = pl.multiple_of(tile * CL, CL)
                states[slot] = dict(
                    begin=pl.multiple_of(starts[tile] * CL, CL),
                    here=here,
                    keys=jnp.concatenate([stacked(k_ref[pl.ds(here, CL), :]), lse_pick], axis=1),
                    values=jnp.concatenate(
                        [stacked(v_ref[pl.ds(here, CL), :]), delta_pick], axis=1
                    ),
                    cols=[
                        as_column(kid_ref[0, half : half + 1, pl.ds(own, CL)]) for half in range(2)
                    ],
                    key_sum=jnp.zeros((2 * CL, 2 * HD), jnp.float32),
                    value_sum=jnp.zeros((2 * CL, 2 * HD), jnp.float32),
                )
            return states[slot]

        def produce(slot, j):
            state = state_of(slot)
            at = pl.multiple_of(state["begin"] + j * KCHUNK, CL)
            scores = back_product(state["keys"], q_ref[pl.ds(at, KCHUNK), :])
            return scores, back_product(state["values"], g_ref[pl.ds(at, KCHUNK), :])

        def consume(slot, j, held):
            state = state_of(slot)
            at = pl.multiple_of(state["begin"] + j * KCHUNK, CL)
            scores, back_probs = held
            probs = jnp.exp2(masked(scores * SCALE2, state["cols"], qid_ref, at))
            back_scores = probs * back_probs
            state["value_sum"] = state["value_sum"] + plain_product(
                probs.astype(jnp.bfloat16), g_ref[pl.ds(at, KCHUNK), : 2 * HD]
            )
            state["key_sum"] = state["key_sum"] + plain_product(
                back_scores.astype(jnp.bfloat16), q_ref[pl.ds(at, KCHUNK), : 2 * HD]
            )
            if j == WINDOW // KCHUNK - 1:
                rows = pl.ds(state["here"], CL)
                out_ref[rows, : 2 * HD] = (
                    unstacked(state["key_sum"]) * HD ** (-0.5)
                ).astype(jnp.bfloat16)
                out_ref[rows, 2 * HD :] = unstacked(state["value_sum"]).astype(jnp.bfloat16)

        ahead(
            [(slot, j) for slot in range(TILES_AT_ONCE) for j in range(WINDOW // KCHUNK)],
            produce,
            consume,
        )
        return carry

    lax.fori_loop(0, tiles // TILES_AT_ONCE, some_tiles, 0)


def lane_block(rows, first, heads=2):
    return pl.BlockSpec((rows, heads * HD), lambda pair, starts: (0, first + pair))


def fixed_lanes(rows, block):
    return pl.BlockSpec((rows, 2 * HD), lambda pair, starts: (0, block))


def row_block(columns, first, heads=2):
    return pl.BlockSpec((1, heads, columns), lambda pair, starts: (first + pair, 0, 0))


UNREAD = pl.BlockSpec(memory_space=pl.ANY)


VMEM_LIMIT = 60 * 1024 * 1024


def strip_call(
    kernel, length, grid, in_specs, out_specs, out_shape, scratch, args, aliases=None
):
    return pl.pallas_call(
        kernel,
        out_shape=out_shape,
        grid_spec=pltpu.PrefetchScalarGridSpec(
            num_scalar_prefetch=1,
            grid=grid,
            in_specs=in_specs,
            out_specs=out_specs,
            scratch_shapes=scratch,
        ),
        input_output_aliases=aliases or {},
        cost_estimate=work(length),
        compiler_params=pltpu.CompilerParams(vmem_limit_bytes=VMEM_LIMIT),
    )(*args)


def project_kernel(parts, weight, *refs):
    for source, target in zip(refs[:parts], refs[-parts:]):
        target[...] = plain_product(source[...], weight[...]).astype(target.dtype)


def project_call(parts, weight, *needs):
    depth, columns = weight.shape
    block = PACK * HD
    return pl.pallas_call(
        functools.partial(project_kernel, len(parts)),
        grid=(columns // block,),
        in_specs=[pl.BlockSpec((depth, block), lambda i: (0, i))]
        + [pl.BlockSpec(part.shape, lambda i: (0, 0)) for part in parts]
        + [UNREAD] * len(needs),
        out_specs=[pl.BlockSpec((part.shape[0], block), lambda i: (0, i)) for part in parts],
        out_shape=[jax.ShapeDtypeStruct((part.shape[0], columns), part.dtype) for part in parts],
        cost_estimate=work(20),
        compiler_params=pltpu.CompilerParams(vmem_limit_bytes=VMEM_LIMIT),
    )(weight, *parts, *needs)


def gelu_terms(value):
    t = 1.0 / (1.0 + (0.3275911 * 0.7071067811865476) * jnp.abs(value))
    bell = jnp.exp2(value * value * (-0.5 * 1.4426950408889634))
    tail = 0.5 * 1.061405429
    for term in (-0.5 * 1.453152027, 0.5 * 1.421413741, -0.5 * 0.284496736, 0.5 * 0.254829592):
        tail = tail * t + term
    tail = tail * t * bell
    cdf = jnp.where(value >= 0.0, 1.0 - tail, tail)
    return value * cdf, cdf + value * (0.3989422804014327 * bell)


def normalised(values):
    mean = jnp.mean(values, axis=-1, keepdims=True)
    centre = values - mean
    rate = lax.rsqrt(jnp.mean(centre * centre, axis=-1, keepdims=True) + EPSILON)
    return centre * rate, rate


def norm_back(scaled, unit, rate):
    first = jnp.mean(scaled, axis=-1, keepdims=True)
    second = jnp.mean(scaled * unit, axis=-1, keepdims=True)
    return rate * (scaled - first - unit * second)


def row_sums(values):
    rows, columns = values.shape
    return jnp.sum(values.reshape(rows // 8, 8, columns), axis=0)


def chain_kernel(
    att_ref,
    tok_ref,
    cot_ref,
    live_ref,
    lse_ref,
    mix_ref,
    up_ref,
    down_ref,
    vec_ref,
    bias_up_ref,
    spread_ref,
    out_ref,
    act_ref,
    upr_ref,
    hid_ref,
    pre_ref,
    mixr_ref,
    mixed_ref,
    back_ref,
    delta_ref,
    sum_ref,
    sum_up_ref,
    slope_ref,
):
    width = up_ref.shape[1]
    bias_mix, bias_down = vec_ref[0:1], vec_ref[1:2]
    gain_one, shift_one = vec_ref[2:3], vec_ref[3:4]
    gain_two, shift_two = vec_ref[4:5], vec_ref[5:6]

    @pl.when(pl.program_id(0) == 0)
    def _():
        sum_ref[...] = jnp.zeros_like(sum_ref)
        sum_up_ref[...] = jnp.zeros_like(sum_up_ref)

    attended = att_ref[...]
    mixed = plain_product(attended, mix_ref[...]) + bias_mix + tok_ref[...].astype(jnp.float32)
    unit_one, rate_one = normalised(mixed)
    hidden = unit_one * gain_one + shift_one
    hidden_rounded = hidden.astype(jnp.bfloat16)
    hid_ref[...] = hidden_rounded
    down_sum = bias_down + hidden
    for f in range(0, width, FCHUNK):
        up_sum = plain_product(hidden_rounded, up_ref[:, f : f + FCHUNK]) + (
            bias_up_ref[0:1, f : f + FCHUNK]
        )
        active, slope = gelu_terms(up_sum)
        active = active.astype(jnp.bfloat16)
        act_ref[:, f : f + FCHUNK] = active
        slope_ref[:, f : f + FCHUNK] = slope
        down_sum = down_sum + plain_product(active, down_ref[f : f + FCHUNK, :])
    unit_two, rate_two = normalised(down_sum)
    out_ref[...] = (unit_two * gain_two + shift_two).astype(jnp.bfloat16)
    cot = cot_ref[...].astype(jnp.float32)
    back_pre = norm_back(cot * gain_two, unit_two, rate_two)
    pre_rounded = back_pre.astype(jnp.bfloat16)
    pre_ref[...] = pre_rounded
    sum_ref[4] += row_sums(cot * unit_two)
    sum_ref[5] += row_sums(cot)
    sum_ref[1] += row_sums(back_pre)
    back_hidden = back_pre
    for f in range(0, width, FCHUNK):
        back_up = back_product(pre_rounded, down_ref[f : f + FCHUNK, :]) * (
            slope_ref[:, f : f + FCHUNK]
        )
        sum_up_ref[:, f : f + FCHUNK] += row_sums(back_up)
        up_rounded = back_up.astype(jnp.bfloat16)
        upr_ref[:, f : f + FCHUNK] = up_rounded
        back_hidden = back_hidden + back_product(up_rounded, up_ref[:, f : f + FCHUNK])
    sum_ref[2] += row_sums(back_hidden * unit_one)
    sum_ref[3] += row_sums(back_hidden)
    back_mixed = norm_back(back_hidden * gain_one, unit_one, rate_one)
    sum_ref[0] += row_sums(back_mixed)
    mixed_ref[...] = back_mixed
    mixed_rounded = back_mixed.astype(jnp.bfloat16)
    mixr_ref[...] = mixed_rounded
    back = back_product(mixed_rounded, mix_ref[...]).astype(jnp.bfloat16)
    back = jnp.where(live_ref[...] > 0.5, back, jnp.zeros_like(back))
    back_ref[:, : back.shape[1]] = back
    terms = back.astype(jnp.float32) * attended.astype(jnp.float32)
    high = terms.astype(jnp.bfloat16)
    low = (terms - high.astype(jnp.float32)).astype(jnp.bfloat16)
    delta = plain_product(high, spread_ref[...]) + plain_product(low, spread_ref[...])
    delta_ref[...] = delta
    lane = lax.broadcasted_iota(jnp.int32, delta.shape, 1)
    term = lane % TERMS
    whole = jnp.where(term < 3, lse_ref[...], delta)
    first = whole.astype(jnp.bfloat16)
    rest = whole - first.astype(jnp.float32)
    second = rest.astype(jnp.bfloat16)
    third = (rest - second.astype(jnp.float32)).astype(jnp.bfloat16)
    picked = jnp.where(
        (term == 0) | (term == 3),
        first.astype(jnp.float32),
        jnp.where((term == 2), third.astype(jnp.float32), second.astype(jnp.float32)),
    )
    picked = jnp.where(lane < TERMS * HEADS, picked, 0.0)
    back_ref[:, back.shape[1] :] = picked.astype(jnp.bfloat16)


def chain_call(att, tok, cot, live, lse, mix, up, down, vectors, bias_up):
    rows, width = tok.shape
    wide = up.shape[1]
    head_of = jnp.arange(width, dtype=jnp.int32)[:, None] // HD
    spread = (head_of == jnp.arange(2 * HD, dtype=jnp.int32)[None, :] // TERMS).astype(jnp.bfloat16)

    def tile(columns):
        return pl.BlockSpec((RTILE, columns), lambda i: (i, 0))

    def fixed(*shape):
        return pl.BlockSpec(shape, lambda i: (0,) * len(shape))

    bf16, f32 = jnp.bfloat16, jnp.float32
    return pl.pallas_call(
        chain_kernel,
        grid=(rows // RTILE,),
        in_specs=[
            tile(width),
            tile(width),
            tile(width),
            tile(1),
            tile(2 * HD),
            fixed(*mix.shape),
            fixed(*up.shape),
            fixed(*down.shape),
            fixed(*vectors.shape),
            fixed(*bias_up.shape),
            fixed(*spread.shape),
        ],
        out_specs=[
            tile(width),
            tile(wide),
            tile(wide),
            tile(width),
            tile(width),
            tile(width),
            tile(width),
            tile(width + 2 * HD),
            tile(2 * HD),
            fixed(6, 8, width),
            fixed(8, wide),
        ],
        out_shape=[
            jax.ShapeDtypeStruct((rows, width), bf16),
            jax.ShapeDtypeStruct((rows, wide), bf16),
            jax.ShapeDtypeStruct((rows, wide), bf16),
            jax.ShapeDtypeStruct((rows, width), bf16),
            jax.ShapeDtypeStruct((rows, width), bf16),
            jax.ShapeDtypeStruct((rows, width), bf16),
            jax.ShapeDtypeStruct((rows, width), f32),
            jax.ShapeDtypeStruct((rows, width + 2 * HD), bf16),
            jax.ShapeDtypeStruct((rows, 2 * HD), f32),
            jax.ShapeDtypeStruct((6, 8, width), f32),
            jax.ShapeDtypeStruct((8, wide), f32),
        ],
        scratch_shapes=[pltpu.VMEM((RTILE, wide), f32)],
        cost_estimate=work(44),
        compiler_params=pltpu.CompilerParams(vmem_limit_bytes=VMEM_LIMIT),
    )(att, tok, cot, live, lse, mix, up, down, vectors, bias_up, spread)


def weight_kernel(n_dp, core_ref, act, pre, hid, upr, att, mixr, small, *refs):
    send, keep, tmp = refs[-3:]
    step = pl.program_id(0)
    core = core_ref[0]
    pieces = FF // D
    down_rows = FF // n_dp
    part_rows = D // n_dp

    def put(x, row, rows, begin):
        mine = pl.multiple_of(begin + core * rows, 16)
        other = pl.multiple_of(begin + (1 - core) * rows, 16)
        keep[pl.ds(x, 1), pl.ds(row, rows), :] = tmp[pl.ds(mine, rows), :][None]
        send[pl.ds(x, 1), pl.ds(row, rows), :] = tmp[pl.ds(other, rows), :][None]

    @pl.when(step < pieces)
    def _():
        tmp[...] = outer_sum(act[...], pre[...]).astype(jnp.bfloat16)
        per = D // down_rows
        for b in range(per):
            block = step * per + b
            x = block // 2
            rows = tmp[b * down_rows : (b + 1) * down_rows, :]

            @pl.when(lax.rem(block, 2) == core)
            def _():
                keep[pl.ds(x, 1), 0:down_rows, :] = rows[None]

            @pl.when(lax.rem(block, 2) != core)
            def _():
                send[pl.ds(x, 1), 0:down_rows, :] = rows[None]

    @pl.when((step >= pieces) & (step < 2 * pieces))
    def _():
        tmp[...] = outer_sum(hid[...], upr[...]).astype(jnp.bfloat16)
        row = pl.multiple_of(down_rows + (step - pieces) * part_rows, 16)
        for x in range(n_dp // 2):
            put(x, row, part_rows, 2 * x * part_rows)

    @pl.when(step == 2 * pieces)
    def _():
        tmp[...] = outer_sum(att[...], mixr[...]).astype(jnp.bfloat16)
        row = down_rows + pieces * part_rows
        for x in range(n_dp // 2):
            put(x, row, part_rows, 2 * x * part_rows)
            last = row + part_rows
            rows = keep.shape[1] - last
            keep[x, last:, :] = small[pl.ds(2 * x + core, 1), :, :][0]
            send[x, last:, :] = small[pl.ds(2 * x + 1 - core, 1), :, :][0]


def weight_call(n_dp, core, act, pre, hid, upr, att, mixr, small, *needs):
    rows = act.shape[0]
    pieces = FF // D
    out_rows = FF // n_dp + (pieces + 1) * (D // n_dp) + small.shape[1]

    def fixed(*shape):
        return pl.BlockSpec(shape, lambda i, c: (0,) * len(shape))

    def stepped(first):
        return pl.BlockSpec((rows, D), lambda i, c: (0, jnp.clip(i - first, 0, pieces - 1)))

    shape = (n_dp // 2, out_rows, D)
    return pl.pallas_call(
        functools.partial(weight_kernel, n_dp),
        out_shape=[jax.ShapeDtypeStruct(shape, jnp.bfloat16)] * 2,
        grid_spec=pltpu.PrefetchScalarGridSpec(
            num_scalar_prefetch=1,
            grid=(2 * pieces + 1,),
            in_specs=[
                stepped(0),
                fixed(rows, D),
                fixed(rows, D),
                stepped(pieces),
                fixed(rows, D),
                fixed(rows, D),
                fixed(*small.shape),
            ]
            + [UNREAD] * len(needs),
            out_specs=[fixed(*shape)] * 2,
            scratch_shapes=[pltpu.VMEM((D, D), jnp.bfloat16)],
        ),
        cost_estimate=work(22),
        compiler_params=pltpu.CompilerParams(vmem_limit_bytes=VMEM_LIMIT),
    )(core, act, pre, hid, upr, att, mixr, small, *needs)


def outer_kernel(n_dp, core_ref, tokens, columns, *refs):
    send, keep, tmp = refs[-3:]
    core = core_ref[0]
    rows = tokens.shape[1] // n_dp
    tmp[...] = outer_sum(tokens[...], columns[...]).astype(tmp.dtype)
    for x in range(n_dp // 2):
        mine = pl.multiple_of((2 * x + core) * rows, 16)
        other = pl.multiple_of((2 * x + 1 - core) * rows, 16)
        keep[x] = tmp[pl.ds(mine, rows), :]
        send[x] = tmp[pl.ds(other, rows), :]


def outer_split(n_dp, core, tokens, columns, first, block, *needs):
    rows, depth = tokens.shape
    steps = columns.shape[1] // block - first
    shape = (n_dp // 2, depth // n_dp, block * steps)
    out = pl.BlockSpec(shape[:2] + (block,), lambda i, c: (0, 0, i))
    return pl.pallas_call(
        functools.partial(outer_kernel, n_dp),
        out_shape=[jax.ShapeDtypeStruct(shape, jnp.bfloat16)] * 2,
        grid_spec=pltpu.PrefetchScalarGridSpec(
            num_scalar_prefetch=1,
            grid=(steps,),
            in_specs=[
                pl.BlockSpec((rows, depth), lambda i, c: (0, 0)),
                pl.BlockSpec((rows, block), lambda i, c: (0, first + i)),
            ]
            + [UNREAD] * len(needs),
            out_specs=[out, out],
            scratch_shapes=[pltpu.VMEM((depth, block), jnp.bfloat16)],
        ),
        cost_estimate=work(4),
        compiler_params=plain_params(),
    )(core, tokens, columns, *needs)


def swap(value, axis, bit):
    devices = lax.axis_size(axis)
    return lax.ppermute(value, axis, [(i, i ^ bit) for i in range(devices)])


def dp_gather(shard, dp_rank):
    blocks = shard[None]
    bit = lax.axis_size("dp") // 2
    while bit >= 1:
        got = swap(blocks, "dp", bit)
        high = ((dp_rank // bit) % 2) == 1
        first = jnp.where(high, got, blocks)
        second = jnp.where(high, blocks, got)
        blocks = jnp.stack([first, second], axis=1).reshape((-1,) + shard.shape)
        bit //= 2
    return blocks.reshape((-1,) + shard.shape[1:])


def work(microseconds):
    return pl.CostEstimate(
        flops=int(microseconds * 0.4e9), transcendentals=0, bytes_accessed=1 << 20
    )


def row_tile(rows, limit=512):
    for size in range(min(rows, limit), 15, -1):
        if rows % size == 0 and size % 16 == 0:
            return size
    return rows


def plain_params():
    return pltpu.CompilerParams(vmem_limit_bytes=VMEM_LIMIT)


def split_add_kernel(which, keep_mine, got_mine, keep_other, got_other, *refs):
    mine, other = refs[-2:]
    mine[...] = (keep_mine[...].astype(jnp.float32) + got_mine[...].astype(jnp.float32)).astype(
        mine.dtype
    )
    other[...] = (keep_other[...].astype(jnp.float32) + got_other[...].astype(jnp.float32)).astype(
        other.dtype
    )


def split_add(keep, got, which, *needs):
    blocks, rows, columns = keep.shape
    tile = row_tile(rows)

    def spec(flip):
        def place(b, i, w):
            bit = 1 - w[0] if flip else w[0]
            return 2 * b + bit, i, 0

        return pl.BlockSpec((1, tile, columns), place)

    out = pl.BlockSpec((1, tile, columns), lambda b, i, w: (b, i, 0))
    shape = jax.ShapeDtypeStruct((blocks // 2, rows, columns), keep.dtype)
    return pl.pallas_call(
        split_add_kernel,
        out_shape=[shape, shape],
        grid_spec=pltpu.PrefetchScalarGridSpec(
            num_scalar_prefetch=1,
            grid=(blocks // 2, rows // tile),
            in_specs=[spec(False), spec(False), spec(True), spec(True)] + [UNREAD] * len(needs),
            out_specs=[out, out],
        ),
        cost_estimate=work(4),
        compiler_params=plain_params(),
    )(which, keep, got, keep, got, *needs)


def add_kernel(left, right, *refs):
    out = refs[-1]
    out[...] = (left[0].astype(jnp.float32) + right[0].astype(jnp.float32)).astype(out.dtype)


def add_blocks(left, right, *needs):
    _, rows, columns = left.shape
    tile = row_tile(rows)
    spec = pl.BlockSpec((1, tile, columns), lambda i: (0, i, 0))
    return pl.pallas_call(
        add_kernel,
        grid=(rows // tile,),
        in_specs=[spec, spec] + [UNREAD] * len(needs),
        out_specs=pl.BlockSpec((tile, columns), lambda i: (i, 0)),
        cost_estimate=work(3),
        out_shape=jax.ShapeDtypeStruct((rows, columns), left.dtype),
        compiler_params=plain_params(),
    )(left, right, *needs)


def pieces_kernel(pieces, *refs):
    out = refs[-1]
    total = pieces[0].astype(jnp.float32)
    for i in range(1, pieces.shape[0]):
        total = total + pieces[i].astype(jnp.float32)
    total = total.astype(out.dtype)
    for i in range(out.shape[0]):
        out[i] = total


def summed_copies(pieces, copies, *needs):
    _, rows, columns = pieces.shape
    return pl.pallas_call(
        pieces_kernel,
        in_specs=[pl.BlockSpec(memory_space=pltpu.VMEM)] + [UNREAD] * len(needs),
        out_specs=pl.BlockSpec(memory_space=pltpu.VMEM),
        out_shape=jax.ShapeDtypeStruct((copies, rows, columns), pieces.dtype),
        cost_estimate=work(2),
        compiler_params=plain_params(),
    )(pieces, *needs)


def gate_kernel(value, *refs):
    refs[-1][...] = value[...]


def gated(value, *needs):
    return pl.pallas_call(
        gate_kernel,
        in_specs=[pl.BlockSpec(memory_space=pltpu.VMEM)] + [UNREAD] * len(needs),
        out_specs=pl.BlockSpec(memory_space=pltpu.VMEM),
        out_shape=jax.ShapeDtypeStruct(value.shape, value.dtype),
        cost_estimate=work(1),
        compiler_params=plain_params(),
    )(value, *needs)


def cluster_ids(group_order, own_start, span):
    padded = jnp.pad(group_order, ((0, 0), (HALO, HALO)), constant_values=-(1 << 24))
    wanted = lax.dynamic_slice_in_dim(padded, own_start, span, 1) - (own_start - HALO)
    tile_of = wanted >> 7
    lane_of_token = wanted & (CL - 1)
    cluster = (jnp.arange(span, dtype=jnp.int32) >> 7) + 1
    tile_hot = jnp.where(
        tile_of[:, :, None] == jnp.arange(span // CL, dtype=jnp.int32), cluster[None, :, None], 0
    ).astype(jnp.bfloat16)
    lane_hot = (lane_of_token[:, :, None] == jnp.arange(CL, dtype=jnp.int32)).astype(jnp.bfloat16)
    table = jnp.einsum("hpt,hpl->htl", tile_hot, lane_hot, preferred_element_type=jnp.float32)
    return table.reshape(HEADS, span) - 1.0


def on_device(
    tokens,
    input_weight,
    output_weight,
    up_weight,
    down_weight,
    output_bias,
    up_bias,
    down_bias,
    first_gain,
    first_shift,
    second_gain,
    second_shift,
    document_runs,
    document_trim,
    cluster_order,
    cotangent,
):
    bf16, f32 = jnp.bfloat16, jnp.float32
    n_dp = lax.axis_size("dp")
    n_seq = lax.axis_size("seq")
    dp_rank = lax.axis_index("dp")
    seq_rank = lax.axis_index("seq")
    inputs = tokens[0]
    tok_dev = inputs.shape[0]
    tiles = tok_dev // CL
    span = tok_dev + 2 * HALO
    own_start = seq_rank * tok_dev

    token_parts = halo_parts(inputs)
    n_parts = len(token_parts)

    weight_in = lax.all_gather(input_weight, "dp", axis=0, tiled=True)
    weight_up = lax.all_gather(up_weight, "dp", axis=0, tiled=True)
    weight_down = lax.all_gather(down_weight, "dp", axis=0, tiled=True)

    runs = document_runs[0]
    first_cluster = jnp.cumsum(runs) - runs
    own_clusters = seq_rank * tiles + jnp.arange(tiles, dtype=jnp.int32)
    doc_start = jnp.max(
        jnp.where(first_cluster[None, :] <= own_clusters[:, None], first_cluster[None, :], 0), axis=1
    )
    starts = (doc_start - seq_rank * tiles + (MOSTB - 1)).astype(jnp.int32)
    near_left = HALO // CL - tiles
    near = near_left + 2 * tiles * jnp.stack([1 - seq_rank % 2, seq_rank % 2])
    starts = jnp.concatenate([starts, near.astype(jnp.int32)])

    cids = cluster_ids(cluster_order[0], own_start, span)
    positions = own_start - HALO + jnp.arange(span, dtype=jnp.int32)
    live = live_tokens(runs, document_trim[0], positions)
    usable = live[None, :] & (cids >= 0.0)
    key_ids = jnp.where(usable, cids, -1.0).reshape(PAIRS, 2, span)
    query_ids = jnp.where(usable, cids, -2.0).reshape(PAIRS, 2, span)
    own_live = live[HALO : HALO + tok_dev, None].astype(f32)

    own = plain_product(inputs, weight_in).astype(bf16)
    groups = HEADS // PACK
    group_lanes = PACK * HD
    kv_weight = (
        weight_in[:, D:]
        .reshape(D, 2, PAIRS, 2 * HD)
        .transpose(0, 2, 1, 3)
        .reshape(D, 2 * D)
    )
    around = project_call(token_parts[:2] + token_parts[3:], weight_in, kv_weight)
    projected = [*around[:2], own, *around[2:]]
    vectors = [
        output_bias,
        down_bias,
        first_gain,
        first_shift,
        second_gain,
        second_shift,
        up_bias,
    ]
    mix_rows = output_weight.shape[0]
    packed = jnp.concatenate(vectors)
    pad_rows = -(-packed.shape[0] // (16 * D)) * 16
    packed = jnp.pad(packed, (0, pad_rows * D - packed.shape[0])).reshape(pad_rows, D)
    mix_shard = gated(jnp.concatenate([output_weight, packed], 0), own)
    mix_all = dp_gather(mix_shard, dp_rank)
    mix_all = mix_all.reshape(n_dp, mix_rows + pad_rows, D)
    weight_mix = mix_all[:, :mix_rows].reshape(D, D)
    small_all = mix_all[:, mix_rows:].reshape(n_dp, -1).astype(f32)
    vec = small_all[:, : 6 * mix_rows].reshape(n_dp, 6, mix_rows).transpose(1, 0, 2).reshape(6, D)
    vec = jnp.pad(vec, ((0, 2), (0, 0)))
    up_part = up_bias.shape[0]
    bias_up = small_all[:, 6 * mix_rows : 6 * mix_rows + up_part].reshape(1, FF)
    bias_up = jnp.pad(bias_up, ((0, 7), (0, 0)))
    heights = [part.shape[0] for part in token_parts]

    groups = HEADS // PACK
    group_lanes = PACK * HD
    group_key_ids = key_ids.reshape(groups, PACK, span)
    group_query_ids = query_ids.reshape(groups, PACK, span)
    group_scratch = pltpu.VMEM((span, group_lanes), bf16)

    def group_parts(third, first):
        return [lane_block(rows, third * groups + first, PACK) for rows in heights]

    steps = tiles // TILES_AT_ONCE
    step_rows = TILES_AT_ONCE * CL

    def of_group(rows, first):
        return pl.BlockSpec((rows, group_lanes), lambda g, t, starts: (0, first + g))

    def ids_of_group():
        return pl.BlockSpec((1, PACK, span), lambda g, t, starts: (g, 0, 0))

    step_block = pl.BlockSpec((step_rows, group_lanes), lambda g, t, starts: (t, g))
    whole_lanes = pl.BlockSpec((tok_dev, 2 * HD), lambda g, t, starts: (0, 0))
    attended, lse, rate, probs = strip_call(
        functools.partial(attend_kernel, tiles, n_parts),
        52,
        (groups, steps),
        [step_block]
        + [of_group(rows, groups) for rows in heights]
        + [of_group(rows, 2 * groups) for rows in heights]
        + [ids_of_group(), ids_of_group()],
        [
            step_block,
            whole_lanes,
            whole_lanes,
            pl.BlockSpec(
                (1, TILES_AT_ONCE, PACK * CL, WINDOW), lambda g, t, starts: (g, t, 0, 0)
            ),
        ],
        [
            jax.ShapeDtypeStruct((tok_dev, D), bf16),
            jax.ShapeDtypeStruct((tok_dev, 2 * HD), f32),
            jax.ShapeDtypeStruct((tok_dev, 2 * HD), f32),
            jax.ShapeDtypeStruct((groups, tiles, PACK * CL, WINDOW), bf16),
        ],
        [group_scratch, group_scratch]
        + [pltpu.VMEM((PACK * CL, WINDOW), f32)] * TILES_AT_ONCE
        + [pltpu.VMEM((PACK * CL, CL), f32)] * TILES_AT_ONCE,
        (starts, own, *projected, *projected, group_query_ids, group_key_ids),
    )

    (
        result,
        active,
        up_rounded,
        hidden_rounded,
        pre_rounded,
        mixed_rounded,
        back_mixed,
        back_own,
        delta,
        sums,
        sums_up,
    ) = chain_call(
        attended,
        inputs,
        cotangent[0],
        own_live,
        lse,
        weight_mix,
        weight_up,
        weight_down,
        vec,
        bias_up,
    )
    back_parts = halo_parts(back_own)

    small = jnp.concatenate(
        [
            jnp.sum(sums, axis=1).reshape(6, n_dp, mix_rows).transpose(1, 0, 2).reshape(n_dp, -1),
            jnp.sum(sums_up, axis=0).reshape(n_dp, -1),
        ],
        axis=1,
    ).astype(bf16)
    unit = 8 * n_seq
    fixed_rows = FF // n_dp + (FF // D + 1) * (D // n_dp)
    small_rows = -(-(fixed_rows + -(-small.shape[1] // D)) // unit) * unit - fixed_rows
    small = jnp.pad(small, ((0, 0), (0, small_rows * D - small.shape[1])))
    small = small.reshape(n_dp, small_rows, D)
    core = (dp_rank % 2).astype(jnp.int32)
    def query_strip(first, *needs):
        buffer = needs[:1] if first > 0 else ()

        def parts(third):
            return [
                pl.BlockSpec(
                    (rows, group_lanes), lambda t, starts: (0, third * groups + first)
                )
                for rows in heights
            ]

        block = pl.BlockSpec((step_rows, group_lanes), lambda t, starts: (t, first))
        lanes = pl.BlockSpec((step_rows, 2 * HD), lambda t, starts: (t, 0))
        in_specs = (
            parts(1)
            + parts(2)
            + [
                block,
                pl.BlockSpec(
                    (1, TILES_AT_ONCE, PACK * CL, WINDOW), lambda t, starts: (first, t, 0, 0)
                ),
                lanes,
                lanes,
            ]
            + [UNREAD] * len(needs)
        )
        return strip_call(
            functools.partial(query_kernel, tiles, n_parts, first * PACK),
            16,
            (steps,),
            in_specs,
            block,
            jax.ShapeDtypeStruct((tok_dev, D), bf16),
            [group_scratch, group_scratch],
            (starts, *projected, *projected, back_own, probs, rate, delta, *needs),
            {len(in_specs) + 1 - len(needs): 0} if buffer else None,
        )

    pair_scratch = pltpu.VMEM((span, 4 * HD), bf16)

    def key_strip(pair, pairs, *needs):
        buffer = needs[:1] if pair > 0 else ()

        def parts(third):
            return [lane_block(rows, third * PAIRS + pair) for rows in heights]

        in_specs = (
            [lane_block(tok_dev, PAIRS + pair), lane_block(tok_dev, 2 * PAIRS + pair)]
            + parts(0)
            + parts(0)
            + [fixed_lanes(rows, PAIRS) for rows in heights]
            + [row_block(span, pair), row_block(span, pair)]
            + [UNREAD] * len(needs)
        )
        return strip_call(
            functools.partial(key_kernel, tiles, n_parts, pair),
            13 * pairs,
            (pairs,),
            in_specs,
            lane_block(tok_dev, pair, 4),
            jax.ShapeDtypeStruct((tok_dev, 2 * D), bf16),
            [pair_scratch, pair_scratch],
            (
                starts,
                own,
                own,
                *projected,
                *back_parts,
                *back_parts,
                query_ids,
                key_ids,
                *needs,
            ),
            {len(in_specs) + 1 - len(needs): 0} if buffer else None,
        )

    def scatter(share):
        rows, columns = share.shape
        return lax.all_to_all(
            share.reshape(n_seq, rows // n_seq, columns), "seq", split_axis=0, concat_axis=0
        )

    def everyone(copies):
        got = lax.all_to_all(copies, "seq", split_axis=0, concat_axis=0)
        return got.reshape(-1, copies.shape[-1])

    def first_split(keep, got, *needs):
        bit = 2
        while True:
            which = ((dp_rank // bit) % 2).astype(jnp.int32).reshape(1)
            mine, other = split_add(keep, got, which, *needs)
            got = swap(other, "dp", bit)
            if mine.shape[0] == 1:
                return mine, got
            keep, bit, needs = mine, bit * 2, ()

    def core_split(grad):
        rows, columns = grad.shape
        blocks = grad.astype(bf16).reshape(n_dp // 2, 2, rows // n_dp, columns)
        return (
            lax.dynamic_index_in_dim(blocks, 1 - core, 1, keepdims=False),
            lax.dynamic_index_in_dim(blocks, core, 1, keepdims=False),
        )

    send, keep = weight_call(
        n_dp,
        core.reshape(1),
        active,
        pre_rounded,
        hidden_rounded,
        up_rounded,
        attended,
        mixed_rounded,
        small,
    )
    core_got = swap(send, "dp", 1)
    back_q = query_strip(0, send)
    mine, x_got = first_split(keep, core_got, back_q)
    back_q = query_strip(1, back_q, mine)
    back_q = query_strip(2, back_q)
    back_kv = key_strip(0, 1, back_q)
    share = add_blocks(mine, x_got, back_kv)
    pieces = scatter(share)
    back_kv = key_strip(1, 2, back_kv, share)
    cut = PAIRS // 2 * 4 * HD
    early_cols = jnp.concatenate([back_q, back_kv[:, :cut]], axis=1)
    early_send, early_keep = core_split(outer_sum(inputs, early_cols))
    early_core = swap(early_send, "dp", 1)
    back_kv = key_strip(3, 1, back_kv, early_send)
    early_mine, early_got = first_split(early_keep, early_core, back_kv)
    back_kv = key_strip(4, 1, back_kv, early_mine)
    copies = summed_copies(pieces, 1, back_kv)
    back_kv = key_strip(5, 1, back_kv, copies)
    early_share = add_blocks(early_mine, early_got, back_kv)
    all_sums = lax.all_gather(copies[0], "seq", axis=0, tiled=True)
    late_send, late_keep = outer_split(
        n_dp, core.reshape(1), inputs, back_kv, 1, cut, early_share
    )
    late_mine, late_got = first_split(late_keep, swap(late_send, "dp", 1))
    late_share = add_blocks(late_mine, late_got, all_sums)
    in_share = jnp.concatenate([early_share, late_share], axis=1)
    in_all = everyone(summed_copies(scatter(in_share), n_seq))

    input_grad = (
        back_mixed + back_product(back_q, weight_in[:, :D]) + back_product(back_kv, kv_weight)
    )
    kv_all = in_all[:, D:].reshape(-1, PAIRS, 2, 2 * HD).transpose(0, 2, 1, 3)
    grad_in_total = jnp.concatenate([in_all[:, :D], kv_all.reshape(-1, 2 * D)], axis=1).astype(f32)
    down_rows = FF // n_dp
    part_rows = D // n_dp
    grad_down = all_sums[:down_rows].astype(f32)
    grad_up = (
        all_sums[down_rows : down_rows + (FF // D) * part_rows]
        .reshape(FF // D, part_rows, D)
        .transpose(1, 0, 2)
        .reshape(part_rows, FF)
        .astype(f32)
    )
    at = down_rows + (FF // D) * part_rows
    grad_mix = all_sums[at : at + part_rows].astype(f32)
    flat = all_sums[at + part_rows :].reshape(-1).astype(f32)
    vectors_out = [flat[i * part_rows : (i + 1) * part_rows] for i in range(6)]
    bias_up_out = flat[6 * part_rows : 6 * part_rows + down_rows]
    return (
        result[None],
        input_grad[None],
        grad_in_total,
        grad_mix,
        grad_up,
        grad_down,
        vectors_out[0],
        bias_up_out,
        vectors_out[1],
        *vectors_out[2:],
    )


def solution(mesh):
    placed = (
        P("dp", "seq", None),
        P("dp", None),
        P("dp", None),
        P("dp", None),
        P("dp", None),
        P("dp"),
        P("dp"),
        P("dp"),
        P("dp"),
        P("dp"),
        P("dp"),
        P("dp"),
        P("dp", None),
        P("dp", None),
        P("dp", None, None),
        P("dp", "seq", None),
    )
    return jax.shard_map(
        on_device,
        mesh=mesh,
        in_specs=placed,
        out_specs=(
            P("dp", "seq", None),
            P("dp", "seq", None),
            P("dp", None),
            P("dp", None),
            P("dp", None),
            P("dp", None),
            P("dp"),
            P("dp"),
            P("dp"),
            P("dp"),
            P("dp"),
            P("dp"),
            P("dp"),
        ),
        check_vma=False,
    )
```

```python
import functools

import jax
import jax.numpy as jnp
from jax import lax
from jax.experimental import pallas as pl
from jax.experimental.pallas import tpu as pltpu
from jax.sharding import PartitionSpec as P

D = 768
HEADS = 12
HD = 64
CL = 128
MOSTB = 16
PAIRS = HEADS // 2
WINDOW = MOSTB * CL
HALO = (MOSTB - 1) * CL
CHUNK = 512
KCHUNK = 512
TILES_AT_ONCE = 2
PACK = 4
NEG = -1e30
TERMS = 5
FF = 3072
RTILE = 256
FCHUNK = 768
SCALE2 = HD ** (-0.5) * 1.4426950408889634

EPSILON = 1e-05


def shifted(value, axis, by):
    devices = lax.axis_size(axis)
    pairs = [(i, i + by) for i in range(devices) if 0 <= i + by < devices]
    return lax.ppermute(value, axis, pairs)


def halo_parts(value):
    own = value.shape[0]
    far = HALO - own
    devices = lax.axis_size("seq")
    assert 0 < far <= own and devices % 2 == 0
    partner = lax.ppermute(value, "seq", [(i, i ^ 1) for i in range(devices)])
    pairs = [(i, i - 1 if i % 2 == 0 else i + 1) for i in range(devices)]
    other = lax.ppermute(value, "seq", [(i, k) for i, k in pairs if 0 <= k < devices])
    before = shifted(value[own - far :], "seq", 2)
    following = shifted(value[:far], "seq", -2)
    return [before, partner, value, other, following]


def places(starts, tiles, parts):
    far, own = parts[0].shape[0], parts[2].shape[0]
    return [
        0,
        pl.multiple_of(starts[tiles] * CL, CL),
        far + own,
        pl.multiple_of(starts[tiles + 1] * CL, CL),
        far + 3 * own,
    ]


def live_tokens(runs, trim, positions):
    ends = jnp.cumsum(runs) * CL
    starts = ends - runs * CL
    lengths = runs * CL - trim
    inside = (positions[..., None] >= starts) & (positions[..., None] < starts + lengths)
    return jnp.any(inside, axis=-1)


def outer_sum(left, right):
    return lax.dot_general(
        left, right, (((0,), (0,)), ((), ())), preferred_element_type=jnp.float32
    )


def back_product(left, right):
    return lax.dot_general(
        left, right, (((1,), (1,)), ((), ())), preferred_element_type=jnp.float32
    )


def plain_product(left, right):
    return jnp.dot(left, right, preferred_element_type=jnp.float32)


def stacked(tile):
    lane = lax.broadcasted_iota(jnp.int32, tile.shape, 1)
    zero = jnp.zeros_like(tile)
    heads = tile.shape[1] // HD
    return jnp.concatenate(
        [
            jnp.where((lane >= h * HD) & (lane < (h + 1) * HD), tile, zero)
            for h in range(heads)
        ],
        axis=0,
    )


def unstacked(stack):
    heads = stack.shape[1] // HD
    lane = lax.broadcasted_iota(jnp.int32, (CL, heads * HD), 1)
    result = stack[:CL]
    for h in range(1, heads):
        result = jnp.where(lane >= h * HD, stack[h * CL : (h + 1) * CL], result)
    return result


def as_column(row):
    return jnp.broadcast_to(row, (CL, CL)).T


def lane_of(tile, lane):
    lanes = lax.broadcasted_iota(jnp.int32, tile.shape, 1)
    return jnp.sum(jnp.where(lanes == lane, tile, 0.0), axis=1, keepdims=True)


def masked(scores, cols, row_ref, begin):
    parts = []
    wide = scores.shape[1]
    for half, one in enumerate(cols):
        row = row_ref[0, half : half + 1, pl.ds(begin, wide)]
        block = scores[half * CL : (half + 1) * CL]
        col = jnp.concatenate([one] * (wide // CL), axis=1)
        parts.append(jnp.where(col == row, block, NEG))
    return jnp.concatenate(parts, axis=0)


def assemble(parts, offsets, whole):
    for part, at in zip(parts, offsets):
        whole[pl.ds(at, part.shape[0]), :] = part[...]


def ahead(steps, produce, consume):
    held = produce(*steps[0])
    for i, step in enumerate(steps):
        following = produce(*steps[i + 1]) if i + 1 < len(steps) else None
        consume(*step, held)
        held = following


def attend_kernel(tiles, n_parts, starts, q_ref, *refs):
    k_parts, refs = refs[:n_parts], refs[n_parts:]
    v_parts, refs = refs[:n_parts], refs[n_parts:]
    qid_ref, kid_ref, out_ref, lse_ref, rate_ref, p_ref, k_ref, v_ref, *slots = refs
    s_refs, top_refs = slots[:TILES_AT_ONCE], slots[TILES_AT_ONCE:]
    group, step = pl.program_id(0), pl.program_id(1)
    heads = q_ref.shape[1] // HD
    chunks = WINDOW // CHUNK

    @pl.when(step == 0)
    def _():
        offsets = places(starts, tiles, k_parts)
        assemble(k_parts, offsets, k_ref)
        assemble(v_parts, offsets, v_ref)

    @pl.when((group == 0) & (step == 0))
    def _():
        lse_ref[...] = jnp.zeros_like(lse_ref)
        rate_ref[...] = jnp.zeros_like(rate_ref)

    def first_half(slot):
        tile = TILES_AT_ONCE * step + slot
        own = pl.multiple_of(HALO + tile * CL, CL)
        return dict(
            begin=pl.multiple_of(starts[tile] * CL, CL),
            query=stacked(q_ref[slot * CL : (slot + 1) * CL, :]),
            cols=[
                as_column(qid_ref[0, half : half + 1, pl.ds(own, CL)]) for half in range(heads)
            ],
        )

    def score(state, slot, j):
        at = pl.multiple_of(state["begin"] + j * CHUNK, CL)
        scores = back_product(state["query"], k_ref[pl.ds(at, CHUNK), :])
        scores = masked(scores, state["cols"], kid_ref, at)
        s_refs[slot][:, j * CHUNK : (j + 1) * CHUNK] = scores
        top = scores[:, :CL]
        for i in range(1, CHUNK // CL):
            top = jnp.maximum(top, scores[:, i * CL : (i + 1) * CL])
        if j > 0:
            top = jnp.maximum(top, top_refs[slot][...])
        top_refs[slot][...] = top

    states = [first_half(0)]
    for j in range(chunks):
        score(states[0], 0, j)
    for slot in range(TILES_AT_ONCE):
        if slot + 1 < TILES_AT_ONCE:
            states.append(first_half(slot + 1))
        state = states[slot]
        peak = jnp.max(top_refs[slot][...], axis=1, keepdims=True)
        total = jnp.zeros((heads * CL, CL), jnp.float32)
        result = jnp.zeros((heads * CL, heads * HD), jnp.float32)
        for j in range(chunks):
            if slot + 1 < TILES_AT_ONCE:
                score(states[slot + 1], slot + 1, j)
            at = pl.multiple_of(state["begin"] + j * CHUNK, CL)
            columns = slice(j * CHUNK, (j + 1) * CHUNK)
            weights = jnp.exp2((s_refs[slot][:, columns] - peak) * SCALE2)
            for i in range(CHUNK // CL):
                total = total + weights[:, i * CL : (i + 1) * CL]
            p_ref[0, slot, :, columns] = weights.astype(jnp.bfloat16)
            result = result + plain_product(
                p_ref[0, slot, :, columns], v_ref[pl.ds(at, CHUNK), :]
            )
        total = jnp.sum(total, axis=1, keepdims=True)
        rate = 1.0 / total
        result = result * rate
        lse = peak + jnp.log(total) * HD**0.5
        live = (state["cols"][0] >= 0.0).astype(jnp.float32)
        live = jnp.concatenate([live] * (heads * HD // CL), axis=1)
        rows = slice(slot * CL, (slot + 1) * CL)
        out_ref[rows, :] = (unstacked(result) * live).astype(jnp.bfloat16)
        here = pl.ds(pl.multiple_of((TILES_AT_ONCE * step + slot) * CL, CL), CL)
        lane = lax.broadcasted_iota(jnp.int32, (CL, CL), 1)
        kept, kept_rate = lse_ref[here, :], rate_ref[here, :]
        for half in range(heads):
            first = (heads * group + half) * TERMS
            inside = (lane >= first) & (lane < first + TERMS)
            part = slice(half * CL, (half + 1) * CL)
            kept = jnp.where(inside, lse[part], kept)
            kept_rate = jnp.where(inside, rate[part], kept_rate)
        lse_ref[here, :] = kept
        rate_ref[here, :] = kept_rate


def query_kernel(tiles, n_parts, first_head, starts, *refs):
    k_parts, refs = refs[:n_parts], refs[n_parts:]
    v_parts, refs = refs[:n_parts], refs[n_parts:]
    g_ref, p_ref, rate_ref, delta_ref = refs[:4]
    out_ref, k_ref, v_ref = refs[-3:]
    step = pl.program_id(0)
    heads = g_ref.shape[1] // HD
    chunks = WINDOW // CHUNK

    @pl.when(step == 0)
    def _():
        offsets = places(starts, tiles, k_parts)
        assemble(k_parts, offsets, k_ref)
        assemble(v_parts, offsets, v_ref)

    states = {}

    def state_of(slot):
        if slot not in states:
            rows = slice(slot * CL, (slot + 1) * CL)
            columns = [
                jnp.concatenate(
                    [lane_of(ref[rows, :], (first_head + half) * TERMS) for half in range(heads)],
                    axis=0,
                )
                for ref in (delta_ref, rate_ref)
            ]
            states[slot] = dict(
                begin=pl.multiple_of(starts[TILES_AT_ONCE * step + slot] * CL, CL),
                back=stacked(g_ref[rows, :]),
                delta=columns[0],
                rate=columns[1],
                result=jnp.zeros((heads * CL, heads * HD), jnp.float32),
            )
        return states[slot]

    def produce(slot, j):
        state = state_of(slot)
        at = pl.multiple_of(state["begin"] + j * CHUNK, CL)
        return back_product(state["back"], v_ref[pl.ds(at, CHUNK), :])

    def consume(slot, j, back_probs):
        state = state_of(slot)
        at = pl.multiple_of(state["begin"] + j * CHUNK, CL)
        weights = p_ref[0, slot, :, j * CHUNK : (j + 1) * CHUNK].astype(jnp.float32)
        back_scores = weights * (back_probs - state["delta"])
        state["result"] = state["result"] + plain_product(
            back_scores.astype(jnp.bfloat16), k_ref[pl.ds(at, CHUNK), :]
        )
        if j == chunks - 1:
            out_ref[slot * CL : (slot + 1) * CL, :] = unstacked(
                state["result"] * (state["rate"] * HD ** (-0.5))
            ).astype(jnp.bfloat16)

    ahead(
        [(slot, j) for slot in range(TILES_AT_ONCE) for j in range(chunks)], produce, consume
    )


def key_kernel(tiles, n_parts, first_pair, starts, k_ref, v_ref, *refs):
    q_parts, refs = refs[:n_parts], refs[n_parts:]
    g_parts, refs = refs[:n_parts], refs[n_parts:]
    a_parts, refs = refs[:n_parts], refs[n_parts:]
    qid_ref, kid_ref = refs[:2]
    out_ref, q_ref, g_ref = refs[-3:]
    pair = first_pair + pl.program_id(0)
    offsets = places(starts, tiles, q_parts)
    for at, q_part, g_part, a_part in zip(offsets, q_parts, g_parts, a_parts):
        rows = pl.ds(at, q_part.shape[0])
        q_ref[rows, : 2 * HD] = q_part[...]
        q_ref[rows, 2 * HD :] = a_part[...]
        g_ref[rows, : 2 * HD] = g_part[...]
        g_ref[rows, 2 * HD :] = a_part[...]

    lane = lax.broadcasted_iota(jnp.int32, (CL, CL), 1)
    lse_pick, delta_pick = [], []
    for half in range(2):
        first = (2 * pair + half) * TERMS
        lse_pick.append(jnp.where((lane >= first) & (lane < first + 3), -1.0, 0.0))
        delta_pick.append(jnp.where((lane >= first + 3) & (lane < first + TERMS), -1.0, 0.0))
    lse_pick = jnp.concatenate(lse_pick, axis=0).astype(jnp.bfloat16)
    delta_pick = jnp.concatenate(delta_pick, axis=0).astype(jnp.bfloat16)

    def some_tiles(step, carry):
        states = {}

        def state_of(slot):
            if slot not in states:
                tile = TILES_AT_ONCE * step + slot
                own = pl.multiple_of(HALO + tile * CL, CL)
                here = pl.multiple_of(tile * CL, CL)
                states[slot] = dict(
                    begin=pl.multiple_of(starts[tile] * CL, CL),
                    here=here,
                    keys=jnp.concatenate([stacked(k_ref[pl.ds(here, CL), :]), lse_pick], axis=1),
                    values=jnp.concatenate(
                        [stacked(v_ref[pl.ds(here, CL), :]), delta_pick], axis=1
                    ),
                    cols=[
                        as_column(kid_ref[0, half : half + 1, pl.ds(own, CL)]) for half in range(2)
                    ],
                    key_sum=jnp.zeros((2 * CL, 2 * HD), jnp.float32),
                    value_sum=jnp.zeros((2 * CL, 2 * HD), jnp.float32),
                )
            return states[slot]

        def produce(slot, j):
            state = state_of(slot)
            at = pl.multiple_of(state["begin"] + j * KCHUNK, CL)
            scores = back_product(state["keys"], q_ref[pl.ds(at, KCHUNK), :])
            return scores, back_product(state["values"], g_ref[pl.ds(at, KCHUNK), :])

        def consume(slot, j, held):
            state = state_of(slot)
            at = pl.multiple_of(state["begin"] + j * KCHUNK, CL)
            scores, back_probs = held
            probs = jnp.exp2(masked(scores * SCALE2, state["cols"], qid_ref, at))
            back_scores = probs * back_probs
            state["value_sum"] = state["value_sum"] + plain_product(
                probs.astype(jnp.bfloat16), g_ref[pl.ds(at, KCHUNK), : 2 * HD]
            )
            state["key_sum"] = state["key_sum"] + plain_product(
                back_scores.astype(jnp.bfloat16), q_ref[pl.ds(at, KCHUNK), : 2 * HD]
            )
            if j == WINDOW // KCHUNK - 1:
                rows = pl.ds(state["here"], CL)
                out_ref[rows, : 2 * HD] = (
                    unstacked(state["key_sum"]) * HD ** (-0.5)
                ).astype(jnp.bfloat16)
                out_ref[rows, 2 * HD :] = unstacked(state["value_sum"]).astype(jnp.bfloat16)

        ahead(
            [(slot, j) for slot in range(TILES_AT_ONCE) for j in range(WINDOW // KCHUNK)],
            produce,
            consume,
        )
        return carry

    lax.fori_loop(0, tiles // TILES_AT_ONCE, some_tiles, 0)


def lane_block(rows, first, heads=2):
    return pl.BlockSpec((rows, heads * HD), lambda pair, starts: (0, first + pair))


def fixed_lanes(rows, block):
    return pl.BlockSpec((rows, 2 * HD), lambda pair, starts: (0, block))


def row_block(columns, first, heads=2):
    return pl.BlockSpec((1, heads, columns), lambda pair, starts: (first + pair, 0, 0))


UNREAD = pl.BlockSpec(memory_space=pl.ANY)


VMEM_LIMIT = 60 * 1024 * 1024


def strip_call(
    kernel, length, grid, in_specs, out_specs, out_shape, scratch, args, aliases=None
):
    return pl.pallas_call(
        kernel,
        out_shape=out_shape,
        grid_spec=pltpu.PrefetchScalarGridSpec(
            num_scalar_prefetch=1,
            grid=grid,
            in_specs=in_specs,
            out_specs=out_specs,
            scratch_shapes=scratch,
        ),
        input_output_aliases=aliases or {},
        cost_estimate=work(length),
        compiler_params=pltpu.CompilerParams(vmem_limit_bytes=VMEM_LIMIT),
    )(*args)


def project_kernel(parts, weight, *refs):
    for source, target in zip(refs[:parts], refs[-parts:]):
        target[...] = plain_product(source[...], weight[...]).astype(target.dtype)


def project_call(parts, weight, *needs):
    depth, columns = weight.shape
    block = PACK * HD
    return pl.pallas_call(
        functools.partial(project_kernel, len(parts)),
        grid=(columns // block,),
        in_specs=[pl.BlockSpec((depth, block), lambda i: (0, i))]
        + [pl.BlockSpec(part.shape, lambda i: (0, 0)) for part in parts]
        + [UNREAD] * len(needs),
        out_specs=[pl.BlockSpec((part.shape[0], block), lambda i: (0, i)) for part in parts],
        out_shape=[jax.ShapeDtypeStruct((part.shape[0], columns), part.dtype) for part in parts],
        cost_estimate=work(20),
        compiler_params=pltpu.CompilerParams(vmem_limit_bytes=VMEM_LIMIT),
    )(weight, *parts, *needs)


def gelu_terms(value):
    t = 1.0 / (1.0 + (0.3275911 * 0.7071067811865476) * jnp.abs(value))
    bell = jnp.exp2(value * value * (-0.5 * 1.4426950408889634))
    tail = 0.5 * 1.061405429
    for term in (-0.5 * 1.453152027, 0.5 * 1.421413741, -0.5 * 0.284496736, 0.5 * 0.254829592):
        tail = tail * t + term
    tail = tail * t * bell
    cdf = jnp.where(value >= 0.0, 1.0 - tail, tail)
    return value * cdf, cdf + value * (0.3989422804014327 * bell)


def normalised(values):
    mean = jnp.mean(values, axis=-1, keepdims=True)
    centre = values - mean
    rate = lax.rsqrt(jnp.mean(centre * centre, axis=-1, keepdims=True) + EPSILON)
    return centre * rate, rate


def norm_back(scaled, unit, rate):
    first = jnp.mean(scaled, axis=-1, keepdims=True)
    second = jnp.mean(scaled * unit, axis=-1, keepdims=True)
    return rate * (scaled - first - unit * second)


def row_sums(values):
    rows, columns = values.shape
    return jnp.sum(values.reshape(rows // 8, 8, columns), axis=0)


def chain_kernel(
    att_ref,
    tok_ref,
    cot_ref,
    live_ref,
    lse_ref,
    mix_ref,
    up_ref,
    down_ref,
    vec_ref,
    bias_up_ref,
    spread_ref,
    out_ref,
    act_ref,
    upr_ref,
    hid_ref,
    pre_ref,
    mixr_ref,
    mixed_ref,
    back_ref,
    delta_ref,
    sum_ref,
    sum_up_ref,
    slope_ref,
):
    width = up_ref.shape[1]
    bias_mix, bias_down = vec_ref[0:1], vec_ref[1:2]
    gain_one, shift_one = vec_ref[2:3], vec_ref[3:4]
    gain_two, shift_two = vec_ref[4:5], vec_ref[5:6]

    @pl.when(pl.program_id(0) == 0)
    def _():
        sum_ref[...] = jnp.zeros_like(sum_ref)
        sum_up_ref[...] = jnp.zeros_like(sum_up_ref)

    attended = att_ref[...]
    mixed = plain_product(attended, mix_ref[...]) + bias_mix + tok_ref[...].astype(jnp.float32)
    unit_one, rate_one = normalised(mixed)
    hidden = unit_one * gain_one + shift_one
    hidden_rounded = hidden.astype(jnp.bfloat16)
    hid_ref[...] = hidden_rounded
    down_sum = bias_down + hidden
    for f in range(0, width, FCHUNK):
        up_sum = plain_product(hidden_rounded, up_ref[:, f : f + FCHUNK]) + (
            bias_up_ref[0:1, f : f + FCHUNK]
        )
        active, slope = gelu_terms(up_sum)
        active = active.astype(jnp.bfloat16)
        act_ref[:, f : f + FCHUNK] = active
        slope_ref[:, f : f + FCHUNK] = slope
        down_sum = down_sum + plain_product(active, down_ref[f : f + FCHUNK, :])
    unit_two, rate_two = normalised(down_sum)
    out_ref[...] = (unit_two * gain_two + shift_two).astype(jnp.bfloat16)
    cot = cot_ref[...].astype(jnp.float32)
    back_pre = norm_back(cot * gain_two, unit_two, rate_two)
    pre_rounded = back_pre.astype(jnp.bfloat16)
    pre_ref[...] = pre_rounded
    sum_ref[4] += row_sums(cot * unit_two)
    sum_ref[5] += row_sums(cot)
    sum_ref[1] += row_sums(back_pre)
    back_hidden = back_pre
    for f in range(0, width, FCHUNK):
        back_up = back_product(pre_rounded, down_ref[f : f + FCHUNK, :]) * (
            slope_ref[:, f : f + FCHUNK]
        )
        sum_up_ref[:, f : f + FCHUNK] += row_sums(back_up)
        up_rounded = back_up.astype(jnp.bfloat16)
        upr_ref[:, f : f + FCHUNK] = up_rounded
        back_hidden = back_hidden + back_product(up_rounded, up_ref[:, f : f + FCHUNK])
    sum_ref[2] += row_sums(back_hidden * unit_one)
    sum_ref[3] += row_sums(back_hidden)
    back_mixed = norm_back(back_hidden * gain_one, unit_one, rate_one)
    sum_ref[0] += row_sums(back_mixed)
    mixed_ref[...] = back_mixed
    mixed_rounded = back_mixed.astype(jnp.bfloat16)
    mixr_ref[...] = mixed_rounded
    back = back_product(mixed_rounded, mix_ref[...]).astype(jnp.bfloat16)
    back = jnp.where(live_ref[...] > 0.5, back, jnp.zeros_like(back))
    back_ref[:, : back.shape[1]] = back
    terms = back.astype(jnp.float32) * attended.astype(jnp.float32)
    high = terms.astype(jnp.bfloat16)
    low = (terms - high.astype(jnp.float32)).astype(jnp.bfloat16)
    delta = plain_product(high, spread_ref[...]) + plain_product(low, spread_ref[...])
    delta_ref[...] = delta
    lane = lax.broadcasted_iota(jnp.int32, delta.shape, 1)
    term = lane % TERMS
    whole = jnp.where(term < 3, lse_ref[...], delta)
    first = whole.astype(jnp.bfloat16)
    rest = whole - first.astype(jnp.float32)
    second = rest.astype(jnp.bfloat16)
    third = (rest - second.astype(jnp.float32)).astype(jnp.bfloat16)
    picked = jnp.where(
        (term == 0) | (term == 3),
        first.astype(jnp.float32),
        jnp.where((term == 2), third.astype(jnp.float32), second.astype(jnp.float32)),
    )
    picked = jnp.where(lane < TERMS * HEADS, picked, 0.0)
    back_ref[:, back.shape[1] :] = picked.astype(jnp.bfloat16)


def chain_call(att, tok, cot, live, lse, mix, up, down, vectors, bias_up):
    rows, width = tok.shape
    wide = up.shape[1]
    head_of = jnp.arange(width, dtype=jnp.int32)[:, None] // HD
    spread = (head_of == jnp.arange(2 * HD, dtype=jnp.int32)[None, :] // TERMS).astype(jnp.bfloat16)

    def tile(columns):
        return pl.BlockSpec((RTILE, columns), lambda i: (i, 0))

    def fixed(*shape):
        return pl.BlockSpec(shape, lambda i: (0,) * len(shape))

    bf16, f32 = jnp.bfloat16, jnp.float32
    return pl.pallas_call(
        chain_kernel,
        grid=(rows // RTILE,),
        in_specs=[
            tile(width),
            tile(width),
            tile(width),
            tile(1),
            tile(2 * HD),
            fixed(*mix.shape),
            fixed(*up.shape),
            fixed(*down.shape),
            fixed(*vectors.shape),
            fixed(*bias_up.shape),
            fixed(*spread.shape),
        ],
        out_specs=[
            tile(width),
            tile(wide),
            tile(wide),
            tile(width),
            tile(width),
            tile(width),
            tile(width),
            tile(width + 2 * HD),
            tile(2 * HD),
            fixed(6, 8, width),
            fixed(8, wide),
        ],
        out_shape=[
            jax.ShapeDtypeStruct((rows, width), bf16),
            jax.ShapeDtypeStruct((rows, wide), bf16),
            jax.ShapeDtypeStruct((rows, wide), bf16),
            jax.ShapeDtypeStruct((rows, width), bf16),
            jax.ShapeDtypeStruct((rows, width), bf16),
            jax.ShapeDtypeStruct((rows, width), bf16),
            jax.ShapeDtypeStruct((rows, width), f32),
            jax.ShapeDtypeStruct((rows, width + 2 * HD), bf16),
            jax.ShapeDtypeStruct((rows, 2 * HD), f32),
            jax.ShapeDtypeStruct((6, 8, width), f32),
            jax.ShapeDtypeStruct((8, wide), f32),
        ],
        scratch_shapes=[pltpu.VMEM((RTILE, wide), f32)],
        cost_estimate=work(44),
        compiler_params=pltpu.CompilerParams(vmem_limit_bytes=VMEM_LIMIT),
    )(att, tok, cot, live, lse, mix, up, down, vectors, bias_up, spread)


def weight_kernel(n_dp, core_ref, act, pre, hid, upr, att, mixr, small, *refs):
    send, keep, tmp = refs[-3:]
    step = pl.program_id(0)
    core = core_ref[0]
    pieces = FF // D
    down_rows = FF // n_dp
    part_rows = D // n_dp

    def put(x, row, rows, begin):
        mine = pl.multiple_of(begin + core * rows, 16)
        other = pl.multiple_of(begin + (1 - core) * rows, 16)
        keep[pl.ds(x, 1), pl.ds(row, rows), :] = tmp[pl.ds(mine, rows), :][None]
        send[pl.ds(x, 1), pl.ds(row, rows), :] = tmp[pl.ds(other, rows), :][None]

    @pl.when(step < pieces)
    def _():
        tmp[...] = outer_sum(act[...], pre[...]).astype(jnp.bfloat16)
        per = D // down_rows
        for b in range(per):
            block = step * per + b
            x = block // 2
            rows = tmp[b * down_rows : (b + 1) * down_rows, :]

            @pl.when(lax.rem(block, 2) == core)
            def _():
                keep[pl.ds(x, 1), 0:down_rows, :] = rows[None]

            @pl.when(lax.rem(block, 2) != core)
            def _():
                send[pl.ds(x, 1), 0:down_rows, :] = rows[None]

    @pl.when((step >= pieces) & (step < 2 * pieces))
    def _():
        tmp[...] = outer_sum(hid[...], upr[...]).astype(jnp.bfloat16)
        row = pl.multiple_of(down_rows + (step - pieces) * part_rows, 16)
        for x in range(n_dp // 2):
            put(x, row, part_rows, 2 * x * part_rows)

    @pl.when(step == 2 * pieces)
    def _():
        tmp[...] = outer_sum(att[...], mixr[...]).astype(jnp.bfloat16)
        row = down_rows + pieces * part_rows
        for x in range(n_dp // 2):
            put(x, row, part_rows, 2 * x * part_rows)
            last = row + part_rows
            rows = keep.shape[1] - last
            keep[x, last:, :] = small[pl.ds(2 * x + core, 1), :, :][0]
            send[x, last:, :] = small[pl.ds(2 * x + 1 - core, 1), :, :][0]


def weight_call(n_dp, core, act, pre, hid, upr, att, mixr, small, *needs):
    rows = act.shape[0]
    pieces = FF // D
    out_rows = FF // n_dp + (pieces + 1) * (D // n_dp) + small.shape[1]

    def fixed(*shape):
        return pl.BlockSpec(shape, lambda i, c: (0,) * len(shape))

    def stepped(first):
        return pl.BlockSpec((rows, D), lambda i, c: (0, jnp.clip(i - first, 0, pieces - 1)))

    shape = (n_dp // 2, out_rows, D)
    return pl.pallas_call(
        functools.partial(weight_kernel, n_dp),
        out_shape=[jax.ShapeDtypeStruct(shape, jnp.bfloat16)] * 2,
        grid_spec=pltpu.PrefetchScalarGridSpec(
            num_scalar_prefetch=1,
            grid=(2 * pieces + 1,),
            in_specs=[
                stepped(0),
                fixed(rows, D),
                fixed(rows, D),
                stepped(pieces),
                fixed(rows, D),
                fixed(rows, D),
                fixed(*small.shape),
            ]
            + [UNREAD] * len(needs),
            out_specs=[fixed(*shape)] * 2,
            scratch_shapes=[pltpu.VMEM((D, D), jnp.bfloat16)],
        ),
        cost_estimate=work(22),
        compiler_params=pltpu.CompilerParams(vmem_limit_bytes=VMEM_LIMIT),
    )(core, act, pre, hid, upr, att, mixr, small, *needs)


def outer_kernel(n_dp, core_ref, tokens, columns, *refs):
    send, keep, tmp = refs[-3:]
    core = core_ref[0]
    rows = tokens.shape[1] // n_dp
    tmp[...] = outer_sum(tokens[...], columns[...]).astype(tmp.dtype)
    for x in range(n_dp // 2):
        mine = pl.multiple_of((2 * x + core) * rows, 16)
        other = pl.multiple_of((2 * x + 1 - core) * rows, 16)
        keep[x] = tmp[pl.ds(mine, rows), :]
        send[x] = tmp[pl.ds(other, rows), :]


def outer_split(n_dp, core, tokens, columns, first, block, *needs):
    rows, depth = tokens.shape
    steps = columns.shape[1] // block - first
    shape = (n_dp // 2, depth // n_dp, block * steps)
    out = pl.BlockSpec(shape[:2] + (block,), lambda i, c: (0, 0, i))
    return pl.pallas_call(
        functools.partial(outer_kernel, n_dp),
        out_shape=[jax.ShapeDtypeStruct(shape, jnp.bfloat16)] * 2,
        grid_spec=pltpu.PrefetchScalarGridSpec(
            num_scalar_prefetch=1,
            grid=(steps,),
            in_specs=[
                pl.BlockSpec((rows, depth), lambda i, c: (0, 0)),
                pl.BlockSpec((rows, block), lambda i, c: (0, first + i)),
            ]
            + [UNREAD] * len(needs),
            out_specs=[out, out],
            scratch_shapes=[pltpu.VMEM((depth, block), jnp.bfloat16)],
        ),
        cost_estimate=work(4),
        compiler_params=plain_params(),
    )(core, tokens, columns, *needs)


def swap(value, axis, bit):
    devices = lax.axis_size(axis)
    return lax.ppermute(value, axis, [(i, i ^ bit) for i in range(devices)])


def dp_gather(shard, dp_rank):
    blocks = shard[None]
    bit = lax.axis_size("dp") // 2
    while bit >= 1:
        got = swap(blocks, "dp", bit)
        high = ((dp_rank // bit) % 2) == 1
        first = jnp.where(high, got, blocks)
        second = jnp.where(high, blocks, got)
        blocks = jnp.stack([first, second], axis=1).reshape((-1,) + shard.shape)
        bit //= 2
    return blocks.reshape((-1,) + shard.shape[1:])


def work(microseconds):
    return pl.CostEstimate(
        flops=int(microseconds * 0.4e9), transcendentals=0, bytes_accessed=1 << 20
    )


def row_tile(rows, limit=512):
    for size in range(min(rows, limit), 15, -1):
        if rows % size == 0 and size % 16 == 0:
            return size
    return rows


def plain_params():
    return pltpu.CompilerParams(vmem_limit_bytes=VMEM_LIMIT)


def split_add_kernel(which, keep_mine, got_mine, keep_other, got_other, *refs):
    mine, other = refs[-2:]
    mine[...] = (keep_mine[...].astype(jnp.float32) + got_mine[...].astype(jnp.float32)).astype(
        mine.dtype
    )
    other[...] = (keep_other[...].astype(jnp.float32) + got_other[...].astype(jnp.float32)).astype(
        other.dtype
    )


def split_add(keep, got, which, *needs):
    blocks, rows, columns = keep.shape
    tile = row_tile(rows)

    def spec(flip):
        def place(b, i, w):
            bit = 1 - w[0] if flip else w[0]
            return 2 * b + bit, i, 0

        return pl.BlockSpec((1, tile, columns), place)

    out = pl.BlockSpec((1, tile, columns), lambda b, i, w: (b, i, 0))
    shape = jax.ShapeDtypeStruct((blocks // 2, rows, columns), keep.dtype)
    return pl.pallas_call(
        split_add_kernel,
        out_shape=[shape, shape],
        grid_spec=pltpu.PrefetchScalarGridSpec(
            num_scalar_prefetch=1,
            grid=(blocks // 2, rows // tile),
            in_specs=[spec(False), spec(False), spec(True), spec(True)] + [UNREAD] * len(needs),
            out_specs=[out, out],
        ),
        cost_estimate=work(4),
        compiler_params=plain_params(),
    )(which, keep, got, keep, got, *needs)


def add_kernel(left, right, *refs):
    out = refs[-1]
    out[...] = (left[0].astype(jnp.float32) + right[0].astype(jnp.float32)).astype(out.dtype)


def add_blocks(left, right, *needs):
    _, rows, columns = left.shape
    tile = row_tile(rows)
    spec = pl.BlockSpec((1, tile, columns), lambda i: (0, i, 0))
    return pl.pallas_call(
        add_kernel,
        grid=(rows // tile,),
        in_specs=[spec, spec] + [UNREAD] * len(needs),
        out_specs=pl.BlockSpec((tile, columns), lambda i: (i, 0)),
        cost_estimate=work(3),
        out_shape=jax.ShapeDtypeStruct((rows, columns), left.dtype),
        compiler_params=plain_params(),
    )(left, right, *needs)


def pieces_kernel(pieces, *refs):
    out = refs[-1]
    total = pieces[0].astype(jnp.float32)
    for i in range(1, pieces.shape[0]):
        total = total + pieces[i].astype(jnp.float32)
    total = total.astype(out.dtype)
    for i in range(out.shape[0]):
        out[i] = total


def summed_copies(pieces, copies, *needs):
    _, rows, columns = pieces.shape
    return pl.pallas_call(
        pieces_kernel,
        in_specs=[pl.BlockSpec(memory_space=pltpu.VMEM)] + [UNREAD] * len(needs),
        out_specs=pl.BlockSpec(memory_space=pltpu.VMEM),
        out_shape=jax.ShapeDtypeStruct((copies, rows, columns), pieces.dtype),
        cost_estimate=work(2),
        compiler_params=plain_params(),
    )(pieces, *needs)


def two_pieces_kernel(left, right, *refs):
    out = refs[-1]
    at = 0
    for pieces in (left, right):
        total = pieces[0].astype(jnp.float32)
        for i in range(1, pieces.shape[0]):
            total = total + pieces[i].astype(jnp.float32)
        total = total.astype(out.dtype)
        for i in range(out.shape[0]):
            out[i, :, at : at + pieces.shape[2]] = total
        at += pieces.shape[2]


def summed_two(left, right, copies, *needs):
    _, rows, columns = left.shape
    shape = (copies, rows, columns + right.shape[2])
    return pl.pallas_call(
        two_pieces_kernel,
        in_specs=[pl.BlockSpec(memory_space=pltpu.VMEM)] * 2 + [UNREAD] * len(needs),
        out_specs=pl.BlockSpec(memory_space=pltpu.VMEM),
        out_shape=jax.ShapeDtypeStruct(shape, left.dtype),
        cost_estimate=work(2),
        compiler_params=plain_params(),
    )(left, right, *needs)


def gate_kernel(value, *refs):
    refs[-1][...] = value[...]


def gated(value, *needs):
    return pl.pallas_call(
        gate_kernel,
        in_specs=[pl.BlockSpec(memory_space=pltpu.VMEM)] + [UNREAD] * len(needs),
        out_specs=pl.BlockSpec(memory_space=pltpu.VMEM),
        out_shape=jax.ShapeDtypeStruct(value.shape, value.dtype),
        cost_estimate=work(1),
        compiler_params=plain_params(),
    )(value, *needs)


def cluster_ids(group_order, own_start, span):
    padded = jnp.pad(group_order, ((0, 0), (HALO, HALO)), constant_values=-(1 << 24))
    wanted = lax.dynamic_slice_in_dim(padded, own_start, span, 1) - (own_start - HALO)
    tile_of = wanted >> 7
    lane_of_token = wanted & (CL - 1)
    cluster = (jnp.arange(span, dtype=jnp.int32) >> 7) + 1
    tile_hot = jnp.where(
        tile_of[:, :, None] == jnp.arange(span // CL, dtype=jnp.int32), cluster[None, :, None], 0
    ).astype(jnp.bfloat16)
    lane_hot = (lane_of_token[:, :, None] == jnp.arange(CL, dtype=jnp.int32)).astype(jnp.bfloat16)
    table = jnp.einsum("hpt,hpl->htl", tile_hot, lane_hot, preferred_element_type=jnp.float32)
    return table.reshape(HEADS, span) - 1.0


def on_device(
    tokens,
    input_weight,
    output_weight,
    up_weight,
    down_weight,
    output_bias,
    up_bias,
    down_bias,
    first_gain,
    first_shift,
    second_gain,
    second_shift,
    document_runs,
    document_trim,
    cluster_order,
    cotangent,
):
    bf16, f32 = jnp.bfloat16, jnp.float32
    n_dp = lax.axis_size("dp")
    n_seq = lax.axis_size("seq")
    dp_rank = lax.axis_index("dp")
    seq_rank = lax.axis_index("seq")
    inputs = tokens[0]
    tok_dev = inputs.shape[0]
    tiles = tok_dev // CL
    span = tok_dev + 2 * HALO
    own_start = seq_rank * tok_dev

    token_parts = halo_parts(inputs)
    n_parts = len(token_parts)

    weight_in = lax.all_gather(input_weight, "dp", axis=0, tiled=True)
    weight_up = lax.all_gather(up_weight, "dp", axis=0, tiled=True)
    weight_down = lax.all_gather(down_weight, "dp", axis=0, tiled=True)

    runs = document_runs[0]
    first_cluster = jnp.cumsum(runs) - runs
    own_clusters = seq_rank * tiles + jnp.arange(tiles, dtype=jnp.int32)
    doc_start = jnp.max(
        jnp.where(first_cluster[None, :] <= own_clusters[:, None], first_cluster[None, :], 0), axis=1
    )
    starts = (doc_start - seq_rank * tiles + (MOSTB - 1)).astype(jnp.int32)
    near_left = HALO // CL - tiles
    near = near_left + 2 * tiles * jnp.stack([1 - seq_rank % 2, seq_rank % 2])
    starts = jnp.concatenate([starts, near.astype(jnp.int32)])

    cids = cluster_ids(cluster_order[0], own_start, span)
    positions = own_start - HALO + jnp.arange(span, dtype=jnp.int32)
    live = live_tokens(runs, document_trim[0], positions)
    usable = live[None, :] & (cids >= 0.0)
    key_ids = jnp.where(usable, cids, -1.0).reshape(PAIRS, 2, span)
    query_ids = jnp.where(usable, cids, -2.0).reshape(PAIRS, 2, span)
    own_live = live[HALO : HALO + tok_dev, None].astype(f32)

    own = plain_product(inputs, weight_in).astype(bf16)
    groups = HEADS // PACK
    group_lanes = PACK * HD
    kv_weight = (
        weight_in[:, D:]
        .reshape(D, 2, PAIRS, 2 * HD)
        .transpose(0, 2, 1, 3)
        .reshape(D, 2 * D)
    )
    around = project_call(token_parts[:2] + token_parts[3:], weight_in, kv_weight)
    projected = [*around[:2], own, *around[2:]]
    vectors = [
        output_bias,
        down_bias,
        first_gain,
        first_shift,
        second_gain,
        second_shift,
        up_bias,
    ]
    mix_rows = output_weight.shape[0]
    packed = jnp.concatenate(vectors)
    pad_rows = -(-packed.shape[0] // (16 * D)) * 16
    packed = jnp.pad(packed, (0, pad_rows * D - packed.shape[0])).reshape(pad_rows, D)
    mix_shard = gated(jnp.concatenate([output_weight, packed], 0), own)
    mix_all = dp_gather(mix_shard, dp_rank)
    mix_all = mix_all.reshape(n_dp, mix_rows + pad_rows, D)
    weight_mix = mix_all[:, :mix_rows].reshape(D, D)
    small_all = mix_all[:, mix_rows:].reshape(n_dp, -1).astype(f32)
    vec = small_all[:, : 6 * mix_rows].reshape(n_dp, 6, mix_rows).transpose(1, 0, 2).reshape(6, D)
    vec = jnp.pad(vec, ((0, 2), (0, 0)))
    up_part = up_bias.shape[0]
    bias_up = small_all[:, 6 * mix_rows : 6 * mix_rows + up_part].reshape(1, FF)
    bias_up = jnp.pad(bias_up, ((0, 7), (0, 0)))
    heights = [part.shape[0] for part in token_parts]

    groups = HEADS // PACK
    group_lanes = PACK * HD
    group_key_ids = key_ids.reshape(groups, PACK, span)
    group_query_ids = query_ids.reshape(groups, PACK, span)
    group_scratch = pltpu.VMEM((span, group_lanes), bf16)

    def group_parts(third, first):
        return [lane_block(rows, third * groups + first, PACK) for rows in heights]

    steps = tiles // TILES_AT_ONCE
    step_rows = TILES_AT_ONCE * CL

    def of_group(rows, first):
        return pl.BlockSpec((rows, group_lanes), lambda g, t, starts: (0, first + g))

    def ids_of_group():
        return pl.BlockSpec((1, PACK, span), lambda g, t, starts: (g, 0, 0))

    step_block = pl.BlockSpec((step_rows, group_lanes), lambda g, t, starts: (t, g))
    whole_lanes = pl.BlockSpec((tok_dev, 2 * HD), lambda g, t, starts: (0, 0))
    attended, lse, rate, probs = strip_call(
        functools.partial(attend_kernel, tiles, n_parts),
        52,
        (groups, steps),
        [step_block]
        + [of_group(rows, groups) for rows in heights]
        + [of_group(rows, 2 * groups) for rows in heights]
        + [ids_of_group(), ids_of_group()],
        [
            step_block,
            whole_lanes,
            whole_lanes,
            pl.BlockSpec(
                (1, TILES_AT_ONCE, PACK * CL, WINDOW), lambda g, t, starts: (g, t, 0, 0)
            ),
        ],
        [
            jax.ShapeDtypeStruct((tok_dev, D), bf16),
            jax.ShapeDtypeStruct((tok_dev, 2 * HD), f32),
            jax.ShapeDtypeStruct((tok_dev, 2 * HD), f32),
            jax.ShapeDtypeStruct((groups, tiles, PACK * CL, WINDOW), bf16),
        ],
        [group_scratch, group_scratch]
        + [pltpu.VMEM((PACK * CL, WINDOW), f32)] * TILES_AT_ONCE
        + [pltpu.VMEM((PACK * CL, CL), f32)] * TILES_AT_ONCE,
        (starts, own, *projected, *projected, group_query_ids, group_key_ids),
    )

    (
        result,
        active,
        up_rounded,
        hidden_rounded,
        pre_rounded,
        mixed_rounded,
        back_mixed,
        back_own,
        delta,
        sums,
        sums_up,
    ) = chain_call(
        attended,
        inputs,
        cotangent[0],
        own_live,
        lse,
        weight_mix,
        weight_up,
        weight_down,
        vec,
        bias_up,
    )
    back_parts = halo_parts(back_own)

    small = jnp.concatenate(
        [
            jnp.sum(sums, axis=1).reshape(6, n_dp, mix_rows).transpose(1, 0, 2).reshape(n_dp, -1),
            jnp.sum(sums_up, axis=0).reshape(n_dp, -1),
        ],
        axis=1,
    ).astype(bf16)
    unit = 8 * n_seq
    fixed_rows = FF // n_dp + (FF // D + 1) * (D // n_dp)
    small_rows = -(-(fixed_rows + -(-small.shape[1] // D)) // unit) * unit - fixed_rows
    small = jnp.pad(small, ((0, 0), (0, small_rows * D - small.shape[1])))
    small = small.reshape(n_dp, small_rows, D)
    core = (dp_rank % 2).astype(jnp.int32)
    def query_strip(first, *needs):
        buffer = needs[:1] if first > 0 else ()

        def parts(third):
            return [
                pl.BlockSpec(
                    (rows, group_lanes), lambda t, starts: (0, third * groups + first)
                )
                for rows in heights
            ]

        block = pl.BlockSpec((step_rows, group_lanes), lambda t, starts: (t, first))
        lanes = pl.BlockSpec((step_rows, 2 * HD), lambda t, starts: (t, 0))
        in_specs = (
            parts(1)
            + parts(2)
            + [
                block,
                pl.BlockSpec(
                    (1, TILES_AT_ONCE, PACK * CL, WINDOW), lambda t, starts: (first, t, 0, 0)
                ),
                lanes,
                lanes,
            ]
            + [UNREAD] * len(needs)
        )
        return strip_call(
            functools.partial(query_kernel, tiles, n_parts, first * PACK),
            16,
            (steps,),
            in_specs,
            block,
            jax.ShapeDtypeStruct((tok_dev, D), bf16),
            [group_scratch, group_scratch],
            (starts, *projected, *projected, back_own, probs, rate, delta, *needs),
            {len(in_specs) + 1 - len(needs): 0} if buffer else None,
        )

    pair_scratch = pltpu.VMEM((span, 4 * HD), bf16)

    def key_strip(pair, pairs, *needs):
        buffer = needs[:1] if pair > 0 else ()

        def parts(third):
            return [lane_block(rows, third * PAIRS + pair) for rows in heights]

        in_specs = (
            [lane_block(tok_dev, PAIRS + pair), lane_block(tok_dev, 2 * PAIRS + pair)]
            + parts(0)
            + parts(0)
            + [fixed_lanes(rows, PAIRS) for rows in heights]
            + [row_block(span, pair), row_block(span, pair)]
            + [UNREAD] * len(needs)
        )
        return strip_call(
            functools.partial(key_kernel, tiles, n_parts, pair),
            13 * pairs,
            (pairs,),
            in_specs,
            lane_block(tok_dev, pair, 4),
            jax.ShapeDtypeStruct((tok_dev, 2 * D), bf16),
            [pair_scratch, pair_scratch],
            (
                starts,
                own,
                own,
                *projected,
                *back_parts,
                *back_parts,
                query_ids,
                key_ids,
                *needs,
            ),
            {len(in_specs) + 1 - len(needs): 0} if buffer else None,
        )

    def scatter(share):
        rows, columns = share.shape
        return lax.all_to_all(
            share.reshape(n_seq, rows // n_seq, columns), "seq", split_axis=0, concat_axis=0
        )

    def everyone(copies):
        got = lax.all_to_all(copies, "seq", split_axis=0, concat_axis=0)
        return got.reshape(-1, copies.shape[-1])

    def first_split(keep, got, *needs):
        bit = 2
        while True:
            which = ((dp_rank // bit) % 2).astype(jnp.int32).reshape(1)
            mine, other = split_add(keep, got, which, *needs)
            got = swap(other, "dp", bit)
            if mine.shape[0] == 1:
                return mine, got
            keep, bit, needs = mine, bit * 2, ()

    def core_split(grad):
        rows, columns = grad.shape
        blocks = grad.astype(bf16).reshape(n_dp // 2, 2, rows // n_dp, columns)
        return (
            lax.dynamic_index_in_dim(blocks, 1 - core, 1, keepdims=False),
            lax.dynamic_index_in_dim(blocks, core, 1, keepdims=False),
        )

    send, keep = weight_call(
        n_dp,
        core.reshape(1),
        active,
        pre_rounded,
        hidden_rounded,
        up_rounded,
        attended,
        mixed_rounded,
        small,
    )
    core_got = swap(send, "dp", 1)
    back_q = query_strip(0, send)
    mine, x_got = first_split(keep, core_got, back_q)
    back_q = query_strip(1, back_q, mine)
    back_q = query_strip(2, back_q)
    back_kv = key_strip(0, 1, back_q)
    share = add_blocks(mine, x_got, back_kv)
    pieces = scatter(share)
    back_kv = key_strip(1, 2, back_kv, share)
    cut = PAIRS // 2 * 4 * HD
    early_cols = jnp.concatenate([back_q, back_kv[:, :cut]], axis=1)
    early_send, early_keep = core_split(outer_sum(inputs, early_cols))
    early_core = swap(early_send, "dp", 1)
    back_kv = key_strip(3, 1, back_kv, early_send)
    early_mine, early_got = first_split(early_keep, early_core, back_kv)
    back_kv = key_strip(4, 1, back_kv, early_mine)
    copies = summed_copies(pieces, 1, back_kv)
    back_kv = key_strip(5, 1, back_kv, copies)
    early_share = add_blocks(early_mine, early_got, back_kv)
    all_sums = lax.all_gather(copies[0], "seq", axis=0, tiled=True)
    late_send, late_keep = outer_split(
        n_dp, core.reshape(1), inputs, back_kv, 1, cut, early_share
    )
    late_mine, late_got = first_split(late_keep, swap(late_send, "dp", 1))
    late_share = add_blocks(late_mine, late_got)
    early_pieces, late_pieces = scatter(early_share), scatter(late_share)
    in_all = everyone(summed_two(early_pieces, late_pieces, n_seq, all_sums))

    input_grad = (
        back_mixed + back_product(back_q, weight_in[:, :D]) + back_product(back_kv, kv_weight)
    )
    kv_all = in_all[:, D:].reshape(-1, PAIRS, 2, 2 * HD).transpose(0, 2, 1, 3)
    grad_in_total = jnp.concatenate([in_all[:, :D], kv_all.reshape(-1, 2 * D)], axis=1).astype(f32)
    down_rows = FF // n_dp
    part_rows = D // n_dp
    grad_down = all_sums[:down_rows].astype(f32)
    grad_up = (
        all_sums[down_rows : down_rows + (FF // D) * part_rows]
        .reshape(FF // D, part_rows, D)
        .transpose(1, 0, 2)
        .reshape(part_rows, FF)
        .astype(f32)
    )
    at = down_rows + (FF // D) * part_rows
    grad_mix = all_sums[at : at + part_rows].astype(f32)
    flat = all_sums[at + part_rows :].reshape(-1).astype(f32)
    vectors_out = [flat[i * part_rows : (i + 1) * part_rows] for i in range(6)]
    bias_up_out = flat[6 * part_rows : 6 * part_rows + down_rows]
    return (
        result[None],
        input_grad[None],
        grad_in_total,
        grad_mix,
        grad_up,
        grad_down,
        vectors_out[0],
        bias_up_out,
        vectors_out[1],
        *vectors_out[2:],
    )


def solution(mesh):
    placed = (
        P("dp", "seq", None),
        P("dp", None),
        P("dp", None),
        P("dp", None),
        P("dp", None),
        P("dp"),
        P("dp"),
        P("dp"),
        P("dp"),
        P("dp"),
        P("dp"),
        P("dp"),
        P("dp", None),
        P("dp", None),
        P("dp", None, None),
        P("dp", "seq", None),
    )
    return jax.shard_map(
        on_device,
        mesh=mesh,
        in_specs=placed,
        out_specs=(
            P("dp", "seq", None),
            P("dp", "seq", None),
            P("dp", None),
            P("dp", None),
            P("dp", None),
            P("dp", None),
            P("dp"),
            P("dp"),
            P("dp"),
            P("dp"),
            P("dp"),
            P("dp"),
            P("dp"),
        ),
        check_vma=False,
    )
```

```python
import functools

import jax
import jax.numpy as jnp
from jax import lax
from jax.experimental import pallas as pl
from jax.experimental.pallas import tpu as pltpu
from jax.sharding import PartitionSpec as P

D = 768
HEADS = 12
HD = 64
CL = 128
MOSTB = 16
PAIRS = HEADS // 2
WINDOW = MOSTB * CL
HALO = (MOSTB - 1) * CL
CHUNK = 1024
KCHUNK = 1024
TILES_AT_ONCE = 2
PACK = 4
NEG = -1e30
TERMS = 5
FF = 3072
RTILE = 256
FCHUNK = 768
SCALE2 = HD ** (-0.5) * 1.4426950408889634

EPSILON = 1e-05


def shifted(value, axis, by):
    devices = lax.axis_size(axis)
    pairs = [(i, i + by) for i in range(devices) if 0 <= i + by < devices]
    return lax.ppermute(value, axis, pairs)


def halo_parts(value):
    own = value.shape[0]
    far = HALO - own
    devices = lax.axis_size("seq")
    assert 0 < far <= own and devices % 2 == 0
    partner = lax.ppermute(value, "seq", [(i, i ^ 1) for i in range(devices)])
    pairs = [(i, i - 1 if i % 2 == 0 else i + 1) for i in range(devices)]
    other = lax.ppermute(value, "seq", [(i, k) for i, k in pairs if 0 <= k < devices])
    before = shifted(value[own - far :], "seq", 2)
    following = shifted(value[:far], "seq", -2)
    return [before, partner, value, other, following]


def places(starts, tiles, parts):
    far, own = parts[0].shape[0], parts[2].shape[0]
    return [
        0,
        pl.multiple_of(starts[tiles] * CL, CL),
        far + own,
        pl.multiple_of(starts[tiles + 1] * CL, CL),
        far + 3 * own,
    ]


def live_tokens(runs, trim, positions):
    ends = jnp.cumsum(runs) * CL
    starts = ends - runs * CL
    lengths = runs * CL - trim
    inside = (positions[..., None] >= starts) & (positions[..., None] < starts + lengths)
    return jnp.any(inside, axis=-1)


def outer_sum(left, right):
    return lax.dot_general(
        left, right, (((0,), (0,)), ((), ())), preferred_element_type=jnp.float32
    )


def back_product(left, right):
    return lax.dot_general(
        left, right, (((1,), (1,)), ((), ())), preferred_element_type=jnp.float32
    )


def plain_product(left, right):
    return jnp.dot(left, right, preferred_element_type=jnp.float32)


def stacked(tile):
    lane = lax.broadcasted_iota(jnp.int32, tile.shape, 1)
    zero = jnp.zeros_like(tile)
    heads = tile.shape[1] // HD
    return jnp.concatenate(
        [
            jnp.where((lane >= h * HD) & (lane < (h + 1) * HD), tile, zero)
            for h in range(heads)
        ],
        axis=0,
    )


def unstacked(stack):
    heads = stack.shape[1] // HD
    lane = lax.broadcasted_iota(jnp.int32, (CL, heads * HD), 1)
    result = stack[:CL]
    for h in range(1, heads):
        result = jnp.where(lane >= h * HD, stack[h * CL : (h + 1) * CL], result)
    return result


def as_column(row):
    return jnp.broadcast_to(row, (CL, CL)).T


def lane_of(tile, lane):
    lanes = lax.broadcasted_iota(jnp.int32, tile.shape, 1)
    return jnp.sum(jnp.where(lanes == lane, tile, 0.0), axis=1, keepdims=True)


def masked(scores, cols, row_ref, begin):
    parts = []
    wide = scores.shape[1]
    for half, one in enumerate(cols):
        row = row_ref[0, half : half + 1, pl.ds(begin, wide)]
        block = scores[half * CL : (half + 1) * CL]
        col = jnp.concatenate([one] * (wide // CL), axis=1)
        parts.append(jnp.where(col == row, block, NEG))
    return jnp.concatenate(parts, axis=0)


def assemble(parts, offsets, whole):
    for part, at in zip(parts, offsets):
        whole[pl.ds(at, part.shape[0]), :] = part[...]


def ahead(steps, produce, consume):
    held = produce(*steps[0])
    for i, step in enumerate(steps):
        following = produce(*steps[i + 1]) if i + 1 < len(steps) else None
        consume(*step, held)
        held = following


def attend_kernel(tiles, n_parts, starts, q_ref, *refs):
    k_parts, refs = refs[:n_parts], refs[n_parts:]
    v_parts, refs = refs[:n_parts], refs[n_parts:]
    qid_ref, kid_ref, out_ref, lse_ref, rate_ref, p_ref, k_ref, v_ref, *slots = refs
    s_refs, top_refs = slots[:TILES_AT_ONCE], slots[TILES_AT_ONCE:]
    group, step = pl.program_id(0), pl.program_id(1)
    heads = q_ref.shape[1] // HD
    chunks = WINDOW // CHUNK

    @pl.when(step == 0)
    def _():
        offsets = places(starts, tiles, k_parts)
        assemble(k_parts, offsets, k_ref)
        assemble(v_parts, offsets, v_ref)

    @pl.when((group == 0) & (step == 0))
    def _():
        lse_ref[...] = jnp.zeros_like(lse_ref)
        rate_ref[...] = jnp.zeros_like(rate_ref)

    def first_half(slot):
        tile = TILES_AT_ONCE * step + slot
        own = pl.multiple_of(HALO + tile * CL, CL)
        return dict(
            begin=pl.multiple_of(starts[tile] * CL, CL),
            query=stacked(q_ref[slot * CL : (slot + 1) * CL, :]),
            cols=[
                as_column(qid_ref[0, half : half + 1, pl.ds(own, CL)]) for half in range(heads)
            ],
        )

    def score(state, slot, j):
        at = pl.multiple_of(state["begin"] + j * CHUNK, CL)
        scores = back_product(state["query"], k_ref[pl.ds(at, CHUNK), :])
        scores = masked(scores, state["cols"], kid_ref, at)
        s_refs[slot][:, j * CHUNK : (j + 1) * CHUNK] = scores
        top = scores[:, :CL]
        for i in range(1, CHUNK // CL):
            top = jnp.maximum(top, scores[:, i * CL : (i + 1) * CL])
        if j > 0:
            top = jnp.maximum(top, top_refs[slot][...])
        top_refs[slot][...] = top

    states = [first_half(0)]
    for j in range(chunks):
        score(states[0], 0, j)
    for slot in range(TILES_AT_ONCE):
        if slot + 1 < TILES_AT_ONCE:
            states.append(first_half(slot + 1))
        state = states[slot]
        peak = jnp.max(top_refs[slot][...], axis=1, keepdims=True)
        total = jnp.zeros((heads * CL, CL), jnp.float32)
        result = jnp.zeros((heads * CL, heads * HD), jnp.float32)
        for j in range(chunks):
            if slot + 1 < TILES_AT_ONCE:
                score(states[slot + 1], slot + 1, j)
            at = pl.multiple_of(state["begin"] + j * CHUNK, CL)
            columns = slice(j * CHUNK, (j + 1) * CHUNK)
            weights = jnp.exp2((s_refs[slot][:, columns] - peak) * SCALE2)
            for i in range(CHUNK // CL):
                total = total + weights[:, i * CL : (i + 1) * CL]
            p_ref[0, slot, :, columns] = weights.astype(jnp.bfloat16)
            result = result + plain_product(
                p_ref[0, slot, :, columns], v_ref[pl.ds(at, CHUNK), :]
            )
        total = jnp.sum(total, axis=1, keepdims=True)
        rate = 1.0 / total
        result = result * rate
        lse = peak + jnp.log(total) * HD**0.5
        live = (state["cols"][0] >= 0.0).astype(jnp.float32)
        live = jnp.concatenate([live] * (heads * HD // CL), axis=1)
        rows = slice(slot * CL, (slot + 1) * CL)
        out_ref[rows, :] = (unstacked(result) * live).astype(jnp.bfloat16)
        here = pl.ds(pl.multiple_of((TILES_AT_ONCE * step + slot) * CL, CL), CL)
        lane = lax.broadcasted_iota(jnp.int32, (CL, CL), 1)
        kept, kept_rate = lse_ref[here, :], rate_ref[here, :]
        for half in range(heads):
            first = (heads * group + half) * TERMS
            inside = (lane >= first) & (lane < first + TERMS)
            part = slice(half * CL, (half + 1) * CL)
            kept = jnp.where(inside, lse[part], kept)
            kept_rate = jnp.where(inside, rate[part], kept_rate)
        lse_ref[here, :] = kept
        rate_ref[here, :] = kept_rate


def query_kernel(tiles, n_parts, first_head, starts, *refs):
    k_parts, refs = refs[:n_parts], refs[n_parts:]
    v_parts, refs = refs[:n_parts], refs[n_parts:]
    g_ref, p_ref, rate_ref, delta_ref = refs[:4]
    out_ref, k_ref, v_ref = refs[-3:]
    step = pl.program_id(0)
    heads = g_ref.shape[1] // HD
    chunks = WINDOW // CHUNK

    @pl.when(step == 0)
    def _():
        offsets = places(starts, tiles, k_parts)
        assemble(k_parts, offsets, k_ref)
        assemble(v_parts, offsets, v_ref)

    states = {}

    def state_of(slot):
        if slot not in states:
            rows = slice(slot * CL, (slot + 1) * CL)
            columns = [
                jnp.concatenate(
                    [lane_of(ref[rows, :], (first_head + half) * TERMS) for half in range(heads)],
                    axis=0,
                )
                for ref in (delta_ref, rate_ref)
            ]
            states[slot] = dict(
                begin=pl.multiple_of(starts[TILES_AT_ONCE * step + slot] * CL, CL),
                back=stacked(g_ref[rows, :]),
                delta=columns[0],
                rate=columns[1],
                result=jnp.zeros((heads * CL, heads * HD), jnp.float32),
            )
        return states[slot]

    def produce(slot, j):
        state = state_of(slot)
        at = pl.multiple_of(state["begin"] + j * CHUNK, CL)
        return back_product(state["back"], v_ref[pl.ds(at, CHUNK), :])

    def consume(slot, j, back_probs):
        state = state_of(slot)
        at = pl.multiple_of(state["begin"] + j * CHUNK, CL)
        weights = p_ref[0, slot, :, j * CHUNK : (j + 1) * CHUNK].astype(jnp.float32)
        back_scores = weights * (back_probs - state["delta"])
        state["result"] = state["result"] + plain_product(
            back_scores.astype(jnp.bfloat16), k_ref[pl.ds(at, CHUNK), :]
        )
        if j == chunks - 1:
            out_ref[slot * CL : (slot + 1) * CL, :] = unstacked(
                state["result"] * (state["rate"] * HD ** (-0.5))
            ).astype(jnp.bfloat16)

    ahead(
        [(slot, j) for slot in range(TILES_AT_ONCE) for j in range(chunks)], produce, consume
    )


def key_kernel(tiles, n_parts, first_pair, starts, k_ref, v_ref, *refs):
    q_parts, refs = refs[:n_parts], refs[n_parts:]
    g_parts, refs = refs[:n_parts], refs[n_parts:]
    a_parts, refs = refs[:n_parts], refs[n_parts:]
    qid_ref, kid_ref = refs[:2]
    out_ref, q_ref, g_ref = refs[-3:]
    pair = first_pair + pl.program_id(0)
    offsets = places(starts, tiles, q_parts)
    for at, q_part, g_part, a_part in zip(offsets, q_parts, g_parts, a_parts):
        rows = pl.ds(at, q_part.shape[0])
        q_ref[rows, : 2 * HD] = q_part[...]
        q_ref[rows, 2 * HD :] = a_part[...]
        g_ref[rows, : 2 * HD] = g_part[...]
        g_ref[rows, 2 * HD :] = a_part[...]

    lane = lax.broadcasted_iota(jnp.int32, (CL, CL), 1)
    lse_pick, delta_pick = [], []
    for half in range(2):
        first = (2 * pair + half) * TERMS
        lse_pick.append(jnp.where((lane >= first) & (lane < first + 3), -1.0, 0.0))
        delta_pick.append(jnp.where((lane >= first + 3) & (lane < first + TERMS), -1.0, 0.0))
    lse_pick = jnp.concatenate(lse_pick, axis=0).astype(jnp.bfloat16)
    delta_pick = jnp.concatenate(delta_pick, axis=0).astype(jnp.bfloat16)

    def some_tiles(step, carry):
        states = {}

        def state_of(slot):
            if slot not in states:
                tile = TILES_AT_ONCE * step + slot
                own = pl.multiple_of(HALO + tile * CL, CL)
                here = pl.multiple_of(tile * CL, CL)
                states[slot] = dict(
                    begin=pl.multiple_of(starts[tile] * CL, CL),
                    here=here,
                    keys=jnp.concatenate([stacked(k_ref[pl.ds(here, CL), :]), lse_pick], axis=1),
                    values=jnp.concatenate(
                        [stacked(v_ref[pl.ds(here, CL), :]), delta_pick], axis=1
                    ),
                    cols=[
                        as_column(kid_ref[0, half : half + 1, pl.ds(own, CL)]) for half in range(2)
                    ],
                    key_sum=jnp.zeros((2 * CL, 2 * HD), jnp.float32),
                    value_sum=jnp.zeros((2 * CL, 2 * HD), jnp.float32),
                )
            return states[slot]

        def produce(slot, j):
            state = state_of(slot)
            at = pl.multiple_of(state["begin"] + j * KCHUNK, CL)
            scores = back_product(state["keys"], q_ref[pl.ds(at, KCHUNK), :])
            return scores, back_product(state["values"], g_ref[pl.ds(at, KCHUNK), :])

        def consume(slot, j, held):
            state = state_of(slot)
            at = pl.multiple_of(state["begin"] + j * KCHUNK, CL)
            scores, back_probs = held
            probs = jnp.exp2(masked(scores * SCALE2, state["cols"], qid_ref, at))
            back_scores = probs * back_probs
            state["value_sum"] = state["value_sum"] + plain_product(
                probs.astype(jnp.bfloat16), g_ref[pl.ds(at, KCHUNK), : 2 * HD]
            )
            state["key_sum"] = state["key_sum"] + plain_product(
                back_scores.astype(jnp.bfloat16), q_ref[pl.ds(at, KCHUNK), : 2 * HD]
            )
            if j == WINDOW // KCHUNK - 1:
                rows = pl.ds(state["here"], CL)
                out_ref[rows, : 2 * HD] = (
                    unstacked(state["key_sum"]) * HD ** (-0.5)
                ).astype(jnp.bfloat16)
                out_ref[rows, 2 * HD :] = unstacked(state["value_sum"]).astype(jnp.bfloat16)

        ahead(
            [(slot, j) for slot in range(TILES_AT_ONCE) for j in range(WINDOW // KCHUNK)],
            produce,
            consume,
        )
        return carry

    lax.fori_loop(0, tiles // TILES_AT_ONCE, some_tiles, 0)


def lane_block(rows, first, heads=2):
    return pl.BlockSpec((rows, heads * HD), lambda pair, starts: (0, first + pair))


def fixed_lanes(rows, block):
    return pl.BlockSpec((rows, 2 * HD), lambda pair, starts: (0, block))


def row_block(columns, first, heads=2):
    return pl.BlockSpec((1, heads, columns), lambda pair, starts: (first + pair, 0, 0))


UNREAD = pl.BlockSpec(memory_space=pl.ANY)


VMEM_LIMIT = 60 * 1024 * 1024


def strip_call(
    kernel, length, grid, in_specs, out_specs, out_shape, scratch, args, aliases=None
):
    return pl.pallas_call(
        kernel,
        out_shape=out_shape,
        grid_spec=pltpu.PrefetchScalarGridSpec(
            num_scalar_prefetch=1,
            grid=grid,
            in_specs=in_specs,
            out_specs=out_specs,
            scratch_shapes=scratch,
        ),
        input_output_aliases=aliases or {},
        cost_estimate=work(length),
        compiler_params=pltpu.CompilerParams(vmem_limit_bytes=VMEM_LIMIT),
    )(*args)


def project_kernel(parts, weight, *refs):
    for source, target in zip(refs[:parts], refs[-parts:]):
        target[...] = plain_product(source[...], weight[...]).astype(target.dtype)


def project_call(parts, weight, *needs):
    depth, columns = weight.shape
    block = PACK * HD
    return pl.pallas_call(
        functools.partial(project_kernel, len(parts)),
        grid=(columns // block,),
        in_specs=[pl.BlockSpec((depth, block), lambda i: (0, i))]
        + [pl.BlockSpec(part.shape, lambda i: (0, 0)) for part in parts]
        + [UNREAD] * len(needs),
        out_specs=[pl.BlockSpec((part.shape[0], block), lambda i: (0, i)) for part in parts],
        out_shape=[jax.ShapeDtypeStruct((part.shape[0], columns), part.dtype) for part in parts],
        cost_estimate=work(20),
        compiler_params=pltpu.CompilerParams(vmem_limit_bytes=VMEM_LIMIT),
    )(weight, *parts, *needs)


def gelu_terms(value):
    t = 1.0 / (1.0 + (0.3275911 * 0.7071067811865476) * jnp.abs(value))
    bell = jnp.exp2(value * value * (-0.5 * 1.4426950408889634))
    tail = 0.5 * 1.061405429
    for term in (-0.5 * 1.453152027, 0.5 * 1.421413741, -0.5 * 0.284496736, 0.5 * 0.254829592):
        tail = tail * t + term
    tail = tail * t * bell
    cdf = jnp.where(value >= 0.0, 1.0 - tail, tail)
    return value * cdf, cdf + value * (0.3989422804014327 * bell)


def normalised(values):
    mean = jnp.mean(values, axis=-1, keepdims=True)
    centre = values - mean
    rate = lax.rsqrt(jnp.mean(centre * centre, axis=-1, keepdims=True) + EPSILON)
    return centre * rate, rate


def norm_back(scaled, unit, rate):
    first = jnp.mean(scaled, axis=-1, keepdims=True)
    second = jnp.mean(scaled * unit, axis=-1, keepdims=True)
    return rate * (scaled - first - unit * second)


def row_sums(values):
    rows, columns = values.shape
    return jnp.sum(values.reshape(rows // 8, 8, columns), axis=0)


def chain_kernel(
    att_ref,
    tok_ref,
    cot_ref,
    live_ref,
    lse_ref,
    mix_ref,
    up_ref,
    down_ref,
    vec_ref,
    bias_up_ref,
    spread_ref,
    out_ref,
    act_ref,
    upr_ref,
    hid_ref,
    pre_ref,
    mixr_ref,
    mixed_ref,
    back_ref,
    delta_ref,
    sum_ref,
    sum_up_ref,
    slope_ref,
):
    width = up_ref.shape[1]
    bias_mix, bias_down = vec_ref[0:1], vec_ref[1:2]
    gain_one, shift_one = vec_ref[2:3], vec_ref[3:4]
    gain_two, shift_two = vec_ref[4:5], vec_ref[5:6]

    @pl.when(pl.program_id(0) == 0)
    def _():
        sum_ref[...] = jnp.zeros_like(sum_ref)
        sum_up_ref[...] = jnp.zeros_like(sum_up_ref)

    attended = att_ref[...]
    mixed = plain_product(attended, mix_ref[...]) + bias_mix + tok_ref[...].astype(jnp.float32)
    unit_one, rate_one = normalised(mixed)
    hidden = unit_one * gain_one + shift_one
    hidden_rounded = hidden.astype(jnp.bfloat16)
    hid_ref[...] = hidden_rounded
    down_sum = bias_down + hidden
    for f in range(0, width, FCHUNK):
        up_sum = plain_product(hidden_rounded, up_ref[:, f : f + FCHUNK]) + (
            bias_up_ref[0:1, f : f + FCHUNK]
        )
        active, slope = gelu_terms(up_sum)
        active = active.astype(jnp.bfloat16)
        act_ref[:, f : f + FCHUNK] = active
        slope_ref[:, f : f + FCHUNK] = slope
        down_sum = down_sum + plain_product(active, down_ref[f : f + FCHUNK, :])
    unit_two, rate_two = normalised(down_sum)
    out_ref[...] = (unit_two * gain_two + shift_two).astype(jnp.bfloat16)
    cot = cot_ref[...].astype(jnp.float32)
    back_pre = norm_back(cot * gain_two, unit_two, rate_two)
    pre_rounded = back_pre.astype(jnp.bfloat16)
    pre_ref[...] = pre_rounded
    sum_ref[4] += row_sums(cot * unit_two)
    sum_ref[5] += row_sums(cot)
    sum_ref[1] += row_sums(back_pre)
    back_hidden = back_pre
    for f in range(0, width, FCHUNK):
        back_up = back_product(pre_rounded, down_ref[f : f + FCHUNK, :]) * (
            slope_ref[:, f : f + FCHUNK]
        )
        sum_up_ref[:, f : f + FCHUNK] += row_sums(back_up)
        up_rounded = back_up.astype(jnp.bfloat16)
        upr_ref[:, f : f + FCHUNK] = up_rounded
        back_hidden = back_hidden + back_product(up_rounded, up_ref[:, f : f + FCHUNK])
    sum_ref[2] += row_sums(back_hidden * unit_one)
    sum_ref[3] += row_sums(back_hidden)
    back_mixed = norm_back(back_hidden * gain_one, unit_one, rate_one)
    sum_ref[0] += row_sums(back_mixed)
    mixed_ref[...] = back_mixed
    mixed_rounded = back_mixed.astype(jnp.bfloat16)
    mixr_ref[...] = mixed_rounded
    back = back_product(mixed_rounded, mix_ref[...]).astype(jnp.bfloat16)
    back = jnp.where(live_ref[...] > 0.5, back, jnp.zeros_like(back))
    back_ref[:, : back.shape[1]] = back
    terms = back.astype(jnp.float32) * attended.astype(jnp.float32)
    high = terms.astype(jnp.bfloat16)
    low = (terms - high.astype(jnp.float32)).astype(jnp.bfloat16)
    delta = plain_product(high, spread_ref[...]) + plain_product(low, spread_ref[...])
    delta_ref[...] = delta
    lane = lax.broadcasted_iota(jnp.int32, delta.shape, 1)
    term = lane % TERMS
    whole = jnp.where(term < 3, lse_ref[...], delta)
    first = whole.astype(jnp.bfloat16)
    rest = whole - first.astype(jnp.float32)
    second = rest.astype(jnp.bfloat16)
    third = (rest - second.astype(jnp.float32)).astype(jnp.bfloat16)
    picked = jnp.where(
        (term == 0) | (term == 3),
        first.astype(jnp.float32),
        jnp.where((term == 2), third.astype(jnp.float32), second.astype(jnp.float32)),
    )
    picked = jnp.where(lane < TERMS * HEADS, picked, 0.0)
    back_ref[:, back.shape[1] :] = picked.astype(jnp.bfloat16)


def chain_call(att, tok, cot, live, lse, mix, up, down, vectors, bias_up):
    rows, width = tok.shape
    wide = up.shape[1]
    head_of = jnp.arange(width, dtype=jnp.int32)[:, None] // HD
    spread = (head_of == jnp.arange(2 * HD, dtype=jnp.int32)[None, :] // TERMS).astype(jnp.bfloat16)

    def tile(columns):
        return pl.BlockSpec((RTILE, columns), lambda i: (i, 0))

    def fixed(*shape):
        return pl.BlockSpec(shape, lambda i: (0,) * len(shape))

    bf16, f32 = jnp.bfloat16, jnp.float32
    return pl.pallas_call(
        chain_kernel,
        grid=(rows // RTILE,),
        in_specs=[
            tile(width),
            tile(width),
            tile(width),
            tile(1),
            tile(2 * HD),
            fixed(*mix.shape),
            fixed(*up.shape),
            fixed(*down.shape),
            fixed(*vectors.shape),
            fixed(*bias_up.shape),
            fixed(*spread.shape),
        ],
        out_specs=[
            tile(width),
            tile(wide),
            tile(wide),
            tile(width),
            tile(width),
            tile(width),
            tile(width),
            tile(width + 2 * HD),
            tile(2 * HD),
            fixed(6, 8, width),
            fixed(8, wide),
        ],
        out_shape=[
            jax.ShapeDtypeStruct((rows, width), bf16),
            jax.ShapeDtypeStruct((rows, wide), bf16),
            jax.ShapeDtypeStruct((rows, wide), bf16),
            jax.ShapeDtypeStruct((rows, width), bf16),
            jax.ShapeDtypeStruct((rows, width), bf16),
            jax.ShapeDtypeStruct((rows, width), bf16),
            jax.ShapeDtypeStruct((rows, width), f32),
            jax.ShapeDtypeStruct((rows, width + 2 * HD), bf16),
            jax.ShapeDtypeStruct((rows, 2 * HD), f32),
            jax.ShapeDtypeStruct((6, 8, width), f32),
            jax.ShapeDtypeStruct((8, wide), f32),
        ],
        scratch_shapes=[pltpu.VMEM((RTILE, wide), f32)],
        cost_estimate=work(44),
        compiler_params=pltpu.CompilerParams(vmem_limit_bytes=VMEM_LIMIT),
    )(att, tok, cot, live, lse, mix, up, down, vectors, bias_up, spread)


def weight_kernel(n_dp, core_ref, act, pre, hid, upr, att, mixr, small, *refs):
    send, keep, tmp = refs[-3:]
    step = pl.program_id(0)
    core = core_ref[0]
    pieces = FF // D
    down_rows = FF // n_dp
    part_rows = D // n_dp

    def put(x, row, rows, begin):
        mine = pl.multiple_of(begin + core * rows, 16)
        other = pl.multiple_of(begin + (1 - core) * rows, 16)
        keep[pl.ds(x, 1), pl.ds(row, rows), :] = tmp[pl.ds(mine, rows), :][None]
        send[pl.ds(x, 1), pl.ds(row, rows), :] = tmp[pl.ds(other, rows), :][None]

    @pl.when(step < pieces)
    def _():
        tmp[...] = outer_sum(act[...], pre[...]).astype(jnp.bfloat16)
        per = D // down_rows
        for b in range(per):
            block = step * per + b
            x = block // 2
            rows = tmp[b * down_rows : (b + 1) * down_rows, :]

            @pl.when(lax.rem(block, 2) == core)
            def _():
                keep[pl.ds(x, 1), 0:down_rows, :] = rows[None]

            @pl.when(lax.rem(block, 2) != core)
            def _():
                send[pl.ds(x, 1), 0:down_rows, :] = rows[None]

    @pl.when((step >= pieces) & (step < 2 * pieces))
    def _():
        tmp[...] = outer_sum(hid[...], upr[...]).astype(jnp.bfloat16)
        row = pl.multiple_of(down_rows + (step - pieces) * part_rows, 16)
        for x in range(n_dp // 2):
            put(x, row, part_rows, 2 * x * part_rows)

    @pl.when(step == 2 * pieces)
    def _():
        tmp[...] = outer_sum(att[...], mixr[...]).astype(jnp.bfloat16)
        row = down_rows + pieces * part_rows
        for x in range(n_dp // 2):
            put(x, row, part_rows, 2 * x * part_rows)
            last = row + part_rows
            rows = keep.shape[1] - last
            keep[x, last:, :] = small[pl.ds(2 * x + core, 1), :, :][0]
            send[x, last:, :] = small[pl.ds(2 * x + 1 - core, 1), :, :][0]


def weight_call(n_dp, core, act, pre, hid, upr, att, mixr, small, *needs):
    rows = act.shape[0]
    pieces = FF // D
    out_rows = FF // n_dp + (pieces + 1) * (D // n_dp) + small.shape[1]

    def fixed(*shape):
        return pl.BlockSpec(shape, lambda i, c: (0,) * len(shape))

    def stepped(first):
        return pl.BlockSpec((rows, D), lambda i, c: (0, jnp.clip(i - first, 0, pieces - 1)))

    shape = (n_dp // 2, out_rows, D)
    return pl.pallas_call(
        functools.partial(weight_kernel, n_dp),
        out_shape=[jax.ShapeDtypeStruct(shape, jnp.bfloat16)] * 2,
        grid_spec=pltpu.PrefetchScalarGridSpec(
            num_scalar_prefetch=1,
            grid=(2 * pieces + 1,),
            in_specs=[
                stepped(0),
                fixed(rows, D),
                fixed(rows, D),
                stepped(pieces),
                fixed(rows, D),
                fixed(rows, D),
                fixed(*small.shape),
            ]
            + [UNREAD] * len(needs),
            out_specs=[fixed(*shape)] * 2,
            scratch_shapes=[pltpu.VMEM((D, D), jnp.bfloat16)],
        ),
        cost_estimate=work(22),
        compiler_params=pltpu.CompilerParams(vmem_limit_bytes=VMEM_LIMIT),
    )(core, act, pre, hid, upr, att, mixr, small, *needs)


def outer_kernel(n_dp, core_ref, tokens, columns, *refs):
    send, keep, tmp = refs[-3:]
    core = core_ref[0]
    rows = tokens.shape[1] // n_dp
    tmp[...] = outer_sum(tokens[...], columns[...]).astype(tmp.dtype)
    for x in range(n_dp // 2):
        mine = pl.multiple_of((2 * x + core) * rows, 16)
        other = pl.multiple_of((2 * x + 1 - core) * rows, 16)
        keep[x] = tmp[pl.ds(mine, rows), :]
        send[x] = tmp[pl.ds(other, rows), :]


def outer_split(n_dp, core, tokens, columns, first, block, *needs):
    rows, depth = tokens.shape
    steps = columns.shape[1] // block - first
    shape = (n_dp // 2, depth // n_dp, block * steps)
    out = pl.BlockSpec(shape[:2] + (block,), lambda i, c: (0, 0, i))
    return pl.pallas_call(
        functools.partial(outer_kernel, n_dp),
        out_shape=[jax.ShapeDtypeStruct(shape, jnp.bfloat16)] * 2,
        grid_spec=pltpu.PrefetchScalarGridSpec(
            num_scalar_prefetch=1,
            grid=(steps,),
            in_specs=[
                pl.BlockSpec((rows, depth), lambda i, c: (0, 0)),
                pl.BlockSpec((rows, block), lambda i, c: (0, first + i)),
            ]
            + [UNREAD] * len(needs),
            out_specs=[out, out],
            scratch_shapes=[pltpu.VMEM((depth, block), jnp.bfloat16)],
        ),
        cost_estimate=work(4),
        compiler_params=plain_params(),
    )(core, tokens, columns, *needs)


def swap(value, axis, bit):
    devices = lax.axis_size(axis)
    return lax.ppermute(value, axis, [(i, i ^ bit) for i in range(devices)])


def dp_gather(shard, dp_rank):
    blocks = shard[None]
    bit = lax.axis_size("dp") // 2
    while bit >= 1:
        got = swap(blocks, "dp", bit)
        high = ((dp_rank // bit) % 2) == 1
        first = jnp.where(high, got, blocks)
        second = jnp.where(high, blocks, got)
        blocks = jnp.stack([first, second], axis=1).reshape((-1,) + shard.shape)
        bit //= 2
    return blocks.reshape((-1,) + shard.shape[1:])


def work(microseconds):
    return pl.CostEstimate(
        flops=int(microseconds * 0.4e9), transcendentals=0, bytes_accessed=1 << 20
    )


def row_tile(rows, limit=512):
    for size in range(min(rows, limit), 15, -1):
        if rows % size == 0 and size % 16 == 0:
            return size
    return rows


def plain_params():
    return pltpu.CompilerParams(vmem_limit_bytes=VMEM_LIMIT)


def split_add_kernel(which, keep_mine, got_mine, keep_other, got_other, *refs):
    mine, other = refs[-2:]
    mine[...] = (keep_mine[...].astype(jnp.float32) + got_mine[...].astype(jnp.float32)).astype(
        mine.dtype
    )
    other[...] = (keep_other[...].astype(jnp.float32) + got_other[...].astype(jnp.float32)).astype(
        other.dtype
    )


def split_add(keep, got, which, *needs):
    blocks, rows, columns = keep.shape
    tile = row_tile(rows)

    def spec(flip):
        def place(b, i, w):
            bit = 1 - w[0] if flip else w[0]
            return 2 * b + bit, i, 0

        return pl.BlockSpec((1, tile, columns), place)

    out = pl.BlockSpec((1, tile, columns), lambda b, i, w: (b, i, 0))
    shape = jax.ShapeDtypeStruct((blocks // 2, rows, columns), keep.dtype)
    return pl.pallas_call(
        split_add_kernel,
        out_shape=[shape, shape],
        grid_spec=pltpu.PrefetchScalarGridSpec(
            num_scalar_prefetch=1,
            grid=(blocks // 2, rows // tile),
            in_specs=[spec(False), spec(False), spec(True), spec(True)] + [UNREAD] * len(needs),
            out_specs=[out, out],
        ),
        cost_estimate=work(4),
        compiler_params=plain_params(),
    )(which, keep, got, keep, got, *needs)


def add_kernel(left, right, *refs):
    out = refs[-1]
    out[...] = (left[0].astype(jnp.float32) + right[0].astype(jnp.float32)).astype(out.dtype)


def add_blocks(left, right, *needs):
    _, rows, columns = left.shape
    tile = row_tile(rows)
    spec = pl.BlockSpec((1, tile, columns), lambda i: (0, i, 0))
    return pl.pallas_call(
        add_kernel,
        grid=(rows // tile,),
        in_specs=[spec, spec] + [UNREAD] * len(needs),
        out_specs=pl.BlockSpec((tile, columns), lambda i: (i, 0)),
        cost_estimate=work(3),
        out_shape=jax.ShapeDtypeStruct((rows, columns), left.dtype),
        compiler_params=plain_params(),
    )(left, right, *needs)


def pieces_kernel(pieces, *refs):
    out = refs[-1]
    total = pieces[0].astype(jnp.float32)
    for i in range(1, pieces.shape[0]):
        total = total + pieces[i].astype(jnp.float32)
    total = total.astype(out.dtype)
    for i in range(out.shape[0]):
        out[i] = total


def summed_copies(pieces, copies, *needs):
    _, rows, columns = pieces.shape
    return pl.pallas_call(
        pieces_kernel,
        in_specs=[pl.BlockSpec(memory_space=pltpu.VMEM)] + [UNREAD] * len(needs),
        out_specs=pl.BlockSpec(memory_space=pltpu.VMEM),
        out_shape=jax.ShapeDtypeStruct((copies, rows, columns), pieces.dtype),
        cost_estimate=work(2),
        compiler_params=plain_params(),
    )(pieces, *needs)


def two_pieces_kernel(left, right, *refs):
    out = refs[-1]
    at = 0
    for pieces in (left, right):
        total = pieces[0].astype(jnp.float32)
        for i in range(1, pieces.shape[0]):
            total = total + pieces[i].astype(jnp.float32)
        total = total.astype(out.dtype)
        for i in range(out.shape[0]):
            out[i, :, at : at + pieces.shape[2]] = total
        at += pieces.shape[2]


def summed_two(left, right, copies, *needs):
    _, rows, columns = left.shape
    shape = (copies, rows, columns + right.shape[2])
    return pl.pallas_call(
        two_pieces_kernel,
        in_specs=[pl.BlockSpec(memory_space=pltpu.VMEM)] * 2 + [UNREAD] * len(needs),
        out_specs=pl.BlockSpec(memory_space=pltpu.VMEM),
        out_shape=jax.ShapeDtypeStruct(shape, left.dtype),
        cost_estimate=work(2),
        compiler_params=plain_params(),
    )(left, right, *needs)


def gate_kernel(value, *refs):
    refs[-1][...] = value[...]


def gated(value, *needs):
    return pl.pallas_call(
        gate_kernel,
        in_specs=[pl.BlockSpec(memory_space=pltpu.VMEM)] + [UNREAD] * len(needs),
        out_specs=pl.BlockSpec(memory_space=pltpu.VMEM),
        out_shape=jax.ShapeDtypeStruct(value.shape, value.dtype),
        cost_estimate=work(1),
        compiler_params=plain_params(),
    )(value, *needs)


def cluster_ids(group_order, own_start, span):
    padded = jnp.pad(group_order, ((0, 0), (HALO, HALO)), constant_values=-(1 << 24))
    wanted = lax.dynamic_slice_in_dim(padded, own_start, span, 1) - (own_start - HALO)
    tile_of = wanted >> 7
    lane_of_token = wanted & (CL - 1)
    cluster = (jnp.arange(span, dtype=jnp.int32) >> 7) + 1
    tile_hot = jnp.where(
        tile_of[:, :, None] == jnp.arange(span // CL, dtype=jnp.int32), cluster[None, :, None], 0
    ).astype(jnp.bfloat16)
    lane_hot = (lane_of_token[:, :, None] == jnp.arange(CL, dtype=jnp.int32)).astype(jnp.bfloat16)
    table = jnp.einsum("hpt,hpl->htl", tile_hot, lane_hot, preferred_element_type=jnp.float32)
    return table.reshape(HEADS, span) - 1.0


def on_device(
    tokens,
    input_weight,
    output_weight,
    up_weight,
    down_weight,
    output_bias,
    up_bias,
    down_bias,
    first_gain,
    first_shift,
    second_gain,
    second_shift,
    document_runs,
    document_trim,
    cluster_order,
    cotangent,
):
    bf16, f32 = jnp.bfloat16, jnp.float32
    n_dp = lax.axis_size("dp")
    n_seq = lax.axis_size("seq")
    dp_rank = lax.axis_index("dp")
    seq_rank = lax.axis_index("seq")
    inputs = tokens[0]
    tok_dev = inputs.shape[0]
    tiles = tok_dev // CL
    span = tok_dev + 2 * HALO
    own_start = seq_rank * tok_dev

    token_parts = halo_parts(inputs)
    n_parts = len(token_parts)

    weight_in = lax.all_gather(input_weight, "dp", axis=0, tiled=True)
    weight_up = lax.all_gather(up_weight, "dp", axis=0, tiled=True)
    weight_down = lax.all_gather(down_weight, "dp", axis=0, tiled=True)

    runs = document_runs[0]
    first_cluster = jnp.cumsum(runs) - runs
    own_clusters = seq_rank * tiles + jnp.arange(tiles, dtype=jnp.int32)
    doc_start = jnp.max(
        jnp.where(first_cluster[None, :] <= own_clusters[:, None], first_cluster[None, :], 0), axis=1
    )
    starts = (doc_start - seq_rank * tiles + (MOSTB - 1)).astype(jnp.int32)
    near_left = HALO // CL - tiles
    near = near_left + 2 * tiles * jnp.stack([1 - seq_rank % 2, seq_rank % 2])
    starts = jnp.concatenate([starts, near.astype(jnp.int32)])

    cids = cluster_ids(cluster_order[0], own_start, span)
    positions = own_start - HALO + jnp.arange(span, dtype=jnp.int32)
    live = live_tokens(runs, document_trim[0], positions)
    usable = live[None, :] & (cids >= 0.0)
    key_ids = jnp.where(usable, cids, -1.0).reshape(PAIRS, 2, span)
    query_ids = jnp.where(usable, cids, -2.0).reshape(PAIRS, 2, span)
    own_live = live[HALO : HALO + tok_dev, None].astype(f32)

    own = plain_product(inputs, weight_in).astype(bf16)
    groups = HEADS // PACK
    group_lanes = PACK * HD
    kv_weight = (
        weight_in[:, D:]
        .reshape(D, 2, PAIRS, 2 * HD)
        .transpose(0, 2, 1, 3)
        .reshape(D, 2 * D)
    )
    around = project_call(token_parts[:2] + token_parts[3:], weight_in, kv_weight)
    projected = [*around[:2], own, *around[2:]]
    vectors = [
        output_bias,
        down_bias,
        first_gain,
        first_shift,
        second_gain,
        second_shift,
        up_bias,
    ]
    mix_rows = output_weight.shape[0]
    packed = jnp.concatenate(vectors)
    pad_rows = -(-packed.shape[0] // (16 * D)) * 16
    packed = jnp.pad(packed, (0, pad_rows * D - packed.shape[0])).reshape(pad_rows, D)
    mix_shard = gated(jnp.concatenate([output_weight, packed], 0), own)
    mix_all = dp_gather(mix_shard, dp_rank)
    mix_all = mix_all.reshape(n_dp, mix_rows + pad_rows, D)
    weight_mix = mix_all[:, :mix_rows].reshape(D, D)
    small_all = mix_all[:, mix_rows:].reshape(n_dp, -1).astype(f32)
    vec = small_all[:, : 6 * mix_rows].reshape(n_dp, 6, mix_rows).transpose(1, 0, 2).reshape(6, D)
    vec = jnp.pad(vec, ((0, 2), (0, 0)))
    up_part = up_bias.shape[0]
    bias_up = small_all[:, 6 * mix_rows : 6 * mix_rows + up_part].reshape(1, FF)
    bias_up = jnp.pad(bias_up, ((0, 7), (0, 0)))
    heights = [part.shape[0] for part in token_parts]

    groups = HEADS // PACK
    group_lanes = PACK * HD
    group_key_ids = key_ids.reshape(groups, PACK, span)
    group_query_ids = query_ids.reshape(groups, PACK, span)
    group_scratch = pltpu.VMEM((span, group_lanes), bf16)

    def group_parts(third, first):
        return [lane_block(rows, third * groups + first, PACK) for rows in heights]

    steps = tiles // TILES_AT_ONCE
    step_rows = TILES_AT_ONCE * CL

    def of_group(rows, first):
        return pl.BlockSpec((rows, group_lanes), lambda g, t, starts: (0, first + g))

    def ids_of_group():
        return pl.BlockSpec((1, PACK, span), lambda g, t, starts: (g, 0, 0))

    step_block = pl.BlockSpec((step_rows, group_lanes), lambda g, t, starts: (t, g))
    whole_lanes = pl.BlockSpec((tok_dev, 2 * HD), lambda g, t, starts: (0, 0))
    attended, lse, rate, probs = strip_call(
        functools.partial(attend_kernel, tiles, n_parts),
        52,
        (groups, steps),
        [step_block]
        + [of_group(rows, groups) for rows in heights]
        + [of_group(rows, 2 * groups) for rows in heights]
        + [ids_of_group(), ids_of_group()],
        [
            step_block,
            whole_lanes,
            whole_lanes,
            pl.BlockSpec(
                (1, TILES_AT_ONCE, PACK * CL, WINDOW), lambda g, t, starts: (g, t, 0, 0)
            ),
        ],
        [
            jax.ShapeDtypeStruct((tok_dev, D), bf16),
            jax.ShapeDtypeStruct((tok_dev, 2 * HD), f32),
            jax.ShapeDtypeStruct((tok_dev, 2 * HD), f32),
            jax.ShapeDtypeStruct((groups, tiles, PACK * CL, WINDOW), bf16),
        ],
        [group_scratch, group_scratch]
        + [pltpu.VMEM((PACK * CL, WINDOW), f32)] * TILES_AT_ONCE
        + [pltpu.VMEM((PACK * CL, CL), f32)] * TILES_AT_ONCE,
        (starts, own, *projected, *projected, group_query_ids, group_key_ids),
    )

    (
        result,
        active,
        up_rounded,
        hidden_rounded,
        pre_rounded,
        mixed_rounded,
        back_mixed,
        back_own,
        delta,
        sums,
        sums_up,
    ) = chain_call(
        attended,
        inputs,
        cotangent[0],
        own_live,
        lse,
        weight_mix,
        weight_up,
        weight_down,
        vec,
        bias_up,
    )
    back_parts = halo_parts(back_own)

    small = jnp.concatenate(
        [
            jnp.sum(sums, axis=1).reshape(6, n_dp, mix_rows).transpose(1, 0, 2).reshape(n_dp, -1),
            jnp.sum(sums_up, axis=0).reshape(n_dp, -1),
        ],
        axis=1,
    ).astype(bf16)
    unit = 8 * n_seq
    fixed_rows = FF // n_dp + (FF // D + 1) * (D // n_dp)
    small_rows = -(-(fixed_rows + -(-small.shape[1] // D)) // unit) * unit - fixed_rows
    small = jnp.pad(small, ((0, 0), (0, small_rows * D - small.shape[1])))
    small = small.reshape(n_dp, small_rows, D)
    core = (dp_rank % 2).astype(jnp.int32)
    def query_strip(first, *needs):
        buffer = needs[:1] if first > 0 else ()

        def parts(third):
            return [
                pl.BlockSpec(
                    (rows, group_lanes), lambda t, starts: (0, third * groups + first)
                )
                for rows in heights
            ]

        block = pl.BlockSpec((step_rows, group_lanes), lambda t, starts: (t, first))
        lanes = pl.BlockSpec((step_rows, 2 * HD), lambda t, starts: (t, 0))
        in_specs = (
            parts(1)
            + parts(2)
            + [
                block,
                pl.BlockSpec(
                    (1, TILES_AT_ONCE, PACK * CL, WINDOW), lambda t, starts: (first, t, 0, 0)
                ),
                lanes,
                lanes,
            ]
            + [UNREAD] * len(needs)
        )
        return strip_call(
            functools.partial(query_kernel, tiles, n_parts, first * PACK),
            16,
            (steps,),
            in_specs,
            block,
            jax.ShapeDtypeStruct((tok_dev, D), bf16),
            [group_scratch, group_scratch],
            (starts, *projected, *projected, back_own, probs, rate, delta, *needs),
            {len(in_specs) + 1 - len(needs): 0} if buffer else None,
        )

    pair_scratch = pltpu.VMEM((span, 4 * HD), bf16)

    def key_strip(pair, pairs, *needs):
        buffer = needs[:1] if pair > 0 else ()

        def parts(third):
            return [lane_block(rows, third * PAIRS + pair) for rows in heights]

        in_specs = (
            [lane_block(tok_dev, PAIRS + pair), lane_block(tok_dev, 2 * PAIRS + pair)]
            + parts(0)
            + parts(0)
            + [fixed_lanes(rows, PAIRS) for rows in heights]
            + [row_block(span, pair), row_block(span, pair)]
            + [UNREAD] * len(needs)
        )
        return strip_call(
            functools.partial(key_kernel, tiles, n_parts, pair),
            13 * pairs,
            (pairs,),
            in_specs,
            lane_block(tok_dev, pair, 4),
            jax.ShapeDtypeStruct((tok_dev, 2 * D), bf16),
            [pair_scratch, pair_scratch],
            (
                starts,
                own,
                own,
                *projected,
                *back_parts,
                *back_parts,
                query_ids,
                key_ids,
                *needs,
            ),
            {len(in_specs) + 1 - len(needs): 0} if buffer else None,
        )

    def scatter(share):
        rows, columns = share.shape
        return lax.all_to_all(
            share.reshape(n_seq, rows // n_seq, columns), "seq", split_axis=0, concat_axis=0
        )

    def everyone(copies):
        got = lax.all_to_all(copies, "seq", split_axis=0, concat_axis=0)
        return got.reshape(-1, copies.shape[-1])

    def first_split(keep, got, *needs):
        bit = 2
        while True:
            which = ((dp_rank // bit) % 2).astype(jnp.int32).reshape(1)
            mine, other = split_add(keep, got, which, *needs)
            got = swap(other, "dp", bit)
            if mine.shape[0] == 1:
                return mine, got
            keep, bit, needs = mine, bit * 2, ()

    def core_split(grad):
        rows, columns = grad.shape
        blocks = grad.astype(bf16).reshape(n_dp // 2, 2, rows // n_dp, columns)
        return (
            lax.dynamic_index_in_dim(blocks, 1 - core, 1, keepdims=False),
            lax.dynamic_index_in_dim(blocks, core, 1, keepdims=False),
        )

    send, keep = weight_call(
        n_dp,
        core.reshape(1),
        active,
        pre_rounded,
        hidden_rounded,
        up_rounded,
        attended,
        mixed_rounded,
        small,
    )
    core_got = swap(send, "dp", 1)
    back_q = query_strip(0, send)
    mine, x_got = first_split(keep, core_got, back_q)
    back_q = query_strip(1, back_q, mine)
    back_q = query_strip(2, back_q)
    back_kv = key_strip(0, 1, back_q)
    share = add_blocks(mine, x_got, back_kv)
    pieces = scatter(share)
    back_kv = key_strip(1, 2, back_kv, share)
    cut = PAIRS // 2 * 4 * HD
    early_cols = jnp.concatenate([back_q, back_kv[:, :cut]], axis=1)
    early_send, early_keep = core_split(outer_sum(inputs, early_cols))
    early_core = swap(early_send, "dp", 1)
    back_kv = key_strip(3, 1, back_kv, early_send)
    early_mine, early_got = first_split(early_keep, early_core, back_kv)
    back_kv = key_strip(4, 1, back_kv, early_mine)
    copies = summed_copies(pieces, 1, back_kv)
    back_kv = key_strip(5, 1, back_kv, copies)
    early_share = add_blocks(early_mine, early_got, back_kv)
    all_sums = lax.all_gather(copies[0], "seq", axis=0, tiled=True)
    late_send, late_keep = outer_split(
        n_dp, core.reshape(1), inputs, back_kv, 1, cut, early_share
    )
    late_mine, late_got = first_split(late_keep, swap(late_send, "dp", 1))
    late_share = add_blocks(late_mine, late_got)
    early_pieces, late_pieces = scatter(early_share), scatter(late_share)
    in_all = everyone(summed_two(early_pieces, late_pieces, n_seq, all_sums))

    input_grad = (
        back_mixed + back_product(back_q, weight_in[:, :D]) + back_product(back_kv, kv_weight)
    )
    kv_all = in_all[:, D:].reshape(-1, PAIRS, 2, 2 * HD).transpose(0, 2, 1, 3)
    grad_in_total = jnp.concatenate([in_all[:, :D], kv_all.reshape(-1, 2 * D)], axis=1).astype(f32)
    down_rows = FF // n_dp
    part_rows = D // n_dp
    grad_down = all_sums[:down_rows].astype(f32)
    grad_up = (
        all_sums[down_rows : down_rows + (FF // D) * part_rows]
        .reshape(FF // D, part_rows, D)
        .transpose(1, 0, 2)
        .reshape(part_rows, FF)
        .astype(f32)
    )
    at = down_rows + (FF // D) * part_rows
    grad_mix = all_sums[at : at + part_rows].astype(f32)
    flat = all_sums[at + part_rows :].reshape(-1).astype(f32)
    vectors_out = [flat[i * part_rows : (i + 1) * part_rows] for i in range(6)]
    bias_up_out = flat[6 * part_rows : 6 * part_rows + down_rows]
    return (
        result[None],
        input_grad[None],
        grad_in_total,
        grad_mix,
        grad_up,
        grad_down,
        vectors_out[0],
        bias_up_out,
        vectors_out[1],
        *vectors_out[2:],
    )


def solution(mesh):
    placed = (
        P("dp", "seq", None),
        P("dp", None),
        P("dp", None),
        P("dp", None),
        P("dp", None),
        P("dp"),
        P("dp"),
        P("dp"),
        P("dp"),
        P("dp"),
        P("dp"),
        P("dp"),
        P("dp", None),
        P("dp", None),
        P("dp", None, None),
        P("dp", "seq", None),
    )
    return jax.shard_map(
        on_device,
        mesh=mesh,
        in_specs=placed,
        out_specs=(
            P("dp", "seq", None),
            P("dp", "seq", None),
            P("dp", None),
            P("dp", None),
            P("dp", None),
            P("dp", None),
            P("dp"),
            P("dp"),
            P("dp"),
            P("dp"),
            P("dp"),
            P("dp"),
            P("dp"),
        ),
        check_vma=False,
    )
```

```python
import functools

import jax
import jax.numpy as jnp
from jax import lax
from jax.experimental import pallas as pl
from jax.experimental.pallas import tpu as pltpu
from jax.sharding import PartitionSpec as P

D = 768
HEADS = 12
HD = 64
CL = 128
MOSTB = 16
PAIRS = HEADS // 2
WINDOW = MOSTB * CL
HALO = (MOSTB - 1) * CL
CHUNK = 1024
KCHUNK = 1024
TILES_AT_ONCE = 2
PACK = 4
NEG = -1e30
TERMS = 5
FF = 3072
RTILE = 256
FCHUNK = 768
SCALE2 = HD ** (-0.5) * 1.4426950408889634

EPSILON = 1e-05


def shifted(value, axis, by):
    devices = lax.axis_size(axis)
    pairs = [(i, i + by) for i in range(devices) if 0 <= i + by < devices]
    return lax.ppermute(value, axis, pairs)


def halo_parts(value):
    own = value.shape[0]
    far = HALO - own
    devices = lax.axis_size("seq")
    assert 0 < far <= own and devices % 2 == 0
    partner = lax.ppermute(value, "seq", [(i, i ^ 1) for i in range(devices)])
    pairs = [(i, i - 1 if i % 2 == 0 else i + 1) for i in range(devices)]
    other = lax.ppermute(value, "seq", [(i, k) for i, k in pairs if 0 <= k < devices])
    before = shifted(value[own - far :], "seq", 2)
    following = shifted(value[:far], "seq", -2)
    return [before, partner, value, other, following]


def places(starts, tiles, parts):
    far, own = parts[0].shape[0], parts[2].shape[0]
    return [
        0,
        pl.multiple_of(starts[tiles] * CL, CL),
        far + own,
        pl.multiple_of(starts[tiles + 1] * CL, CL),
        far + 3 * own,
    ]


def live_tokens(runs, trim, positions):
    ends = jnp.cumsum(runs) * CL
    starts = ends - runs * CL
    lengths = runs * CL - trim
    inside = (positions[..., None] >= starts) & (positions[..., None] < starts + lengths)
    return jnp.any(inside, axis=-1)


def outer_sum(left, right):
    return lax.dot_general(
        left, right, (((0,), (0,)), ((), ())), preferred_element_type=jnp.float32
    )


def back_product(left, right):
    return lax.dot_general(
        left, right, (((1,), (1,)), ((), ())), preferred_element_type=jnp.float32
    )


def plain_product(left, right):
    return jnp.dot(left, right, preferred_element_type=jnp.float32)


def stacked(tile):
    lane = lax.broadcasted_iota(jnp.int32, tile.shape, 1)
    zero = jnp.zeros_like(tile)
    heads = tile.shape[1] // HD
    return jnp.concatenate(
        [
            jnp.where((lane >= h * HD) & (lane < (h + 1) * HD), tile, zero)
            for h in range(heads)
        ],
        axis=0,
    )


def unstacked(stack):
    heads = stack.shape[1] // HD
    lane = lax.broadcasted_iota(jnp.int32, (CL, heads * HD), 1)
    result = stack[:CL]
    for h in range(1, heads):
        result = jnp.where(lane >= h * HD, stack[h * CL : (h + 1) * CL], result)
    return result


def as_column(row):
    return jnp.broadcast_to(row, (CL, CL)).T


def lane_of(tile, lane):
    lanes = lax.broadcasted_iota(jnp.int32, tile.shape, 1)
    return jnp.sum(jnp.where(lanes == lane, tile, 0.0), axis=1, keepdims=True)


def masked(scores, cols, row_ref, begin):
    parts = []
    wide = scores.shape[1]
    for half, one in enumerate(cols):
        row = row_ref[0, half : half + 1, pl.ds(begin, wide)]
        block = scores[half * CL : (half + 1) * CL]
        col = jnp.concatenate([one] * (wide // CL), axis=1)
        parts.append(jnp.where(col == row, block, NEG))
    return jnp.concatenate(parts, axis=0)


def assemble(parts, offsets, whole):
    for part, at in zip(parts, offsets):
        whole[pl.ds(at, part.shape[0]), :] = part[...]


def ahead(steps, produce, consume):
    held = produce(*steps[0])
    for i, step in enumerate(steps):
        following = produce(*steps[i + 1]) if i + 1 < len(steps) else None
        consume(*step, held)
        held = following


def attend_kernel(tiles, n_parts, starts, q_ref, *refs):
    k_parts, refs = refs[:n_parts], refs[n_parts:]
    v_parts, refs = refs[:n_parts], refs[n_parts:]
    qid_ref, kid_ref, out_ref, lse_ref, rate_ref, p_ref, k_ref, v_ref, *slots = refs
    s_refs, top_refs = slots[:TILES_AT_ONCE], slots[TILES_AT_ONCE:]
    group, step = pl.program_id(0), pl.program_id(1)
    heads = q_ref.shape[1] // HD
    chunks = WINDOW // CHUNK

    @pl.when(step == 0)
    def _():
        offsets = places(starts, tiles, k_parts)
        assemble(k_parts, offsets, k_ref)
        assemble(v_parts, offsets, v_ref)

    @pl.when((group == 0) & (step == 0))
    def _():
        lse_ref[...] = jnp.zeros_like(lse_ref)
        rate_ref[...] = jnp.zeros_like(rate_ref)

    def first_half(slot):
        tile = TILES_AT_ONCE * step + slot
        own = pl.multiple_of(HALO + tile * CL, CL)
        return dict(
            begin=pl.multiple_of(starts[tile] * CL, CL),
            query=stacked(q_ref[slot * CL : (slot + 1) * CL, :]),
            cols=[
                as_column(qid_ref[0, half : half + 1, pl.ds(own, CL)]) for half in range(heads)
            ],
        )

    def score(state, slot, j):
        at = pl.multiple_of(state["begin"] + j * CHUNK, CL)
        scores = back_product(state["query"], k_ref[pl.ds(at, CHUNK), :])
        scores = masked(scores, state["cols"], kid_ref, at)
        s_refs[slot][:, j * CHUNK : (j + 1) * CHUNK] = scores
        top = scores[:, :CL]
        for i in range(1, CHUNK // CL):
            top = jnp.maximum(top, scores[:, i * CL : (i + 1) * CL])
        if j > 0:
            top = jnp.maximum(top, top_refs[slot][...])
        top_refs[slot][...] = top

    states = [first_half(0)]
    for j in range(chunks):
        score(states[0], 0, j)
    for slot in range(TILES_AT_ONCE):
        if slot + 1 < TILES_AT_ONCE:
            states.append(first_half(slot + 1))
        state = states[slot]
        peak = jnp.max(top_refs[slot][...], axis=1, keepdims=True)
        total = jnp.zeros((heads * CL, CL), jnp.float32)
        result = jnp.zeros((heads * CL, heads * HD), jnp.float32)
        for j in range(chunks):
            if slot + 1 < TILES_AT_ONCE:
                score(states[slot + 1], slot + 1, j)
            at = pl.multiple_of(state["begin"] + j * CHUNK, CL)
            columns = slice(j * CHUNK, (j + 1) * CHUNK)
            weights = jnp.exp2((s_refs[slot][:, columns] - peak) * SCALE2)
            for i in range(CHUNK // CL):
                total = total + weights[:, i * CL : (i + 1) * CL]
            p_ref[0, slot, :, columns] = weights.astype(jnp.bfloat16)
            result = result + plain_product(
                p_ref[0, slot, :, columns], v_ref[pl.ds(at, CHUNK), :]
            )
        total = jnp.sum(total, axis=1, keepdims=True)
        rate = 1.0 / total
        result = result * rate
        lse = peak + jnp.log(total) * HD**0.5
        live = (state["cols"][0] >= 0.0).astype(jnp.float32)
        live = jnp.concatenate([live] * (heads * HD // CL), axis=1)
        rows = slice(slot * CL, (slot + 1) * CL)
        out_ref[rows, :] = (unstacked(result) * live).astype(jnp.bfloat16)
        here = pl.ds(pl.multiple_of((TILES_AT_ONCE * step + slot) * CL, CL), CL)
        lane = lax.broadcasted_iota(jnp.int32, (CL, CL), 1)
        kept, kept_rate = lse_ref[here, :], rate_ref[here, :]
        for half in range(heads):
            first = (heads * group + half) * TERMS
            inside = (lane >= first) & (lane < first + TERMS)
            part = slice(half * CL, (half + 1) * CL)
            kept = jnp.where(inside, lse[part], kept)
            kept_rate = jnp.where(inside, rate[part], kept_rate)
        lse_ref[here, :] = kept
        rate_ref[here, :] = kept_rate


def query_kernel(tiles, n_parts, first_head, starts, *refs):
    k_parts, refs = refs[:n_parts], refs[n_parts:]
    v_parts, refs = refs[:n_parts], refs[n_parts:]
    g_ref, p_ref, rate_ref, delta_ref = refs[:4]
    out_ref, k_ref, v_ref = refs[-3:]
    step = pl.program_id(0)
    heads = g_ref.shape[1] // HD
    chunks = WINDOW // CHUNK

    @pl.when(step == 0)
    def _():
        offsets = places(starts, tiles, k_parts)
        assemble(k_parts, offsets, k_ref)
        assemble(v_parts, offsets, v_ref)

    states = {}

    def state_of(slot):
        if slot not in states:
            rows = slice(slot * CL, (slot + 1) * CL)
            columns = [
                jnp.concatenate(
                    [lane_of(ref[rows, :], (first_head + half) * TERMS) for half in range(heads)],
                    axis=0,
                )
                for ref in (delta_ref, rate_ref)
            ]
            states[slot] = dict(
                begin=pl.multiple_of(starts[TILES_AT_ONCE * step + slot] * CL, CL),
                back=stacked(g_ref[rows, :]),
                delta=columns[0],
                rate=columns[1],
                result=jnp.zeros((heads * CL, heads * HD), jnp.float32),
            )
        return states[slot]

    def produce(slot, j):
        state = state_of(slot)
        at = pl.multiple_of(state["begin"] + j * CHUNK, CL)
        return back_product(state["back"], v_ref[pl.ds(at, CHUNK), :])

    def consume(slot, j, back_probs):
        state = state_of(slot)
        at = pl.multiple_of(state["begin"] + j * CHUNK, CL)
        weights = p_ref[0, slot, :, j * CHUNK : (j + 1) * CHUNK].astype(jnp.float32)
        back_scores = weights * (back_probs - state["delta"])
        state["result"] = state["result"] + plain_product(
            back_scores.astype(jnp.bfloat16), k_ref[pl.ds(at, CHUNK), :]
        )
        if j == chunks - 1:
            out_ref[slot * CL : (slot + 1) * CL, :] = unstacked(
                state["result"] * (state["rate"] * HD ** (-0.5))
            ).astype(jnp.bfloat16)

    ahead(
        [(slot, j) for slot in range(TILES_AT_ONCE) for j in range(chunks)], produce, consume
    )


def key_kernel(tiles, n_parts, first_pair, starts, k_ref, v_ref, *refs):
    q_parts, refs = refs[:n_parts], refs[n_parts:]
    g_parts, refs = refs[:n_parts], refs[n_parts:]
    a_parts, refs = refs[:n_parts], refs[n_parts:]
    qid_ref, kid_ref = refs[:2]
    out_ref, q_ref, g_ref = refs[-3:]
    pair = first_pair + pl.program_id(0)
    offsets = places(starts, tiles, q_parts)
    for at, q_part, g_part, a_part in zip(offsets, q_parts, g_parts, a_parts):
        rows = pl.ds(at, q_part.shape[0])
        q_ref[rows, : 2 * HD] = q_part[...]
        q_ref[rows, 2 * HD :] = a_part[...]
        g_ref[rows, : 2 * HD] = g_part[...]
        g_ref[rows, 2 * HD :] = a_part[...]

    lane = lax.broadcasted_iota(jnp.int32, (CL, CL), 1)
    lse_pick, delta_pick = [], []
    for half in range(2):
        first = (2 * pair + half) * TERMS
        lse_pick.append(jnp.where((lane >= first) & (lane < first + 3), -1.0, 0.0))
        delta_pick.append(jnp.where((lane >= first + 3) & (lane < first + TERMS), -1.0, 0.0))
    lse_pick = jnp.concatenate(lse_pick, axis=0).astype(jnp.bfloat16)
    delta_pick = jnp.concatenate(delta_pick, axis=0).astype(jnp.bfloat16)

    def some_tiles(step, carry):
        states = {}

        def state_of(slot):
            if slot not in states:
                tile = TILES_AT_ONCE * step + slot
                own = pl.multiple_of(HALO + tile * CL, CL)
                here = pl.multiple_of(tile * CL, CL)
                states[slot] = dict(
                    begin=pl.multiple_of(starts[tile] * CL, CL),
                    here=here,
                    keys=jnp.concatenate([stacked(k_ref[pl.ds(here, CL), :]), lse_pick], axis=1),
                    values=jnp.concatenate(
                        [stacked(v_ref[pl.ds(here, CL), :]), delta_pick], axis=1
                    ),
                    cols=[
                        as_column(kid_ref[0, half : half + 1, pl.ds(own, CL)]) for half in range(2)
                    ],
                    key_sum=jnp.zeros((2 * CL, 2 * HD), jnp.float32),
                    value_sum=jnp.zeros((2 * CL, 2 * HD), jnp.float32),
                )
            return states[slot]

        def produce(slot, j):
            state = state_of(slot)
            at = pl.multiple_of(state["begin"] + j * KCHUNK, CL)
            scores = back_product(state["keys"], q_ref[pl.ds(at, KCHUNK), :])
            return scores, back_product(state["values"], g_ref[pl.ds(at, KCHUNK), :])

        def consume(slot, j, held):
            state = state_of(slot)
            at = pl.multiple_of(state["begin"] + j * KCHUNK, CL)
            scores, back_probs = held
            probs = jnp.exp2(masked(scores * SCALE2, state["cols"], qid_ref, at))
            back_scores = probs * back_probs
            state["value_sum"] = state["value_sum"] + plain_product(
                probs.astype(jnp.bfloat16), g_ref[pl.ds(at, KCHUNK), : 2 * HD]
            )
            state["key_sum"] = state["key_sum"] + plain_product(
                back_scores.astype(jnp.bfloat16), q_ref[pl.ds(at, KCHUNK), : 2 * HD]
            )
            if j == WINDOW // KCHUNK - 1:
                rows = pl.ds(state["here"], CL)
                out_ref[rows, : 2 * HD] = (
                    unstacked(state["key_sum"]) * HD ** (-0.5)
                ).astype(jnp.bfloat16)
                out_ref[rows, 2 * HD :] = unstacked(state["value_sum"]).astype(jnp.bfloat16)

        ahead(
            [(slot, j) for slot in range(TILES_AT_ONCE) for j in range(WINDOW // KCHUNK)],
            produce,
            consume,
        )
        return carry

    lax.fori_loop(0, tiles // TILES_AT_ONCE, some_tiles, 0)


def lane_block(rows, first, heads=2):
    return pl.BlockSpec((rows, heads * HD), lambda pair, starts: (0, first + pair))


def fixed_lanes(rows, block):
    return pl.BlockSpec((rows, 2 * HD), lambda pair, starts: (0, block))


def row_block(columns, first, heads=2):
    return pl.BlockSpec((1, heads, columns), lambda pair, starts: (first + pair, 0, 0))


UNREAD = pl.BlockSpec(memory_space=pl.ANY)


VMEM_LIMIT = 60 * 1024 * 1024


def strip_call(
    kernel, length, grid, in_specs, out_specs, out_shape, scratch, args, aliases=None
):
    return pl.pallas_call(
        kernel,
        out_shape=out_shape,
        grid_spec=pltpu.PrefetchScalarGridSpec(
            num_scalar_prefetch=1,
            grid=grid,
            in_specs=in_specs,
            out_specs=out_specs,
            scratch_shapes=scratch,
        ),
        input_output_aliases=aliases or {},
        cost_estimate=work(length),
        compiler_params=pltpu.CompilerParams(vmem_limit_bytes=VMEM_LIMIT),
    )(*args)


def project_kernel(parts, weight, *refs):
    for source, target in zip(refs[:parts], refs[-parts:]):
        target[...] = plain_product(source[...], weight[...]).astype(target.dtype)


def project_call(parts, weight, *needs):
    depth, columns = weight.shape
    block = PACK * HD
    return pl.pallas_call(
        functools.partial(project_kernel, len(parts)),
        grid=(columns // block,),
        in_specs=[pl.BlockSpec((depth, block), lambda i: (0, i))]
        + [pl.BlockSpec(part.shape, lambda i: (0, 0)) for part in parts]
        + [UNREAD] * len(needs),
        out_specs=[pl.BlockSpec((part.shape[0], block), lambda i: (0, i)) for part in parts],
        out_shape=[jax.ShapeDtypeStruct((part.shape[0], columns), part.dtype) for part in parts],
        cost_estimate=work(20),
        compiler_params=pltpu.CompilerParams(vmem_limit_bytes=VMEM_LIMIT),
    )(weight, *parts, *needs)


def gelu_terms(value):
    t = 1.0 / (1.0 + (0.3275911 * 0.7071067811865476) * jnp.abs(value))
    bell = jnp.exp2(value * value * (-0.5 * 1.4426950408889634))
    tail = 0.5 * 1.061405429
    for term in (-0.5 * 1.453152027, 0.5 * 1.421413741, -0.5 * 0.284496736, 0.5 * 0.254829592):
        tail = tail * t + term
    tail = tail * t * bell
    cdf = jnp.where(value >= 0.0, 1.0 - tail, tail)
    return value * cdf, cdf + value * (0.3989422804014327 * bell)


def normalised(values):
    mean = jnp.mean(values, axis=-1, keepdims=True)
    centre = values - mean
    rate = lax.rsqrt(jnp.mean(centre * centre, axis=-1, keepdims=True) + EPSILON)
    return centre * rate, rate


def norm_back(scaled, unit, rate):
    first = jnp.mean(scaled, axis=-1, keepdims=True)
    second = jnp.mean(scaled * unit, axis=-1, keepdims=True)
    return rate * (scaled - first - unit * second)


def row_sums(values):
    rows, columns = values.shape
    return jnp.sum(values.reshape(rows // 8, 8, columns), axis=0)


def chain_kernel(
    att_ref,
    tok_ref,
    cot_ref,
    live_ref,
    lse_ref,
    mix_ref,
    up_ref,
    down_ref,
    vec_ref,
    bias_up_ref,
    spread_ref,
    out_ref,
    act_ref,
    upr_ref,
    hid_ref,
    pre_ref,
    mixr_ref,
    mixed_ref,
    back_ref,
    delta_ref,
    sum_ref,
    sum_up_ref,
    slope_ref,
):
    width = up_ref.shape[1]
    bias_mix, bias_down = vec_ref[0:1], vec_ref[1:2]
    gain_one, shift_one = vec_ref[2:3], vec_ref[3:4]
    gain_two, shift_two = vec_ref[4:5], vec_ref[5:6]

    @pl.when(pl.program_id(0) == 0)
    def _():
        sum_ref[...] = jnp.zeros_like(sum_ref)
        sum_up_ref[...] = jnp.zeros_like(sum_up_ref)

    attended = att_ref[...]
    mixed = plain_product(attended, mix_ref[...]) + bias_mix + tok_ref[...].astype(jnp.float32)
    unit_one, rate_one = normalised(mixed)
    hidden = unit_one * gain_one + shift_one
    hidden_rounded = hidden.astype(jnp.bfloat16)
    hid_ref[...] = hidden_rounded
    down_sum = bias_down + hidden
    for f in range(0, width, FCHUNK):
        up_sum = plain_product(hidden_rounded, up_ref[:, f : f + FCHUNK]) + (
            bias_up_ref[0:1, f : f + FCHUNK]
        )
        active, slope = gelu_terms(up_sum)
        active = active.astype(jnp.bfloat16)
        act_ref[:, f : f + FCHUNK] = active
        slope_ref[:, f : f + FCHUNK] = slope
        down_sum = down_sum + plain_product(active, down_ref[f : f + FCHUNK, :])
    unit_two, rate_two = normalised(down_sum)
    out_ref[...] = (unit_two * gain_two + shift_two).astype(jnp.bfloat16)
    cot = cot_ref[...].astype(jnp.float32)
    back_pre = norm_back(cot * gain_two, unit_two, rate_two)
    pre_rounded = back_pre.astype(jnp.bfloat16)
    pre_ref[...] = pre_rounded
    sum_ref[4] += row_sums(cot * unit_two)
    sum_ref[5] += row_sums(cot)
    sum_ref[1] += row_sums(back_pre)
    back_hidden = back_pre
    for f in range(0, width, FCHUNK):
        back_up = back_product(pre_rounded, down_ref[f : f + FCHUNK, :]) * (
            slope_ref[:, f : f + FCHUNK]
        )
        sum_up_ref[:, f : f + FCHUNK] += row_sums(back_up)
        up_rounded = back_up.astype(jnp.bfloat16)
        upr_ref[:, f : f + FCHUNK] = up_rounded
        back_hidden = back_hidden + back_product(up_rounded, up_ref[:, f : f + FCHUNK])
    sum_ref[2] += row_sums(back_hidden * unit_one)
    sum_ref[3] += row_sums(back_hidden)
    back_mixed = norm_back(back_hidden * gain_one, unit_one, rate_one)
    sum_ref[0] += row_sums(back_mixed)
    mixed_ref[...] = back_mixed
    mixed_rounded = back_mixed.astype(jnp.bfloat16)
    mixr_ref[...] = mixed_rounded
    back = back_product(mixed_rounded, mix_ref[...]).astype(jnp.bfloat16)
    back = jnp.where(live_ref[...] > 0.5, back, jnp.zeros_like(back))
    back_ref[:, : back.shape[1]] = back
    terms = back.astype(jnp.float32) * attended.astype(jnp.float32)
    high = terms.astype(jnp.bfloat16)
    low = (terms - high.astype(jnp.float32)).astype(jnp.bfloat16)
    delta = plain_product(high, spread_ref[...]) + plain_product(low, spread_ref[...])
    delta_ref[...] = delta
    lane = lax.broadcasted_iota(jnp.int32, delta.shape, 1)
    term = lane % TERMS
    whole = jnp.where(term < 3, lse_ref[...], delta)
    first = whole.astype(jnp.bfloat16)
    rest = whole - first.astype(jnp.float32)
    second = rest.astype(jnp.bfloat16)
    third = (rest - second.astype(jnp.float32)).astype(jnp.bfloat16)
    picked = jnp.where(
        (term == 0) | (term == 3),
        first.astype(jnp.float32),
        jnp.where((term == 2), third.astype(jnp.float32), second.astype(jnp.float32)),
    )
    picked = jnp.where(lane < TERMS * HEADS, picked, 0.0)
    back_ref[:, back.shape[1] :] = picked.astype(jnp.bfloat16)


def chain_call(att, tok, cot, live, lse, mix, up, down, vectors, bias_up):
    rows, width = tok.shape
    wide = up.shape[1]
    head_of = jnp.arange(width, dtype=jnp.int32)[:, None] // HD
    spread = (head_of == jnp.arange(2 * HD, dtype=jnp.int32)[None, :] // TERMS).astype(jnp.bfloat16)

    def tile(columns):
        return pl.BlockSpec((RTILE, columns), lambda i: (i, 0))

    def fixed(*shape):
        return pl.BlockSpec(shape, lambda i: (0,) * len(shape))

    bf16, f32 = jnp.bfloat16, jnp.float32
    return pl.pallas_call(
        chain_kernel,
        grid=(rows // RTILE,),
        in_specs=[
            tile(width),
            tile(width),
            tile(width),
            tile(1),
            tile(2 * HD),
            fixed(*mix.shape),
            fixed(*up.shape),
            fixed(*down.shape),
            fixed(*vectors.shape),
            fixed(*bias_up.shape),
            fixed(*spread.shape),
        ],
        out_specs=[
            tile(width),
            tile(wide),
            tile(wide),
            tile(width),
            tile(width),
            tile(width),
            tile(width),
            tile(width + 2 * HD),
            tile(2 * HD),
            fixed(6, 8, width),
            fixed(8, wide),
        ],
        out_shape=[
            jax.ShapeDtypeStruct((rows, width), bf16),
            jax.ShapeDtypeStruct((rows, wide), bf16),
            jax.ShapeDtypeStruct((rows, wide), bf16),
            jax.ShapeDtypeStruct((rows, width), bf16),
            jax.ShapeDtypeStruct((rows, width), bf16),
            jax.ShapeDtypeStruct((rows, width), bf16),
            jax.ShapeDtypeStruct((rows, width), f32),
            jax.ShapeDtypeStruct((rows, width + 2 * HD), bf16),
            jax.ShapeDtypeStruct((rows, 2 * HD), f32),
            jax.ShapeDtypeStruct((6, 8, width), f32),
            jax.ShapeDtypeStruct((8, wide), f32),
        ],
        scratch_shapes=[pltpu.VMEM((RTILE, wide), f32)],
        cost_estimate=work(44),
        compiler_params=pltpu.CompilerParams(vmem_limit_bytes=VMEM_LIMIT),
    )(att, tok, cot, live, lse, mix, up, down, vectors, bias_up, spread)


def weight_kernel(n_dp, core_ref, act, pre, hid, upr, att, mixr, small, *refs):
    send, keep, tmp = refs[-3:]
    step = pl.program_id(0)
    core = core_ref[0]
    pieces = FF // D
    down_rows = FF // n_dp
    part_rows = D // n_dp

    def put(x, row, rows, begin):
        mine = pl.multiple_of(begin + core * rows, 16)
        other = pl.multiple_of(begin + (1 - core) * rows, 16)
        keep[pl.ds(x, 1), pl.ds(row, rows), :] = tmp[pl.ds(mine, rows), :][None]
        send[pl.ds(x, 1), pl.ds(row, rows), :] = tmp[pl.ds(other, rows), :][None]

    @pl.when(step < pieces)
    def _():
        tmp[...] = outer_sum(act[...], pre[...]).astype(jnp.bfloat16)
        per = D // down_rows
        for b in range(per):
            block = step * per + b
            x = block // 2
            rows = tmp[b * down_rows : (b + 1) * down_rows, :]

            @pl.when(lax.rem(block, 2) == core)
            def _():
                keep[pl.ds(x, 1), 0:down_rows, :] = rows[None]

            @pl.when(lax.rem(block, 2) != core)
            def _():
                send[pl.ds(x, 1), 0:down_rows, :] = rows[None]

    @pl.when((step >= pieces) & (step < 2 * pieces))
    def _():
        tmp[...] = outer_sum(hid[...], upr[...]).astype(jnp.bfloat16)
        row = pl.multiple_of(down_rows + (step - pieces) * part_rows, 16)
        for x in range(n_dp // 2):
            put(x, row, part_rows, 2 * x * part_rows)

    @pl.when(step == 2 * pieces)
    def _():
        tmp[...] = outer_sum(att[...], mixr[...]).astype(jnp.bfloat16)
        row = down_rows + pieces * part_rows
        for x in range(n_dp // 2):
            put(x, row, part_rows, 2 * x * part_rows)
            last = row + part_rows
            rows = keep.shape[1] - last
            keep[x, last:, :] = small[pl.ds(2 * x + core, 1), :, :][0]
            send[x, last:, :] = small[pl.ds(2 * x + 1 - core, 1), :, :][0]


def weight_call(n_dp, core, act, pre, hid, upr, att, mixr, small, *needs):
    rows = act.shape[0]
    pieces = FF // D
    out_rows = FF // n_dp + (pieces + 1) * (D // n_dp) + small.shape[1]

    def fixed(*shape):
        return pl.BlockSpec(shape, lambda i, c: (0,) * len(shape))

    def stepped(first):
        return pl.BlockSpec((rows, D), lambda i, c: (0, jnp.clip(i - first, 0, pieces - 1)))

    shape = (n_dp // 2, out_rows, D)
    return pl.pallas_call(
        functools.partial(weight_kernel, n_dp),
        out_shape=[jax.ShapeDtypeStruct(shape, jnp.bfloat16)] * 2,
        grid_spec=pltpu.PrefetchScalarGridSpec(
            num_scalar_prefetch=1,
            grid=(2 * pieces + 1,),
            in_specs=[
                stepped(0),
                fixed(rows, D),
                fixed(rows, D),
                stepped(pieces),
                fixed(rows, D),
                fixed(rows, D),
                fixed(*small.shape),
            ]
            + [UNREAD] * len(needs),
            out_specs=[fixed(*shape)] * 2,
            scratch_shapes=[pltpu.VMEM((D, D), jnp.bfloat16)],
        ),
        cost_estimate=work(22),
        compiler_params=pltpu.CompilerParams(vmem_limit_bytes=VMEM_LIMIT),
    )(core, act, pre, hid, upr, att, mixr, small, *needs)


def outer_kernel(n_dp, core_ref, tokens, columns, *refs):
    send, keep, tmp = refs[-3:]
    core = core_ref[0]
    rows = tokens.shape[1] // n_dp
    tmp[...] = outer_sum(tokens[...], columns[...]).astype(tmp.dtype)
    for x in range(n_dp // 2):
        mine = pl.multiple_of((2 * x + core) * rows, 16)
        other = pl.multiple_of((2 * x + 1 - core) * rows, 16)
        keep[x] = tmp[pl.ds(mine, rows), :]
        send[x] = tmp[pl.ds(other, rows), :]


def outer_split(n_dp, core, tokens, columns, first, block, *needs):
    rows, depth = tokens.shape
    steps = columns.shape[1] // block - first
    shape = (n_dp // 2, depth // n_dp, block * steps)
    out = pl.BlockSpec(shape[:2] + (block,), lambda i, c: (0, 0, i))
    return pl.pallas_call(
        functools.partial(outer_kernel, n_dp),
        out_shape=[jax.ShapeDtypeStruct(shape, jnp.bfloat16)] * 2,
        grid_spec=pltpu.PrefetchScalarGridSpec(
            num_scalar_prefetch=1,
            grid=(steps,),
            in_specs=[
                pl.BlockSpec((rows, depth), lambda i, c: (0, 0)),
                pl.BlockSpec((rows, block), lambda i, c: (0, first + i)),
            ]
            + [UNREAD] * len(needs),
            out_specs=[out, out],
            scratch_shapes=[pltpu.VMEM((depth, block), jnp.bfloat16)],
        ),
        cost_estimate=work(4),
        compiler_params=plain_params(),
    )(core, tokens, columns, *needs)


def swap(value, axis, bit):
    devices = lax.axis_size(axis)
    return lax.ppermute(value, axis, [(i, i ^ bit) for i in range(devices)])


def dp_gather(shard, dp_rank):
    blocks = shard[None]
    bit = lax.axis_size("dp") // 2
    while bit >= 1:
        got = swap(blocks, "dp", bit)
        high = ((dp_rank // bit) % 2) == 1
        first = jnp.where(high, got, blocks)
        second = jnp.where(high, blocks, got)
        blocks = jnp.stack([first, second], axis=1).reshape((-1,) + shard.shape)
        bit //= 2
    return blocks.reshape((-1,) + shard.shape[1:])


def work(microseconds):
    return pl.CostEstimate(
        flops=int(microseconds * 0.4e9), transcendentals=0, bytes_accessed=1 << 20
    )


def row_tile(rows, limit=1024):
    for size in range(min(rows, limit), 15, -1):
        if rows % size == 0 and size % 16 == 0:
            return size
    return rows


def plain_params():
    return pltpu.CompilerParams(vmem_limit_bytes=VMEM_LIMIT)


def split_add_kernel(which, keep_mine, got_mine, keep_other, got_other, *refs):
    mine, other = refs[-2:]
    mine[...] = (keep_mine[...].astype(jnp.float32) + got_mine[...].astype(jnp.float32)).astype(
        mine.dtype
    )
    other[...] = (keep_other[...].astype(jnp.float32) + got_other[...].astype(jnp.float32)).astype(
        other.dtype
    )


def split_add(keep, got, which, *needs):
    blocks, rows, columns = keep.shape
    tile = row_tile(rows)

    def spec(flip):
        def place(b, i, w):
            bit = 1 - w[0] if flip else w[0]
            return 2 * b + bit, i, 0

        return pl.BlockSpec((1, tile, columns), place)

    out = pl.BlockSpec((1, tile, columns), lambda b, i, w: (b, i, 0))
    shape = jax.ShapeDtypeStruct((blocks // 2, rows, columns), keep.dtype)
    return pl.pallas_call(
        split_add_kernel,
        out_shape=[shape, shape],
        grid_spec=pltpu.PrefetchScalarGridSpec(
            num_scalar_prefetch=1,
            grid=(blocks // 2, rows // tile),
            in_specs=[spec(False), spec(False), spec(True), spec(True)] + [UNREAD] * len(needs),
            out_specs=[out, out],
        ),
        cost_estimate=work(4),
        compiler_params=plain_params(),
    )(which, keep, got, keep, got, *needs)


def add_kernel(left, right, *refs):
    out = refs[-1]
    out[...] = (left[0].astype(jnp.float32) + right[0].astype(jnp.float32)).astype(out.dtype)


def add_blocks(left, right, *needs):
    _, rows, columns = left.shape
    tile = row_tile(rows)
    spec = pl.BlockSpec((1, tile, columns), lambda i: (0, i, 0))
    return pl.pallas_call(
        add_kernel,
        grid=(rows // tile,),
        in_specs=[spec, spec] + [UNREAD] * len(needs),
        out_specs=pl.BlockSpec((tile, columns), lambda i: (i, 0)),
        cost_estimate=work(3),
        out_shape=jax.ShapeDtypeStruct((rows, columns), left.dtype),
        compiler_params=plain_params(),
    )(left, right, *needs)


def pieces_kernel(pieces, *refs):
    out = refs[-1]
    total = pieces[0].astype(jnp.float32)
    for i in range(1, pieces.shape[0]):
        total = total + pieces[i].astype(jnp.float32)
    total = total.astype(out.dtype)
    for i in range(out.shape[0]):
        out[i] = total


def summed_copies(pieces, copies, *needs):
    _, rows, columns = pieces.shape
    return pl.pallas_call(
        pieces_kernel,
        in_specs=[pl.BlockSpec(memory_space=pltpu.VMEM)] + [UNREAD] * len(needs),
        out_specs=pl.BlockSpec(memory_space=pltpu.VMEM),
        out_shape=jax.ShapeDtypeStruct((copies, rows, columns), pieces.dtype),
        cost_estimate=work(2),
        compiler_params=plain_params(),
    )(pieces, *needs)


def two_pieces_kernel(left, right, *refs):
    out = refs[-1]
    at = 0
    for pieces in (left, right):
        total = pieces[0].astype(jnp.float32)
        for i in range(1, pieces.shape[0]):
            total = total + pieces[i].astype(jnp.float32)
        total = total.astype(out.dtype)
        for i in range(out.shape[0]):
            out[i, :, at : at + pieces.shape[2]] = total
        at += pieces.shape[2]


def summed_two(left, right, copies, *needs):
    _, rows, columns = left.shape
    shape = (copies, rows, columns + right.shape[2])
    return pl.pallas_call(
        two_pieces_kernel,
        in_specs=[pl.BlockSpec(memory_space=pltpu.VMEM)] * 2 + [UNREAD] * len(needs),
        out_specs=pl.BlockSpec(memory_space=pltpu.VMEM),
        out_shape=jax.ShapeDtypeStruct(shape, left.dtype),
        cost_estimate=work(2),
        compiler_params=plain_params(),
    )(left, right, *needs)


def gate_kernel(value, *refs):
    refs[-1][...] = value[...]


def gated(value, *needs):
    return pl.pallas_call(
        gate_kernel,
        in_specs=[pl.BlockSpec(memory_space=pltpu.VMEM)] + [UNREAD] * len(needs),
        out_specs=pl.BlockSpec(memory_space=pltpu.VMEM),
        out_shape=jax.ShapeDtypeStruct(value.shape, value.dtype),
        cost_estimate=work(1),
        compiler_params=plain_params(),
    )(value, *needs)


def cluster_ids(group_order, own_start, span):
    padded = jnp.pad(group_order, ((0, 0), (HALO, HALO)), constant_values=-(1 << 24))
    wanted = lax.dynamic_slice_in_dim(padded, own_start, span, 1) - (own_start - HALO)
    tile_of = wanted >> 7
    lane_of_token = wanted & (CL - 1)
    cluster = (jnp.arange(span, dtype=jnp.int32) >> 7) + 1
    tile_hot = jnp.where(
        tile_of[:, :, None] == jnp.arange(span // CL, dtype=jnp.int32), cluster[None, :, None], 0
    ).astype(jnp.bfloat16)
    lane_hot = (lane_of_token[:, :, None] == jnp.arange(CL, dtype=jnp.int32)).astype(jnp.bfloat16)
    table = jnp.einsum("hpt,hpl->htl", tile_hot, lane_hot, preferred_element_type=jnp.float32)
    return table.reshape(HEADS, span) - 1.0


def on_device(
    tokens,
    input_weight,
    output_weight,
    up_weight,
    down_weight,
    output_bias,
    up_bias,
    down_bias,
    first_gain,
    first_shift,
    second_gain,
    second_shift,
    document_runs,
    document_trim,
    cluster_order,
    cotangent,
):
    bf16, f32 = jnp.bfloat16, jnp.float32
    n_dp = lax.axis_size("dp")
    n_seq = lax.axis_size("seq")
    dp_rank = lax.axis_index("dp")
    seq_rank = lax.axis_index("seq")
    inputs = tokens[0]
    tok_dev = inputs.shape[0]
    tiles = tok_dev // CL
    span = tok_dev + 2 * HALO
    own_start = seq_rank * tok_dev

    token_parts = halo_parts(inputs)
    n_parts = len(token_parts)

    weight_in = lax.all_gather(input_weight, "dp", axis=0, tiled=True)
    weight_up = lax.all_gather(up_weight, "dp", axis=0, tiled=True)
    weight_down = lax.all_gather(down_weight, "dp", axis=0, tiled=True)

    runs = document_runs[0]
    first_cluster = jnp.cumsum(runs) - runs
    own_clusters = seq_rank * tiles + jnp.arange(tiles, dtype=jnp.int32)
    doc_start = jnp.max(
        jnp.where(first_cluster[None, :] <= own_clusters[:, None], first_cluster[None, :], 0), axis=1
    )
    starts = (doc_start - seq_rank * tiles + (MOSTB - 1)).astype(jnp.int32)
    near_left = HALO // CL - tiles
    near = near_left + 2 * tiles * jnp.stack([1 - seq_rank % 2, seq_rank % 2])
    starts = jnp.concatenate([starts, near.astype(jnp.int32)])

    cids = cluster_ids(cluster_order[0], own_start, span)
    positions = own_start - HALO + jnp.arange(span, dtype=jnp.int32)
    live = live_tokens(runs, document_trim[0], positions)
    usable = live[None, :] & (cids >= 0.0)
    key_ids = jnp.where(usable, cids, -1.0).reshape(PAIRS, 2, span)
    query_ids = jnp.where(usable, cids, -2.0).reshape(PAIRS, 2, span)
    own_live = live[HALO : HALO + tok_dev, None].astype(f32)

    own = plain_product(inputs, weight_in).astype(bf16)
    groups = HEADS // PACK
    group_lanes = PACK * HD
    kv_weight = (
        weight_in[:, D:]
        .reshape(D, 2, PAIRS, 2 * HD)
        .transpose(0, 2, 1, 3)
        .reshape(D, 2 * D)
    )
    around = project_call(token_parts[:2] + token_parts[3:], weight_in, kv_weight)
    projected = [*around[:2], own, *around[2:]]
    vectors = [
        output_bias,
        down_bias,
        first_gain,
        first_shift,
        second_gain,
        second_shift,
        up_bias,
    ]
    mix_rows = output_weight.shape[0]
    packed = jnp.concatenate(vectors)
    pad_rows = -(-packed.shape[0] // (16 * D)) * 16
    packed = jnp.pad(packed, (0, pad_rows * D - packed.shape[0])).reshape(pad_rows, D)
    mix_shard = gated(jnp.concatenate([output_weight, packed], 0), own)
    mix_all = dp_gather(mix_shard, dp_rank)
    mix_all = mix_all.reshape(n_dp, mix_rows + pad_rows, D)
    weight_mix = mix_all[:, :mix_rows].reshape(D, D)
    small_all = mix_all[:, mix_rows:].reshape(n_dp, -1).astype(f32)
    vec = small_all[:, : 6 * mix_rows].reshape(n_dp, 6, mix_rows).transpose(1, 0, 2).reshape(6, D)
    vec = jnp.pad(vec, ((0, 2), (0, 0)))
    up_part = up_bias.shape[0]
    bias_up = small_all[:, 6 * mix_rows : 6 * mix_rows + up_part].reshape(1, FF)
    bias_up = jnp.pad(bias_up, ((0, 7), (0, 0)))
    heights = [part.shape[0] for part in token_parts]

    groups = HEADS // PACK
    group_lanes = PACK * HD
    group_key_ids = key_ids.reshape(groups, PACK, span)
    group_query_ids = query_ids.reshape(groups, PACK, span)
    group_scratch = pltpu.VMEM((span, group_lanes), bf16)

    def group_parts(third, first):
        return [lane_block(rows, third * groups + first, PACK) for rows in heights]

    steps = tiles // TILES_AT_ONCE
    step_rows = TILES_AT_ONCE * CL

    def of_group(rows, first):
        return pl.BlockSpec((rows, group_lanes), lambda g, t, starts: (0, first + g))

    def ids_of_group():
        return pl.BlockSpec((1, PACK, span), lambda g, t, starts: (g, 0, 0))

    step_block = pl.BlockSpec((step_rows, group_lanes), lambda g, t, starts: (t, g))
    whole_lanes = pl.BlockSpec((tok_dev, 2 * HD), lambda g, t, starts: (0, 0))
    attended, lse, rate, probs = strip_call(
        functools.partial(attend_kernel, tiles, n_parts),
        52,
        (groups, steps),
        [step_block]
        + [of_group(rows, groups) for rows in heights]
        + [of_group(rows, 2 * groups) for rows in heights]
        + [ids_of_group(), ids_of_group()],
        [
            step_block,
            whole_lanes,
            whole_lanes,
            pl.BlockSpec(
                (1, TILES_AT_ONCE, PACK * CL, WINDOW), lambda g, t, starts: (g, t, 0, 0)
            ),
        ],
        [
            jax.ShapeDtypeStruct((tok_dev, D), bf16),
            jax.ShapeDtypeStruct((tok_dev, 2 * HD), f32),
            jax.ShapeDtypeStruct((tok_dev, 2 * HD), f32),
            jax.ShapeDtypeStruct((groups, tiles, PACK * CL, WINDOW), bf16),
        ],
        [group_scratch, group_scratch]
        + [pltpu.VMEM((PACK * CL, WINDOW), f32)] * TILES_AT_ONCE
        + [pltpu.VMEM((PACK * CL, CL), f32)] * TILES_AT_ONCE,
        (starts, own, *projected, *projected, group_query_ids, group_key_ids),
    )

    (
        result,
        active,
        up_rounded,
        hidden_rounded,
        pre_rounded,
        mixed_rounded,
        back_mixed,
        back_own,
        delta,
        sums,
        sums_up,
    ) = chain_call(
        attended,
        inputs,
        cotangent[0],
        own_live,
        lse,
        weight_mix,
        weight_up,
        weight_down,
        vec,
        bias_up,
    )
    back_parts = halo_parts(back_own)

    small = jnp.concatenate(
        [
            jnp.sum(sums, axis=1).reshape(6, n_dp, mix_rows).transpose(1, 0, 2).reshape(n_dp, -1),
            jnp.sum(sums_up, axis=0).reshape(n_dp, -1),
        ],
        axis=1,
    ).astype(bf16)
    unit = 8 * n_seq
    fixed_rows = FF // n_dp + (FF // D + 1) * (D // n_dp)
    small_rows = -(-(fixed_rows + -(-small.shape[1] // D)) // unit) * unit - fixed_rows
    small = jnp.pad(small, ((0, 0), (0, small_rows * D - small.shape[1])))
    small = small.reshape(n_dp, small_rows, D)
    core = (dp_rank % 2).astype(jnp.int32)
    def query_strip(first, *needs):
        buffer = needs[:1] if first > 0 else ()

        def parts(third):
            return [
                pl.BlockSpec(
                    (rows, group_lanes), lambda t, starts: (0, third * groups + first)
                )
                for rows in heights
            ]

        block = pl.BlockSpec((step_rows, group_lanes), lambda t, starts: (t, first))
        lanes = pl.BlockSpec((step_rows, 2 * HD), lambda t, starts: (t, 0))
        in_specs = (
            parts(1)
            + parts(2)
            + [
                block,
                pl.BlockSpec(
                    (1, TILES_AT_ONCE, PACK * CL, WINDOW), lambda t, starts: (first, t, 0, 0)
                ),
                lanes,
                lanes,
            ]
            + [UNREAD] * len(needs)
        )
        return strip_call(
            functools.partial(query_kernel, tiles, n_parts, first * PACK),
            16,
            (steps,),
            in_specs,
            block,
            jax.ShapeDtypeStruct((tok_dev, D), bf16),
            [group_scratch, group_scratch],
            (starts, *projected, *projected, back_own, probs, rate, delta, *needs),
            {len(in_specs) + 1 - len(needs): 0} if buffer else None,
        )

    pair_scratch = pltpu.VMEM((span, 4 * HD), bf16)

    def key_strip(pair, pairs, *needs):
        buffer = needs[:1] if pair > 0 else ()

        def parts(third):
            return [lane_block(rows, third * PAIRS + pair) for rows in heights]

        in_specs = (
            [lane_block(tok_dev, PAIRS + pair), lane_block(tok_dev, 2 * PAIRS + pair)]
            + parts(0)
            + parts(0)
            + [fixed_lanes(rows, PAIRS) for rows in heights]
            + [row_block(span, pair), row_block(span, pair)]
            + [UNREAD] * len(needs)
        )
        return strip_call(
            functools.partial(key_kernel, tiles, n_parts, pair),
            13 * pairs,
            (pairs,),
            in_specs,
            lane_block(tok_dev, pair, 4),
            jax.ShapeDtypeStruct((tok_dev, 2 * D), bf16),
            [pair_scratch, pair_scratch],
            (
                starts,
                own,
                own,
                *projected,
                *back_parts,
                *back_parts,
                query_ids,
                key_ids,
                *needs,
            ),
            {len(in_specs) + 1 - len(needs): 0} if buffer else None,
        )

    def scatter(share):
        rows, columns = share.shape
        return lax.all_to_all(
            share.reshape(n_seq, rows // n_seq, columns), "seq", split_axis=0, concat_axis=0
        )

    def everyone(copies):
        got = lax.all_to_all(copies, "seq", split_axis=0, concat_axis=0)
        return got.reshape(-1, copies.shape[-1])

    def first_split(keep, got, *needs):
        bit = 2
        while True:
            which = ((dp_rank // bit) % 2).astype(jnp.int32).reshape(1)
            mine, other = split_add(keep, got, which, *needs)
            got = swap(other, "dp", bit)
            if mine.shape[0] == 1:
                return mine, got
            keep, bit, needs = mine, bit * 2, ()

    def core_split(grad):
        rows, columns = grad.shape
        blocks = grad.astype(bf16).reshape(n_dp // 2, 2, rows // n_dp, columns)
        return (
            lax.dynamic_index_in_dim(blocks, 1 - core, 1, keepdims=False),
            lax.dynamic_index_in_dim(blocks, core, 1, keepdims=False),
        )

    send, keep = weight_call(
        n_dp,
        core.reshape(1),
        active,
        pre_rounded,
        hidden_rounded,
        up_rounded,
        attended,
        mixed_rounded,
        small,
    )
    core_got = swap(send, "dp", 1)
    back_q = query_strip(0, send)
    mine, x_got = first_split(keep, core_got, back_q)
    back_q = query_strip(1, back_q, mine)
    back_q = query_strip(2, back_q)
    back_kv = key_strip(0, 1, back_q)
    share = add_blocks(mine, x_got, back_kv)
    pieces = scatter(share)
    back_kv = key_strip(1, 2, back_kv, share)
    cut = PAIRS // 2 * 4 * HD
    early_cols = jnp.concatenate([back_q, back_kv[:, :cut]], axis=1)
    early_send, early_keep = core_split(outer_sum(inputs, early_cols))
    early_core = swap(early_send, "dp", 1)
    back_kv = key_strip(3, 1, back_kv, early_send)
    early_mine, early_got = first_split(early_keep, early_core, back_kv)
    back_kv = key_strip(4, 1, back_kv, early_mine)
    copies = summed_copies(pieces, 1, back_kv)
    back_kv = key_strip(5, 1, back_kv, copies)
    early_share = add_blocks(early_mine, early_got, back_kv)
    all_sums = lax.all_gather(copies[0], "seq", axis=0, tiled=True)
    late_send, late_keep = outer_split(
        n_dp, core.reshape(1), inputs, back_kv, 1, cut, early_share
    )
    late_mine, late_got = first_split(late_keep, swap(late_send, "dp", 1))
    late_share = add_blocks(late_mine, late_got)
    early_pieces, late_pieces = scatter(early_share), scatter(late_share)
    in_all = everyone(summed_two(early_pieces, late_pieces, n_seq, all_sums))

    input_grad = (
        back_mixed + back_product(back_q, weight_in[:, :D]) + back_product(back_kv, kv_weight)
    )
    kv_all = in_all[:, D:].reshape(-1, PAIRS, 2, 2 * HD).transpose(0, 2, 1, 3)
    grad_in_total = jnp.concatenate([in_all[:, :D], kv_all.reshape(-1, 2 * D)], axis=1).astype(f32)
    down_rows = FF // n_dp
    part_rows = D // n_dp
    grad_down = all_sums[:down_rows].astype(f32)
    grad_up = (
        all_sums[down_rows : down_rows + (FF // D) * part_rows]
        .reshape(FF // D, part_rows, D)
        .transpose(1, 0, 2)
        .reshape(part_rows, FF)
        .astype(f32)
    )
    at = down_rows + (FF // D) * part_rows
    grad_mix = all_sums[at : at + part_rows].astype(f32)
    flat = all_sums[at + part_rows :].reshape(-1).astype(f32)
    vectors_out = [flat[i * part_rows : (i + 1) * part_rows] for i in range(6)]
    bias_up_out = flat[6 * part_rows : 6 * part_rows + down_rows]
    return (
        result[None],
        input_grad[None],
        grad_in_total,
        grad_mix,
        grad_up,
        grad_down,
        vectors_out[0],
        bias_up_out,
        vectors_out[1],
        *vectors_out[2:],
    )


def solution(mesh):
    placed = (
        P("dp", "seq", None),
        P("dp", None),
        P("dp", None),
        P("dp", None),
        P("dp", None),
        P("dp"),
        P("dp"),
        P("dp"),
        P("dp"),
        P("dp"),
        P("dp"),
        P("dp"),
        P("dp", None),
        P("dp", None),
        P("dp", None, None),
        P("dp", "seq", None),
    )
    return jax.shard_map(
        on_device,
        mesh=mesh,
        in_specs=placed,
        out_specs=(
            P("dp", "seq", None),
            P("dp", "seq", None),
            P("dp", None),
            P("dp", None),
            P("dp", None),
            P("dp", None),
            P("dp"),
            P("dp"),
            P("dp"),
            P("dp"),
            P("dp"),
            P("dp"),
            P("dp"),
        ),
        check_vma=False,
    )
```
